32 devices in a mesh: section: 4 (over x, core), expert: 8 (over z, y).
Axes of the slice: x: 2, y: 2, z: 4, core: 2. Of those that a mesh axis runs over, the one named last changes fastest.
Arguments:
- ahead_rows: bfloat16 [4, 384, 7168], P('section', None, 'expert'), may hold values from -6 to 6
- behind_rows: bfloat16 [4, 384, 7168], P('section', None, 'expert'), may hold values from -6 to 6
- behind_grad: bfloat16 [4, 384, 7168], P('section', None, 'expert'), may hold values from -6 to 6
- route_scores: float32 [4, 2, 384], P('section'), may hold values from 0.1 to 1
- route_counts: int32 [4, 2], P('section'), may hold values from 96 to 384, as said below
- gate_up: bfloat16 [4, 8, 2, 1024, 1792], P('section', 'expert'), may hold values from -0.0625 to 0.0625
- down_proj: bfloat16 [4, 8, 1024, 1792], P('section', 'expert'), may hold values from -0.125 to 0.125
Outputs:
- ahead_sent: bfloat16 [4, 384, 7168], P('section', None, 'expert')
- behind_sent: bfloat16 [4, 384, 7168], P('section', None, 'expert')
The draws below stay inside these ranges and needn't reach their ends.
Inputs may be any that keep to these rules, and one draw needn't show every extreme that they name: `route_counts`: live slots of each section's expert per micro-batch; in each micro-batch some section has all 384 slots live.
All inputs are finite; a program needn't handle non-finite values.
Results may differ from the reference program's by a relative error of at most 0.02.
Values may be sent and summed in bfloat16 or wider, within the bound.
No kernel may reach another device: no remote copies, remote signals or barrier semaphores. Data moves between devices by JAX's collectives and lax.ppermute only.
A program may use at most 64 MiB of HBM per device.

```python
import math
import jax
import jax.numpy as jnp
from jax import lax

D = 7168
FF = 2048
CAP = 384
DBLOCKS = 4
FGROUPS = 2
UNITS = 1024
QWIDTH = 1792
N_SECTION = 4
N_EXPERT = 8


def draw_route_counts(key, part):
    first_key, second_key = jax.random.split(jax.random.fold_in(key, 11))
    base = jax.random.randint(first_key, (N_SECTION, 2), CAP // 4, CAP + 1)
    chosen = jax.random.randint(second_key, (2,), 0, N_SECTION)
    sections = jnp.arange(N_SECTION, dtype=jnp.int32)[:, None]
    return jnp.where(sections == chosen[None, :], CAP, base).astype(jnp.int32)


def block_levels(stream_key, dims, pieces, least, top_value):
    def one(position, shards_of):
        steps = jax.random.uniform(jax.random.fold_in(jax.random.fold_in(stream_key, 6), position), (shards_of,), jnp.float32, least / len(pieces), top_value / len(pieces))
        return jnp.repeat(jnp.exp(steps), dims[position] // shards_of).reshape((-1,) + (1,) * (len(dims) - position - 1))

    factor_of = one(*pieces[0])
    for cut in pieces[1:]:
        factor_of = factor_of * one(*cut)
    return factor_of


def scatter_about(own_key, dims, scale, bound, cuts=(), kind=jnp.bfloat16):
    array = jax.random.normal(own_key, dims, jnp.float32) * scale
    if len(cuts) > 0:
        array = block_levels(own_key, dims, cuts, -0.22, 0.18) * array
    return jnp.clip(array, min=-bound, max=bound).astype(kind)


def setup_inputs(seed: int = 0) -> dict:
    splits = jax.random.split(jax.random.key(seed), 8)
    ahead_rows = scatter_about(splits[0], (N_SECTION, CAP, D), 1.0, 6.0, ((0, 4), (2, 8)))
    behind_rows = scatter_about(splits[1], (N_SECTION, CAP, D), 1.0, 6.0, ((0, 4), (2, 8)))
    behind_grad = scatter_about(splits[2], (N_SECTION, CAP, D), 1.0, 6.0, ((0, 4), (2, 8)))
    route_scores = jnp.clip(jnp.exp(math.log(1.0) - 2.3025851 * jax.random.uniform(splits[3], (N_SECTION, 2, CAP), jnp.float32) ** block_levels(splits[3], (N_SECTION, 2, CAP), ((0, 4),), -0.2, 0.2)), 0.1, 1.0)
    route_counts = draw_route_counts(jax.random.fold_in(splits[7], 71), 0)
    gate_up = scatter_about(splits[5], (N_SECTION, N_EXPERT, 2, UNITS, QWIDTH), D ** -0.5, 0.0625, ((0, 4), (1, 8)))
    down_proj = scatter_about(splits[6], (N_SECTION, N_EXPERT, UNITS, QWIDTH), FF ** -0.5, 0.125, ((0, 4), (1, 8)))
    return {"ahead_rows": ahead_rows, "behind_rows": behind_rows, "behind_grad": behind_grad, "route_scores": route_scores, "route_counts": route_counts, "gate_up": gate_up, "down_proj": down_proj}


def silu_float(value):
    return value * jax.nn.sigmoid(value)


def expand_inner(tiles):
    blocks = tiles.astype(jnp.float32).reshape(DBLOCKS, FGROUPS, 2, UNITS, QWIDTH)
    return jnp.transpose(blocks, (2, 1, 3, 0, 4)).reshape(2, FF, D)


def expand_outer(tiles):
    blocks = tiles.astype(jnp.float32).reshape(DBLOCKS, FGROUPS, UNITS, QWIDTH)
    return jnp.transpose(blocks, (1, 2, 0, 3)).reshape(FF, D)


def section_pass(operands):
    ahead, behind, grad_in, scores, counts, gate_tiles, down_tiles = operands
    slots = jnp.arange(CAP, dtype=jnp.int32)
    scale_ahead = scores[0] * (slots < counts[0]).astype(jnp.float32)
    scale_behind = scores[1] * (slots < counts[1]).astype(jnp.float32)
    gate_wide = expand_inner(gate_tiles)
    down_wide = expand_outer(down_tiles)
    scaled_grad = (grad_in.astype(jnp.float32) * scale_behind[:, None]).astype(jnp.bfloat16)
    pre_ahead = jnp.einsum("cd,kfd->ckf", ahead.astype(jnp.float32), gate_wide)
    pre_behind = jnp.einsum("cd,kfd->ckf", behind.astype(jnp.float32), gate_wide)
    expanded = jnp.einsum("cd,fd->cf", scaled_grad.astype(jnp.float32), down_wide)
    hidden = (silu_float(pre_ahead[:, 0]) * pre_ahead[:, 1]).astype(jnp.bfloat16)
    gate_val = pre_behind[:, 0]
    up_val = pre_behind[:, 1]
    sigmoid_gate = jax.nn.sigmoid(gate_val)
    grad_gate = (expanded * up_val * sigmoid_gate * (1.0 + gate_val * (1.0 - sigmoid_gate))).astype(jnp.bfloat16)
    grad_up = (expanded * gate_val * sigmoid_gate).astype(jnp.bfloat16)
    summed_ahead = jnp.einsum("cf,fd->cd", hidden.astype(jnp.float32), down_wide)
    ahead_out = (summed_ahead * scale_ahead[:, None]).astype(jnp.bfloat16)
    stacked = jnp.stack([grad_gate, grad_up], axis=1).astype(jnp.float32)
    behind_out = jnp.einsum("ckf,kfd->cd", stacked, gate_wide).astype(jnp.bfloat16)
    return ahead_out, behind_out


def reference(ahead_rows, behind_rows, behind_grad, route_scores, route_counts, gate_up, down_proj):
    ahead_out, behind_out = lax.map(section_pass, (ahead_rows, behind_rows, behind_grad, route_scores, route_counts, gate_up, down_proj))
    blank = jnp.zeros_like(ahead_out[:1])
    ahead_sent = jnp.concatenate([blank, ahead_out[:-1]], axis=0)
    behind_sent = jnp.concatenate([behind_out[1:], blank], axis=0)
    return (ahead_sent, behind_sent)
```

```python
import jax
import jax.numpy as jnp
from jax import lax
from jax.sharding import PartitionSpec as P

DBLOCKS = 4
BF16 = jnp.bfloat16
F32 = jnp.float32


def shift(shard, axis, by):
    devices = lax.axis_size(axis)
    pairs = [(i, i + by) for i in range(devices) if 0 <= i + by < devices]
    return lax.ppermute(shard, axis, pairs)


def body(ahead_rows, behind_rows, behind_grad, route_scores, route_counts, gate_up, down_proj):
    groups = lax.axis_size("expert")
    fgroups = groups // DBLOCKS
    low = [[q * fgroups + f for f in range(fgroups)] for q in range(DBLOCKS)]
    high = [[q * fgroups + f for q in range(DBLOCKS)] for f in range(fgroups)]
    height = ahead_rows.shape[1]
    weights_in = gate_up[0, 0]
    weights_out = down_proj[0, 0]
    units = weights_in.shape[1]
    part = units // DBLOCKS
    own = lax.axis_index("expert")
    block = own // fgroups

    def wide(rows):
        return lax.all_gather(rows, "expert", axis_index_groups=low, axis=1, tiled=True)

    def reduced(partials):
        flat = partials.reshape(-1, partials.shape[-1])
        total = lax.psum_scatter(
            flat, "expert", axis_index_groups=high, scatter_dimension=0, tiled=True
        )
        return total.astype(F32).reshape(partials.shape[1:])

    def spread(values):
        return lax.all_gather(values, "expert", axis_index_groups=high, axis=0, tiled=False)

    def narrowed(values):
        return lax.psum_scatter(
            values.astype(BF16), "expert", axis_index_groups=low, scatter_dimension=1, tiled=True
        )

    slot_ids = jnp.arange(height, dtype=jnp.int32)
    scale_ahead = route_scores[0, 0] * (slot_ids < route_counts[0, 0]).astype(F32)
    scale_behind = route_scores[0, 1] * (slot_ids < route_counts[0, 1]).astype(F32)
    gates = weights_in.reshape(2, DBLOCKS, part, -1)
    downs = weights_out.reshape(DBLOCKS, part, -1)

    ahead_wide = wide(ahead_rows[0])
    pre_a = jnp.einsum("cd,kqfd->qkcf", ahead_wide, gates, preferred_element_type=F32).astype(BF16)
    sum_a = reduced(pre_a)
    hidden = (sum_a[0] * jax.nn.sigmoid(sum_a[0]) * sum_a[1]).astype(BF16)
    hidden_all = spread(hidden)

    behind_wide = wide(behind_rows[0])
    grad_wide = wide(behind_grad[0])
    pre_b = jnp.einsum("cd,kqfd->qkcf", behind_wide, gates, preferred_element_type=F32).astype(BF16)
    exp_b = jnp.einsum("cd,qfd->qcf", grad_wide, downs, preferred_element_type=F32).astype(BF16)
    sum_b = reduced(jnp.concatenate([pre_b, exp_b[:, None]], axis=1))
    gate, up, expanded = sum_b[0], sum_b[1], sum_b[2] * scale_behind[:, None]
    sig = jax.nn.sigmoid(gate)
    grad_gate = (expanded * up * sig * (1.0 + gate * (1.0 - sig))).astype(BF16)
    grad_up = (expanded * gate * sig).astype(BF16)
    grads_all = spread(jnp.stack([grad_gate, grad_up]))

    out_a = jnp.einsum("qcf,qfd->cd", hidden_all, downs, preferred_element_type=F32)
    ahead_out = (narrowed(out_a).astype(F32) * scale_ahead[:, None]).astype(BF16)
    moved_ahead = shift(ahead_out, "section", 1)
    out_b = jnp.einsum("qkcf,kqfd->cd", grads_all, gates, preferred_element_type=F32)
    behind_out = narrowed(out_b)
    moved_behind = shift(behind_out, "section", -1)
    return (moved_ahead[None], moved_behind[None])


def solution(mesh):
    in_specs = (
        P("section", None, "expert"),
        P("section", None, "expert"),
        P("section", None, "expert"),
        P("section", None, None),
        P("section", None),
        P("section", "expert", None, None, None),
        P("section", "expert", None, None),
    )
    out_specs = (P("section", None, "expert"), P("section", None, "expert"))
    return jax.shard_map(body, mesh=mesh, in_specs=in_specs, out_specs=out_specs, check_vma=False)
```

```python
import functools

import jax
import jax.numpy as jnp
from jax import lax
from jax.experimental import pallas as pl
from jax.experimental.pallas import tpu as pltpu
from jax.sharding import PartitionSpec as P

DBLOCKS = 4
BF16 = jnp.bfloat16
F32 = jnp.float32
VMEM_LIMIT = 40 * 1024 * 1024


def shift(shard, axis, by):
    devices = lax.axis_size(axis)
    pairs = [(i, i + by) for i in range(devices) if 0 <= i + by < devices]
    return lax.ppermute(shard, axis, pairs)


def call(kernel, flops, size, **kwargs):
    return pl.pallas_call(
        kernel,
        compiler_params=pltpu.CompilerParams(vmem_limit_bytes=VMEM_LIMIT),
        cost_estimate=pl.CostEstimate(flops=flops, bytes_accessed=size, transcendentals=0),
        **kwargs,
    )


def join_rows(own_col, width, own, partner, joined):
    at = pl.multiple_of(own_col * width, 128)
    other = pl.multiple_of((1 - own_col) * width, 128)
    joined[:, pl.ds(at, width)] = own[...]
    joined[:, pl.ds(other, width)] = partner[...]


def times_transposed(rows, tile):
    return lax.dot_general(
        rows, tile, (((1,), (1,)), ((), ())), preferred_element_type=F32
    ).astype(BF16)


def ahead_first_kernel(width, which, own, partner, gates, out, joined):
    @pl.when((pl.program_id(0) == 0) & (pl.program_id(1) == 0))
    def _():
        join_rows(which[1], width, own, partner, joined)

    out[0] = times_transposed(joined[...], gates[0])


def behind_first_kernel(
    width, which, own, partner, grad_own, grad_partner, gates, downs, out, joined, grad_joined
):
    @pl.when((pl.program_id(0) == 0) & (pl.program_id(1) == 0))
    def _():
        join_rows(which[1], width, own, partner, joined)
        join_rows(which[1], width, grad_own, grad_partner, grad_joined)

    @pl.when(pl.program_id(0) < 2)
    def _():
        out[0] = times_transposed(joined[...], gates[0])

    @pl.when(pl.program_id(0) == 2)
    def _():
        out[0] = times_transposed(grad_joined[...], downs[...])


def first_product(which, rows, grads, gate_up, down):
    slots, width = rows[0].shape
    units, features = gate_up.shape[1:]
    half = units // 2
    tile = min(256, half)
    steps = half // tile
    parts = 3 if grads else 2
    row_spec = pl.BlockSpec((slots, width), lambda k, j, w: (0, 0))

    def gate_at(k, j, w):
        return (jnp.minimum(k, 1), w[0] * steps + jnp.where(k < 2, j, steps - 1), 0)

    def down_at(k, j, w):
        return (w[0] * steps + jnp.where(k < 2, 0, j), 0)

    in_specs = [row_spec] * (2 * (parts - 1)) + [pl.BlockSpec((1, tile, features), gate_at)]
    operands = [*rows, *(grads or ()), gate_up]
    if grads:
        in_specs.append(pl.BlockSpec((tile, features), down_at))
        operands.append(down)
    kernel = behind_first_kernel if grads else ahead_first_kernel
    return call(
        functools.partial(kernel, width),
        2 * slots * features * half * parts,
        2 * (features * half * parts + slots * half * parts + slots * features * (parts - 1)),
        out_shape=jax.ShapeDtypeStruct((parts, slots, half), BF16),
        grid_spec=pltpu.PrefetchScalarGridSpec(
            num_scalar_prefetch=1,
            grid=(parts, steps),
            in_specs=in_specs,
            out_specs=pl.BlockSpec((1, slots, tile), lambda k, j, w: (k, 0, j)),
            scratch_shapes=[pltpu.VMEM((slots, features), BF16)] * (parts - 1),
        ),
    )(which, *operands)


def ahead_act_kernel(near, arrived, out):
    gate = near[0].astype(F32) + arrived[0].astype(F32)
    up = near[1].astype(F32) + arrived[1].astype(F32)
    out[0] = (gate * jax.nn.sigmoid(gate) * up).astype(BF16)


def behind_act_kernel(near, arrived, scale, out):
    gate = near[0].astype(F32) + arrived[0].astype(F32)
    up = near[1].astype(F32) + arrived[1].astype(F32)
    expanded = (near[2].astype(F32) + arrived[2].astype(F32)) * scale[...]
    sig = jax.nn.sigmoid(gate)
    out[0] = (expanded * up * sig * (1.0 + gate * (1.0 - sig))).astype(BF16)
    out[1] = (expanded * gate * sig).astype(BF16)


def activation(near, arrived, scale):
    parts, slots, half = near.shape
    kernel = ahead_act_kernel if scale is None else behind_act_kernel
    operands = (near, arrived) if scale is None else (near, arrived, scale)
    return call(
        kernel,
        10 * slots * half,
        2 * (3 * parts - 1) * slots * half,
        out_shape=jax.ShapeDtypeStruct((parts - 1, slots, half), BF16),
    )(*operands)


def second_kernel(kinds, which, own, one, two, three, tile, out, total):
    far = pl.program_id(0)
    kind = pl.program_id(1)
    last = (far == 1) & (kind == kinds - 1)
    at_end = which[2] == 1

    def add(values):
        product = jnp.dot(
            values[0], tile[0], preferred_element_type=F32
        )

        @pl.when((far == 0) & (kind == 0))
        def _():
            total[...] = product

        @pl.when((far == 1) | (kind > 0))
        def _():
            total[...] += product

    near_value = jnp.where(at_end, own[...], one[...])
    far_value = jnp.where(at_end, three[...], two[...])
    add(jnp.where(far == 0, near_value, far_value))

    @pl.when(last)
    def _():
        out[...] = total[...].astype(out.dtype)


def second_product(which, column, values, weights, dtype):
    kinds, slots, half = values[0].shape
    width = weights.shape[2] // 2

    def tile_at(far, kind, w):
        return (kind, jnp.where(far == 0, w[0], 1 - w[0]), jnp.where(column, w[1], 1 - w[1]))

    value_spec = pl.BlockSpec((1, slots, half), lambda far, kind, w: (kind, 0, 0))
    return call(
        functools.partial(second_kernel, kinds),
        4 * slots * half * width * kinds,
        2 * (2 * half * width * kinds + slots * width * 2 + 4 * slots * half * kinds),
        out_shape=jax.ShapeDtypeStruct((slots, width), dtype),
        grid_spec=pltpu.PrefetchScalarGridSpec(
            num_scalar_prefetch=1,
            grid=(2, kinds),
            in_specs=[value_spec] * 4 + [pl.BlockSpec((1, half, width), tile_at)],
            out_specs=pl.BlockSpec((slots, width), lambda far, kind, w: (0, 0)),
            scratch_shapes=[pltpu.VMEM((slots, width), F32)],
        ),
    )(which, *values, weights)


def added(mine, arrived):
    return (mine.astype(F32) + arrived.astype(F32)).astype(BF16)


def piece_body(ahead_rows, behind_rows, behind_grad, route_scores, route_counts, gate_up, down_proj):
    height = ahead_rows.shape[1]
    gates = gate_up[0, 0]
    downs = down_proj[0, 0]
    own = lax.axis_index("expert")
    block, group = own // 2, own % 2
    near = (block >= DBLOCKS // 2).astype(jnp.int32)
    at_end = ((block == 0) | (block == DBLOCKS - 1)).astype(jnp.int32)
    near_which = jnp.stack([near, group, at_end])
    far_which = jnp.stack([1 - near, group, at_end])

    def over_blocks(value, pairs):
        full = [(a * 2 + f, b * 2 + f) for a, b in pairs for f in range(2)]
        return lax.ppermute(value, "expert", full)

    def inward(value):
        return over_blocks(value, [(0, 1), (3, 2)])

    def across(value):
        return over_blocks(value, [(1, 2), (2, 1)])

    def outward(value):
        return over_blocks(value, [(1, 0), (2, 3)])

    def partner(value):
        return lax.ppermute(value, "expert", [(i, i ^ 1) for i in range(2 * DBLOCKS)])

    slot_ids = jnp.arange(height, dtype=jnp.int32)[None]
    live = slot_ids < route_counts[0][:, None]
    scales = jnp.where(live, route_scores[0], 0.0)[:, :, None]

    def piece(kind, start, size):
        def cut(array):
            return array[0, start : start + size]

        scale = scales[kind, start : start + size]
        if kind == 0:
            rows = cut(ahead_rows)
            rows, grads = (rows, partner(rows)), None
        else:
            rows, grads = cut(behind_rows), cut(behind_grad)
            rows, grads = (rows, partner(rows)), (grads, partner(grads))
        far = first_product(far_which, rows, grads, gates, downs)
        arrived = inward(far)
        near = first_product(near_which, rows, grads, gates, downs)
        arrived = across(added(far, arrived))
        arrived = outward(added(near, arrived))
        act = activation(near, arrived, None if kind == 0 else scale)
        one = inward(act)
        two = across(one)
        three = outward(two)
        weights = downs[None] if kind == 0 else gates
        values = (act, one, two, three)
        give = second_product(near_which, 0, values, weights, BF16)
        given = partner(give)
        keep = second_product(near_which, 1, values, weights, F32)
        total = keep + given.astype(F32)
        if kind == 0:
            total = total * scale
        return shift(total.astype(BF16), "section", 1 if kind == 0 else -1)

    size = height // 2
    order = [(0, 0), (1, 0), (1, 1), (0, 1)]
    done = {(kind, i): piece(kind, i * size, size) for kind, i in order}
    return tuple(jnp.concatenate([done[kind, 0], done[kind, 1]])[None] for kind in (0, 1))


def body(ahead_rows, behind_rows, behind_grad, route_scores, route_counts, gate_up, down_proj):
    groups = lax.axis_size("expert")
    fgroups = groups // DBLOCKS
    low = [[q * fgroups + f for f in range(fgroups)] for q in range(DBLOCKS)]
    high = [[q * fgroups + f for q in range(DBLOCKS)] for f in range(fgroups)]
    height = ahead_rows.shape[1]
    weights_in = gate_up[0, 0]
    weights_out = down_proj[0, 0]
    units = weights_in.shape[1]
    part = units // DBLOCKS

    def wide(rows):
        return lax.all_gather(rows, "expert", axis_index_groups=low, axis=1, tiled=True)

    def reduced(partials):
        flat = partials.reshape(-1, partials.shape[-1])
        total = lax.psum_scatter(
            flat, "expert", axis_index_groups=high, scatter_dimension=0, tiled=True
        )
        return total.astype(F32).reshape(partials.shape[1:])

    def spread(values):
        return lax.all_gather(values, "expert", axis_index_groups=high, axis=0, tiled=False)

    def narrowed(values):
        return lax.psum_scatter(
            values.astype(BF16), "expert", axis_index_groups=low, scatter_dimension=1, tiled=True
        )

    slot_ids = jnp.arange(height, dtype=jnp.int32)
    scale_ahead = route_scores[0, 0] * (slot_ids < route_counts[0, 0]).astype(F32)
    scale_behind = route_scores[0, 1] * (slot_ids < route_counts[0, 1]).astype(F32)
    gates = weights_in.reshape(2, DBLOCKS, part, -1)
    downs = weights_out.reshape(DBLOCKS, part, -1)

    ahead_wide = wide(ahead_rows[0])
    pre_a = jnp.einsum("cd,kqfd->qkcf", ahead_wide, gates, preferred_element_type=F32).astype(BF16)
    sum_a = reduced(pre_a)
    hidden = (sum_a[0] * jax.nn.sigmoid(sum_a[0]) * sum_a[1]).astype(BF16)
    hidden_all = spread(hidden)

    behind_wide = wide(behind_rows[0])
    grad_wide = wide(behind_grad[0])
    pre_b = jnp.einsum("cd,kqfd->qkcf", behind_wide, gates, preferred_element_type=F32).astype(BF16)
    exp_b = jnp.einsum("cd,qfd->qcf", grad_wide, downs, preferred_element_type=F32).astype(BF16)
    sum_b = reduced(jnp.concatenate([pre_b, exp_b[:, None]], axis=1))
    gate, up, expanded = sum_b[0], sum_b[1], sum_b[2] * scale_behind[:, None]
    sig = jax.nn.sigmoid(gate)
    grad_gate = (expanded * up * sig * (1.0 + gate * (1.0 - sig))).astype(BF16)
    grad_up = (expanded * gate * sig).astype(BF16)
    grads_all = spread(jnp.stack([grad_gate, grad_up]))

    out_a = jnp.einsum("qcf,qfd->cd", hidden_all, downs, preferred_element_type=F32)
    ahead_out = (narrowed(out_a).astype(F32) * scale_ahead[:, None]).astype(BF16)
    moved_ahead = shift(ahead_out, "section", 1)
    out_b = jnp.einsum("qkcf,kqfd->cd", grads_all, gates, preferred_element_type=F32)
    behind_out = narrowed(out_b)
    moved_behind = shift(behind_out, "section", -1)
    return (moved_ahead[None], moved_behind[None])


def solution(mesh):
    in_specs = (
        P("section", None, "expert"),
        P("section", None, "expert"),
        P("section", None, "expert"),
        P("section", None, None),
        P("section", None),
        P("section", "expert", None, None, None),
        P("section", "expert", None, None),
    )
    out_specs = (P("section", None, "expert"), P("section", None, "expert"))
    chosen = piece_body if mesh.shape["expert"] == 2 * DBLOCKS else body
    return jax.shard_map(chosen, mesh=mesh, in_specs=in_specs, out_specs=out_specs, check_vma=False)
```

```python
import functools

import jax
import jax.numpy as jnp
from jax import lax
from jax.experimental import pallas as pl
from jax.experimental.pallas import tpu as pltpu
from jax.sharding import PartitionSpec as P

DBLOCKS = 4
BF16 = jnp.bfloat16
F32 = jnp.float32
VMEM_LIMIT = 40 * 1024 * 1024

ROW_PIECES = {"F": 1, "B": 1}
UNIT_PIECES = {"F": 2, "B": 2}
ORDER = (
    "YX0", "YG0", "YF0", "B00g.mf", "B01g.mf", "B01g.P1", "B00g.P1", "B00g.mn", "B01g.mn",
    "B01g.a1", "B01g.P2", "B01e.mf", "B00e.mn", "B01e.mn", "B01e.P1", "B00e.mf", "B00e.P1",
    "B00g.a1", "B00g.P2", "B01g.a2", "B01g.P3", "B01e.a1", "B01e.P2", "F00.mf", "F00.P1", "F00.mn",
    "B00g.a2", "B00g.P3", "B00e.a1", "B00e.P2", "B01e.a2", "F01.mf", "F01.P1", "B01e.P3", "F00.a1",
    "F00.P2", "B00e.a2", "B00e.P3", "F01.mn", "B01.act", "B01.Q1", "F01.a1", "F01.P2", "F00.a2",
    "F00.P3", "B00.act", "B00.Q1", "B01.Q2", "F01.a2", "F01.P3", "F00.act", "F00.Q1", "B00.Q2",
    "B01.Q3", "F00.Q2", "F01.act", "F01.Q1", "B00.Q3", "F01.Q2", "F00.Q3", "F01.Q3", "OB00.ms",
    "OB00.Y", "OB00.mk", "OB00.X", "OF00.mk", "OF00.X", "OF00.ms", "OF00.Y", "OB00.add",
    "OF00.add",
)


def shift(shard, axis, by):
    devices = lax.axis_size(axis)
    pairs = [(i, i + by) for i in range(devices) if 0 <= i + by < devices]
    return lax.ppermute(shard, axis, pairs)


ANY = pl.BlockSpec(memory_space=pl.ANY)


def call(kernel, micros, operands, after, out_shape, scalars=(), grid=(), in_specs=None, out_specs=None, scratch=()):
    count, unread = len(scalars) + len(operands), len(after)

    def run(*refs):
        kernel(*refs[:count], *refs[count + unread :])

    if in_specs is None:
        in_specs = [pl.BlockSpec(o.shape, functools.partial(lambda n, *_: (0,) * n, o.ndim)) for o in operands]
    if out_specs is None:
        out_specs = pl.BlockSpec(out_shape.shape, functools.partial(lambda n, *_: (0,) * n, len(out_shape.shape)))
    return pl.pallas_call(
        run,
        compiler_params=pltpu.CompilerParams(vmem_limit_bytes=VMEM_LIMIT),
        cost_estimate=pl.CostEstimate(flops=int(micros * 1.1e9), bytes_accessed=1024, transcendentals=0),
        out_shape=out_shape,
        grid_spec=pltpu.PrefetchScalarGridSpec(
            num_scalar_prefetch=len(scalars),
            grid=grid or (1,),
            in_specs=[*in_specs, *[ANY] * unread],
            out_specs=out_specs,
            scratch_shapes=list(scratch),
        ),
    )(*scalars, *operands, *after)


def first_kernel(width, which, own, partner, tile, out, joined):
    @pl.when((pl.program_id(0) == 0) & (pl.program_id(1) == 0))
    def _():
        at = pl.multiple_of(which[1] * width, 128)
        other = pl.multiple_of((1 - which[1]) * width, 128)
        joined[:, pl.ds(at, width)] = own[...]
        joined[:, pl.ds(other, width)] = partner[...]

    out[0] = lax.dot_general(
        joined[...], tile[0], (((1,), (1,)), ((), ())), preferred_element_type=F32
    ).astype(BF16)


def first_product(which, rows, weights, piece, pieces, after):
    slots, width = rows[0].shape
    kinds, units, features = weights.shape
    half = units // 2
    size = half // pieces
    tile = min(256, size)
    steps = size // tile

    def tile_at(k, j, w):
        return (k, (w[0] * pieces + piece) * steps + j, 0)

    return call(
        functools.partial(first_kernel, width),
        0.5 + 2.1 * kinds / 2 / pieces,
        (*rows, weights),
        after,
        jax.ShapeDtypeStruct((kinds, slots, size), BF16),
        scalars=(which,),
        grid=(kinds, steps),
        in_specs=[pl.BlockSpec((slots, width), lambda k, j, w: (0, 0))] * 2
        + [pl.BlockSpec((1, tile, features), tile_at)],
        out_specs=pl.BlockSpec((1, slots, tile), lambda k, j, w: (k, 0, j)),
        scratch=[pltpu.VMEM((slots, features), BF16)],
    )


def add_kernel(mine, arrived, out):
    out[...] = (mine[...].astype(F32) + arrived[...].astype(F32)).astype(BF16)


def added(mine, arrived, after):
    return call(add_kernel, 0.4, (mine, arrived), after, jax.ShapeDtypeStruct(mine.shape, BF16))


def ahead_act_kernel(near, arrived, out):
    gate = near[0].astype(F32) + arrived[0].astype(F32)
    up = near[1].astype(F32) + arrived[1].astype(F32)
    out[0] = (gate * jax.nn.sigmoid(gate) * up).astype(BF16)


def behind_act_kernel(near, arrived, near_e, arrived_e, scale, out):
    gate = near[0].astype(F32) + arrived[0].astype(F32)
    up = near[1].astype(F32) + arrived[1].astype(F32)
    expanded = (near_e[0].astype(F32) + arrived_e[0].astype(F32)) * scale[...]
    sig = jax.nn.sigmoid(gate)
    out[0] = (expanded * up * sig * (1.0 + gate * (1.0 - sig))).astype(BF16)
    out[1] = (expanded * gate * sig).astype(BF16)


def second_kernel(kinds, pieces, scaled, which, *refs):
    values, refs = refs[: 4 * pieces], refs[4 * pieces :]
    scale, refs = (refs[0], refs[1:]) if scaled else (None, refs)
    tile, out, total = refs
    far, kind = pl.program_id(0), pl.program_id(1)
    at_end = which[2] == 1
    product = None
    for piece in range(pieces):
        own, one, two, three = values[4 * piece : 4 * piece + 4]
        size = own.shape[2]
        near_value = jnp.where(at_end, own[0], one[0])
        far_value = jnp.where(at_end, three[0], two[0])
        value = jnp.where(far == 0, near_value, far_value)
        part = jnp.dot(value, tile[0, piece * size : (piece + 1) * size], preferred_element_type=F32)
        product = part if product is None else product + part
    first = (far == 0) & (kind == 0)
    last = (far == 1) & (kind == kinds - 1)

    @pl.when(first)
    def _():
        total[...] = product

    @pl.when(jnp.logical_not(first) & jnp.logical_not(last))
    def _():
        total[...] += product

    @pl.when(last)
    def _():
        result = total[...] + product
        if scaled:
            result = result * scale[...]
        out[...] = result.astype(BF16)


def second_product(which, partner, values, scale, weights, after):
    kinds, slots = values[0][0].shape[:2]
    half = weights.shape[1] // 2
    width = weights.shape[2] // 2

    def tile_at(far, kind, w):
        return (kind, jnp.where(far == 0, w[0], 1 - w[0]), (1 - w[1]) if partner else w[1])

    flat = [v for four in values for v in four]
    specs = [pl.BlockSpec((1, slots, v.shape[2]), lambda far, kind, w: (kind, 0, 0)) for v in flat]
    if scale is not None:
        flat.append(scale)
        specs.append(pl.BlockSpec((slots, 1), lambda far, kind, w: (0, 0)))
    return call(
        functools.partial(second_kernel, kinds, len(values), scale is not None),
        0.5 + 1.2 * kinds,
        (*flat, weights),
        after,
        jax.ShapeDtypeStruct((slots, width), BF16),
        scalars=(which,),
        grid=(2, kinds),
        in_specs=[*specs, pl.BlockSpec((1, half, width), tile_at)],
        out_specs=pl.BlockSpec((slots, width), lambda far, kind, w: (0, 0)),
        scratch=[pltpu.VMEM((slots, width), F32)],
    )


def piece_body(ahead_rows, behind_rows, behind_grad, route_scores, route_counts, gate_up, down_proj):
    height = ahead_rows.shape[1]
    gates = gate_up[0, 0]
    downs = down_proj[0]
    own = lax.axis_index("expert")
    sections = lax.axis_size("section")
    block, group = own // 2, own % 2
    near = (block >= DBLOCKS // 2).astype(jnp.int32)
    at_end = ((block == 0) | (block == DBLOCKS - 1)).astype(jnp.int32)
    near_which = jnp.stack([near, group, at_end])
    far_which = jnp.stack([1 - near, group, at_end])
    slot_ids = jnp.arange(height, dtype=jnp.int32)[None]
    live = slot_ids < route_counts[0][:, None]
    scales = jnp.where(live, route_scores[0], 0.0)[:, :, None]

    def over_blocks(value, pairs):
        full = [(a * 2 + f, b * 2 + f) for a, b in pairs for f in range(2)]
        return lax.ppermute(value, "expert", full)

    def to_section(value, by, flip):
        devices = 2 * DBLOCKS
        pairs = [
            (s * devices + e, (s + by) * devices + (e ^ flip))
            for s in range(sections)
            if 0 <= s + by < sections
            for e in range(devices)
        ]
        return lax.ppermute(value, ("section", "expert"), pairs)

    hops = {
        "1": [(0, 1), (3, 2)],
        "2": [(1, 2), (2, 1)],
        "3": [(1, 0), (2, 3)],
    }
    inputs = {"F": ahead_rows[0], "g": behind_rows[0], "e": behind_grad[0]}
    got = {}
    recent = []

    def rows_of(kind, i):
        pieces = ROW_PIECES["F" if kind == "F" else "B"]
        size = height // pieces
        return inputs[kind][i * size : (i + 1) * size]

    def scale_of(kind, i):
        size = height // ROW_PIECES[kind]
        return scales["FB".index(kind), i * size : (i + 1) * size]

    def exchanged(name):
        kind = {"YF": "F", "YX": "g", "YG": "e"}[name[:2]]
        rows = rows_of(kind, int(name[2]))
        pairs = [(i, i ^ 1) for i in range(2 * DBLOCKS)]
        got[kind, int(name[2])] = (rows, lax.ppermute(rows, "expert", pairs))

    def step(name):
        if name[0] == "Y":
            return exchanged(name)
        piece, op = name.split(".")
        if op in ("Y", "X"):
            source = got[piece + (".ms" if op == "Y" else ".mk")]
            got[name] = to_section(source, 1 if piece[1] == "F" else -1, op == "Y")
            return
        if op[0] in "PQ":
            before = {"P1": "mf", "P2": "a1", "P3": "a2", "Q1": "act", "Q2": "Q1", "Q3": "Q2"}[op]
            got[name] = over_blocks(got[piece + "." + before], hops[op[1]])
            return
        kind = piece[0]
        if op in ("mf", "mn"):
            rows = got[piece[3] if kind == "B" else "F", int(piece[1])]
            weights = downs if piece[3:] == "e" else gates
            which = far_which if op == "mf" else near_which
            made = first_product(which, rows, weights, int(piece[2]), UNIT_PIECES[kind], recent)
        elif op == "a1":
            made = added(got[piece + ".mf"], got[piece + ".P1"], recent)
        elif op == "a2":
            made = added(got[piece + ".mn"], got[piece + ".P2"], recent)
        elif op == "act":
            parts = [piece] if kind == "F" else [piece + "g", piece + "e"]
            operands = [got[p + s] for p in parts for s in (".mn", ".P3")]
            if kind == "B":
                operands.append(scale_of(kind, int(piece[1])))
            shape = (1 if kind == "F" else 2, *operands[0].shape[1:])
            kernel = ahead_act_kernel if kind == "F" else behind_act_kernel
            made = call(kernel, 0.6, operands, recent, jax.ShapeDtypeStruct(shape, BF16))
        elif op in ("ms", "mk"):
            kind, i = piece[1], piece[2]
            values = [
                [got[f"{kind}{i}{u}.{s}"] for s in ("act", "Q1", "Q2", "Q3")]
                for u in range(UNIT_PIECES[kind])
            ]
            scale = scale_of(kind, int(i)) if kind == "F" else None
            weights = downs if kind == "F" else gates
            made = second_product(near_which, op == "ms", values, scale, weights, recent)
        got[name] = made
        recent[:] = [made]

    for name in ORDER:
        if not name.endswith(".add"):
            step(name)

    def result(kind):
        shares = [
            (got[f"O{kind}{i}0.Y"].astype(F32) + got[f"O{kind}{i}0.X"].astype(F32)).astype(BF16)
            for i in range(ROW_PIECES[kind])
        ]
        return (shares[0] if len(shares) == 1 else jnp.concatenate(shares))[None]

    return result("F"), result("B")


def body(ahead_rows, behind_rows, behind_grad, route_scores, route_counts, gate_up, down_proj):
    groups = lax.axis_size("expert")
    fgroups = groups // DBLOCKS
    low = [[q * fgroups + f for f in range(fgroups)] for q in range(DBLOCKS)]
    high = [[q * fgroups + f for q in range(DBLOCKS)] for f in range(fgroups)]
    height = ahead_rows.shape[1]
    weights_in = gate_up[0, 0]
    weights_out = down_proj[0, 0]
    units = weights_in.shape[1]
    part = units // DBLOCKS

    def wide(rows):
        return lax.all_gather(rows, "expert", axis_index_groups=low, axis=1, tiled=True)

    def reduced(partials):
        flat = partials.reshape(-1, partials.shape[-1])
        total = lax.psum_scatter(
            flat, "expert", axis_index_groups=high, scatter_dimension=0, tiled=True
        )
        return total.astype(F32).reshape(partials.shape[1:])

    def spread(values):
        return lax.all_gather(values, "expert", axis_index_groups=high, axis=0, tiled=False)

    def narrowed(values):
        return lax.psum_scatter(
            values.astype(BF16), "expert", axis_index_groups=low, scatter_dimension=1, tiled=True
        )

    slot_ids = jnp.arange(height, dtype=jnp.int32)
    scale_ahead = route_scores[0, 0] * (slot_ids < route_counts[0, 0]).astype(F32)
    scale_behind = route_scores[0, 1] * (slot_ids < route_counts[0, 1]).astype(F32)
    gates = weights_in.reshape(2, DBLOCKS, part, -1)
    downs = weights_out.reshape(DBLOCKS, part, -1)

    ahead_wide = wide(ahead_rows[0])
    pre_a = jnp.einsum("cd,kqfd->qkcf", ahead_wide, gates, preferred_element_type=F32).astype(BF16)
    sum_a = reduced(pre_a)
    hidden = (sum_a[0] * jax.nn.sigmoid(sum_a[0]) * sum_a[1]).astype(BF16)
    hidden_all = spread(hidden)

    behind_wide = wide(behind_rows[0])
    grad_wide = wide(behind_grad[0])
    pre_b = jnp.einsum("cd,kqfd->qkcf", behind_wide, gates, preferred_element_type=F32).astype(BF16)
    exp_b = jnp.einsum("cd,qfd->qcf", grad_wide, downs, preferred_element_type=F32).astype(BF16)
    sum_b = reduced(jnp.concatenate([pre_b, exp_b[:, None]], axis=1))
    gate, up, expanded = sum_b[0], sum_b[1], sum_b[2] * scale_behind[:, None]
    sig = jax.nn.sigmoid(gate)
    grad_gate = (expanded * up * sig * (1.0 + gate * (1.0 - sig))).astype(BF16)
    grad_up = (expanded * gate * sig).astype(BF16)
    grads_all = spread(jnp.stack([grad_gate, grad_up]))

    out_a = jnp.einsum("qcf,qfd->cd", hidden_all, downs, preferred_element_type=F32)
    ahead_out = (narrowed(out_a).astype(F32) * scale_ahead[:, None]).astype(BF16)
    moved_ahead = shift(ahead_out, "section", 1)
    out_b = jnp.einsum("qkcf,kqfd->cd", grads_all, gates, preferred_element_type=F32)
    behind_out = narrowed(out_b)
    moved_behind = shift(behind_out, "section", -1)
    return (moved_ahead[None], moved_behind[None])


def solution(mesh):
    in_specs = (
        P("section", None, "expert"),
        P("section", None, "expert"),
        P("section", None, "expert"),
        P("section", None, None),
        P("section", None),
        P("section", "expert", None, None, None),
        P("section", "expert", None, None),
    )
    out_specs = (P("section", None, "expert"), P("section", None, "expert"))
    chosen = piece_body if mesh.shape["expert"] == 2 * DBLOCKS else body
    return jax.shard_map(chosen, mesh=mesh, in_specs=in_specs, out_specs=out_specs, check_vma=False)
```

```python
import functools

import jax
import jax.numpy as jnp
from jax import lax
from jax.experimental import pallas as pl
from jax.experimental.pallas import tpu as pltpu
from jax.sharding import PartitionSpec as P

DBLOCKS = 4
BF16 = jnp.bfloat16
F32 = jnp.float32
MIB = 1024 * 1024


def shift(shard, axis, by):
    devices = lax.axis_size(axis)
    pairs = [(i, i + by) for i in range(devices) if 0 <= i + by < devices]
    return lax.ppermute(shard, axis, pairs)


def whole(array):
    return pl.BlockSpec(array.shape, functools.partial(lambda n, *_: (0,) * n, array.ndim))


def call(kernel, micros, operands, after, out_shape, scalars=(), grid=(1,), in_specs=None, out_specs=None, scratch=(), limit=16):
    count, unread = len(scalars) + len(operands), len(after)

    def run(*refs):
        kernel(*refs[:count], *refs[count + unread :])

    if in_specs is None:
        in_specs = [whole(o) for o in operands]
    if out_specs is None:
        out_specs = jax.tree.map(whole, out_shape)
    return pl.pallas_call(
        run,
        compiler_params=pltpu.CompilerParams(vmem_limit_bytes=limit * MIB),
        cost_estimate=pl.CostEstimate(flops=int(micros * 4e9), bytes_accessed=1024, transcendentals=0),
        out_shape=out_shape,
        grid_spec=pltpu.PrefetchScalarGridSpec(
            num_scalar_prefetch=len(scalars),
            grid=grid,
            in_specs=[*in_specs, *[pl.BlockSpec(memory_space=pl.ANY)] * unread],
            out_specs=out_specs,
            scratch_shapes=list(scratch),
        ),
    )(*scalars, *operands, *after)


def first_kernel(width, where, own, partner, tile, out, joined):
    @pl.when((pl.program_id(0) == 0) & (pl.program_id(1) == 0))
    def _():
        at = pl.multiple_of(where[1] * width, 128)
        other = pl.multiple_of((1 - where[1]) * width, 128)
        joined[:, pl.ds(at, width)] = own[...]
        joined[:, pl.ds(other, width)] = partner[...]

    out[0, 0] = lax.dot_general(
        joined[...], tile[0], (((1,), (1,)), ((), ())), preferred_element_type=F32
    ).astype(BF16)


def first_product(where, rows, weights, quarters, after):
    slots, width = rows[0].shape
    kinds, units, features = weights.shape
    size = units // DBLOCKS

    def tile_at(q, k, w):
        return (k, quarters(q, w), 0)

    count = DBLOCKS if quarters is natural else 1
    return call(
        functools.partial(first_kernel, width),
        0.5 + 0.65 * kinds * count,
        (*rows, weights),
        after,
        jax.ShapeDtypeStruct((count, kinds, slots, size), BF16),
        scalars=(where,),
        grid=(count, kinds),
        in_specs=[pl.BlockSpec((slots, width), lambda q, k, w: (0, 0))] * 2
        + [pl.BlockSpec((1, size, features), tile_at)],
        out_specs=pl.BlockSpec((1, 1, slots, size), lambda q, k, w: (q, k, 0, 0)),
        scratch=[pltpu.VMEM((slots, features), BF16)],
    )


def natural(q, w):
    return q


def other_block(mask):
    return lambda q, w: w[0] ^ mask


def total_of(refs, kind):
    total = refs[0][0, kind].astype(F32)
    for ref in refs[1:]:
        total += ref[0, kind].astype(F32)
    return total


def ahead_act_kernel(*refs):
    terms, out = refs[:-1], refs[-1]
    gate, up = total_of(terms, 0), total_of(terms, 1)
    out[...] = (gate * jax.nn.sigmoid(gate) * up).astype(BF16)


def behind_act_kernel(sums, scale, *refs):
    terms, out = refs[:-1], refs[-1]
    gate, up = sums[0].astype(F32), sums[1].astype(F32)
    expanded = total_of(terms, 0) * scale[...]
    sig = jax.nn.sigmoid(gate)
    out[0] = (expanded * up * sig * (1.0 + gate * (1.0 - sig))).astype(BF16)
    out[1] = (expanded * gate * sig).astype(BF16)


def second_dot(joined, tile):
    kinds, units, width = tile.shape
    return jnp.dot(joined[...], tile[...].reshape(kinds * units, width), preferred_element_type=F32)


def store_share(share, give, keep):
    @pl.when(pl.program_id(0) == 0)
    def _():
        give[...] = share.astype(BF16)

    @pl.when(pl.program_id(0) == 1)
    def _():
        keep[...] = share.astype(BF16)


def ahead_second_kernel(where, *refs):
    values, (scale, tile, give, keep, joined) = refs[:DBLOCKS], refs[DBLOCKS:]

    @pl.when(pl.program_id(0) == 0)
    def _():
        for mask, value in enumerate(values):
            size = value.shape[1]
            at = pl.multiple_of((where[0] ^ mask) * size, 128)
            joined[:, pl.ds(at, size)] = value[...]

    store_share(second_dot(joined, tile) * scale[...], give, keep)


def behind_second_kernel(where, values, tile, give, keep, joined):
    @pl.when(pl.program_id(0) == 0)
    def _():
        quarters, kinds, _, size = values.shape
        for kind in range(kinds):
            for q in range(quarters):
                at = (kind * quarters + q) * size
                joined[:, at : at + size] = values[q, kind]

    store_share(second_dot(joined, tile), give, keep)


def second_product(kernel, where, values, weights, after):
    kinds, units, features = weights.shape
    slots = values[0].shape[-2]
    width = features // 2

    def tile_at(own, w):
        return (0, 0, jnp.where(own == 0, 1 - w[1], w[1]))

    share = jax.ShapeDtypeStruct((slots, width), BF16)
    return call(
        kernel,
        1 + 3 * kinds,
        (*values, weights),
        after,
        (share, share),
        scalars=(where,),
        grid=(2,),
        in_specs=[*[whole(v) for v in values], pl.BlockSpec((kinds, units, width), tile_at)],
        scratch=[pltpu.VMEM((slots, kinds * units), BF16)],
        limit=28,
    )


def direct_body(ahead_rows, behind_rows, behind_grad, route_scores, route_counts, gate_up, down_proj):
    height = ahead_rows.shape[1]
    gates = gate_up[0, 0]
    downs = down_proj[0]
    units = gates.shape[1]
    size = units // DBLOCKS
    own = lax.axis_index("expert")
    sections = lax.axis_size("section")
    devices = 2 * DBLOCKS
    where = jnp.stack([own // 2, own % 2])
    high = [[q * 2 + f for q in range(DBLOCKS)] for f in range(2)]
    slot_ids = jnp.arange(height, dtype=jnp.int32)[None]
    live = slot_ids < route_counts[0][:, None]
    scales = jnp.where(live, route_scores[0], 0.0)[:, :, None]

    def swapped(value, mask):
        return lax.ppermute(value, "expert", [(i, i ^ mask) for i in range(devices)])

    def to_section(value, by, flip):
        pairs = [
            (s * devices + e, (s + by) * devices + (e ^ flip))
            for s in range(sections)
            if 0 <= s + by < sections
            for e in range(devices)
        ]
        return lax.ppermute(value, ("section", "expert"), pairs)

    def joined(shares, by):
        give, keep = shares
        arrived = to_section(give, by, 1).astype(F32) + to_section(keep, by, 0).astype(F32)
        return arrived.astype(BF16)[None]

    rows = {"b": behind_rows[0], "a": ahead_rows[0], "g": behind_grad[0]}
    rows = {name: (value, swapped(value, 1)) for name, value in rows.items()}

    pre_b = first_product(where, rows["b"], gates, natural, [])
    sum_b = lax.psum_scatter(
        pre_b.reshape(-1, size), "expert", axis_index_groups=high, scatter_dimension=0, tiled=True
    ).reshape(2, height, size)

    def direct(rows, weights, after):
        terms = []
        for mask in (2, 3, 1, 0):
            term = first_product(where, rows, weights, other_block(mask), after)
            after = [term]
            terms.append(swapped(term, 2 * mask) if mask else term)
        return terms, after

    pre_a, after = direct(rows["a"], gates, [pre_b])
    exp_b, after = direct(rows["g"], downs, after)
    grads = call(
        behind_act_kernel,
        2,
        (sum_b, scales[1], *exp_b),
        after,
        jax.ShapeDtypeStruct((2, height, size), BF16),
    )
    grads_all = lax.all_gather(grads, "expert", axis_index_groups=high, axis=0, tiled=False)
    hidden = call(
        ahead_act_kernel, 2, pre_a, [grads], jax.ShapeDtypeStruct((height, size), BF16)
    )
    hidden_all = [hidden, *[swapped(hidden, 2 * mask) for mask in (1, 2, 3)]]
    shares_a = second_product(ahead_second_kernel, where, [*hidden_all, scales[0]], downs, [])
    shares_b = second_product(behind_second_kernel, where, [grads_all], gates, [shares_a[0]])
    return joined(shares_a, 1), joined(shares_b, -1)


def body(ahead_rows, behind_rows, behind_grad, route_scores, route_counts, gate_up, down_proj):
    groups = lax.axis_size("expert")
    fgroups = groups // DBLOCKS
    low = [[q * fgroups + f for f in range(fgroups)] for q in range(DBLOCKS)]
    high = [[q * fgroups + f for q in range(DBLOCKS)] for f in range(fgroups)]
    height = ahead_rows.shape[1]
    weights_in = gate_up[0, 0]
    weights_out = down_proj[0, 0]
    units = weights_in.shape[1]
    part = units // DBLOCKS

    def wide(rows):
        return lax.all_gather(rows, "expert", axis_index_groups=low, axis=1, tiled=True)

    def reduced(partials):
        flat = partials.reshape(-1, partials.shape[-1])
        total = lax.psum_scatter(
            flat, "expert", axis_index_groups=high, scatter_dimension=0, tiled=True
        )
        return total.astype(F32).reshape(partials.shape[1:])

    def spread(values):
        return lax.all_gather(values, "expert", axis_index_groups=high, axis=0, tiled=False)

    def narrowed(values):
        return lax.psum_scatter(
            values.astype(BF16), "expert", axis_index_groups=low, scatter_dimension=1, tiled=True
        )

    slot_ids = jnp.arange(height, dtype=jnp.int32)
    scale_ahead = route_scores[0, 0] * (slot_ids < route_counts[0, 0]).astype(F32)
    scale_behind = route_scores[0, 1] * (slot_ids < route_counts[0, 1]).astype(F32)
    gates = weights_in.reshape(2, DBLOCKS, part, -1)
    downs = weights_out.reshape(DBLOCKS, part, -1)

    ahead_wide = wide(ahead_rows[0])
    pre_a = jnp.einsum("cd,kqfd->qkcf", ahead_wide, gates, preferred_element_type=F32).astype(BF16)
    sum_a = reduced(pre_a)
    hidden = (sum_a[0] * jax.nn.sigmoid(sum_a[0]) * sum_a[1]).astype(BF16)
    hidden_all = spread(hidden)

    behind_wide = wide(behind_rows[0])
    grad_wide = wide(behind_grad[0])
    pre_b = jnp.einsum("cd,kqfd->qkcf", behind_wide, gates, preferred_element_type=F32).astype(BF16)
    exp_b = jnp.einsum("cd,qfd->qcf", grad_wide, downs, preferred_element_type=F32).astype(BF16)
    sum_b = reduced(jnp.concatenate([pre_b, exp_b[:, None]], axis=1))
    gate, up, expanded = sum_b[0], sum_b[1], sum_b[2] * scale_behind[:, None]
    sig = jax.nn.sigmoid(gate)
    grad_gate = (expanded * up * sig * (1.0 + gate * (1.0 - sig))).astype(BF16)
    grad_up = (expanded * gate * sig).astype(BF16)
    grads_all = spread(jnp.stack([grad_gate, grad_up]))

    out_a = jnp.einsum("qcf,qfd->cd", hidden_all, downs, preferred_element_type=F32)
    ahead_out = (narrowed(out_a).astype(F32) * scale_ahead[:, None]).astype(BF16)
    moved_ahead = shift(ahead_out, "section", 1)
    out_b = jnp.einsum("qkcf,kqfd->cd", grads_all, gates, preferred_element_type=F32)
    behind_out = narrowed(out_b)
    moved_behind = shift(behind_out, "section", -1)
    return (moved_ahead[None], moved_behind[None])


def solution(mesh):
    in_specs = (
        P("section", None, "expert"),
        P("section", None, "expert"),
        P("section", None, "expert"),
        P("section", None, None),
        P("section", None),
        P("section", "expert", None, None, None),
        P("section", "expert", None, None),
    )
    out_specs = (P("section", None, "expert"), P("section", None, "expert"))
    chosen = direct_body if mesh.shape["expert"] == 2 * DBLOCKS else body
    return jax.shard_map(chosen, mesh=mesh, in_specs=in_specs, out_specs=out_specs, check_vma=False)
```

```python
import functools

import jax
import jax.numpy as jnp
from jax import lax
from jax.experimental import pallas as pl
from jax.experimental.pallas import tpu as pltpu
from jax.sharding import PartitionSpec as P

DBLOCKS = 4
BF16 = jnp.bfloat16
F32 = jnp.float32
MIB = 1024 * 1024
PIECES = 2


def shift(shard, axis, by):
    devices = lax.axis_size(axis)
    pairs = [(i, i + by) for i in range(devices) if 0 <= i + by < devices]
    return lax.ppermute(shard, axis, pairs)


def whole(array):
    return pl.BlockSpec(array.shape, functools.partial(lambda n, *_: (0,) * n, array.ndim))


def call(kernel, micros, operands, after, out_shape, scalars=(), grid=(1,), in_specs=None, out_specs=None, scratch=(), limit=24):
    count, unread = len(scalars) + len(operands), len(after)

    def run(*refs):
        kernel(*refs[:count], *refs[count + unread :])

    if in_specs is None:
        in_specs = [whole(o) for o in operands]
    if out_specs is None:
        out_specs = jax.tree.map(whole, out_shape)
    return pl.pallas_call(
        run,
        compiler_params=pltpu.CompilerParams(vmem_limit_bytes=limit * MIB),
        cost_estimate=pl.CostEstimate(flops=int(micros * 4e9), bytes_accessed=1024, transcendentals=0),
        out_shape=out_shape,
        grid_spec=pltpu.PrefetchScalarGridSpec(
            num_scalar_prefetch=len(scalars),
            grid=grid,
            in_specs=[*in_specs, *[pl.BlockSpec(memory_space=pl.ANY)] * unread],
            out_specs=out_specs,
            scratch_shapes=list(scratch),
        ),
    )(*scalars, *operands, *after)


def first_kernel(width, where, own, partner, tile, out, joined):
    @pl.when((pl.program_id(0) == 0) & (pl.program_id(1) == 0))
    def _():
        at = pl.multiple_of(where[1] * width, 128)
        other = pl.multiple_of((1 - where[1]) * width, 128)
        joined[:, pl.ds(at, width)] = own[...]
        joined[:, pl.ds(other, width)] = partner[...]

    out[0] = lax.dot_general(
        joined[...], tile[0], (((1,), (1,)), ((), ())), preferred_element_type=F32
    ).astype(BF16)


def behind_first_kernel(width, where, own, partner, grad, grad_partner, tile, down, out, joined, joined_grad):
    at = pl.multiple_of(where[1] * width, 128)
    other = pl.multiple_of((1 - where[1]) * width, 128)

    @pl.when((pl.program_id(0) == 0) & (pl.program_id(1) == 0))
    def _():
        joined[:, pl.ds(at, width)] = own[...]
        joined[:, pl.ds(other, width)] = partner[...]
        joined_grad[:, pl.ds(at, width)] = grad[...]
        joined_grad[:, pl.ds(other, width)] = grad_partner[...]

    @pl.when(pl.program_id(0) < 2)
    def _():
        out[0] = lax.dot_general(
            joined[...], tile[0], (((1,), (1,)), ((), ())), preferred_element_type=F32
        ).astype(BF16)

    @pl.when(pl.program_id(0) == 2)
    def _():
        out[0] = lax.dot_general(
            joined_grad[...], down[...], (((1,), (1,)), ((), ())), preferred_element_type=F32
        ).astype(BF16)


def first_product(where, far, rows, gates, downs, after):
    slots, width = rows[0].shape
    units, features = gates.shape[1:]
    half = units // 2
    tile = min(256, half)
    steps = half // tile
    parts = 1 + len(rows) // 2

    def side(w):
        return (1 - w[0]) * steps if far else w[0] * steps

    def gate_at(k, j, w):
        return (jnp.minimum(k, 1), side(w) + jnp.where(k < 2, j, steps - 1), 0)

    def down_at(k, j, w):
        return (side(w) + jnp.where(k < 2, 0, j), 0)

    in_specs = [whole(r) for r in rows] + [pl.BlockSpec((1, tile, features), gate_at)]
    operands = [*rows, gates]
    if parts == 3:
        in_specs.append(pl.BlockSpec((tile, features), down_at))
        operands.append(downs)
    return call(
        functools.partial(behind_first_kernel if parts == 3 else first_kernel, width),
        1.3 * parts,
        operands,
        after,
        jax.ShapeDtypeStruct((parts, slots, half), BF16),
        scalars=(where,),
        grid=(parts, steps),
        in_specs=in_specs,
        out_specs=pl.BlockSpec((1, slots, tile), lambda k, j, w: (k, 0, j)),
        scratch=[pltpu.VMEM((slots, features), BF16)] * (parts - 1),
    )


def sum_kernel(mine, arrived, out):
    out[...] = (mine[...].astype(F32) + arrived[...].astype(F32)).astype(BF16)


def end_or_sum_kernel(where, at_end, mine, arrived, out):
    @pl.when(where[2] == 1)
    def _():
        parts = at_end.shape[0]
        out[:parts] = at_end[...]
        if parts < out.shape[0]:
            out[parts:] = jnp.zeros_like(out[parts:])

    @pl.when(where[2] == 0)
    def _():
        out[...] = (mine[...].astype(F32) + arrived[...].astype(F32)).astype(BF16)


def end_or_pass_kernel(where, at_end, passed, out):
    @pl.when(where[2] == 1)
    def _():
        out[...] = at_end[...]

    @pl.when(where[2] == 0)
    def _():
        out[...] = passed[...]


def ahead_act_kernel(near, arrived, out):
    gate = near[0].astype(F32) + arrived[0].astype(F32)
    up = near[1].astype(F32) + arrived[1].astype(F32)
    out[0] = (gate * jax.nn.sigmoid(gate) * up).astype(BF16)


def behind_act_kernel(near, arrived, scale, out):
    gate = near[0].astype(F32) + arrived[0].astype(F32)
    up = near[1].astype(F32) + arrived[1].astype(F32)
    expanded = (near[2].astype(F32) + arrived[2].astype(F32)) * scale[...]
    sig = jax.nn.sigmoid(gate)
    out[0] = (expanded * up * sig * (1.0 + gate * (1.0 - sig))).astype(BF16)
    out[1] = (expanded * gate * sig).astype(BF16)


def second_kernel(scaled, where, act, one, two, three, *refs):
    scale, refs = (refs[0], refs[1:]) if scaled else (None, refs)
    tile, give, keep, joined = refs
    kinds, _, half = act.shape

    def place(near, far):
        for kind in range(kinds):
            at = pl.multiple_of((2 * kind + where[0]) * half, 128)
            other = pl.multiple_of((2 * kind + 1 - where[0]) * half, 128)
            joined[:, pl.ds(at, half)] = near[kind]
            joined[:, pl.ds(other, half)] = far[kind]

    first = pl.program_id(0) == 0

    @pl.when(first & (where[2] == 1))
    def _():
        place(act, three)

    @pl.when(first & (where[2] == 0))
    def _():
        place(one, two)

    kinds, units, width = tile.shape
    share = jnp.dot(
        joined[...], tile[...].reshape(kinds * units, width), preferred_element_type=F32
    )
    if scaled:
        share = share * scale[...]

    @pl.when(first)
    def _():
        give[...] = share.astype(BF16)

    @pl.when(pl.program_id(0) == 1)
    def _():
        keep[...] = share.astype(BF16)


def second_product(where, values, scale, weights, after):
    kinds, units, features = weights.shape
    slots = values[0].shape[1]
    width = features // 2

    def tile_at(own, w):
        return (0, 0, jnp.where(own == 0, 1 - w[1], w[1]))

    operands = [*values] + ([] if scale is None else [scale])
    share = jax.ShapeDtypeStruct((slots, width), BF16)
    return call(
        functools.partial(second_kernel, scale is not None),
        1 + 2 * kinds,
        (*operands, weights),
        after,
        (share, share),
        scalars=(where,),
        grid=(2,),
        in_specs=[*[whole(v) for v in operands], pl.BlockSpec((kinds, units, width), tile_at)],
        scratch=[pltpu.VMEM((slots, kinds * units), BF16)],
    )


def chain_body(ahead_rows, behind_rows, behind_grad, route_scores, route_counts, gate_up, down_proj):
    height = ahead_rows.shape[1]
    gates = gate_up[0, 0]
    downs = down_proj[0]
    own = lax.axis_index("expert")
    sections = lax.axis_size("section")
    devices = 2 * DBLOCKS
    block, group = own // 2, own % 2
    near_half = (block >= DBLOCKS // 2).astype(jnp.int32)
    at_end = ((block == 0) | (block == DBLOCKS - 1)).astype(jnp.int32)
    where = jnp.stack([near_half, group, at_end])
    slot_ids = jnp.arange(height, dtype=jnp.int32)[None]
    live = slot_ids < route_counts[0][:, None]
    scales = jnp.where(live, route_scores[0], 0.0)[:, :, None]

    def between(value, to):
        pairs = [(q * 2 + f, to[q] * 2 + f) for q in range(DBLOCKS) for f in range(2)]
        return lax.ppermute(value, "expert", pairs)

    def outer(value):
        return between(value, (1, 0, 3, 2))

    def middle(value):
        return between(value, (0, 2, 1, 3))

    def swapped(value):
        return lax.ppermute(value, "expert", [(i, i ^ 1) for i in range(devices)])

    def to_section(value, by, flip):
        pairs = [
            (s * devices + e, (s + by) * devices + (e ^ flip))
            for s in range(sections)
            if 0 <= s + by < sections
            for e in range(devices)
        ]
        return lax.ppermute(value, ("section", "expert"), pairs)

    recent = []

    def kernel_call(kernel, micros, operands, shape, scalars=()):
        made = call(kernel, micros, operands, list(recent), jax.ShapeDtypeStruct(shape, BF16), scalars)
        recent[:] = [made]
        return made

    class Chain:
        def __init__(self, inputs, scale, by):
            self.inputs, self.scale, self.by = inputs, scale, by
            self.parts = 1 + len(inputs)
            self.rows, self.far, self.near, self.act = {}, {}, {}, {}
            self.out, self.mid, self.one, self.shares = {}, {}, {}, {}

        def cut(self, array, c):
            size = height // PIECES
            return array[c * size : (c + 1) * size]

        def fetch(self, c):
            rows = [self.cut(array, c) for array in self.inputs]
            self.rows[c] = [r for row in rows for r in (row, swapped(row))]

        def product(self, c, far):
            made = first_product(where, far, self.rows[c], gates, downs[0], list(recent))
            recent[:] = [made]
            (self.far if far else self.near)[c] = made

        def outer_sum(self, c):
            if c == 0:
                value = self.far[0]
            else:
                first = self.far[c] if c < PIECES else self.act[0]
                mine = self.near[c - 1]
                value = kernel_call(
                    end_or_sum_kernel, 0.4, (first, mine, self.mid[c - 1]), mine.shape, (where,)
                )
            self.out[c] = outer(value)

        def middle_sum(self, c):
            mine = self.far[c]
            self.mid[c] = middle(kernel_call(sum_kernel, 0.4, (mine, self.out[c]), mine.shape))

        def activate(self, c):
            near = self.near[c]
            operands = [near, self.out[c + 1]]
            kernel = ahead_act_kernel
            if self.parts == 3:
                operands.append(self.cut(self.scale, c))
                kernel = behind_act_kernel
            shape = (self.parts - 1, *near.shape[1:])
            self.act[c] = kernel_call(kernel, 0.8, operands, shape)

        def outer_pass(self, c):
            value = self.mid[PIECES + c - 1]
            if c < PIECES:
                value = kernel_call(
                    end_or_pass_kernel, 0.3, (self.act[c], value), value.shape, (where,)
                )
            self.out[PIECES + c] = outer(value)

        def middle_pass(self, c):
            value = self.out[PIECES + c]
            if c == 0:
                value = value[: self.parts - 1]
            self.one[c] = value
            self.mid[PIECES + c] = middle(value)

        def finish(self, c):
            values = [
                self.act[c],
                self.one[c],
                self.mid[PIECES + c],
                self.out[PIECES + c + 1],
            ]
            scaled = self.parts == 2
            scale = self.cut(self.scale, c) if scaled else None
            weights = downs if scaled else gates
            give, keep = second_product(where, values, scale, weights, list(recent))
            recent[:] = [give]
            arrived = to_section(give, self.by, 1), to_section(keep, self.by, 0)
            self.shares[c] = arrived

        def result(self):
            sums = [
                (a.astype(F32) + b.astype(F32)).astype(BF16)
                for a, b in (self.shares[c] for c in range(PIECES))
            ]
            return jnp.concatenate(sums)[None]

    ahead = Chain([ahead_rows[0]], scales[0], 1)
    behind = Chain([behind_rows[0], behind_grad[0]], scales[1], -1)
    both = (ahead, behind)
    for c in range(PIECES):
        for chain in both:
            chain.fetch(c)
    for chain in both:
        chain.product(0, True)
        chain.outer_sum(0)
        chain.product(0, False)
    for c in range(PIECES):
        for chain in both:
            chain.middle_sum(c)
            if c > 0:
                chain.activate(c - 1)
            if c + 1 < PIECES:
                chain.product(c + 1, True)
        for chain in both:
            chain.outer_sum(c + 1)
            if c + 1 < PIECES:
                chain.product(c + 1, False)
    for c in range(PIECES):
        for chain in both:
            chain.middle_pass(c)
            if c == 0:
                chain.activate(PIECES - 1)
            else:
                chain.finish(c - 1)
        for chain in both:
            chain.outer_pass(c + 1)
    for chain in both:
        chain.finish(PIECES - 1)
    return ahead.result(), behind.result()


def body(ahead_rows, behind_rows, behind_grad, route_scores, route_counts, gate_up, down_proj):
    groups = lax.axis_size("expert")
    fgroups = groups // DBLOCKS
    low = [[q * fgroups + f for f in range(fgroups)] for q in range(DBLOCKS)]
    high = [[q * fgroups + f for q in range(DBLOCKS)] for f in range(fgroups)]
    height = ahead_rows.shape[1]
    weights_in = gate_up[0, 0]
    weights_out = down_proj[0, 0]
    units = weights_in.shape[1]
    part = units // DBLOCKS

    def wide(rows):
        return lax.all_gather(rows, "expert", axis_index_groups=low, axis=1, tiled=True)

    def reduced(partials):
        flat = partials.reshape(-1, partials.shape[-1])
        total = lax.psum_scatter(
            flat, "expert", axis_index_groups=high, scatter_dimension=0, tiled=True
        )
        return total.astype(F32).reshape(partials.shape[1:])

    def spread(values):
        return lax.all_gather(values, "expert", axis_index_groups=high, axis=0, tiled=False)

    def narrowed(values):
        return lax.psum_scatter(
            values.astype(BF16), "expert", axis_index_groups=low, scatter_dimension=1, tiled=True
        )

    slot_ids = jnp.arange(height, dtype=jnp.int32)
    scale_ahead = route_scores[0, 0] * (slot_ids < route_counts[0, 0]).astype(F32)
    scale_behind = route_scores[0, 1] * (slot_ids < route_counts[0, 1]).astype(F32)
    gates = weights_in.reshape(2, DBLOCKS, part, -1)
    downs = weights_out.reshape(DBLOCKS, part, -1)

    ahead_wide = wide(ahead_rows[0])
    pre_a = jnp.einsum("cd,kqfd->qkcf", ahead_wide, gates, preferred_element_type=F32).astype(BF16)
    sum_a = reduced(pre_a)
    hidden = (sum_a[0] * jax.nn.sigmoid(sum_a[0]) * sum_a[1]).astype(BF16)
    hidden_all = spread(hidden)

    behind_wide = wide(behind_rows[0])
    grad_wide = wide(behind_grad[0])
    pre_b = jnp.einsum("cd,kqfd->qkcf", behind_wide, gates, preferred_element_type=F32).astype(BF16)
    exp_b = jnp.einsum("cd,qfd->qcf", grad_wide, downs, preferred_element_type=F32).astype(BF16)
    sum_b = reduced(jnp.concatenate([pre_b, exp_b[:, None]], axis=1))
    gate, up, expanded = sum_b[0], sum_b[1], sum_b[2] * scale_behind[:, None]
    sig = jax.nn.sigmoid(gate)
    grad_gate = (expanded * up * sig * (1.0 + gate * (1.0 - sig))).astype(BF16)
    grad_up = (expanded * gate * sig).astype(BF16)
    grads_all = spread(jnp.stack([grad_gate, grad_up]))

    out_a = jnp.einsum("qcf,qfd->cd", hidden_all, downs, preferred_element_type=F32)
    ahead_out = (narrowed(out_a).astype(F32) * scale_ahead[:, None]).astype(BF16)
    moved_ahead = shift(ahead_out, "section", 1)
    out_b = jnp.einsum("qkcf,kqfd->cd", grads_all, gates, preferred_element_type=F32)
    behind_out = narrowed(out_b)
    moved_behind = shift(behind_out, "section", -1)
    return (moved_ahead[None], moved_behind[None])


def solution(mesh):
    in_specs = (
        P("section", None, "expert"),
        P("section", None, "expert"),
        P("section", None, "expert"),
        P("section", None, None),
        P("section", None),
        P("section", "expert", None, None, None),
        P("section", "expert", None, None),
    )
    out_specs = (P("section", None, "expert"), P("section", None, "expert"))
    chosen = chain_body if mesh.shape["expert"] == 2 * DBLOCKS else body
    return jax.shard_map(chosen, mesh=mesh, in_specs=in_specs, out_specs=out_specs, check_vma=False)
```

```python
import functools

import jax
import jax.numpy as jnp
from jax import lax
from jax.experimental import pallas as pl
from jax.experimental.pallas import tpu as pltpu
from jax.sharding import PartitionSpec as P

DBLOCKS = 4
BF16 = jnp.bfloat16
F32 = jnp.float32
MIB = 1024 * 1024
PIECES = 2
ROWS, SMALL, ACT, FIRST, AHEAD_OUT, BEHIND_OUT = 20, 1.6, 10, 5.2, 12, 20


def shift(shard, axis, by):
    devices = lax.axis_size(axis)
    pairs = [(i, i + by) for i in range(devices) if 0 <= i + by < devices]
    return lax.ppermute(shard, axis, pairs)


def whole(array):
    return pl.BlockSpec(array.shape, functools.partial(lambda n, *_: (0,) * n, array.ndim))


def call(kernel, micros, operands, after, out_shape, scalars=(), grid=(1,), in_specs=None, out_specs=None, scratch=(), limit=24, name=None):
    count, unread = len(scalars) + len(operands), len(after)

    def run(*refs):
        kernel(*refs[:count], *refs[count + unread :])

    if in_specs is None:
        in_specs = [whole(o) for o in operands]
    if out_specs is None:
        out_specs = jax.tree.map(whole, out_shape)
    return pl.pallas_call(
        run,
        compiler_params=pltpu.CompilerParams(vmem_limit_bytes=limit * MIB),
        cost_estimate=pl.CostEstimate(flops=int(micros * 1e9), bytes_accessed=1024, transcendentals=0),
        out_shape=out_shape,
        name=name,
        grid_spec=pltpu.PrefetchScalarGridSpec(
            num_scalar_prefetch=len(scalars),
            grid=grid,
            in_specs=[*in_specs, *[pl.BlockSpec(memory_space=pl.ANY)] * unread],
            out_specs=out_specs,
            scratch_shapes=list(scratch),
        ),
    )(*scalars, *operands, *after)


def cut_kernel(rows, out):
    out[...] = rows[...]


def cut_first_kernel(value, out):
    out[...] = value[: out.shape[0]]


def first_kernel(width, where, own, partner, tile, out, joined):
    @pl.when((pl.program_id(0) == 0) & (pl.program_id(1) == 0))
    def _():
        at = pl.multiple_of(where[1] * width, 128)
        other = pl.multiple_of((1 - where[1]) * width, 128)
        joined[:, pl.ds(at, width)] = own[...]
        joined[:, pl.ds(other, width)] = partner[...]

    out[0] = lax.dot_general(
        joined[...], tile[0], (((1,), (1,)), ((), ())), preferred_element_type=F32
    ).astype(BF16)


def first_product(name, where, far, rows, weights, after):
    slots, width = rows[0].shape
    parts, units, features = weights.shape
    half = units // 2
    tile = min(256, half)
    steps = half // tile

    def tile_at(k, j, w):
        return (k, ((1 - w[0]) if far else w[0]) * steps + j, 0)

    return call(
        functools.partial(first_kernel, width),
        FIRST * parts,
        (*rows, weights),
        after,
        jax.ShapeDtypeStruct((parts, slots, half), BF16),
        scalars=(where,),
        grid=(parts, steps),
        in_specs=[*[whole(r) for r in rows], pl.BlockSpec((1, tile, features), tile_at)],
        out_specs=pl.BlockSpec((1, slots, tile), lambda k, j, w: (k, 0, j)),
        scratch=[pltpu.VMEM((slots, features), BF16)],
        name=name,
    )


def sum_kernel(mine, arrived, out):
    out[...] = (mine[...].astype(F32) + arrived[...].astype(F32)).astype(BF16)


def end_or_sum_kernel(where, at_end, mine, arrived, out):
    @pl.when(where[2] == 1)
    def _():
        parts = at_end.shape[0]
        out[:parts] = at_end[...]
        if parts < out.shape[0]:
            out[parts:] = jnp.zeros_like(out[parts:])

    @pl.when(where[2] == 0)
    def _():
        out[...] = (mine[...].astype(F32) + arrived[...].astype(F32)).astype(BF16)


def end_or_pass_kernel(where, at_end, passed, out):
    @pl.when(where[2] == 1)
    def _():
        out[...] = at_end[...]

    @pl.when(where[2] == 0)
    def _():
        out[...] = passed[...]


def ahead_act_kernel(near, arrived, out):
    gate = near[0].astype(F32) + arrived[0].astype(F32)
    up = near[1].astype(F32) + arrived[1].astype(F32)
    out[0] = (gate * jax.nn.sigmoid(gate) * up).astype(BF16)


def behind_act_kernel(near, arrived, near_e, arrived_e, scale, out):
    gate = near[0].astype(F32) + arrived[0].astype(F32)
    up = near[1].astype(F32) + arrived[1].astype(F32)
    expanded = (near_e[0].astype(F32) + arrived_e[0].astype(F32)) * scale[...]
    sig = jax.nn.sigmoid(gate)
    out[0] = (expanded * up * sig * (1.0 + gate * (1.0 - sig))).astype(BF16)
    out[1] = (expanded * gate * sig).astype(BF16)


def second_kernel(scaled, where, act, one, two, three, *refs):
    scale, refs = (refs[0], refs[1:]) if scaled else (None, refs)
    tile, give, keep, joined = refs
    kinds, _, half = act.shape

    def place(near, far):
        for kind in range(kinds):
            at = pl.multiple_of((2 * kind + where[0]) * half, 128)
            other = pl.multiple_of((2 * kind + 1 - where[0]) * half, 128)
            joined[:, pl.ds(at, half)] = near[kind]
            joined[:, pl.ds(other, half)] = far[kind]

    first = pl.program_id(0) == 0

    @pl.when(first & (where[2] == 1))
    def _():
        place(act, three)

    @pl.when(first & (where[2] == 0))
    def _():
        place(one, two)

    kinds, units, width = tile.shape
    share = jnp.dot(
        joined[...], tile[...].reshape(kinds * units, width), preferred_element_type=F32
    )
    if scaled:
        share = share * scale[...]

    @pl.when(first)
    def _():
        give[...] = share.astype(BF16)

    @pl.when(pl.program_id(0) == 1)
    def _():
        keep[...] = share.astype(BF16)


def second_product(name, where, values, scale, weights, after):
    kinds, units, features = weights.shape
    slots = values[0].shape[1]
    width = features // 2

    def tile_at(own, w):
        return (0, 0, jnp.where(own == 0, 1 - w[1], w[1]))

    operands = [*values] + ([] if scale is None else [scale])
    share = jax.ShapeDtypeStruct((slots, width), BF16)
    return call(
        functools.partial(second_kernel, scale is not None),
        AHEAD_OUT if kinds == 1 else BEHIND_OUT,
        (*operands, weights),
        after,
        (share, share),
        scalars=(where,),
        grid=(2,),
        in_specs=[*[whole(v) for v in operands], pl.BlockSpec((kinds, units, width), tile_at)],
        scratch=[pltpu.VMEM((slots, kinds * units), BF16)],
        name=name,
    )


def chain_body(ahead_rows, behind_rows, behind_grad, route_scores, route_counts, gate_up, down_proj):
    height = ahead_rows.shape[1]
    gates = gate_up[0, 0]
    downs = down_proj[0]
    own = lax.axis_index("expert")
    sections = lax.axis_size("section")
    devices = 2 * DBLOCKS
    block, group = own // 2, own % 2
    near_half = (block >= DBLOCKS // 2).astype(jnp.int32)
    at_end = ((block == 0) | (block == DBLOCKS - 1)).astype(jnp.int32)
    where = jnp.stack([near_half, group, at_end])
    slot_ids = jnp.arange(height, dtype=jnp.int32)[None]
    live = slot_ids < route_counts[0][:, None]
    scales = jnp.where(live, route_scores[0], 0.0)[:, :, None]

    def between(value, to):
        pairs = [(q * 2 + f, to[q] * 2 + f) for q in range(DBLOCKS) for f in range(2)]
        return lax.ppermute(value, "expert", pairs)

    def outer(value):
        return between(value, (1, 0, 3, 2))

    def middle(value):
        return between(value, (0, 2, 1, 3))

    def swapped(value):
        return lax.ppermute(value, "expert", [(i, i ^ 1) for i in range(devices)])

    def to_section(value, by, flip):
        pairs = [
            (s * devices + e, (s + by) * devices + (e ^ flip))
            for s in range(sections)
            if 0 <= s + by < sections
            for e in range(devices)
        ]
        return lax.ppermute(value, ("section", "expert"), pairs)

    recent = []

    def kernel_call(name, kernel, micros, operands, shape, scalars=()):
        made = call(
            kernel, micros, operands, list(recent), jax.ShapeDtypeStruct(shape, BF16), scalars, name=name
        )
        recent[:] = [made]
        return made

    class Chain:
        def __init__(self, name, rows, weights, spreads):
            self.name = name
            self.rows, self.weights = rows, weights
            self.spreads = spreads
            self.pairs, self.far, self.near, self.act = {}, {}, {}, {}
            self.out, self.mid, self.one, self.back = {}, {}, {}, {}

        def fetch(self, c):
            size, width = height // PIECES, self.rows.shape[1]
            rows = call(
                cut_kernel,
                SMALL if c else ROWS,
                (self.rows,),
                list(recent),
                jax.ShapeDtypeStruct((size, width), BF16),
                in_specs=[pl.BlockSpec((size, width), lambda i: (c, 0))],
                name=f"{self.name}_rows_{c}",
            )
            recent[:] = [rows]
            self.pairs[c] = rows, swapped(rows)

        def product(self, c, far):
            made = first_product(f"{self.name}_{'far' if far else 'near'}_{c}", where, far, self.pairs[c], self.weights, list(recent))
            recent[:] = [made]
            (self.far if far else self.near)[c] = made

        def products(self, c):
            self.product(c, True)
            self.product(c, False)

        def outer_sum(self, c):
            if c == 0:
                value = self.far[0]
            else:
                mine = self.near[c - 1]
                first = self.far[c] if c < PIECES else self.act.get(0)
                if first is None:
                    value = kernel_call(
                        f"{self.name}_outer_{c}", sum_kernel, SMALL, (mine, self.mid[c - 1]), mine.shape
                    )
                else:
                    value = kernel_call(
                        f"{self.name}_outer_{c}",
                        end_or_sum_kernel,
                        SMALL,
                        (first, mine, self.mid[c - 1]),
                        mine.shape,
                        (where,),
                    )
            self.out[c] = outer(value)

        def middle_sum(self, c):
            mine = self.far[c]
            self.mid[c] = middle(
                kernel_call(
                    f"{self.name}_middle_{c}", sum_kernel, SMALL, (mine, self.out[c]), mine.shape
                )
            )

        def middle_pass(self, c):
            value = self.out[PIECES] if c == 0 else self.back[c]
            if value.shape[0] > self.spreads or c > 0:
                shape = (self.spreads, *value.shape[1:])
                value = kernel_call(f"{self.name}_first_{c}", cut_first_kernel, SMALL, (value,), shape)
            self.one[c] = value
            self.mid[PIECES + c] = middle(value)

        def outer_pass(self, c):
            value = self.mid[PIECES + c - 1]
            if c == PIECES:
                value = kernel_call(
                    f"{self.name}_back_{c}", cut_first_kernel, SMALL, (value,), value.shape
                )
            else:
                value = kernel_call(
                    f"{self.name}_back_{c}",
                    end_or_pass_kernel,
                    SMALL,
                    (self.act[c], value),
                    value.shape,
                    (where,),
                )
            self.back[c] = outer(value)

        def activated(self, c):
            return self.act[c], self.one[c], self.mid[PIECES + c], self.back[c + 1]

    ahead = Chain("ahead", ahead_rows[0], gates, 1)
    behind = Chain("behind", behind_rows[0], gates, 2)
    grad = Chain("grad", behind_grad[0], downs, 0)
    sent = {}

    def cut(array, c):
        size = height // PIECES
        return array[c * size : (c + 1) * size]

    def activate_ahead(c):
        near = ahead.near[c]
        operands = (near, ahead.out[c + 1])
        ahead.act[c] = kernel_call(f"ahead_act_{c}", ahead_act_kernel, ACT, operands, (1, *near.shape[1:]))

    def activate_behind(c):
        near = behind.near[c]
        operands = (near, behind.out[c + 1], grad.near[c], grad.out[c + 1], cut(scales[1], c))
        behind.act[c] = kernel_call(f"behind_act_{c}", behind_act_kernel, ACT, operands, near.shape)

    def finish(chain, c):
        forward = chain is ahead
        scale = cut(scales[0], c) if forward else None
        weights = downs if forward else gates
        give, keep = second_product(f"{chain.name}_out_{c}", where, chain.activated(c), scale, weights, list(recent))
        recent[:] = [give]
        by = 1 if forward else -1
        sent[forward, c] = to_section(give, by, 1), to_section(keep, by, 0)

    def result(forward):
        sums = [
            (a.astype(F32) + b.astype(F32)).astype(BF16)
            for a, b in (sent[forward, c] for c in range(PIECES))
        ]
        return jnp.concatenate(sums)[None]

    chains = (behind, grad, ahead)
    last = PIECES - 1
    for chain in chains:
        chain.fetch(0)
    for chain in chains:
        chain.product(0, True)
        chain.outer_sum(0)
        chain.product(0, False)
        if chain is not ahead:
            chain.fetch(1)
    for c in range(PIECES):
        for chain in chains:
            chain.middle_sum(c)
            if chain is grad and c > 0:
                activate_behind(c - 1)
            if chain is ahead and c > 0:
                activate_ahead(c - 1)
            if c == 0 and chain is behind:
                ahead.fetch(1)
            if c < last:
                chain.product(c + 1, True)
        for chain in chains:
            chain.outer_sum(c + 1)
            if c < last:
                chain.product(c + 1, False)
    for c in range(PIECES):
        behind.middle_pass(c)
        if c == 0:
            activate_behind(last)
        else:
            finish(behind, c - 1)
        ahead.middle_pass(c)
        if c == 0:
            activate_ahead(last)
        else:
            finish(ahead, c - 1)
        behind.outer_pass(c + 1)
        ahead.outer_pass(c + 1)
    finish(behind, last)
    finish(ahead, last)
    return result(True), result(False)


def body(ahead_rows, behind_rows, behind_grad, route_scores, route_counts, gate_up, down_proj):
    groups = lax.axis_size("expert")
    fgroups = groups // DBLOCKS
    low = [[q * fgroups + f for f in range(fgroups)] for q in range(DBLOCKS)]
    high = [[q * fgroups + f for q in range(DBLOCKS)] for f in range(fgroups)]
    height = ahead_rows.shape[1]
    weights_in = gate_up[0, 0]
    weights_out = down_proj[0, 0]
    units = weights_in.shape[1]
    part = units // DBLOCKS

    def wide(rows):
        return lax.all_gather(rows, "expert", axis_index_groups=low, axis=1, tiled=True)

    def reduced(partials):
        flat = partials.reshape(-1, partials.shape[-1])
        total = lax.psum_scatter(
            flat, "expert", axis_index_groups=high, scatter_dimension=0, tiled=True
        )
        return total.astype(F32).reshape(partials.shape[1:])

    def spread(values):
        return lax.all_gather(values, "expert", axis_index_groups=high, axis=0, tiled=False)

    def narrowed(values):
        return lax.psum_scatter(
            values.astype(BF16), "expert", axis_index_groups=low, scatter_dimension=1, tiled=True
        )

    slot_ids = jnp.arange(height, dtype=jnp.int32)
    scale_ahead = route_scores[0, 0] * (slot_ids < route_counts[0, 0]).astype(F32)
    scale_behind = route_scores[0, 1] * (slot_ids < route_counts[0, 1]).astype(F32)
    gates = weights_in.reshape(2, DBLOCKS, part, -1)
    downs = weights_out.reshape(DBLOCKS, part, -1)

    ahead_wide = wide(ahead_rows[0])
    pre_a = jnp.einsum("cd,kqfd->qkcf", ahead_wide, gates, preferred_element_type=F32).astype(BF16)
    sum_a = reduced(pre_a)
    hidden = (sum_a[0] * jax.nn.sigmoid(sum_a[0]) * sum_a[1]).astype(BF16)
    hidden_all = spread(hidden)

    behind_wide = wide(behind_rows[0])
    grad_wide = wide(behind_grad[0])
    pre_b = jnp.einsum("cd,kqfd->qkcf", behind_wide, gates, preferred_element_type=F32).astype(BF16)
    exp_b = jnp.einsum("cd,qfd->qcf", grad_wide, downs, preferred_element_type=F32).astype(BF16)
    sum_b = reduced(jnp.concatenate([pre_b, exp_b[:, None]], axis=1))
    gate, up, expanded = sum_b[0], sum_b[1], sum_b[2] * scale_behind[:, None]
    sig = jax.nn.sigmoid(gate)
    grad_gate = (expanded * up * sig * (1.0 + gate * (1.0 - sig))).astype(BF16)
    grad_up = (expanded * gate * sig).astype(BF16)
    grads_all = spread(jnp.stack([grad_gate, grad_up]))

    out_a = jnp.einsum("qcf,qfd->cd", hidden_all, downs, preferred_element_type=F32)
    ahead_out = (narrowed(out_a).astype(F32) * scale_ahead[:, None]).astype(BF16)
    moved_ahead = shift(ahead_out, "section", 1)
    out_b = jnp.einsum("qkcf,kqfd->cd", grads_all, gates, preferred_element_type=F32)
    behind_out = narrowed(out_b)
    moved_behind = shift(behind_out, "section", -1)
    return (moved_ahead[None], moved_behind[None])


def solution(mesh):
    in_specs = (
        P("section", None, "expert"),
        P("section", None, "expert"),
        P("section", None, "expert"),
        P("section", None, None),
        P("section", None),
        P("section", "expert", None, None, None),
        P("section", "expert", None, None),
    )
    out_specs = (P("section", None, "expert"), P("section", None, "expert"))
    chosen = chain_body if mesh.shape["expert"] == 2 * DBLOCKS else body
    return jax.shard_map(chosen, mesh=mesh, in_specs=in_specs, out_specs=out_specs, check_vma=False)
```

```python
import functools

import jax
import jax.numpy as jnp
from jax import lax
from jax.experimental import pallas as pl
from jax.experimental.pallas import tpu as pltpu
from jax.sharding import PartitionSpec as P

DBLOCKS = 4
BF16 = jnp.bfloat16
F32 = jnp.float32
MIB = 1024 * 1024
PIECES = 2
ROWS, SMALL, ACT, FIRST, AHEAD_OUT, BEHIND_OUT = 20, 6, 10, 5.2, 3, 20


def shift(shard, axis, by):
    devices = lax.axis_size(axis)
    pairs = [(i, i + by) for i in range(devices) if 0 <= i + by < devices]
    return lax.ppermute(shard, axis, pairs)


def whole(array):
    return pl.BlockSpec(array.shape, functools.partial(lambda n, *_: (0,) * n, array.ndim))


def call(kernel, micros, operands, after, out_shape, scalars=(), grid=(1,), in_specs=None, out_specs=None, scratch=(), limit=24, name=None):
    count, unread = len(scalars) + len(operands), len(after)

    def run(*refs):
        kernel(*refs[:count], *refs[count + unread :])

    if in_specs is None:
        in_specs = [whole(o) for o in operands]
    if out_specs is None:
        out_specs = jax.tree.map(whole, out_shape)
    return pl.pallas_call(
        run,
        compiler_params=pltpu.CompilerParams(vmem_limit_bytes=limit * MIB),
        cost_estimate=pl.CostEstimate(flops=int(micros * 1e9), bytes_accessed=1024, transcendentals=0),
        out_shape=out_shape,
        name=name,
        grid_spec=pltpu.PrefetchScalarGridSpec(
            num_scalar_prefetch=len(scalars),
            grid=grid,
            in_specs=[*in_specs, *[pl.BlockSpec(memory_space=pl.ANY)] * unread],
            out_specs=out_specs,
            scratch_shapes=list(scratch),
        ),
    )(*scalars, *operands, *after)


def cut_kernel(rows, out):
    out[...] = rows[...]


def touch_kernel(out):
    out[...] = jnp.zeros_like(out)


def cut_first_kernel(value, out):
    out[...] = value[: out.shape[0]]


def first_kernel(width, far, where, own, partner, weights, out, joined, tiles, sems):
    parts, slots, half = out.shape
    tile = tiles.shape[1]
    steps = half // tile
    side = 1 - where[0] if far else where[0]
    copies = []
    for k in range(parts):
        for j in range(steps):
            at = pl.multiple_of((side * steps + j) * tile, tile)
            copy = pltpu.make_async_copy(
                weights.at[k, pl.ds(at, tile)], tiles.at[k * steps + j], sems.at[k * steps + j]
            )
            copy.start()
            copies.append(copy)
    at = pl.multiple_of(where[1] * width, 128)
    other = pl.multiple_of((1 - where[1]) * width, 128)
    joined[:slots, pl.ds(at, width)] = own[...]
    joined[:slots, pl.ds(other, width)] = partner[...]
    for k in range(parts):
        for j in range(steps):
            copies[k * steps + j].wait()
            product = lax.dot_general(
                tiles[k * steps + j],
                joined[...],
                (((1,), (1,)), ((), ())),
                preferred_element_type=F32,
            )
            out[k, :, j * tile : (j + 1) * tile] = product.T[:slots].astype(BF16)


def first_product(name, where, far, rows, weights, after):
    slots, width = rows[0].shape
    parts, units, features = weights.shape
    half = units // 2
    tile = min(256, half)
    steps = half // tile
    return call(
        functools.partial(first_kernel, width, far),
        FIRST * parts,
        (*rows, weights),
        after,
        jax.ShapeDtypeStruct((parts, slots, half), BF16),
        scalars=(where,),
        in_specs=[*[whole(r) for r in rows], pl.BlockSpec(memory_space=pltpu.HBM)],
        scratch=[
            pltpu.VMEM((-(-slots // 128) * 128, features), BF16),
            pltpu.VMEM((parts * steps, tile, features), BF16),
            pltpu.SemaphoreType.DMA((parts * steps,)),
        ],
        name=name,
    )


def sum_kernel(mine, arrived, out):
    out[...] = (mine[...].astype(F32) + arrived[...].astype(F32)).astype(BF16)


def end_or_sum_kernel(where, at_end, mine, arrived, out):
    @pl.when(where[2] == 1)
    def _():
        parts = at_end.shape[0]
        out[:parts] = at_end[...]
        if parts < out.shape[0]:
            out[parts:] = jnp.zeros_like(out[parts:])

    @pl.when(where[2] == 0)
    def _():
        out[...] = (mine[...].astype(F32) + arrived[...].astype(F32)).astype(BF16)


def end_or_pass_kernel(where, at_end, passed, out):
    @pl.when(where[2] == 1)
    def _():
        out[...] = at_end[...]

    @pl.when(where[2] == 0)
    def _():
        out[...] = passed[...]


def ahead_act_kernel(near, arrived, out):
    gate = near[0].astype(F32) + arrived[0].astype(F32)
    up = near[1].astype(F32) + arrived[1].astype(F32)
    out[0] = (gate * jax.nn.sigmoid(gate) * up).astype(BF16)


def behind_act_kernel(near, arrived, near_e, arrived_e, scale, out):
    gate = near[0].astype(F32) + arrived[0].astype(F32)
    up = near[1].astype(F32) + arrived[1].astype(F32)
    expanded = (near_e[0].astype(F32) + arrived_e[0].astype(F32)) * scale[...]
    sig = jax.nn.sigmoid(gate)
    out[0] = (expanded * up * sig * (1.0 + gate * (1.0 - sig))).astype(BF16)
    out[1] = (expanded * gate * sig).astype(BF16)


def second_kernel(scaled, where, act, one, two, three, *refs):
    scale, refs = (refs[0], refs[1:]) if scaled else (None, refs)
    weights, give, keep, joined, tiles, sems = refs
    kinds, _, half = act.shape
    _, _, units, width = tiles.shape
    copies = []
    for own in range(2):
        at = pl.multiple_of((where[1] if own else 1 - where[1]) * width, 128)
        copy = pltpu.make_async_copy(
            weights.at[:, :, pl.ds(at, width)], tiles.at[own], sems.at[own]
        )
        copy.start()
        copies.append(copy)

    def place(near, far):
        for kind in range(kinds):
            at = pl.multiple_of((2 * kind + where[0]) * half, 128)
            other = pl.multiple_of((2 * kind + 1 - where[0]) * half, 128)
            joined[:, pl.ds(at, half)] = near[kind]
            joined[:, pl.ds(other, half)] = far[kind]

    @pl.when(where[2] == 1)
    def _():
        place(act, three)

    @pl.when(where[2] == 0)
    def _():
        place(one, two)

    for own, out in enumerate((give, keep)):
        copies[own].wait()
        share = jnp.dot(
            joined[...], tiles[own].reshape(kinds * units, width), preferred_element_type=F32
        )
        if scaled:
            share = share * scale[...]
        out[...] = share.astype(BF16)


def second_product(name, where, values, scale, weights, after):
    kinds, units, features = weights.shape
    slots = values[0].shape[1]
    width = features // 2
    operands = [*values] + ([] if scale is None else [scale])
    share = jax.ShapeDtypeStruct((slots, width), BF16)
    return call(
        functools.partial(second_kernel, scale is not None),
        AHEAD_OUT if kinds == 1 else BEHIND_OUT,
        (*operands, weights),
        after,
        (share, share),
        scalars=(where,),
        in_specs=[*[whole(v) for v in operands], pl.BlockSpec(memory_space=pltpu.HBM)],
        scratch=[
            pltpu.VMEM((slots, kinds * units), BF16),
            pltpu.VMEM((2, kinds, units, width), BF16),
            pltpu.SemaphoreType.DMA((2,)),
        ],
        name=name,
    )


def chain_body(ahead_rows, behind_rows, behind_grad, route_scores, route_counts, gate_up, down_proj):
    height = ahead_rows.shape[1]
    gates = gate_up[0, 0]
    downs = down_proj[0]
    own = lax.axis_index("expert")
    sections = lax.axis_size("section")
    devices = 2 * DBLOCKS
    block, group = own // 2, own % 2
    near_half = (block >= DBLOCKS // 2).astype(jnp.int32)
    at_end = ((block == 0) | (block == DBLOCKS - 1)).astype(jnp.int32)
    where = jnp.stack([near_half, group, at_end])
    slot_ids = jnp.arange(height, dtype=jnp.int32)[None]
    live = slot_ids < route_counts[0][:, None]
    scales = jnp.where(live, route_scores[0], 0.0)[:, :, None]

    def between(value, to):
        pairs = [(q * 2 + f, to[q] * 2 + f) for q in range(DBLOCKS) for f in range(2)]
        return lax.ppermute(value, "expert", pairs)

    def outer(value):
        return between(value, (1, 0, 3, 2))

    def middle(value):
        return between(value, (0, 2, 1, 3))

    def swapped(value):
        return lax.ppermute(value, "expert", [(i, i ^ 1) for i in range(devices)])

    def to_section(value, by, flip):
        pairs = [
            (s * devices + e, (s + by) * devices + (e ^ flip))
            for s in range(sections)
            if 0 <= s + by < sections
            for e in range(devices)
        ]
        return lax.ppermute(value, ("section", "expert"), pairs)

    recent = []

    def kernel_call(name, kernel, micros, operands, shape, scalars=()):
        made = call(
            kernel, micros, operands, list(recent), jax.ShapeDtypeStruct(shape, BF16), scalars, name=name
        )
        recent[:] = [made]
        return made

    class Chain:
        def __init__(self, name, rows, weights, spreads):
            self.name = name
            self.rows, self.weights = rows, weights
            self.spreads = spreads
            self.pairs, self.far, self.near, self.act = {}, {}, {}, {}
            self.out, self.mid, self.one, self.back = {}, {}, {}, {}

        def fetch(self, c):
            size, width = height // PIECES, self.rows.shape[1]
            rows = call(
                cut_kernel,
                SMALL if c else ROWS,
                (self.rows,),
                list(recent),
                jax.ShapeDtypeStruct((size, width), BF16),
                in_specs=[pl.BlockSpec((size, width), lambda i: (c, 0))],
                name=f"{self.name}_rows_{c}",
            )
            recent[:] = [rows]
            self.pairs[c] = rows, swapped(rows)

        def product(self, c, far):
            made = first_product(f"{self.name}_{'far' if far else 'near'}_{c}", where, far, self.pairs[c], self.weights, list(recent))
            recent[:] = [made]
            (self.far if far else self.near)[c] = made

        def products(self, c):
            self.product(c, True)
            self.product(c, False)

        def outer_sum(self, c):
            if c == 0:
                value = self.far[0]
            else:
                mine = self.near[c - 1]
                first = self.far[c] if c < PIECES else self.act.get(0)
                if first is None:
                    value = kernel_call(
                        f"{self.name}_outer_{c}", sum_kernel, SMALL, (mine, self.mid[c - 1]), mine.shape
                    )
                else:
                    value = kernel_call(
                        f"{self.name}_outer_{c}",
                        end_or_sum_kernel,
                        SMALL,
                        (first, mine, self.mid[c - 1]),
                        mine.shape,
                        (where,),
                    )
            self.out[c] = outer(value)

        def middle_sum(self, c):
            mine = self.far[c]
            self.mid[c] = middle(
                kernel_call(
                    f"{self.name}_middle_{c}", sum_kernel, SMALL, (mine, self.out[c]), mine.shape
                )
            )

        def middle_pass(self, c):
            value = self.out[PIECES] if c == 0 else self.back[c]
            if value.shape[0] > self.spreads or c > 0:
                shape = (self.spreads, *value.shape[1:])
                value = kernel_call(f"{self.name}_first_{c}", cut_first_kernel, SMALL, (value,), shape)
            self.one[c] = value
            self.mid[PIECES + c] = middle(value)

        def outer_pass(self, c):
            value = self.mid[PIECES + c - 1]
            if c == PIECES:
                value = kernel_call(
                    f"{self.name}_back_{c}", cut_first_kernel, SMALL, (value,), value.shape
                )
            else:
                value = kernel_call(
                    f"{self.name}_back_{c}",
                    end_or_pass_kernel,
                    SMALL,
                    (self.act[c], value),
                    value.shape,
                    (where,),
                )
            self.back[c] = outer(value)

        def activated(self, c):
            return self.act[c], self.one[c], self.mid[PIECES + c], self.back[c + 1]

    ahead = Chain("ahead", ahead_rows[0], gates, 1)
    behind = Chain("behind", behind_rows[0], gates, 2)
    grad = Chain("grad", behind_grad[0], downs, 0)
    sent = {}

    def cut(array, c):
        size = height // PIECES
        return array[c * size : (c + 1) * size]

    def activate_ahead(c):
        near = ahead.near[c]
        operands = (near, ahead.out[c + 1])
        ahead.act[c] = kernel_call(f"ahead_act_{c}", ahead_act_kernel, ACT, operands, (1, *near.shape[1:]))

    def activate_behind(c):
        near = behind.near[c]
        operands = (near, behind.out[c + 1], grad.near[c], grad.out[c + 1], cut(scales[1], c))
        behind.act[c] = kernel_call(f"behind_act_{c}", behind_act_kernel, ACT, operands, near.shape)

    def finish(chain, c):
        forward = chain is ahead
        scale = cut(scales[0], c) if forward else None
        weights = downs if forward else gates
        give, keep = second_product(f"{chain.name}_out_{c}", where, chain.activated(c), scale, weights, list(recent))
        recent[:] = [give]
        by = 1 if forward else -1
        sent[forward, c] = to_section(give, by, 1), to_section(keep, by, 0)

    def result(forward):
        sums = [
            (a.astype(F32) + b.astype(F32)).astype(BF16)
            for a, b in (sent[forward, c] for c in range(PIECES))
        ]
        return jnp.concatenate(sums)[None]

    for chain in (behind, grad, ahead):
        chain.fetch(0)
    touched = call(
        touch_kernel, ROWS, (), [*recent, gates, downs], jax.ShapeDtypeStruct((8, 128), F32), name="touch"
    )
    recent[:] = [touched]
    behind.product(0, True)
    behind.outer_sum(0)
    behind.fetch(1)
    grad.product(0, True)
    grad.outer_sum(0)
    behind.product(0, False)
    behind.middle_sum(0)
    grad.fetch(1)
    ahead.product(0, True)
    ahead.outer_sum(0)
    grad.middle_sum(0)
    grad.product(0, False)
    behind.product(1, True)
    behind.outer_sum(1)
    ahead.fetch(1)
    ahead.product(0, False)
    ahead.middle_sum(0)
    grad.product(1, True)
    grad.outer_sum(1)
    behind.product(1, False)
    behind.middle_sum(1)
    ahead.product(1, True)
    ahead.outer_sum(1)
    grad.middle_sum(1)
    activate_behind(0)
    grad.product(1, False)
    behind.outer_sum(2)
    ahead.product(1, False)
    ahead.middle_sum(1)
    activate_ahead(0)
    grad.outer_sum(2)
    behind.middle_pass(0)
    ahead.outer_sum(2)
    activate_behind(1)
    behind.outer_pass(1)
    ahead.middle_pass(0)
    activate_ahead(1)
    ahead.outer_pass(1)
    behind.middle_pass(1)
    finish(behind, 0)
    ahead.middle_pass(1)
    behind.outer_pass(2)
    ahead.outer_pass(2)
    finish(ahead, 0)
    finish(behind, 1)
    finish(ahead, 1)
    return result(True), result(False)


def body(ahead_rows, behind_rows, behind_grad, route_scores, route_counts, gate_up, down_proj):
    groups = lax.axis_size("expert")
    fgroups = groups // DBLOCKS
    low = [[q * fgroups + f for f in range(fgroups)] for q in range(DBLOCKS)]
    high = [[q * fgroups + f for q in range(DBLOCKS)] for f in range(fgroups)]
    height = ahead_rows.shape[1]
    weights_in = gate_up[0, 0]
    weights_out = down_proj[0, 0]
    units = weights_in.shape[1]
    part = units // DBLOCKS

    def wide(rows):
        return lax.all_gather(rows, "expert", axis_index_groups=low, axis=1, tiled=True)

    def reduced(partials):
        flat = partials.reshape(-1, partials.shape[-1])
        total = lax.psum_scatter(
            flat, "expert", axis_index_groups=high, scatter_dimension=0, tiled=True
        )
        return total.astype(F32).reshape(partials.shape[1:])

    def spread(values):
        return lax.all_gather(values, "expert", axis_index_groups=high, axis=0, tiled=False)

    def narrowed(values):
        return lax.psum_scatter(
            values.astype(BF16), "expert", axis_index_groups=low, scatter_dimension=1, tiled=True
        )

    slot_ids = jnp.arange(height, dtype=jnp.int32)
    scale_ahead = route_scores[0, 0] * (slot_ids < route_counts[0, 0]).astype(F32)
    scale_behind = route_scores[0, 1] * (slot_ids < route_counts[0, 1]).astype(F32)
    gates = weights_in.reshape(2, DBLOCKS, part, -1)
    downs = weights_out.reshape(DBLOCKS, part, -1)

    ahead_wide = wide(ahead_rows[0])
    pre_a = jnp.einsum("cd,kqfd->qkcf", ahead_wide, gates, preferred_element_type=F32).astype(BF16)
    sum_a = reduced(pre_a)
    hidden = (sum_a[0] * jax.nn.sigmoid(sum_a[0]) * sum_a[1]).astype(BF16)
    hidden_all = spread(hidden)

    behind_wide = wide(behind_rows[0])
    grad_wide = wide(behind_grad[0])
    pre_b = jnp.einsum("cd,kqfd->qkcf", behind_wide, gates, preferred_element_type=F32).astype(BF16)
    exp_b = jnp.einsum("cd,qfd->qcf", grad_wide, downs, preferred_element_type=F32).astype(BF16)
    sum_b = reduced(jnp.concatenate([pre_b, exp_b[:, None]], axis=1))
    gate, up, expanded = sum_b[0], sum_b[1], sum_b[2] * scale_behind[:, None]
    sig = jax.nn.sigmoid(gate)
    grad_gate = (expanded * up * sig * (1.0 + gate * (1.0 - sig))).astype(BF16)
    grad_up = (expanded * gate * sig).astype(BF16)
    grads_all = spread(jnp.stack([grad_gate, grad_up]))

    out_a = jnp.einsum("qcf,qfd->cd", hidden_all, downs, preferred_element_type=F32)
    ahead_out = (narrowed(out_a).astype(F32) * scale_ahead[:, None]).astype(BF16)
    moved_ahead = shift(ahead_out, "section", 1)
    out_b = jnp.einsum("qkcf,kqfd->cd", grads_all, gates, preferred_element_type=F32)
    behind_out = narrowed(out_b)
    moved_behind = shift(behind_out, "section", -1)
    return (moved_ahead[None], moved_behind[None])


def solution(mesh):
    in_specs = (
        P("section", None, "expert"),
        P("section", None, "expert"),
        P("section", None, "expert"),
        P("section", None, None),
        P("section", None),
        P("section", "expert", None, None, None),
        P("section", "expert", None, None),
    )
    out_specs = (P("section", None, "expert"), P("section", None, "expert"))
    chosen = chain_body if mesh.shape["expert"] == 2 * DBLOCKS else body
    return jax.shard_map(chosen, mesh=mesh, in_specs=in_specs, out_specs=out_specs, check_vma=False)
```

```python
import functools

import jax
import jax.numpy as jnp
from jax import lax
from jax.experimental import pallas as pl
from jax.experimental.pallas import tpu as pltpu
from jax.sharding import PartitionSpec as P

DBLOCKS = 4
BF16 = jnp.bfloat16
F32 = jnp.float32
MIB = 1024 * 1024
PIECES = 2
ROWS, SMALL, ACT, FIRST, AHEAD_OUT, BEHIND_OUT = 20, 6, 10, 5.2, 3, 20


def shift(shard, axis, by):
    devices = lax.axis_size(axis)
    pairs = [(i, i + by) for i in range(devices) if 0 <= i + by < devices]
    return lax.ppermute(shard, axis, pairs)


def whole(array):
    return pl.BlockSpec(array.shape, functools.partial(lambda n, *_: (0,) * n, array.ndim))


def call(kernel, micros, operands, after, out_shape, scalars=(), grid=(1,), in_specs=None, out_specs=None, scratch=(), limit=24, name=None):
    count, unread = len(scalars) + len(operands), len(after)

    def run(*refs):
        kernel(*refs[:count], *refs[count + unread :])

    if in_specs is None:
        in_specs = [whole(o) for o in operands]
    if out_specs is None:
        out_specs = jax.tree.map(whole, out_shape)
    return pl.pallas_call(
        run,
        compiler_params=pltpu.CompilerParams(vmem_limit_bytes=limit * MIB),
        cost_estimate=pl.CostEstimate(flops=int(micros * 1e9), bytes_accessed=1024, transcendentals=0),
        out_shape=out_shape,
        name=name,
        grid_spec=pltpu.PrefetchScalarGridSpec(
            num_scalar_prefetch=len(scalars),
            grid=grid,
            in_specs=[*in_specs, *[pl.BlockSpec(memory_space=pl.ANY)] * unread],
            out_specs=out_specs,
            scratch_shapes=list(scratch),
        ),
    )(*scalars, *operands, *after)


def cut_kernel(rows, out):
    out[...] = rows[...]


def cut_first_kernel(value, out):
    out[...] = value[: out.shape[0]]


def first_kernel(width, where, own, partner, tile, out, joined):
    @pl.when((pl.program_id(0) == 0) & (pl.program_id(1) == 0))
    def _():
        at = pl.multiple_of(where[1] * width, 128)
        other = pl.multiple_of((1 - where[1]) * width, 128)
        joined[:, pl.ds(at, width)] = own[...]
        joined[:, pl.ds(other, width)] = partner[...]

    out[0] = lax.dot_general(
        joined[...], tile[0], (((1,), (1,)), ((), ())), preferred_element_type=F32
    ).astype(BF16)


def first_product(name, where, far, rows, weights, after):
    slots, width = rows[0].shape
    parts, units, features = weights.shape
    half = units // 2
    tile = min(256, half)
    steps = half // tile

    def tile_at(k, j, w):
        return (k, ((1 - w[0]) if far else w[0]) * steps + j, 0)

    return call(
        functools.partial(first_kernel, width),
        FIRST * parts,
        (*rows, weights),
        after,
        jax.ShapeDtypeStruct((parts, slots, half), BF16),
        scalars=(where,),
        grid=(parts, steps),
        in_specs=[*[whole(r) for r in rows], pl.BlockSpec((1, tile, features), tile_at)],
        out_specs=pl.BlockSpec((1, slots, tile), lambda k, j, w: (k, 0, j)),
        scratch=[pltpu.VMEM((slots, features), BF16)],
        name=name,
    )


def sum_kernel(mine, arrived, out):
    out[...] = (mine[...].astype(F32) + arrived[...].astype(F32)).astype(BF16)


def end_or_sum_kernel(where, at_end, mine, arrived, out):
    @pl.when(where[2] == 1)
    def _():
        parts = at_end.shape[0]
        out[:parts] = at_end[...]
        if parts < out.shape[0]:
            out[parts:] = jnp.zeros_like(out[parts:])

    @pl.when(where[2] == 0)
    def _():
        out[...] = (mine[...].astype(F32) + arrived[...].astype(F32)).astype(BF16)


def end_or_pass_kernel(where, at_end, passed, out):
    @pl.when(where[2] == 1)
    def _():
        out[...] = at_end[...]

    @pl.when(where[2] == 0)
    def _():
        out[...] = passed[...]


def ahead_act_kernel(near, arrived, out):
    gate = near[0].astype(F32) + arrived[0].astype(F32)
    up = near[1].astype(F32) + arrived[1].astype(F32)
    out[0] = (gate * jax.nn.sigmoid(gate) * up).astype(BF16)


def behind_act_kernel(near, arrived, near_e, arrived_e, scale, out):
    gate = near[0].astype(F32) + arrived[0].astype(F32)
    up = near[1].astype(F32) + arrived[1].astype(F32)
    expanded = (near_e[0].astype(F32) + arrived_e[0].astype(F32)) * scale[...]
    sig = jax.nn.sigmoid(gate)
    out[0] = (expanded * up * sig * (1.0 + gate * (1.0 - sig))).astype(BF16)
    out[1] = (expanded * gate * sig).astype(BF16)


def shares_kernel(one, two, out):
    out[...] = (one[...].astype(F32) + two[...].astype(F32)).astype(BF16)


def result_kernel(first, one, two, out):
    size = first.shape[0]
    out[:size] = first[...]
    out[size:] = (one[...].astype(F32) + two[...].astype(F32)).astype(BF16)


def second_kernel(scaled, where, act, one, two, three, *refs):
    scale, refs = (refs[0], refs[1:]) if scaled else (None, refs)
    weights, give, keep, joined, tiles, sems = refs
    kinds, _, half = act.shape
    _, _, units, width = tiles.shape
    copies = []
    for own in range(2):
        at = pl.multiple_of((where[1] if own else 1 - where[1]) * width, 128)
        copy = pltpu.make_async_copy(
            weights.at[:, :, pl.ds(at, width)], tiles.at[own], sems.at[own]
        )
        copy.start()
        copies.append(copy)

    def place(near, far):
        for kind in range(kinds):
            at = pl.multiple_of((2 * kind + where[0]) * half, 128)
            other = pl.multiple_of((2 * kind + 1 - where[0]) * half, 128)
            joined[:, pl.ds(at, half)] = near[kind]
            joined[:, pl.ds(other, half)] = far[kind]

    @pl.when(where[2] == 1)
    def _():
        place(act, three)

    @pl.when(where[2] == 0)
    def _():
        place(one, two)

    for own, out in enumerate((give, keep)):
        copies[own].wait()
        share = jnp.dot(
            joined[...], tiles[own].reshape(kinds * units, width), preferred_element_type=F32
        )
        if scaled:
            share = share * scale[...]
        out[...] = share.astype(BF16)


def second_product(name, where, values, scale, weights, after):
    kinds, units, features = weights.shape
    slots = values[0].shape[1]
    width = features // 2
    operands = [*values] + ([] if scale is None else [scale])
    share = jax.ShapeDtypeStruct((slots, width), BF16)
    return call(
        functools.partial(second_kernel, scale is not None),
        AHEAD_OUT if kinds == 1 else BEHIND_OUT,
        (*operands, weights),
        after,
        (share, share),
        scalars=(where,),
        in_specs=[*[whole(v) for v in operands], pl.BlockSpec(memory_space=pltpu.HBM)],
        scratch=[
            pltpu.VMEM((slots, kinds * units), BF16),
            pltpu.VMEM((2, kinds, units, width), BF16),
            pltpu.SemaphoreType.DMA((2,)),
        ],
        name=name,
    )


def chain_body(ahead_rows, behind_rows, behind_grad, route_scores, route_counts, gate_up, down_proj):
    height = ahead_rows.shape[1]
    gates = gate_up[0, 0]
    downs = down_proj[0]
    own = lax.axis_index("expert")
    sections = lax.axis_size("section")
    devices = 2 * DBLOCKS
    block, group = own // 2, own % 2
    near_half = (block >= DBLOCKS // 2).astype(jnp.int32)
    at_end = ((block == 0) | (block == DBLOCKS - 1)).astype(jnp.int32)
    where = jnp.stack([near_half, group, at_end])
    slot_ids = jnp.arange(height, dtype=jnp.int32)[None]
    live = slot_ids < route_counts[0][:, None]
    scales = jnp.where(live, route_scores[0], 0.0)[:, :, None]

    def between(value, to):
        pairs = [(q * 2 + f, to[q] * 2 + f) for q in range(DBLOCKS) for f in range(2)]
        return lax.ppermute(value, "expert", pairs)

    def outer(value):
        return between(value, (1, 0, 3, 2))

    def middle(value):
        return between(value, (0, 2, 1, 3))

    def swapped(value):
        return lax.ppermute(value, "expert", [(i, i ^ 1) for i in range(devices)])

    def to_section(value, by, flip):
        pairs = [
            (s * devices + e, (s + by) * devices + (e ^ flip))
            for s in range(sections)
            if 0 <= s + by < sections
            for e in range(devices)
        ]
        return lax.ppermute(value, ("section", "expert"), pairs)

    recent = []

    def kernel_call(name, kernel, micros, operands, shape, scalars=()):
        made = call(
            kernel, micros, operands, list(recent), jax.ShapeDtypeStruct(shape, BF16), scalars, name=name
        )
        recent[:] = [made]
        return made

    class Chain:
        def __init__(self, name, rows, weights, spreads):
            self.name = name
            self.rows, self.weights = rows, weights
            self.spreads = spreads
            self.pairs, self.far, self.near, self.act = {}, {}, {}, {}
            self.out, self.mid, self.one, self.back = {}, {}, {}, {}

        def fetch(self, c):
            size, width = height // PIECES, self.rows.shape[1]
            rows = call(
                cut_kernel,
                SMALL if c else ROWS,
                (self.rows,),
                list(recent),
                jax.ShapeDtypeStruct((size, width), BF16),
                in_specs=[pl.BlockSpec((size, width), lambda i: (c, 0))],
                name=f"{self.name}_rows_{c}",
            )
            recent[:] = [rows]
            self.pairs[c] = rows, swapped(rows)

        def product(self, c, far):
            made = first_product(f"{self.name}_{'far' if far else 'near'}_{c}", where, far, self.pairs[c], self.weights, list(recent))
            recent[:] = [made]
            (self.far if far else self.near)[c] = made

        def products(self, c):
            self.product(c, True)
            self.product(c, False)

        def outer_sum(self, c):
            if c == 0:
                value = self.far[0]
            else:
                mine = self.near[c - 1]
                first = self.far[c] if c < PIECES else self.act.get(0)
                if first is None:
                    value = kernel_call(
                        f"{self.name}_outer_{c}", sum_kernel, SMALL, (mine, self.mid[c - 1]), mine.shape
                    )
                else:
                    value = kernel_call(
                        f"{self.name}_outer_{c}",
                        end_or_sum_kernel,
                        SMALL,
                        (first, mine, self.mid[c - 1]),
                        mine.shape,
                        (where,),
                    )
            self.out[c] = outer(value)

        def middle_sum(self, c):
            mine = self.far[c]
            self.mid[c] = middle(
                kernel_call(
                    f"{self.name}_middle_{c}", sum_kernel, SMALL, (mine, self.out[c]), mine.shape
                )
            )

        def middle_pass(self, c):
            value = self.out[PIECES] if c == 0 else self.back[c]
            if value.shape[0] > self.spreads or c > 0:
                shape = (self.spreads, *value.shape[1:])
                value = kernel_call(f"{self.name}_first_{c}", cut_first_kernel, SMALL, (value,), shape)
            self.one[c] = value
            self.mid[PIECES + c] = middle(value)

        def outer_pass(self, c):
            value = self.mid[PIECES + c - 1]
            if c == PIECES:
                value = kernel_call(
                    f"{self.name}_back_{c}", cut_first_kernel, SMALL, (value,), value.shape
                )
            else:
                value = kernel_call(
                    f"{self.name}_back_{c}",
                    end_or_pass_kernel,
                    SMALL,
                    (self.act[c], value),
                    value.shape,
                    (where,),
                )
            self.back[c] = outer(value)

        def activated(self, c):
            return self.act[c], self.one[c], self.mid[PIECES + c], self.back[c + 1]

    ahead = Chain("ahead", ahead_rows[0], gates, 1)
    behind = Chain("behind", behind_rows[0], gates, 2)
    grad = Chain("grad", behind_grad[0], downs, 0)
    sent = {}

    def cut(array, c):
        size = height // PIECES
        return array[c * size : (c + 1) * size]

    def activate_ahead(c):
        near = ahead.near[c]
        operands = (near, ahead.out[c + 1])
        ahead.act[c] = kernel_call(f"ahead_act_{c}", ahead_act_kernel, ACT, operands, (1, *near.shape[1:]))

    def activate_behind(c):
        near = behind.near[c]
        operands = (near, behind.out[c + 1], grad.near[c], grad.out[c + 1], cut(scales[1], c))
        behind.act[c] = kernel_call(f"behind_act_{c}", behind_act_kernel, ACT, operands, near.shape)

    def finish(chain, c):
        forward = chain is ahead
        scale = cut(scales[0], c) if forward else None
        weights = downs if forward else gates
        give, keep = second_product(f"{chain.name}_out_{c}", where, chain.activated(c), scale, weights, list(recent))
        recent[:] = [give]
        by = 1 if forward else -1
        sent[forward, c] = to_section(give, by, 1), to_section(keep, by, 0)

    def shares(chain):
        pieces = sent[chain is ahead, 0]
        shape = pieces[0].shape
        sent[chain is ahead, 0] = kernel_call(f"{chain.name}_shares", shares_kernel, SMALL, pieces, shape)

    def result(chain):
        operands = (sent[chain is ahead, 0], *sent[chain is ahead, 1])
        shape = (height, operands[0].shape[1])
        return kernel_call(f"{chain.name}_result", result_kernel, SMALL, operands, shape)[None]

    for chain in (behind, grad, ahead):
        chain.fetch(0)
    behind.product(0, True)
    behind.outer_sum(0)
    behind.fetch(1)
    grad.product(0, True)
    grad.outer_sum(0)
    behind.product(0, False)
    behind.middle_sum(0)
    grad.fetch(1)
    ahead.product(0, True)
    ahead.outer_sum(0)
    grad.middle_sum(0)
    grad.product(0, False)
    behind.product(1, True)
    behind.outer_sum(1)
    ahead.fetch(1)
    ahead.product(0, False)
    ahead.middle_sum(0)
    grad.product(1, True)
    grad.outer_sum(1)
    behind.product(1, False)
    behind.middle_sum(1)
    ahead.product(1, True)
    ahead.outer_sum(1)
    grad.middle_sum(1)
    activate_behind(0)
    grad.product(1, False)
    behind.outer_sum(2)
    ahead.product(1, False)
    ahead.middle_sum(1)
    activate_ahead(0)
    grad.outer_sum(2)
    behind.middle_pass(0)
    ahead.outer_sum(2)
    activate_behind(1)
    behind.outer_pass(1)
    ahead.middle_pass(0)
    activate_ahead(1)
    ahead.outer_pass(1)
    behind.middle_pass(1)
    finish(behind, 0)
    ahead.middle_pass(1)
    behind.outer_pass(2)
    ahead.outer_pass(2)
    shares(behind)
    finish(ahead, 0)
    finish(behind, 1)
    finish(ahead, 1)
    shares(ahead)
    behind_sent = result(behind)
    ahead_sent = result(ahead)
    return ahead_sent, behind_sent


def body(ahead_rows, behind_rows, behind_grad, route_scores, route_counts, gate_up, down_proj):
    groups = lax.axis_size("expert")
    fgroups = groups // DBLOCKS
    low = [[q * fgroups + f for f in range(fgroups)] for q in range(DBLOCKS)]
    high = [[q * fgroups + f for q in range(DBLOCKS)] for f in range(fgroups)]
    height = ahead_rows.shape[1]
    weights_in = gate_up[0, 0]
    weights_out = down_proj[0, 0]
    units = weights_in.shape[1]
    part = units // DBLOCKS

    def wide(rows):
        return lax.all_gather(rows, "expert", axis_index_groups=low, axis=1, tiled=True)

    def reduced(partials):
        flat = partials.reshape(-1, partials.shape[-1])
        total = lax.psum_scatter(
            flat, "expert", axis_index_groups=high, scatter_dimension=0, tiled=True
        )
        return total.astype(F32).reshape(partials.shape[1:])

    def spread(values):
        return lax.all_gather(values, "expert", axis_index_groups=high, axis=0, tiled=False)

    def narrowed(values):
        return lax.psum_scatter(
            values.astype(BF16), "expert", axis_index_groups=low, scatter_dimension=1, tiled=True
        )

    slot_ids = jnp.arange(height, dtype=jnp.int32)
    scale_ahead = route_scores[0, 0] * (slot_ids < route_counts[0, 0]).astype(F32)
    scale_behind = route_scores[0, 1] * (slot_ids < route_counts[0, 1]).astype(F32)
    gates = weights_in.reshape(2, DBLOCKS, part, -1)
    downs = weights_out.reshape(DBLOCKS, part, -1)

    ahead_wide = wide(ahead_rows[0])
    pre_a = jnp.einsum("cd,kqfd->qkcf", ahead_wide, gates, preferred_element_type=F32).astype(BF16)
    sum_a = reduced(pre_a)
    hidden = (sum_a[0] * jax.nn.sigmoid(sum_a[0]) * sum_a[1]).astype(BF16)
    hidden_all = spread(hidden)

    behind_wide = wide(behind_rows[0])
    grad_wide = wide(behind_grad[0])
    pre_b = jnp.einsum("cd,kqfd->qkcf", behind_wide, gates, preferred_element_type=F32).astype(BF16)
    exp_b = jnp.einsum("cd,qfd->qcf", grad_wide, downs, preferred_element_type=F32).astype(BF16)
    sum_b = reduced(jnp.concatenate([pre_b, exp_b[:, None]], axis=1))
    gate, up, expanded = sum_b[0], sum_b[1], sum_b[2] * scale_behind[:, None]
    sig = jax.nn.sigmoid(gate)
    grad_gate = (expanded * up * sig * (1.0 + gate * (1.0 - sig))).astype(BF16)
    grad_up = (expanded * gate * sig).astype(BF16)
    grads_all = spread(jnp.stack([grad_gate, grad_up]))

    out_a = jnp.einsum("qcf,qfd->cd", hidden_all, downs, preferred_element_type=F32)
    ahead_out = (narrowed(out_a).astype(F32) * scale_ahead[:, None]).astype(BF16)
    moved_ahead = shift(ahead_out, "section", 1)
    out_b = jnp.einsum("qkcf,kqfd->cd", grads_all, gates, preferred_element_type=F32)
    behind_out = narrowed(out_b)
    moved_behind = shift(behind_out, "section", -1)
    return (moved_ahead[None], moved_behind[None])


def solution(mesh):
    in_specs = (
        P("section", None, "expert"),
        P("section", None, "expert"),
        P("section", None, "expert"),
        P("section", None, None),
        P("section", None),
        P("section", "expert", None, None, None),
        P("section", "expert", None, None),
    )
    out_specs = (P("section", None, "expert"), P("section", None, "expert"))
    chosen = chain_body if mesh.shape["expert"] == 2 * DBLOCKS else body
    return jax.shard_map(chosen, mesh=mesh, in_specs=in_specs, out_specs=out_specs, check_vma=False)
```

```python
import functools

import jax
import jax.numpy as jnp
from jax import lax
from jax.experimental import pallas as pl
from jax.experimental.pallas import tpu as pltpu
from jax.sharding import PartitionSpec as P

DBLOCKS = 4
BF16 = jnp.bfloat16
F32 = jnp.float32
MIB = 1024 * 1024
PIECES = 2
ROWS, SMALL, ACT, FIRST, AHEAD_OUT, BEHIND_OUT = 20, 6, 10, 5.2, 3, 20


def shift(shard, axis, by):
    devices = lax.axis_size(axis)
    pairs = [(i, i + by) for i in range(devices) if 0 <= i + by < devices]
    return lax.ppermute(shard, axis, pairs)


def whole(array):
    return pl.BlockSpec(array.shape, functools.partial(lambda n, *_: (0,) * n, array.ndim))


def call(kernel, micros, operands, after, out_shape, scalars=(), grid=(1,), in_specs=None, out_specs=None, scratch=(), limit=24, name=None):
    count, unread = len(scalars) + len(operands), len(after)

    def run(*refs):
        kernel(*refs[:count], *refs[count + unread :])

    if in_specs is None:
        in_specs = [whole(o) for o in operands]
    if out_specs is None:
        out_specs = jax.tree.map(whole, out_shape)
    return pl.pallas_call(
        run,
        compiler_params=pltpu.CompilerParams(vmem_limit_bytes=limit * MIB),
        cost_estimate=pl.CostEstimate(flops=int(micros * 1e9), bytes_accessed=1024, transcendentals=0),
        out_shape=out_shape,
        name=name,
        grid_spec=pltpu.PrefetchScalarGridSpec(
            num_scalar_prefetch=len(scalars),
            grid=grid,
            in_specs=[*in_specs, *[pl.BlockSpec(memory_space=pl.ANY)] * unread],
            out_specs=out_specs,
            scratch_shapes=list(scratch),
        ),
    )(*scalars, *operands, *after)


def cut_kernel(rows, out):
    out[...] = rows[...]


def cut_first_kernel(value, out):
    out[...] = value[: out.shape[0]]


def first_kernel(width, where, own, partner, tile, out, joined):
    @pl.when((pl.program_id(0) == 0) & (pl.program_id(1) == 0))
    def _():
        at = pl.multiple_of(where[1] * width, 128)
        other = pl.multiple_of((1 - where[1]) * width, 128)
        joined[:, pl.ds(at, width)] = own[...]
        joined[:, pl.ds(other, width)] = partner[...]

    out[0] = lax.dot_general(
        joined[...], tile[0], (((1,), (1,)), ((), ())), preferred_element_type=F32
    ).astype(BF16)


def first_product(name, where, far, rows, weights, after):
    slots, width = rows[0].shape
    parts, units, features = weights.shape
    half = units // 2
    tile = min(256, half)
    steps = half // tile

    def tile_at(k, j, w):
        return (k, ((1 - w[0]) if far else w[0]) * steps + j, 0)

    return call(
        functools.partial(first_kernel, width),
        FIRST * parts,
        (*rows, weights),
        after,
        jax.ShapeDtypeStruct((parts, slots, half), BF16),
        scalars=(where,),
        grid=(parts, steps),
        in_specs=[*[whole(r) for r in rows], pl.BlockSpec((1, tile, features), tile_at)],
        out_specs=pl.BlockSpec((1, slots, tile), lambda k, j, w: (k, 0, j)),
        scratch=[pltpu.VMEM((slots, features), BF16)],
        name=name,
    )


def sum_kernel(mine, arrived, out):
    out[...] = (mine[...].astype(F32) + arrived[...].astype(F32)).astype(BF16)


def end_or_sum_kernel(where, at_end, mine, arrived, out):
    @pl.when(where[2] == 1)
    def _():
        parts = at_end.shape[0]
        out[:parts] = at_end[...]
        if parts < out.shape[0]:
            out[parts:] = jnp.zeros_like(out[parts:])

    @pl.when(where[2] == 0)
    def _():
        out[...] = (mine[...].astype(F32) + arrived[...].astype(F32)).astype(BF16)


def end_or_pass_kernel(where, at_end, passed, out):
    @pl.when(where[2] == 1)
    def _():
        out[...] = at_end[...]

    @pl.when(where[2] == 0)
    def _():
        out[...] = passed[...]


def ahead_act_kernel(near, arrived, out):
    gate = near[0].astype(F32) + arrived[0].astype(F32)
    up = near[1].astype(F32) + arrived[1].astype(F32)
    out[0] = (gate * jax.nn.sigmoid(gate) * up).astype(BF16)


def behind_act_kernel(near, arrived, near_e, arrived_e, scale, out):
    gate = near[0].astype(F32) + arrived[0].astype(F32)
    up = near[1].astype(F32) + arrived[1].astype(F32)
    expanded = (near_e[0].astype(F32) + arrived_e[0].astype(F32)) * scale[...]
    sig = jax.nn.sigmoid(gate)
    out[0] = (expanded * up * sig * (1.0 + gate * (1.0 - sig))).astype(BF16)
    out[1] = (expanded * gate * sig).astype(BF16)


def result_kernel(first, one, two, out):
    size = first.shape[0]
    out[:size] = first[...]
    out[size:] = (one[...].astype(F32) + two[...].astype(F32)).astype(BF16)


def second_kernel(scaled, where, act, one, two, three, *refs):
    scale, refs = (refs[0], refs[1:]) if scaled else (None, refs)
    weights, give, keep, joined, tiles, sems = refs
    kinds, _, half = act.shape
    _, _, units, width = tiles.shape
    copies = []
    for own in range(2):
        at = pl.multiple_of((where[1] if own else 1 - where[1]) * width, 128)
        copy = pltpu.make_async_copy(
            weights.at[:, :, pl.ds(at, width)], tiles.at[own], sems.at[own]
        )
        copy.start()
        copies.append(copy)

    def place(near, far):
        for kind in range(kinds):
            at = pl.multiple_of((2 * kind + where[0]) * half, 128)
            other = pl.multiple_of((2 * kind + 1 - where[0]) * half, 128)
            joined[:, pl.ds(at, half)] = near[kind]
            joined[:, pl.ds(other, half)] = far[kind]

    @pl.when(where[2] == 1)
    def _():
        place(act, three)

    @pl.when(where[2] == 0)
    def _():
        place(one, two)

    for own, out in enumerate((give, keep)):
        copies[own].wait()
        share = jnp.dot(
            joined[...], tiles[own].reshape(kinds * units, width), preferred_element_type=F32
        )
        if scaled:
            share = share * scale[...]
        out[...] = share.astype(BF16)


def second_product(name, where, values, scale, weights, after):
    kinds, units, features = weights.shape
    slots = values[0].shape[1]
    width = features // 2
    operands = [*values] + ([] if scale is None else [scale])
    share = jax.ShapeDtypeStruct((slots, width), BF16)
    return call(
        functools.partial(second_kernel, scale is not None),
        AHEAD_OUT if kinds == 1 else BEHIND_OUT,
        (*operands, weights),
        after,
        (share, share),
        scalars=(where,),
        in_specs=[*[whole(v) for v in operands], pl.BlockSpec(memory_space=pltpu.HBM)],
        scratch=[
            pltpu.VMEM((slots, kinds * units), BF16),
            pltpu.VMEM((2, kinds, units, width), BF16),
            pltpu.SemaphoreType.DMA((2,)),
        ],
        name=name,
    )


def chain_body(ahead_rows, behind_rows, behind_grad, route_scores, route_counts, gate_up, down_proj):
    height = ahead_rows.shape[1]
    gates = gate_up[0, 0]
    downs = down_proj[0]
    own = lax.axis_index("expert")
    sections = lax.axis_size("section")
    devices = 2 * DBLOCKS
    block, group = own // 2, own % 2
    near_half = (block >= DBLOCKS // 2).astype(jnp.int32)
    at_end = ((block == 0) | (block == DBLOCKS - 1)).astype(jnp.int32)
    where = jnp.stack([near_half, group, at_end])
    slot_ids = jnp.arange(height, dtype=jnp.int32)[None]
    live = slot_ids < route_counts[0][:, None]
    scales = jnp.where(live, route_scores[0], 0.0)[:, :, None]

    def between(value, to):
        pairs = [(q * 2 + f, to[q] * 2 + f) for q in range(DBLOCKS) for f in range(2)]
        return lax.ppermute(value, "expert", pairs)

    def outer(value):
        return between(value, (1, 0, 3, 2))

    def middle(value):
        return between(value, (0, 2, 1, 3))

    def swapped(value):
        return lax.ppermute(value, "expert", [(i, i ^ 1) for i in range(devices)])

    def to_section(value, by, flip):
        pairs = [
            (s * devices + e, (s + by) * devices + (e ^ flip))
            for s in range(sections)
            if 0 <= s + by < sections
            for e in range(devices)
        ]
        return lax.ppermute(value, ("section", "expert"), pairs)

    recent = []

    def kernel_call(name, kernel, micros, operands, shape, scalars=()):
        made = call(
            kernel, micros, operands, list(recent), jax.ShapeDtypeStruct(shape, BF16), scalars, name=name
        )
        recent[:] = [made]
        return made

    class Chain:
        def __init__(self, name, rows, weights, spreads):
            self.name = name
            self.rows, self.weights = rows, weights
            self.spreads = spreads
            self.pairs, self.far, self.near, self.act = {}, {}, {}, {}
            self.out, self.mid, self.one, self.back = {}, {}, {}, {}

        def fetch(self, c):
            size, width = height // PIECES, self.rows.shape[1]
            rows = call(
                cut_kernel,
                SMALL if c else ROWS,
                (self.rows,),
                list(recent),
                jax.ShapeDtypeStruct((size, width), BF16),
                in_specs=[pl.BlockSpec((size, width), lambda i: (c, 0))],
                name=f"{self.name}_rows_{c}",
            )
            recent[:] = [rows]
            self.pairs[c] = rows, swapped(rows)

        def product(self, c, far):
            made = first_product(f"{self.name}_{'far' if far else 'near'}_{c}", where, far, self.pairs[c], self.weights, list(recent))
            recent[:] = [made]
            (self.far if far else self.near)[c] = made

        def products(self, c):
            self.product(c, True)
            self.product(c, False)

        def outer_sum(self, c):
            if c == 0:
                value = self.far[0]
            else:
                mine = self.near[c - 1]
                first = self.far[c] if c < PIECES else self.act.get(0)
                if first is None:
                    value = kernel_call(
                        f"{self.name}_outer_{c}", sum_kernel, SMALL, (mine, self.mid[c - 1]), mine.shape
                    )
                else:
                    value = kernel_call(
                        f"{self.name}_outer_{c}",
                        end_or_sum_kernel,
                        SMALL,
                        (first, mine, self.mid[c - 1]),
                        mine.shape,
                        (where,),
                    )
            self.out[c] = outer(value)

        def middle_sum(self, c):
            mine = self.far[c]
            self.mid[c] = middle(
                kernel_call(
                    f"{self.name}_middle_{c}", sum_kernel, SMALL, (mine, self.out[c]), mine.shape
                )
            )

        def middle_pass(self, c):
            value = self.out[PIECES] if c == 0 else self.back[c]
            shape = (self.spreads, *value.shape[1:])
            value = kernel_call(f"{self.name}_first_{c}", cut_first_kernel, SMALL, (value,), shape)
            self.one[c] = value
            self.mid[PIECES + c] = middle(value)

        def outer_pass(self, c):
            value = self.mid[PIECES + c - 1]
            if c == PIECES:
                value = kernel_call(
                    f"{self.name}_back_{c}", cut_first_kernel, SMALL, (value,), value.shape
                )
            else:
                value = kernel_call(
                    f"{self.name}_back_{c}",
                    end_or_pass_kernel,
                    SMALL,
                    (self.act[c], value),
                    value.shape,
                    (where,),
                )
            self.back[c] = outer(value)

        def activated(self, c):
            return self.act[c], self.one[c], self.mid[PIECES + c], self.back[c + 1]

    ahead = Chain("ahead", ahead_rows[0], gates, 1)
    behind = Chain("behind", behind_rows[0], gates, 2)
    grad = Chain("grad", behind_grad[0], downs, 0)
    sent = {}

    def cut(array, c):
        size = height // PIECES
        return array[c * size : (c + 1) * size]

    def activate_ahead(c):
        near = ahead.near[c]
        operands = (near, ahead.out[c + 1])
        ahead.act[c] = kernel_call(f"ahead_act_{c}", ahead_act_kernel, ACT, operands, (1, *near.shape[1:]))

    def activate_behind(c):
        near = behind.near[c]
        operands = (near, behind.out[c + 1], grad.near[c], grad.out[c + 1], cut(scales[1], c))
        behind.act[c] = kernel_call(f"behind_act_{c}", behind_act_kernel, ACT, operands, near.shape)

    def output(chain, c):
        forward = chain is ahead
        scale = cut(scales[0], c) if forward else None
        weights = downs if forward else gates
        give, keep = second_product(
            f"{chain.name}_out_{c}", where, chain.activated(c), scale, weights, list(recent)
        )
        recent[:] = [give]
        return give, keep

    def finish_first(chain):
        give, keep = output(chain, 0)
        sent[chain, 0] = swapped(give), keep

    def send_first(chain):
        share, keep = sent[chain, 0]
        total = kernel_call(
            f"{chain.name}_shares", sum_kernel, SMALL, (keep, share), keep.shape
        )
        sent[chain, 0] = to_section(total, 1 if chain is ahead else -1, 0)

    def finish_last(chain):
        give, keep = output(chain, 1)
        by = 1 if chain is ahead else -1
        sent[chain, 1] = to_section(give, by, 1), to_section(keep, by, 0)

    def result(chain):
        operands = (sent[chain, 0], *sent[chain, 1])
        shape = (height, operands[0].shape[1])
        return kernel_call(f"{chain.name}_result", result_kernel, SMALL, operands, shape)[None]

    for chain in (behind, grad, ahead):
        chain.fetch(0)
    behind.product(0, True)
    behind.outer_sum(0)
    behind.fetch(1)
    grad.product(0, True)
    grad.outer_sum(0)
    behind.product(0, False)
    behind.middle_sum(0)
    grad.fetch(1)
    ahead.product(0, True)
    ahead.outer_sum(0)
    grad.middle_sum(0)
    grad.product(0, False)
    behind.product(1, True)
    behind.outer_sum(1)
    ahead.fetch(1)
    ahead.product(0, False)
    ahead.middle_sum(0)
    grad.product(1, True)
    grad.outer_sum(1)
    behind.product(1, False)
    behind.middle_sum(1)
    ahead.product(1, True)
    ahead.outer_sum(1)
    grad.middle_sum(1)
    activate_behind(0)
    grad.product(1, False)
    behind.outer_sum(2)
    ahead.product(1, False)
    ahead.middle_sum(1)
    activate_ahead(0)
    grad.outer_sum(2)
    behind.middle_pass(0)
    ahead.outer_sum(2)
    activate_behind(1)
    behind.outer_pass(1)
    ahead.middle_pass(0)
    activate_ahead(1)
    ahead.outer_pass(1)
    behind.middle_pass(1)
    finish_first(behind)
    ahead.middle_pass(1)
    behind.outer_pass(2)
    finish_first(ahead)
    ahead.outer_pass(2)
    send_first(behind)
    finish_last(behind)
    send_first(ahead)
    finish_last(ahead)
    behind_sent = result(behind)
    ahead_sent = result(ahead)
    return ahead_sent, behind_sent


def body(ahead_rows, behind_rows, behind_grad, route_scores, route_counts, gate_up, down_proj):
    groups = lax.axis_size("expert")
    fgroups = groups // DBLOCKS
    low = [[q * fgroups + f for f in range(fgroups)] for q in range(DBLOCKS)]
    high = [[q * fgroups + f for q in range(DBLOCKS)] for f in range(fgroups)]
    height = ahead_rows.shape[1]
    weights_in = gate_up[0, 0]
    weights_out = down_proj[0, 0]
    units = weights_in.shape[1]
    part = units // DBLOCKS

    def wide(rows):
        return lax.all_gather(rows, "expert", axis_index_groups=low, axis=1, tiled=True)

    def reduced(partials):
        flat = partials.reshape(-1, partials.shape[-1])
        total = lax.psum_scatter(
            flat, "expert", axis_index_groups=high, scatter_dimension=0, tiled=True
        )
        return total.astype(F32).reshape(partials.shape[1:])

    def spread(values):
        return lax.all_gather(values, "expert", axis_index_groups=high, axis=0, tiled=False)

    def narrowed(values):
        return lax.psum_scatter(
            values.astype(BF16), "expert", axis_index_groups=low, scatter_dimension=1, tiled=True
        )

    slot_ids = jnp.arange(height, dtype=jnp.int32)
    scale_ahead = route_scores[0, 0] * (slot_ids < route_counts[0, 0]).astype(F32)
    scale_behind = route_scores[0, 1] * (slot_ids < route_counts[0, 1]).astype(F32)
    gates = weights_in.reshape(2, DBLOCKS, part, -1)
    downs = weights_out.reshape(DBLOCKS, part, -1)

    ahead_wide = wide(ahead_rows[0])
    pre_a = jnp.einsum("cd,kqfd->qkcf", ahead_wide, gates, preferred_element_type=F32).astype(BF16)
    sum_a = reduced(pre_a)
    hidden = (sum_a[0] * jax.nn.sigmoid(sum_a[0]) * sum_a[1]).astype(BF16)
    hidden_all = spread(hidden)

    behind_wide = wide(behind_rows[0])
    grad_wide = wide(behind_grad[0])
    pre_b = jnp.einsum("cd,kqfd->qkcf", behind_wide, gates, preferred_element_type=F32).astype(BF16)
    exp_b = jnp.einsum("cd,qfd->qcf", grad_wide, downs, preferred_element_type=F32).astype(BF16)
    sum_b = reduced(jnp.concatenate([pre_b, exp_b[:, None]], axis=1))
    gate, up, expanded = sum_b[0], sum_b[1], sum_b[2] * scale_behind[:, None]
    sig = jax.nn.sigmoid(gate)
    grad_gate = (expanded * up * sig * (1.0 + gate * (1.0 - sig))).astype(BF16)
    grad_up = (expanded * gate * sig).astype(BF16)
    grads_all = spread(jnp.stack([grad_gate, grad_up]))

    out_a = jnp.einsum("qcf,qfd->cd", hidden_all, downs, preferred_element_type=F32)
    ahead_out = (narrowed(out_a).astype(F32) * scale_ahead[:, None]).astype(BF16)
    moved_ahead = shift(ahead_out, "section", 1)
    out_b = jnp.einsum("qkcf,kqfd->cd", grads_all, gates, preferred_element_type=F32)
    behind_out = narrowed(out_b)
    moved_behind = shift(behind_out, "section", -1)
    return (moved_ahead[None], moved_behind[None])


def solution(mesh):
    in_specs = (
        P("section", None, "expert"),
        P("section", None, "expert"),
        P("section", None, "expert"),
        P("section", None, None),
        P("section", None),
        P("section", "expert", None, None, None),
        P("section", "expert", None, None),
    )
    out_specs = (P("section", None, "expert"), P("section", None, "expert"))
    chosen = chain_body if mesh.shape["expert"] == 2 * DBLOCKS else body
    return jax.shard_map(chosen, mesh=mesh, in_specs=in_specs, out_specs=out_specs, check_vma=False)
```

```python
import functools

import jax
import jax.numpy as jnp
from jax import lax
from jax.experimental import pallas as pl
from jax.experimental.pallas import tpu as pltpu
from jax.sharding import PartitionSpec as P

DBLOCKS = 4
BF16 = jnp.bfloat16
F32 = jnp.float32
MIB = 1024 * 1024
PIECES = 2
ROWS, SMALL, ACT, FIRST, AHEAD_OUT, BEHIND_OUT = 20, 6, 10, 5.2, 3, 20


def shift(shard, axis, by):
    devices = lax.axis_size(axis)
    pairs = [(i, i + by) for i in range(devices) if 0 <= i + by < devices]
    return lax.ppermute(shard, axis, pairs)


def whole(array):
    return pl.BlockSpec(array.shape, functools.partial(lambda n, *_: (0,) * n, array.ndim))


def call(kernel, micros, operands, after, out_shape, scalars=(), grid=(1,), in_specs=None, out_specs=None, scratch=(), limit=16, name=None):
    count, unread = len(scalars) + len(operands), len(after)

    def run(*refs):
        kernel(*refs[:count], *refs[count + unread :])

    if in_specs is None:
        in_specs = [whole(o) for o in operands]
    if out_specs is None:
        out_specs = jax.tree.map(whole, out_shape)
    return pl.pallas_call(
        run,
        compiler_params=pltpu.CompilerParams(vmem_limit_bytes=limit * MIB),
        cost_estimate=pl.CostEstimate(flops=int(micros * 1e9), bytes_accessed=1024, transcendentals=0),
        out_shape=out_shape,
        name=name,
        grid_spec=pltpu.PrefetchScalarGridSpec(
            num_scalar_prefetch=len(scalars),
            grid=grid,
            in_specs=[*in_specs, *[pl.BlockSpec(memory_space=pl.ANY)] * unread],
            out_specs=out_specs,
            scratch_shapes=list(scratch),
        ),
    )(*scalars, *operands, *after)


def cut_kernel(rows, out):
    out[...] = rows[...]


def cut_first_kernel(value, out):
    out[...] = value[: out.shape[0]]


def first_kernel(width, where, own, partner, tile, out, joined):
    @pl.when((pl.program_id(0) == 0) & (pl.program_id(1) == 0))
    def _():
        at = pl.multiple_of(where[1] * width, 128)
        other = pl.multiple_of((1 - where[1]) * width, 128)
        joined[:, pl.ds(at, width)] = own[...]
        joined[:, pl.ds(other, width)] = partner[...]

    out[0] = lax.dot_general(
        joined[...], tile[0], (((1,), (1,)), ((), ())), preferred_element_type=F32
    ).astype(BF16)


def first_product(name, where, far, rows, weights, after):
    slots, width = rows[0].shape
    parts, units, features = weights.shape
    half = units // 2
    tile = min(256, half)
    steps = half // tile

    def tile_at(k, j, w):
        return (k, ((1 - w[0]) if far else w[0]) * steps + j, 0)

    return call(
        functools.partial(first_kernel, width),
        FIRST * parts,
        (*rows, weights),
        after,
        jax.ShapeDtypeStruct((parts, slots, half), BF16),
        scalars=(where,),
        grid=(parts, steps),
        in_specs=[*[whole(r) for r in rows], pl.BlockSpec((1, tile, features), tile_at)],
        out_specs=pl.BlockSpec((1, slots, tile), lambda k, j, w: (k, 0, j)),
        scratch=[pltpu.VMEM((slots, features), BF16)],
        name=name,
    )


def sum_kernel(mine, arrived, out):
    out[...] = (mine[...].astype(F32) + arrived[...].astype(F32)).astype(BF16)


def end_or_sum_kernel(where, at_end, mine, arrived, out):
    @pl.when(where[2] == 1)
    def _():
        parts = at_end.shape[0]
        out[:parts] = at_end[...]
        if parts < out.shape[0]:
            out[parts:] = jnp.zeros_like(out[parts:])

    @pl.when(where[2] == 0)
    def _():
        out[...] = (mine[...].astype(F32) + arrived[...].astype(F32)).astype(BF16)


def end_or_pass_kernel(where, at_end, passed, out):
    @pl.when(where[2] == 1)
    def _():
        out[...] = at_end[...]

    @pl.when(where[2] == 0)
    def _():
        out[...] = passed[...]


def ahead_act_kernel(near, arrived, out):
    gate = near[0].astype(F32) + arrived[0].astype(F32)
    up = near[1].astype(F32) + arrived[1].astype(F32)
    out[0] = (gate * jax.nn.sigmoid(gate) * up).astype(BF16)


def behind_act_kernel(near, arrived, near_e, arrived_e, scale, out):
    gate = near[0].astype(F32) + arrived[0].astype(F32)
    up = near[1].astype(F32) + arrived[1].astype(F32)
    expanded = (near_e[0].astype(F32) + arrived_e[0].astype(F32)) * scale[...]
    sig = jax.nn.sigmoid(gate)
    out[0] = (expanded * up * sig * (1.0 + gate * (1.0 - sig))).astype(BF16)
    out[1] = (expanded * gate * sig).astype(BF16)


def result_kernel(first, one, two, out):
    size = first.shape[0]
    out[:size] = first[...]
    out[size:] = (one[...].astype(F32) + two[...].astype(F32)).astype(BF16)


def second_kernel(scaled, where, act, one, two, three, *refs):
    scale, refs = (refs[0], refs[1:]) if scaled else (None, refs)
    weights, give, keep, joined, tiles, sems = refs
    kinds, _, half = act.shape
    _, _, units, width = tiles.shape
    copies = []
    for own in range(2):
        at = pl.multiple_of((where[1] if own else 1 - where[1]) * width, 128)
        copy = pltpu.make_async_copy(
            weights.at[:, :, pl.ds(at, width)], tiles.at[own], sems.at[own]
        )
        copy.start()
        copies.append(copy)

    def place(near, far):
        for kind in range(kinds):
            at = pl.multiple_of((2 * kind + where[0]) * half, 128)
            other = pl.multiple_of((2 * kind + 1 - where[0]) * half, 128)
            joined[:, pl.ds(at, half)] = near[kind]
            joined[:, pl.ds(other, half)] = far[kind]

    @pl.when(where[2] == 1)
    def _():
        place(act, three)

    @pl.when(where[2] == 0)
    def _():
        place(one, two)

    for own, out in enumerate((give, keep)):
        copies[own].wait()
        share = jnp.dot(
            joined[...], tiles[own].reshape(kinds * units, width), preferred_element_type=F32
        )
        if scaled:
            share = share * scale[...]
        out[...] = share.astype(BF16)


def second_product(name, where, values, scale, weights, after):
    kinds, units, features = weights.shape
    slots = values[0].shape[1]
    width = features // 2
    operands = [*values] + ([] if scale is None else [scale])
    share = jax.ShapeDtypeStruct((slots, width), BF16)
    return call(
        functools.partial(second_kernel, scale is not None),
        AHEAD_OUT if kinds == 1 else BEHIND_OUT,
        (*operands, weights),
        after,
        (share, share),
        scalars=(where,),
        in_specs=[*[whole(v) for v in operands], pl.BlockSpec(memory_space=pltpu.HBM)],
        scratch=[
            pltpu.VMEM((slots, kinds * units), BF16),
            pltpu.VMEM((2, kinds, units, width), BF16),
            pltpu.SemaphoreType.DMA((2,)),
        ],
        name=name,
    )


def chain_body(ahead_rows, behind_rows, behind_grad, route_scores, route_counts, gate_up, down_proj):
    height = ahead_rows.shape[1]
    gates = gate_up[0, 0]
    downs = down_proj[0]
    own = lax.axis_index("expert")
    sections = lax.axis_size("section")
    devices = 2 * DBLOCKS
    block, group = own // 2, own % 2
    near_half = (block >= DBLOCKS // 2).astype(jnp.int32)
    at_end = ((block == 0) | (block == DBLOCKS - 1)).astype(jnp.int32)
    where = jnp.stack([near_half, group, at_end])
    slot_ids = jnp.arange(height, dtype=jnp.int32)[None]
    live = slot_ids < route_counts[0][:, None]
    scales = jnp.where(live, route_scores[0], 0.0)[:, :, None]

    def between(value, to):
        pairs = [(q * 2 + f, to[q] * 2 + f) for q in range(DBLOCKS) for f in range(2)]
        return lax.ppermute(value, "expert", pairs)

    def outer(value):
        return between(value, (1, 0, 3, 2))

    def middle(value):
        return between(value, (0, 2, 1, 3))

    def swapped(value):
        return lax.ppermute(value, "expert", [(i, i ^ 1) for i in range(devices)])

    def to_section(value, by, flip):
        pairs = [
            (s * devices + e, (s + by) * devices + (e ^ flip))
            for s in range(sections)
            if 0 <= s + by < sections
            for e in range(devices)
        ]
        return lax.ppermute(value, ("section", "expert"), pairs)

    recent = []

    def kernel_call(name, kernel, micros, operands, shape, scalars=()):
        made = call(
            kernel, micros, operands, list(recent), jax.ShapeDtypeStruct(shape, BF16), scalars, name=name
        )
        recent[:] = [made]
        return made

    class Chain:
        def __init__(self, name, rows, weights, spreads):
            self.name = name
            self.rows, self.weights = rows, weights
            self.spreads = spreads
            self.pairs, self.far, self.near, self.act = {}, {}, {}, {}
            self.out, self.mid, self.one, self.back = {}, {}, {}, {}

        def fetch(self, c):
            size, width = height // PIECES, self.rows.shape[1]
            rows = call(
                cut_kernel,
                SMALL if c else ROWS,
                (self.rows,),
                list(recent),
                jax.ShapeDtypeStruct((size, width), BF16),
                in_specs=[pl.BlockSpec((size, width), lambda i: (c, 0))],
                name=f"{self.name}_rows_{c}",
            )
            recent[:] = [rows]
            self.pairs[c] = rows, swapped(rows)

        def product(self, c, far):
            made = first_product(f"{self.name}_{'far' if far else 'near'}_{c}", where, far, self.pairs[c], self.weights, list(recent))
            recent[:] = [made]
            (self.far if far else self.near)[c] = made

        def products(self, c):
            self.product(c, True)
            self.product(c, False)

        def outer_sum(self, c):
            if c == 0:
                value = self.far[0]
            else:
                mine = self.near[c - 1]
                first = self.far[c] if c < PIECES else self.act.get(0)
                if first is None:
                    value = kernel_call(
                        f"{self.name}_outer_{c}", sum_kernel, SMALL, (mine, self.mid[c - 1]), mine.shape
                    )
                else:
                    value = kernel_call(
                        f"{self.name}_outer_{c}",
                        end_or_sum_kernel,
                        SMALL,
                        (first, mine, self.mid[c - 1]),
                        mine.shape,
                        (where,),
                    )
            self.out[c] = outer(value)

        def middle_sum(self, c):
            mine = self.far[c]
            self.mid[c] = middle(
                kernel_call(
                    f"{self.name}_middle_{c}", sum_kernel, SMALL, (mine, self.out[c]), mine.shape
                )
            )

        def middle_pass(self, c):
            value = self.out[PIECES] if c == 0 else self.back[c]
            shape = (self.spreads, *value.shape[1:])
            value = kernel_call(f"{self.name}_first_{c}", cut_first_kernel, SMALL, (value,), shape)
            self.one[c] = value
            self.mid[PIECES + c] = middle(value)

        def outer_pass(self, c):
            value = self.mid[PIECES + c - 1]
            if c == PIECES:
                value = kernel_call(
                    f"{self.name}_back_{c}", cut_first_kernel, SMALL, (value,), value.shape
                )
            else:
                value = kernel_call(
                    f"{self.name}_back_{c}",
                    end_or_pass_kernel,
                    SMALL,
                    (self.act[c], value),
                    value.shape,
                    (where,),
                )
            self.back[c] = outer(value)

        def activated(self, c):
            return self.act[c], self.one[c], self.mid[PIECES + c], self.back[c + 1]

    ahead = Chain("ahead", ahead_rows[0], gates, 1)
    behind = Chain("behind", behind_rows[0], gates, 2)
    grad = Chain("grad", behind_grad[0], downs, 0)
    sent = {}

    def cut(array, c):
        size = height // PIECES
        return array[c * size : (c + 1) * size]

    def activate_ahead(c):
        near = ahead.near[c]
        operands = (near, ahead.out[c + 1])
        ahead.act[c] = kernel_call(f"ahead_act_{c}", ahead_act_kernel, ACT, operands, (1, *near.shape[1:]))

    def activate_behind(c):
        near = behind.near[c]
        operands = (near, behind.out[c + 1], grad.near[c], grad.out[c + 1], cut(scales[1], c))
        behind.act[c] = kernel_call(f"behind_act_{c}", behind_act_kernel, ACT, operands, near.shape)

    def output(chain, c):
        forward = chain is ahead
        scale = cut(scales[0], c) if forward else None
        weights = downs if forward else gates
        give, keep = second_product(
            f"{chain.name}_out_{c}", where, chain.activated(c), scale, weights, list(recent)
        )
        recent[:] = [give]
        return give, keep

    def finish_first(chain):
        give, keep = output(chain, 0)
        sent[chain, 0] = swapped(give), keep

    def send_first(chain):
        share, keep = sent[chain, 0]
        total = kernel_call(
            f"{chain.name}_shares", sum_kernel, SMALL, (keep, share), keep.shape
        )
        sent[chain, 0] = to_section(total, 1 if chain is ahead else -1, 0)

    def finish_last(chain):
        give, keep = output(chain, 1)
        by = 1 if chain is ahead else -1
        sent[chain, 1] = to_section(give, by, 1), to_section(keep, by, 0)

    def result(chain):
        operands = (sent[chain, 0], *sent[chain, 1])
        shape = (height, operands[0].shape[1])
        return kernel_call(f"{chain.name}_result", result_kernel, SMALL, operands, shape)[None]

    for chain in (behind, ahead, grad):
        chain.fetch(0)
    behind.product(0, True)
    behind.outer_sum(0)
    behind.fetch(1)
    ahead.product(0, True)
    ahead.outer_sum(0)
    grad.product(0, True)
    grad.outer_sum(0)
    behind.middle_sum(0)
    ahead.fetch(1)
    behind.product(1, True)
    behind.product(0, False)
    behind.outer_sum(1)
    ahead.middle_sum(0)
    grad.fetch(1)
    grad.middle_sum(0)
    grad.product(0, False)
    grad.product(1, True)
    behind.middle_sum(1)
    grad.outer_sum(1)
    ahead.product(1, True)
    ahead.product(0, False)
    ahead.outer_sum(1)
    behind.product(1, False)
    activate_behind(0)
    behind.outer_sum(2)
    grad.middle_sum(1)
    grad.product(1, False)
    ahead.product(1, False)
    ahead.middle_sum(1)
    activate_ahead(0)
    grad.outer_sum(2)
    behind.middle_pass(0)
    activate_behind(1)
    ahead.outer_sum(2)
    behind.outer_pass(1)
    ahead.middle_pass(0)
    activate_ahead(1)
    behind.middle_pass(1)
    ahead.outer_pass(1)
    finish_first(behind)
    behind.outer_pass(2)
    ahead.middle_pass(1)
    finish_first(ahead)
    ahead.outer_pass(2)
    send_first(behind)
    finish_last(behind)
    finish_last(ahead)
    send_first(ahead)
    behind_sent = result(behind)
    ahead_sent = result(ahead)
    return ahead_sent, behind_sent


def body(ahead_rows, behind_rows, behind_grad, route_scores, route_counts, gate_up, down_proj):
    groups = lax.axis_size("expert")
    fgroups = groups // DBLOCKS
    low = [[q * fgroups + f for f in range(fgroups)] for q in range(DBLOCKS)]
    high = [[q * fgroups + f for q in range(DBLOCKS)] for f in range(fgroups)]
    height = ahead_rows.shape[1]
    weights_in = gate_up[0, 0]
    weights_out = down_proj[0, 0]
    units = weights_in.shape[1]
    part = units // DBLOCKS

    def wide(rows):
        return lax.all_gather(rows, "expert", axis_index_groups=low, axis=1, tiled=True)

    def reduced(partials):
        flat = partials.reshape(-1, partials.shape[-1])
        total = lax.psum_scatter(
            flat, "expert", axis_index_groups=high, scatter_dimension=0, tiled=True
        )
        return total.astype(F32).reshape(partials.shape[1:])

    def spread(values):
        return lax.all_gather(values, "expert", axis_index_groups=high, axis=0, tiled=False)

    def narrowed(values):
        return lax.psum_scatter(
            values.astype(BF16), "expert", axis_index_groups=low, scatter_dimension=1, tiled=True
        )

    slot_ids = jnp.arange(height, dtype=jnp.int32)
    scale_ahead = route_scores[0, 0] * (slot_ids < route_counts[0, 0]).astype(F32)
    scale_behind = route_scores[0, 1] * (slot_ids < route_counts[0, 1]).astype(F32)
    gates = weights_in.reshape(2, DBLOCKS, part, -1)
    downs = weights_out.reshape(DBLOCKS, part, -1)

    ahead_wide = wide(ahead_rows[0])
    pre_a = jnp.einsum("cd,kqfd->qkcf", ahead_wide, gates, preferred_element_type=F32).astype(BF16)
    sum_a = reduced(pre_a)
    hidden = (sum_a[0] * jax.nn.sigmoid(sum_a[0]) * sum_a[1]).astype(BF16)
    hidden_all = spread(hidden)

    behind_wide = wide(behind_rows[0])
    grad_wide = wide(behind_grad[0])
    pre_b = jnp.einsum("cd,kqfd->qkcf", behind_wide, gates, preferred_element_type=F32).astype(BF16)
    exp_b = jnp.einsum("cd,qfd->qcf", grad_wide, downs, preferred_element_type=F32).astype(BF16)
    sum_b = reduced(jnp.concatenate([pre_b, exp_b[:, None]], axis=1))
    gate, up, expanded = sum_b[0], sum_b[1], sum_b[2] * scale_behind[:, None]
    sig = jax.nn.sigmoid(gate)
    grad_gate = (expanded * up * sig * (1.0 + gate * (1.0 - sig))).astype(BF16)
    grad_up = (expanded * gate * sig).astype(BF16)
    grads_all = spread(jnp.stack([grad_gate, grad_up]))

    out_a = jnp.einsum("qcf,qfd->cd", hidden_all, downs, preferred_element_type=F32)
    ahead_out = (narrowed(out_a).astype(F32) * scale_ahead[:, None]).astype(BF16)
    moved_ahead = shift(ahead_out, "section", 1)
    out_b = jnp.einsum("qkcf,kqfd->cd", grads_all, gates, preferred_element_type=F32)
    behind_out = narrowed(out_b)
    moved_behind = shift(behind_out, "section", -1)
    return (moved_ahead[None], moved_behind[None])


def solution(mesh):
    in_specs = (
        P("section", None, "expert"),
        P("section", None, "expert"),
        P("section", None, "expert"),
        P("section", None, None),
        P("section", None),
        P("section", "expert", None, None, None),
        P("section", "expert", None, None),
    )
    out_specs = (P("section", None, "expert"), P("section", None, "expert"))
    chosen = chain_body if mesh.shape["expert"] == 2 * DBLOCKS else body
    return jax.shard_map(chosen, mesh=mesh, in_specs=in_specs, out_specs=out_specs, check_vma=False)
```

```python
import functools

import jax
import jax.numpy as jnp
from jax import lax
from jax.experimental import pallas as pl
from jax.experimental.pallas import tpu as pltpu
from jax.sharding import PartitionSpec as P

DBLOCKS = 4
BF16 = jnp.bfloat16
F32 = jnp.float32
MIB = 1024 * 1024
PIECES = 2
ROWS, SMALL, ACT, FIRST, AHEAD_OUT, BEHIND_OUT = 20, 6, 10, 5.2, 3, 20


def shift(shard, axis, by):
    devices = lax.axis_size(axis)
    pairs = [(i, i + by) for i in range(devices) if 0 <= i + by < devices]
    return lax.ppermute(shard, axis, pairs)


def whole(array):
    return pl.BlockSpec(array.shape, functools.partial(lambda n, *_: (0,) * n, array.ndim))


def row_piece(array, c):
    parts, slots, half = array.shape
    return pl.BlockSpec((parts, slots // PIECES, half), lambda *_: (0, c, 0))


def call(kernel, micros, operands, after, out_shape, scalars=(), grid=(1,), in_specs=None, out_specs=None, scratch=(), limit=24, name=None):
    count, unread = len(scalars) + len(operands), len(after)

    def run(*refs):
        kernel(*refs[:count], *refs[count + unread :])

    if in_specs is None:
        in_specs = [whole(o) for o in operands]
    if out_specs is None:
        out_specs = jax.tree.map(whole, out_shape)
    return pl.pallas_call(
        run,
        compiler_params=pltpu.CompilerParams(vmem_limit_bytes=limit * MIB),
        cost_estimate=pl.CostEstimate(flops=int(micros * 1e9), bytes_accessed=1024, transcendentals=0),
        out_shape=out_shape,
        name=name,
        grid_spec=pltpu.PrefetchScalarGridSpec(
            num_scalar_prefetch=len(scalars),
            grid=grid,
            in_specs=[*in_specs, *[pl.BlockSpec(memory_space=pl.ANY)] * unread],
            out_specs=out_specs,
            scratch_shapes=list(scratch),
        ),
    )(*scalars, *operands, *after)


def cut_kernel(rows, out):
    out[...] = rows[...]


def cut_first_kernel(value, out):
    out[...] = value[: out.shape[0]]


def first_kernel(width, where, *refs):
    rows, (tile, out, joined) = refs[:-3], refs[-3:]

    @pl.when((pl.program_id(0) == 0) & (pl.program_id(1) == 0))
    def _():
        at = pl.multiple_of(where[1] * width, 128)
        other = pl.multiple_of((1 - where[1]) * width, 128)
        slots = rows[0].shape[0]
        for piece in range(len(rows) // 2):
            here = pl.ds(piece * slots, slots)
            joined[here, pl.ds(at, width)] = rows[2 * piece][...]
            joined[here, pl.ds(other, width)] = rows[2 * piece + 1][...]

    out[0] = lax.dot_general(
        joined[...], tile[0], (((1,), (1,)), ((), ())), preferred_element_type=F32
    ).astype(BF16)


def first_product(name, where, far, rows, weights, after):
    slots, width = rows[0].shape
    slots *= len(rows) // 2
    parts, units, features = weights.shape
    half = units // 2
    tile = min(256, half)
    steps = half // tile

    def tile_at(k, j, w):
        return (k, ((1 - w[0]) if far else w[0]) * steps + j, 0)

    return call(
        functools.partial(first_kernel, width),
        FIRST * parts,
        (*rows, weights),
        after,
        jax.ShapeDtypeStruct((parts, slots, half), BF16),
        scalars=(where,),
        grid=(parts, steps),
        in_specs=[*[whole(r) for r in rows], pl.BlockSpec((1, tile, features), tile_at)],
        out_specs=pl.BlockSpec((1, slots, tile), lambda k, j, w: (k, 0, j)),
        scratch=[pltpu.VMEM((slots, features), BF16)],
        name=name,
    )


def sum_kernel(mine, arrived, out):
    out[...] = (mine[...].astype(F32) + arrived[...].astype(F32)).astype(BF16)


def end_or_sum_kernel(where, at_end, mine, arrived, out):
    @pl.when(where[2] == 1)
    def _():
        parts = at_end.shape[0]
        out[:parts] = at_end[...]
        if parts < out.shape[0]:
            out[parts:] = jnp.zeros_like(out[parts:])

    @pl.when(where[2] == 0)
    def _():
        out[...] = (mine[...].astype(F32) + arrived[...].astype(F32)).astype(BF16)


def end_or_pass_kernel(where, at_end, passed, out):
    @pl.when(where[2] == 1)
    def _():
        out[...] = at_end[...]

    @pl.when(where[2] == 0)
    def _():
        out[...] = passed[...]


def ahead_act_kernel(near, arrived, out):
    gate = near[0].astype(F32) + arrived[0].astype(F32)
    up = near[1].astype(F32) + arrived[1].astype(F32)
    out[0] = (gate * jax.nn.sigmoid(gate) * up).astype(BF16)


def behind_act_kernel(near, arrived, near_e, arrived_e, scale, out):
    gate = near[0].astype(F32) + arrived[0].astype(F32)
    up = near[1].astype(F32) + arrived[1].astype(F32)
    expanded = (near_e[0].astype(F32) + arrived_e[0].astype(F32)) * scale[...]
    sig = jax.nn.sigmoid(gate)
    out[0] = (expanded * up * sig * (1.0 + gate * (1.0 - sig))).astype(BF16)
    out[1] = (expanded * gate * sig).astype(BF16)


def result_kernel(first, one, two, out):
    size = first.shape[0]
    out[:size] = first[...]
    out[size:] = (one[...].astype(F32) + two[...].astype(F32)).astype(BF16)


def second_kernel(scaled, where, act, one, two, three, *refs):
    scale, refs = (refs[0], refs[1:]) if scaled else (None, refs)
    weights, give, keep, joined, tiles, sems = refs
    kinds, _, half = act.shape
    _, _, units, width = tiles.shape
    copies = []
    for own in range(2):
        at = pl.multiple_of((where[1] if own else 1 - where[1]) * width, 128)
        copy = pltpu.make_async_copy(
            weights.at[:, :, pl.ds(at, width)], tiles.at[own], sems.at[own]
        )
        copy.start()
        copies.append(copy)

    def place(near, far):
        for kind in range(kinds):
            at = pl.multiple_of((2 * kind + where[0]) * half, 128)
            other = pl.multiple_of((2 * kind + 1 - where[0]) * half, 128)
            joined[:, pl.ds(at, half)] = near[kind]
            joined[:, pl.ds(other, half)] = far[kind]

    @pl.when(where[2] == 1)
    def _():
        place(act, three)

    @pl.when(where[2] == 0)
    def _():
        place(one, two)

    for own, out in enumerate((give, keep)):
        copies[own].wait()
        share = jnp.dot(
            joined[...], tiles[own].reshape(kinds * units, width), preferred_element_type=F32
        )
        if scaled:
            share = share * scale[...]
        out[...] = share.astype(BF16)


def second_product(name, where, values, scale, weights, after):
    kinds, units, features = weights.shape
    slots = values[0].shape[1]
    width = features // 2
    operands = [*values] + ([] if scale is None else [scale])
    share = jax.ShapeDtypeStruct((slots, width), BF16)
    return call(
        functools.partial(second_kernel, scale is not None),
        AHEAD_OUT if kinds == 1 else BEHIND_OUT,
        (*operands, weights),
        after,
        (share, share),
        scalars=(where,),
        in_specs=[*[whole(v) for v in operands], pl.BlockSpec(memory_space=pltpu.HBM)],
        scratch=[
            pltpu.VMEM((slots, kinds * units), BF16),
            pltpu.VMEM((2, kinds, units, width), BF16),
            pltpu.SemaphoreType.DMA((2,)),
        ],
        name=name,
    )


def chain_body(ahead_rows, behind_rows, behind_grad, route_scores, route_counts, gate_up, down_proj):
    height = ahead_rows.shape[1]
    gates = gate_up[0, 0]
    downs = down_proj[0]
    own = lax.axis_index("expert")
    sections = lax.axis_size("section")
    devices = 2 * DBLOCKS
    block, group = own // 2, own % 2
    near_half = (block >= DBLOCKS // 2).astype(jnp.int32)
    at_end = ((block == 0) | (block == DBLOCKS - 1)).astype(jnp.int32)
    where = jnp.stack([near_half, group, at_end])
    slot_ids = jnp.arange(height, dtype=jnp.int32)[None]
    live = slot_ids < route_counts[0][:, None]
    scales = jnp.where(live, route_scores[0], 0.0)[:, :, None]

    def between(value, to):
        pairs = [(q * 2 + f, to[q] * 2 + f) for q in range(DBLOCKS) for f in range(2) if to[q] is not None]
        return lax.ppermute(value, "expert", pairs)

    def outer(value):
        return between(value, (1, 0, 3, 2))

    def inward(value):
        return between(value, (1, None, None, 2))

    def outward(value):
        return between(value, (None, 0, 3, None))

    def middle(value):
        return between(value, (0, 2, 1, 3))

    def swapped(value):
        return lax.ppermute(value, "expert", [(i, i ^ 1) for i in range(devices)])

    def to_section(value, by, flip):
        pairs = [
            (s * devices + e, (s + by) * devices + (e ^ flip))
            for s in range(sections)
            if 0 <= s + by < sections
            for e in range(devices)
        ]
        return lax.ppermute(value, ("section", "expert"), pairs)

    recent = []

    def kernel_call(name, kernel, micros, operands, shape, scalars=()):
        specs, arrays = [], []
        for operand in operands:
            array, c = operand if isinstance(operand, tuple) else (operand, None)
            arrays.append(array)
            specs.append(whole(array) if c is None else row_piece(array, c))
        made = call(
            kernel,
            micros,
            arrays,
            list(recent),
            jax.ShapeDtypeStruct(shape, BF16),
            scalars,
            in_specs=specs,
            name=name,
        )
        recent[:] = [made]
        return made

    class Chain:
        def __init__(self, name, rows, weights, spreads):
            self.name = name
            self.rows, self.weights = rows, weights
            self.spreads = spreads
            self.pairs, self.far, self.near, self.act = {}, {}, {}, {}
            self.out, self.mid, self.one, self.back, self.third = {}, {}, {}, {}, {}

        def fetch(self, c):
            size, width = height // PIECES, self.rows.shape[1]
            rows = call(
                cut_kernel,
                SMALL if c else ROWS,
                (self.rows,),
                list(recent),
                jax.ShapeDtypeStruct((size, width), BF16),
                in_specs=[pl.BlockSpec((size, width), lambda i: (c, 0))],
                name=f"{self.name}_rows_{c}",
            )
            recent[:] = [rows]
            self.pairs[c] = rows, swapped(rows)

        def far_product(self, c):
            name = f"{self.name}_far_{c}"
            made = first_product(name, where, True, self.pairs[c], self.weights, list(recent))
            recent[:] = [made]
            self.far[c] = made

        def near_products(self):
            rows = [row for c in range(PIECES) for row in self.pairs[c]]
            made = first_product(f"{self.name}_near", where, False, rows, self.weights, list(recent))
            recent[:] = [made]
            self.near = {c: (made, c) for c in range(PIECES)}

        def near_sum(self, c):
            operands = (self.near[c], self.mid[c])
            return kernel_call(f"{self.name}_third_{c}", sum_kernel, SMALL, operands, self.far[c].shape)

        def first_hop(self, c):
            self.out[c] = outer(self.far[c]) if c == 0 else inward(self.far[c])

        def third_hop(self, c):
            self.third[c] = outward(self.near_sum(c))

        def merged_hop(self, c, first):
            operands = (first, self.near[c - 1], self.mid[c - 1])
            shape = self.far[0].shape
            self.out[c] = outer(
                kernel_call(f"{self.name}_outer_{c}", end_or_sum_kernel, SMALL, operands, shape, (where,))
            )
            self.third[c - 1] = self.out[c]

        def last_third_hop(self):
            self.third[PIECES - 1] = outer(self.near_sum(PIECES - 1))

        def middle_sum(self, c):
            mine = self.far[c]
            self.mid[c] = middle(
                kernel_call(
                    f"{self.name}_middle_{c}", sum_kernel, SMALL, (mine, self.out[c]), mine.shape
                )
            )

        def middle_pass(self, c):
            value = self.out[PIECES] if c == 0 else self.back[c]
            shape = (self.spreads, *value.shape[1:])
            value = kernel_call(f"{self.name}_first_{c}", cut_first_kernel, SMALL, (value,), shape)
            self.one[c] = value
            self.mid[PIECES + c] = middle(value)

        def outer_pass(self, c):
            value = self.mid[PIECES + c - 1]
            if c == PIECES:
                value = kernel_call(
                    f"{self.name}_back_{c}", cut_first_kernel, SMALL, (value,), value.shape
                )
            else:
                value = kernel_call(
                    f"{self.name}_back_{c}",
                    end_or_pass_kernel,
                    SMALL,
                    (self.act[c], value),
                    value.shape,
                    (where,),
                )
            self.back[c] = outer(value)

        def activated(self, c):
            return self.act[c], self.one[c], self.mid[PIECES + c], self.back[c + 1]

    ahead = Chain("ahead", ahead_rows[0], gates, 1)
    behind = Chain("behind", behind_rows[0], gates, 2)
    grad = Chain("grad", behind_grad[0], downs, 0)
    sent = {}

    def cut(array, c):
        size = height // PIECES
        return array[c * size : (c + 1) * size]

    def activate_ahead(c):
        near = ahead.near[c]
        operands = (near, ahead.third[c])
        ahead.act[c] = kernel_call(f"ahead_act_{c}", ahead_act_kernel, ACT, operands, (1, *ahead.far[c].shape[1:]))

    def activate_behind(c):
        near = behind.near[c]
        operands = (near, behind.third[c], grad.near[c], grad.third[c], cut(scales[1], c))
        behind.act[c] = kernel_call(f"behind_act_{c}", behind_act_kernel, ACT, operands, behind.far[c].shape)

    def output(chain, c):
        forward = chain is ahead
        scale = cut(scales[0], c) if forward else None
        weights = downs if forward else gates
        give, keep = second_product(
            f"{chain.name}_out_{c}", where, chain.activated(c), scale, weights, list(recent)
        )
        recent[:] = [give]
        return give, keep

    def finish_first(chain):
        give, keep = output(chain, 0)
        sent[chain, 0] = swapped(give), keep

    def send_first(chain):
        share, keep = sent[chain, 0]
        total = kernel_call(
            f"{chain.name}_shares", sum_kernel, SMALL, (keep, share), keep.shape
        )
        sent[chain, 0] = to_section(total, 1 if chain is ahead else -1, 0)

    def finish_last(chain):
        give, keep = output(chain, 1)
        by = 1 if chain is ahead else -1
        sent[chain, 1] = to_section(give, by, 1), to_section(keep, by, 0)

    def result(chain):
        operands = (sent[chain, 0], *sent[chain, 1])
        shape = (height, operands[0].shape[1])
        return kernel_call(f"{chain.name}_result", result_kernel, SMALL, operands, shape)[None]

    for chain in (behind, grad, ahead):
        chain.fetch(0)
    behind.far_product(0)
    behind.first_hop(0)
    behind.fetch(1)
    grad.far_product(0)
    grad.first_hop(0)
    ahead.far_product(0)
    ahead.first_hop(0)
    behind.middle_sum(0)
    grad.fetch(1)
    behind.far_product(1)
    behind.first_hop(1)
    grad.middle_sum(0)
    behind.near_products()
    behind.third_hop(0)
    ahead.fetch(1)
    behind.middle_sum(1)
    grad.far_product(1)
    grad.near_products()
    grad.merged_hop(1, grad.far[1])
    ahead.middle_sum(0)
    ahead.far_product(1)
    ahead.first_hop(1)
    ahead.near_products()
    ahead.third_hop(0)
    activate_behind(0)
    behind.merged_hop(2, behind.act[0])
    grad.middle_sum(1)
    ahead.middle_sum(1)
    activate_ahead(0)
    behind.middle_pass(0)
    grad.last_third_hop()
    ahead.merged_hop(2, ahead.act[0])
    activate_behind(1)
    behind.outer_pass(1)
    ahead.middle_pass(0)
    activate_ahead(1)
    behind.middle_pass(1)
    ahead.outer_pass(1)
    finish_first(behind)
    behind.outer_pass(2)
    ahead.middle_pass(1)
    finish_first(ahead)
    ahead.outer_pass(2)
    send_first(behind)
    finish_last(behind)
    finish_last(ahead)
    send_first(ahead)
    behind_sent = result(behind)
    ahead_sent = result(ahead)
    return ahead_sent, behind_sent


def body(ahead_rows, behind_rows, behind_grad, route_scores, route_counts, gate_up, down_proj):
    groups = lax.axis_size("expert")
    fgroups = groups // DBLOCKS
    low = [[q * fgroups + f for f in range(fgroups)] for q in range(DBLOCKS)]
    high = [[q * fgroups + f for q in range(DBLOCKS)] for f in range(fgroups)]
    height = ahead_rows.shape[1]
    weights_in = gate_up[0, 0]
    weights_out = down_proj[0, 0]
    units = weights_in.shape[1]
    part = units // DBLOCKS

    def wide(rows):
        return lax.all_gather(rows, "expert", axis_index_groups=low, axis=1, tiled=True)

    def reduced(partials):
        flat = partials.reshape(-1, partials.shape[-1])
        total = lax.psum_scatter(
            flat, "expert", axis_index_groups=high, scatter_dimension=0, tiled=True
        )
        return total.astype(F32).reshape(partials.shape[1:])

    def spread(values):
        return lax.all_gather(values, "expert", axis_index_groups=high, axis=0, tiled=False)

    def narrowed(values):
        return lax.psum_scatter(
            values.astype(BF16), "expert", axis_index_groups=low, scatter_dimension=1, tiled=True
        )

    slot_ids = jnp.arange(height, dtype=jnp.int32)
    scale_ahead = route_scores[0, 0] * (slot_ids < route_counts[0, 0]).astype(F32)
    scale_behind = route_scores[0, 1] * (slot_ids < route_counts[0, 1]).astype(F32)
    gates = weights_in.reshape(2, DBLOCKS, part, -1)
    downs = weights_out.reshape(DBLOCKS, part, -1)

    ahead_wide = wide(ahead_rows[0])
    pre_a = jnp.einsum("cd,kqfd->qkcf", ahead_wide, gates, preferred_element_type=F32).astype(BF16)
    sum_a = reduced(pre_a)
    hidden = (sum_a[0] * jax.nn.sigmoid(sum_a[0]) * sum_a[1]).astype(BF16)
    hidden_all = spread(hidden)

    behind_wide = wide(behind_rows[0])
    grad_wide = wide(behind_grad[0])
    pre_b = jnp.einsum("cd,kqfd->qkcf", behind_wide, gates, preferred_element_type=F32).astype(BF16)
    exp_b = jnp.einsum("cd,qfd->qcf", grad_wide, downs, preferred_element_type=F32).astype(BF16)
    sum_b = reduced(jnp.concatenate([pre_b, exp_b[:, None]], axis=1))
    gate, up, expanded = sum_b[0], sum_b[1], sum_b[2] * scale_behind[:, None]
    sig = jax.nn.sigmoid(gate)
    grad_gate = (expanded * up * sig * (1.0 + gate * (1.0 - sig))).astype(BF16)
    grad_up = (expanded * gate * sig).astype(BF16)
    grads_all = spread(jnp.stack([grad_gate, grad_up]))

    out_a = jnp.einsum("qcf,qfd->cd", hidden_all, downs, preferred_element_type=F32)
    ahead_out = (narrowed(out_a).astype(F32) * scale_ahead[:, None]).astype(BF16)
    moved_ahead = shift(ahead_out, "section", 1)
    out_b = jnp.einsum("qkcf,kqfd->cd", grads_all, gates, preferred_element_type=F32)
    behind_out = narrowed(out_b)
    moved_behind = shift(behind_out, "section", -1)
    return (moved_ahead[None], moved_behind[None])


def solution(mesh):
    in_specs = (
        P("section", None, "expert"),
        P("section", None, "expert"),
        P("section", None, "expert"),
        P("section", None, None),
        P("section", None),
        P("section", "expert", None, None, None),
        P("section", "expert", None, None),
    )
    out_specs = (P("section", None, "expert"), P("section", None, "expert"))
    chosen = chain_body if mesh.shape["expert"] == 2 * DBLOCKS else body
    return jax.shard_map(chosen, mesh=mesh, in_specs=in_specs, out_specs=out_specs, check_vma=False)
```

```python
import functools

import jax
import jax.numpy as jnp
from jax import lax
from jax.experimental import pallas as pl
from jax.experimental.pallas import tpu as pltpu
from jax.sharding import PartitionSpec as P

DBLOCKS = 4
BF16 = jnp.bfloat16
F32 = jnp.float32
MIB = 1024 * 1024
PIECES = 2
ROWS, SMALL, ACT, FIRST, AHEAD_OUT, BEHIND_OUT = 20, 6, 10, 5.2, 3, 20


def shift(shard, axis, by):
    devices = lax.axis_size(axis)
    pairs = [(i, i + by) for i in range(devices) if 0 <= i + by < devices]
    return lax.ppermute(shard, axis, pairs)


def whole(array):
    return pl.BlockSpec(array.shape, functools.partial(lambda n, *_: (0,) * n, array.ndim))


def row_piece(array, c):
    parts, slots, half = array.shape
    return pl.BlockSpec((parts, slots // PIECES, half), lambda *_: (0, c, 0))


def call(kernel, micros, operands, after, out_shape, grid=(1,), in_specs=None, out_specs=None, scratch=(), limit=24, name=None):
    count, unread = len(operands), len(after)

    def run(*refs):
        kernel(*refs[:count], *refs[count + unread :])

    if in_specs is None:
        in_specs = [whole(o) for o in operands]
    if out_specs is None:
        out_specs = jax.tree.map(whole, out_shape)
    return pl.pallas_call(
        run,
        compiler_params=pltpu.CompilerParams(vmem_limit_bytes=limit * MIB),
        cost_estimate=pl.CostEstimate(flops=int(micros * 1e9), bytes_accessed=1024, transcendentals=0),
        out_shape=out_shape,
        name=name,
        grid=grid,
        in_specs=[*in_specs, *[pl.BlockSpec(memory_space=pl.ANY)] * unread],
        out_specs=out_specs,
        scratch_shapes=list(scratch),
    )(*operands, *after)


def cut_kernel(rows, out):
    out[...] = rows[...]


def cut_first_kernel(value, out):
    out[...] = value[: out.shape[0]]


def position():
    own = lax.axis_index("expert")
    block = own // 2
    near = jnp.where(block >= DBLOCKS // 2, 1, 0)
    return near, own % 2, (block == 0) | (block == DBLOCKS - 1)


def first_kernel(far, *refs):
    rows, (weights, out, joined, tiles, sems) = refs[:-5], refs[-5:]
    near, group, _ = position()
    side = 1 - near if far else near
    parts, _, half = out.shape
    tile = tiles.shape[1]
    steps = half // tile
    copies = []
    for k in range(parts):
        for j in range(steps):
            n = k * steps + j
            at = pl.multiple_of((side * steps + j) * tile, tile)
            copy = pltpu.make_async_copy(weights.at[k, pl.ds(at, tile)], tiles.at[n], sems.at[n])
            copy.start()
            copies.append(copy)
    slots, width = rows[0].shape
    at = pl.multiple_of(group * width, 128)
    other = pl.multiple_of((1 - group) * width, 128)
    for piece in range(len(rows) // 2):
        here = pl.ds(piece * slots, slots)
        joined[here, pl.ds(at, width)] = rows[2 * piece][...]
        joined[here, pl.ds(other, width)] = rows[2 * piece + 1][...]
    for k in range(parts):
        for j in range(steps):
            n = k * steps + j
            copies[n].wait()
            out[k, :, j * tile : (j + 1) * tile] = lax.dot_general(
                joined[...], tiles[n], (((1,), (1,)), ((), ())), preferred_element_type=F32
            ).astype(BF16)


def first_product(name, far, rows, weights, after):
    slots, width = rows[0].shape
    slots *= len(rows) // 2
    parts, units, features = weights.shape
    half = units // 2
    tile = min(256, half)
    steps = half // tile
    return call(
        functools.partial(first_kernel, far),
        FIRST * parts,
        (*rows, weights),
        after,
        jax.ShapeDtypeStruct((parts, slots, half), BF16),
        in_specs=[*[whole(r) for r in rows], pl.BlockSpec(memory_space=pl.ANY)],
        scratch=[
            pltpu.VMEM((slots, features), BF16),
            pltpu.VMEM((parts * steps, tile, features), BF16),
            pltpu.SemaphoreType.DMA((parts * steps,)),
        ],
        name=name,
    )


def sum_kernel(mine, arrived, out):
    out[...] = (mine[...].astype(F32) + arrived[...].astype(F32)).astype(BF16)


def end_or_sum_kernel(at_end, mine, arrived, out):
    _, _, end = position()

    @pl.when(end)
    def _():
        parts = at_end.shape[0]
        out[:parts] = at_end[...]
        if parts < out.shape[0]:
            out[parts:] = jnp.zeros_like(out[parts:])

    @pl.when(jnp.logical_not(end))
    def _():
        out[...] = (mine[...].astype(F32) + arrived[...].astype(F32)).astype(BF16)


def end_or_pass_kernel(at_end, passed, out):
    _, _, end = position()

    @pl.when(end)
    def _():
        out[...] = at_end[...]

    @pl.when(jnp.logical_not(end))
    def _():
        out[...] = passed[...]


def ahead_act_kernel(near, arrived, out):
    gate = near[0].astype(F32) + arrived[0].astype(F32)
    up = near[1].astype(F32) + arrived[1].astype(F32)
    out[0] = (gate * jax.nn.sigmoid(gate) * up).astype(BF16)


def behind_act_kernel(near, arrived, near_e, arrived_e, scale, out):
    gate = near[0].astype(F32) + arrived[0].astype(F32)
    up = near[1].astype(F32) + arrived[1].astype(F32)
    expanded = (near_e[0].astype(F32) + arrived_e[0].astype(F32)) * scale[...]
    sig = jax.nn.sigmoid(gate)
    out[0] = (expanded * up * sig * (1.0 + gate * (1.0 - sig))).astype(BF16)
    out[1] = (expanded * gate * sig).astype(BF16)


def result_kernel(first, one, two, out):
    size = first.shape[0]
    out[:size] = first[...]
    out[size:] = (one[...].astype(F32) + two[...].astype(F32)).astype(BF16)


def second_kernel(scaled, act, one, two, three, *refs):
    scale, refs = (refs[0], refs[1:]) if scaled else (None, refs)
    weights, give, keep, joined, tiles, sems = refs
    near_half, group, end = position()
    kinds, _, half = act.shape
    _, _, units, width = tiles.shape
    copies = []
    for own in range(2):
        at = pl.multiple_of((group if own else 1 - group) * width, 128)
        copy = pltpu.make_async_copy(
            weights.at[:, :, pl.ds(at, width)], tiles.at[own], sems.at[own]
        )
        copy.start()
        copies.append(copy)

    def place(near, far):
        for kind in range(kinds):
            at = pl.multiple_of((2 * kind + near_half) * half, 128)
            other = pl.multiple_of((2 * kind + 1 - near_half) * half, 128)
            joined[:, pl.ds(at, half)] = near[kind]
            joined[:, pl.ds(other, half)] = far[kind]

    @pl.when(end)
    def _():
        place(act, three)

    @pl.when(jnp.logical_not(end))
    def _():
        place(one, two)

    for own, out in enumerate((give, keep)):
        copies[own].wait()
        share = jnp.dot(
            joined[...], tiles[own].reshape(kinds * units, width), preferred_element_type=F32
        )
        if scaled:
            share = share * scale[...]
        out[...] = share.astype(BF16)


def second_product(name, values, scale, weights, after):
    kinds, units, features = weights.shape
    slots = values[0].shape[1]
    width = features // 2
    operands = [*values] + ([] if scale is None else [scale])
    share = jax.ShapeDtypeStruct((slots, width), BF16)
    return call(
        functools.partial(second_kernel, scale is not None),
        AHEAD_OUT if kinds == 1 else BEHIND_OUT,
        (*operands, weights),
        after,
        (share, share),
        in_specs=[*[whole(v) for v in operands], pl.BlockSpec(memory_space=pl.ANY)],
        scratch=[
            pltpu.VMEM((slots, kinds * units), BF16),
            pltpu.VMEM((2, kinds, units, width), BF16),
            pltpu.SemaphoreType.DMA((2,)),
        ],
        name=name,
    )


def chain_body(ahead_rows, behind_rows, behind_grad, route_scores, route_counts, gate_up, down_proj):
    height = ahead_rows.shape[1]
    gates = gate_up[0, 0]
    downs = down_proj[0]
    sections = lax.axis_size("section")
    devices = 2 * DBLOCKS
    slot_ids = jnp.arange(height, dtype=jnp.int32)[None]
    live = slot_ids < route_counts[0][:, None]
    scales = jnp.where(live, route_scores[0], 0.0)[:, :, None]

    def between(value, to):
        pairs = [(q * 2 + f, to[q] * 2 + f) for q in range(DBLOCKS) for f in range(2) if to[q] is not None]
        return lax.ppermute(value, "expert", pairs)

    def outer(value):
        return between(value, (1, 0, 3, 2))

    def inward(value):
        return between(value, (1, None, None, 2))

    def outward(value):
        return between(value, (None, 0, 3, None))

    def middle(value):
        return between(value, (0, 2, 1, 3))

    def swapped(value):
        return lax.ppermute(value, "expert", [(i, i ^ 1) for i in range(devices)])

    def to_section(value, by, flip):
        pairs = [
            (s * devices + e, (s + by) * devices + (e ^ flip))
            for s in range(sections)
            if 0 <= s + by < sections
            for e in range(devices)
        ]
        return lax.ppermute(value, ("section", "expert"), pairs)

    recent = []

    def kernel_call(name, kernel, micros, operands, shape):
        specs, arrays = [], []
        for operand in operands:
            array, c = operand if isinstance(operand, tuple) else (operand, None)
            arrays.append(array)
            specs.append(whole(array) if c is None else row_piece(array, c))
        made = call(
            kernel,
            micros,
            arrays,
            list(recent),
            jax.ShapeDtypeStruct(shape, BF16),
            in_specs=specs,
            name=name,
        )
        recent[:] = [made]
        return made

    class Chain:
        def __init__(self, name, rows, weights, spreads):
            self.name = name
            self.rows, self.weights = rows, weights
            self.spreads = spreads
            self.pairs, self.far, self.near, self.act = {}, {}, {}, {}
            self.out, self.mid, self.one, self.back, self.third = {}, {}, {}, {}, {}

        def fetch(self, c):
            size, width = height // PIECES, self.rows.shape[1]
            rows = call(
                cut_kernel,
                SMALL if c else ROWS,
                (self.rows,),
                list(recent),
                jax.ShapeDtypeStruct((size, width), BF16),
                in_specs=[pl.BlockSpec((size, width), lambda i: (c, 0))],
                name=f"{self.name}_rows_{c}",
            )
            recent[:] = [rows]
            self.pairs[c] = rows, swapped(rows)

        def far_product(self, c):
            name = f"{self.name}_far_{c}"
            made = first_product(name, True, self.pairs[c], self.weights, list(recent))
            recent[:] = [made]
            self.far[c] = made

        def near_products(self):
            rows = [row for c in range(PIECES) for row in self.pairs[c]]
            made = first_product(f"{self.name}_near", False, rows, self.weights, list(recent))
            recent[:] = [made]
            self.near = {c: (made, c) for c in range(PIECES)}

        def near_sum(self, c):
            operands = (self.near[c], self.mid[c])
            return kernel_call(f"{self.name}_third_{c}", sum_kernel, SMALL, operands, self.far[c].shape)

        def first_hop(self, c):
            self.out[c] = outer(self.far[c]) if c == 0 else inward(self.far[c])

        def third_hop(self, c):
            self.third[c] = outward(self.near_sum(c))

        def merged_hop(self, c, first):
            operands = (first, self.near[c - 1], self.mid[c - 1])
            shape = self.far[0].shape
            self.out[c] = outer(
                kernel_call(f"{self.name}_outer_{c}", end_or_sum_kernel, SMALL, operands, shape)
            )
            self.third[c - 1] = self.out[c]

        def last_third_hop(self):
            self.third[PIECES - 1] = outer(self.near_sum(PIECES - 1))

        def middle_sum(self, c):
            mine = self.far[c]
            self.mid[c] = middle(
                kernel_call(
                    f"{self.name}_middle_{c}", sum_kernel, SMALL, (mine, self.out[c]), mine.shape
                )
            )

        def middle_pass(self, c):
            value = self.out[PIECES] if c == 0 else self.back[c]
            shape = (self.spreads, *value.shape[1:])
            value = kernel_call(f"{self.name}_first_{c}", cut_first_kernel, SMALL, (value,), shape)
            self.one[c] = value
            self.mid[PIECES + c] = middle(value)

        def outer_pass(self, c):
            value = self.mid[PIECES + c - 1]
            if c == PIECES:
                value = kernel_call(
                    f"{self.name}_back_{c}", cut_first_kernel, SMALL, (value,), value.shape
                )
            else:
                value = kernel_call(
                    f"{self.name}_back_{c}",
                    end_or_pass_kernel,
                    SMALL,
                    (self.act[c], value),
                    value.shape,
                )
            self.back[c] = outer(value)

        def activated(self, c):
            return self.act[c], self.one[c], self.mid[PIECES + c], self.back[c + 1]

    ahead = Chain("ahead", ahead_rows[0], gates, 1)
    behind = Chain("behind", behind_rows[0], gates, 2)
    grad = Chain("grad", behind_grad[0], downs, 0)
    sent = {}

    def cut(array, c):
        size = height // PIECES
        return array[c * size : (c + 1) * size]

    def activate_ahead(c):
        near = ahead.near[c]
        operands = (near, ahead.third[c])
        ahead.act[c] = kernel_call(f"ahead_act_{c}", ahead_act_kernel, ACT, operands, (1, *ahead.far[c].shape[1:]))

    def activate_behind(c):
        near = behind.near[c]
        operands = (near, behind.third[c], grad.near[c], grad.third[c], cut(scales[1], c))
        behind.act[c] = kernel_call(f"behind_act_{c}", behind_act_kernel, ACT, operands, behind.far[c].shape)

    def output(chain, c):
        forward = chain is ahead
        scale = cut(scales[0], c) if forward else None
        weights = downs if forward else gates
        give, keep = second_product(
            f"{chain.name}_out_{c}", chain.activated(c), scale, weights, list(recent)
        )
        recent[:] = [give]
        return give, keep

    def finish_first(chain):
        give, keep = output(chain, 0)
        sent[chain, 0] = swapped(give), keep

    def send_first(chain):
        share, keep = sent[chain, 0]
        total = kernel_call(
            f"{chain.name}_shares", sum_kernel, SMALL, (keep, share), keep.shape
        )
        sent[chain, 0] = to_section(total, 1 if chain is ahead else -1, 0)

    def finish_last(chain):
        give, keep = output(chain, 1)
        by = 1 if chain is ahead else -1
        sent[chain, 1] = to_section(give, by, 1), to_section(keep, by, 0)

    def result(chain):
        operands = (sent[chain, 0], *sent[chain, 1])
        shape = (height, operands[0].shape[1])
        return kernel_call(f"{chain.name}_result", result_kernel, SMALL, operands, shape)[None]

    for chain in (behind, grad, ahead):
        chain.fetch(0)
    behind.far_product(0)
    behind.first_hop(0)
    behind.fetch(1)
    grad.far_product(0)
    grad.first_hop(0)
    ahead.far_product(0)
    ahead.first_hop(0)
    behind.middle_sum(0)
    grad.fetch(1)
    grad.middle_sum(0)
    behind.far_product(1)
    behind.near_products()
    behind.merged_hop(1, behind.far[1])
    ahead.fetch(1)
    ahead.middle_sum(0)
    grad.far_product(1)
    grad.near_products()
    grad.merged_hop(1, grad.far[1])
    ahead.far_product(1)
    behind.middle_sum(1)
    ahead.near_products()
    ahead.merged_hop(1, ahead.far[1])
    grad.middle_sum(1)
    activate_behind(0)
    behind.merged_hop(2, behind.act[0])
    ahead.middle_sum(1)
    activate_ahead(0)
    grad.last_third_hop()
    behind.middle_pass(0)
    ahead.merged_hop(2, ahead.act[0])
    activate_behind(1)
    behind.outer_pass(1)
    ahead.middle_pass(0)
    activate_ahead(1)
    behind.middle_pass(1)
    ahead.outer_pass(1)
    finish_first(behind)
    behind.outer_pass(2)
    ahead.middle_pass(1)
    finish_first(ahead)
    ahead.outer_pass(2)
    send_first(behind)
    finish_last(behind)
    finish_last(ahead)
    send_first(ahead)
    behind_sent = result(behind)
    ahead_sent = result(ahead)
    return ahead_sent, behind_sent


def body(ahead_rows, behind_rows, behind_grad, route_scores, route_counts, gate_up, down_proj):
    groups = lax.axis_size("expert")
    fgroups = groups // DBLOCKS
    low = [[q * fgroups + f for f in range(fgroups)] for q in range(DBLOCKS)]
    high = [[q * fgroups + f for q in range(DBLOCKS)] for f in range(fgroups)]
    height = ahead_rows.shape[1]
    weights_in = gate_up[0, 0]
    weights_out = down_proj[0, 0]
    units = weights_in.shape[1]
    part = units // DBLOCKS

    def wide(rows):
        return lax.all_gather(rows, "expert", axis_index_groups=low, axis=1, tiled=True)

    def reduced(partials):
        flat = partials.reshape(-1, partials.shape[-1])
        total = lax.psum_scatter(
            flat, "expert", axis_index_groups=high, scatter_dimension=0, tiled=True
        )
        return total.astype(F32).reshape(partials.shape[1:])

    def spread(values):
        return lax.all_gather(values, "expert", axis_index_groups=high, axis=0, tiled=False)

    def narrowed(values):
        return lax.psum_scatter(
            values.astype(BF16), "expert", axis_index_groups=low, scatter_dimension=1, tiled=True
        )

    slot_ids = jnp.arange(height, dtype=jnp.int32)
    scale_ahead = route_scores[0, 0] * (slot_ids < route_counts[0, 0]).astype(F32)
    scale_behind = route_scores[0, 1] * (slot_ids < route_counts[0, 1]).astype(F32)
    gates = weights_in.reshape(2, DBLOCKS, part, -1)
    downs = weights_out.reshape(DBLOCKS, part, -1)

    ahead_wide = wide(ahead_rows[0])
    pre_a = jnp.einsum("cd,kqfd->qkcf", ahead_wide, gates, preferred_element_type=F32).astype(BF16)
    sum_a = reduced(pre_a)
    hidden = (sum_a[0] * jax.nn.sigmoid(sum_a[0]) * sum_a[1]).astype(BF16)
    hidden_all = spread(hidden)

    behind_wide = wide(behind_rows[0])
    grad_wide = wide(behind_grad[0])
    pre_b = jnp.einsum("cd,kqfd->qkcf", behind_wide, gates, preferred_element_type=F32).astype(BF16)
    exp_b = jnp.einsum("cd,qfd->qcf", grad_wide, downs, preferred_element_type=F32).astype(BF16)
    sum_b = reduced(jnp.concatenate([pre_b, exp_b[:, None]], axis=1))
    gate, up, expanded = sum_b[0], sum_b[1], sum_b[2] * scale_behind[:, None]
    sig = jax.nn.sigmoid(gate)
    grad_gate = (expanded * up * sig * (1.0 + gate * (1.0 - sig))).astype(BF16)
    grad_up = (expanded * gate * sig).astype(BF16)
    grads_all = spread(jnp.stack([grad_gate, grad_up]))

    out_a = jnp.einsum("qcf,qfd->cd", hidden_all, downs, preferred_element_type=F32)
    ahead_out = (narrowed(out_a).astype(F32) * scale_ahead[:, None]).astype(BF16)
    moved_ahead = shift(ahead_out, "section", 1)
    out_b = jnp.einsum("qkcf,kqfd->cd", grads_all, gates, preferred_element_type=F32)
    behind_out = narrowed(out_b)
    moved_behind = shift(behind_out, "section", -1)
    return (moved_ahead[None], moved_behind[None])


def solution(mesh):
    in_specs = (
        P("section", None, "expert"),
        P("section", None, "expert"),
        P("section", None, "expert"),
        P("section", None, None),
        P("section", None),
        P("section", "expert", None, None, None),
        P("section", "expert", None, None),
    )
    out_specs = (P("section", None, "expert"), P("section", None, "expert"))
    chosen = chain_body if mesh.shape["expert"] == 2 * DBLOCKS else body
    return jax.shard_map(chosen, mesh=mesh, in_specs=in_specs, out_specs=out_specs, check_vma=False)
```

```python
import functools

import jax
import jax.numpy as jnp
from jax import lax
from jax.experimental import pallas as pl
from jax.experimental.pallas import tpu as pltpu
from jax.sharding import PartitionSpec as P

DBLOCKS = 4
BF16 = jnp.bfloat16
F32 = jnp.float32
MIB = 1024 * 1024
PIECES = 2
ROWS, SMALL, ACT, FIRST, AHEAD_OUT, BEHIND_OUT = 20, 6, 10, 5.2, 3, 20


def shift(shard, axis, by):
    devices = lax.axis_size(axis)
    pairs = [(i, i + by) for i in range(devices) if 0 <= i + by < devices]
    return lax.ppermute(shard, axis, pairs)


def whole(array):
    return pl.BlockSpec(array.shape, functools.partial(lambda n, *_: (0,) * n, array.ndim))


def row_piece(array, c):
    parts, slots, half = array.shape
    return pl.BlockSpec((parts, slots // PIECES, half), lambda *_: (0, c, 0))


def call(kernel, micros, operands, after, out_shape, grid=(1,), in_specs=None, out_specs=None, scratch=(), limit=24, name=None):
    count, unread = len(operands), len(after)

    def run(*refs):
        kernel(*refs[:count], *refs[count + unread :])

    if in_specs is None:
        in_specs = [whole(o) for o in operands]
    if out_specs is None:
        out_specs = jax.tree.map(whole, out_shape)
    return pl.pallas_call(
        run,
        compiler_params=pltpu.CompilerParams(vmem_limit_bytes=limit * MIB),
        cost_estimate=pl.CostEstimate(flops=int(micros * 1e9), bytes_accessed=1024, transcendentals=0),
        out_shape=out_shape,
        name=name,
        grid=grid,
        in_specs=[*in_specs, *[pl.BlockSpec(memory_space=pl.ANY)] * unread],
        out_specs=out_specs,
        scratch_shapes=list(scratch),
    )(*operands, *after)


def cut_kernel(rows, out):
    out[...] = rows[...]


def cut_first_kernel(value, out):
    out[...] = value[: out.shape[0]]


def position():
    own = lax.axis_index("expert")
    block = own // 2
    near = jnp.where(block >= DBLOCKS // 2, 1, 0)
    return near, own % 2, (block == 0) | (block == DBLOCKS - 1)


def first_kernel(far, *refs):
    rows, (weights, out, joined) = refs[:-3], refs[-3:]
    near, group, _ = position()
    side = 1 - near if far else near
    parts, _, half = out.shape
    slots, width = rows[0].shape
    at = pl.multiple_of(group * width, 128)
    other = pl.multiple_of((1 - group) * width, 128)
    for piece in range(len(rows) // 2):
        here = pl.ds(piece * slots, slots)
        joined[here, pl.ds(at, width)] = rows[2 * piece][...]
        joined[here, pl.ds(other, width)] = rows[2 * piece + 1][...]
    tile = min(256, half)
    for k in range(parts):
        for j in range(half // tile):
            at = pl.multiple_of(side * half + j * tile, tile)
            out[k, :, j * tile : (j + 1) * tile] = lax.dot_general(
                joined[...],
                weights[k, pl.ds(at, tile)],
                (((1,), (1,)), ((), ())),
                preferred_element_type=F32,
            ).astype(BF16)


def first_product(name, far, rows, weights, after):
    slots = rows[0].shape[0] * len(rows) // 2
    parts, units, features = weights.shape
    return call(
        functools.partial(first_kernel, far),
        FIRST * parts,
        (*rows, weights),
        after,
        jax.ShapeDtypeStruct((parts, slots, units // 2), BF16),
        in_specs=[*[whole(r) for r in rows], pl.BlockSpec(memory_space=pltpu.VMEM)],
        scratch=[pltpu.VMEM((slots, features), BF16)],
        name=name,
    )


def sum_kernel(mine, arrived, out):
    out[...] = (mine[...].astype(F32) + arrived[...].astype(F32)).astype(BF16)


def end_or_sum_kernel(at_end, mine, arrived, out):
    _, _, end = position()

    @pl.when(end)
    def _():
        parts = at_end.shape[0]
        out[:parts] = at_end[...]
        if parts < out.shape[0]:
            out[parts:] = jnp.zeros_like(out[parts:])

    @pl.when(jnp.logical_not(end))
    def _():
        out[...] = (mine[...].astype(F32) + arrived[...].astype(F32)).astype(BF16)


def end_or_pass_kernel(at_end, passed, out):
    _, _, end = position()

    @pl.when(end)
    def _():
        out[...] = at_end[...]

    @pl.when(jnp.logical_not(end))
    def _():
        out[...] = passed[...]


def ahead_act_kernel(near, arrived, out):
    gate = near[0].astype(F32) + arrived[0].astype(F32)
    up = near[1].astype(F32) + arrived[1].astype(F32)
    out[0] = (gate * jax.nn.sigmoid(gate) * up).astype(BF16)


def behind_act_kernel(near, arrived, near_e, arrived_e, scale, out):
    gate = near[0].astype(F32) + arrived[0].astype(F32)
    up = near[1].astype(F32) + arrived[1].astype(F32)
    expanded = (near_e[0].astype(F32) + arrived_e[0].astype(F32)) * scale[...]
    sig = jax.nn.sigmoid(gate)
    out[0] = (expanded * up * sig * (1.0 + gate * (1.0 - sig))).astype(BF16)
    out[1] = (expanded * gate * sig).astype(BF16)


def result_kernel(first, one, two, out):
    size = first.shape[0]
    out[:size] = first[...]
    out[size:] = (one[...].astype(F32) + two[...].astype(F32)).astype(BF16)


def second_kernel(scaled, act, one, two, three, *refs):
    scale, refs = (refs[0], refs[1:]) if scaled else (None, refs)
    weights, give, keep, joined = refs
    near_half, group, end = position()
    kinds, _, half = act.shape
    units = weights.shape[1]
    width = give.shape[1]

    def place(near, far):
        for kind in range(kinds):
            at = pl.multiple_of((2 * kind + near_half) * half, 128)
            other = pl.multiple_of((2 * kind + 1 - near_half) * half, 128)
            joined[:, pl.ds(at, half)] = near[kind]
            joined[:, pl.ds(other, half)] = far[kind]

    @pl.when(end)
    def _():
        place(act, three)

    @pl.when(jnp.logical_not(end))
    def _():
        place(one, two)

    for side, out in ((1 - group, give), (group, keep)):
        at = pl.multiple_of(side * width, 128)
        tile = weights[:, :, pl.ds(at, width)].reshape(kinds * units, width)
        share = jnp.dot(joined[...], tile, preferred_element_type=F32)
        if scaled:
            share = share * scale[...]
        out[...] = share.astype(BF16)


def second_product(name, values, scale, weights, after):
    kinds, units, features = weights.shape
    slots = values[0].shape[1]
    operands = [*values] + ([] if scale is None else [scale])
    share = jax.ShapeDtypeStruct((slots, features // 2), BF16)
    return call(
        functools.partial(second_kernel, scale is not None),
        AHEAD_OUT if kinds == 1 else BEHIND_OUT,
        (*operands, weights),
        after,
        (share, share),
        in_specs=[*[whole(v) for v in operands], pl.BlockSpec(memory_space=pltpu.VMEM)],
        scratch=[pltpu.VMEM((slots, kinds * units), BF16)],
        name=name,
    )


def chain_body(ahead_rows, behind_rows, behind_grad, route_scores, route_counts, gate_up, down_proj):
    height = ahead_rows.shape[1]
    gates = gate_up[0, 0]
    downs = down_proj[0]
    sections = lax.axis_size("section")
    devices = 2 * DBLOCKS
    slot_ids = jnp.arange(height, dtype=jnp.int32)[None]
    live = slot_ids < route_counts[0][:, None]
    scales = jnp.where(live, route_scores[0], 0.0)[:, :, None]

    def between(value, to):
        pairs = [(q * 2 + f, to[q] * 2 + f) for q in range(DBLOCKS) for f in range(2) if to[q] is not None]
        return lax.ppermute(value, "expert", pairs)

    def outer(value):
        return between(value, (1, 0, 3, 2))

    def inward(value):
        return between(value, (1, None, None, 2))

    def outward(value):
        return between(value, (None, 0, 3, None))

    def middle(value):
        return between(value, (0, 2, 1, 3))

    def swapped(value):
        return lax.ppermute(value, "expert", [(i, i ^ 1) for i in range(devices)])

    def to_section(value, by, flip):
        pairs = [
            (s * devices + e, (s + by) * devices + (e ^ flip))
            for s in range(sections)
            if 0 <= s + by < sections
            for e in range(devices)
        ]
        return lax.ppermute(value, ("section", "expert"), pairs)

    recent = []

    def kernel_call(name, kernel, micros, operands, shape):
        specs, arrays = [], []
        for operand in operands:
            array, c = operand if isinstance(operand, tuple) else (operand, None)
            arrays.append(array)
            specs.append(whole(array) if c is None else row_piece(array, c))
        made = call(
            kernel,
            micros,
            arrays,
            list(recent),
            jax.ShapeDtypeStruct(shape, BF16),
            in_specs=specs,
            name=name,
        )
        recent[:] = [made]
        return made

    class Chain:
        def __init__(self, name, rows, weights, spreads):
            self.name = name
            self.rows, self.weights = rows, weights
            self.spreads = spreads
            self.pairs, self.far, self.near, self.act = {}, {}, {}, {}
            self.out, self.mid, self.one, self.back, self.third = {}, {}, {}, {}, {}

        def fetch(self, c):
            size, width = height // PIECES, self.rows.shape[1]
            rows = call(
                cut_kernel,
                SMALL if c else ROWS,
                (self.rows,),
                list(recent),
                jax.ShapeDtypeStruct((size, width), BF16),
                in_specs=[pl.BlockSpec((size, width), lambda i: (c, 0))],
                name=f"{self.name}_rows_{c}",
            )
            recent[:] = [rows]
            self.pairs[c] = rows, swapped(rows)

        def far_product(self, c):
            name = f"{self.name}_far_{c}"
            made = first_product(name, True, self.pairs[c], self.weights, list(recent))
            recent[:] = [made]
            self.far[c] = made

        def near_products(self):
            rows = [row for c in range(PIECES) for row in self.pairs[c]]
            made = first_product(f"{self.name}_near", False, rows, self.weights, list(recent))
            recent[:] = [made]
            self.near = {c: (made, c) for c in range(PIECES)}

        def near_sum(self, c):
            operands = (self.near[c], self.mid[c])
            return kernel_call(f"{self.name}_third_{c}", sum_kernel, SMALL, operands, self.far[c].shape)

        def first_hop(self, c):
            self.out[c] = outer(self.far[c]) if c == 0 else inward(self.far[c])

        def third_hop(self, c):
            self.third[c] = outward(self.near_sum(c))

        def merged_hop(self, c, first):
            operands = (first, self.near[c - 1], self.mid[c - 1])
            shape = self.far[0].shape
            self.out[c] = outer(
                kernel_call(f"{self.name}_outer_{c}", end_or_sum_kernel, SMALL, operands, shape)
            )
            self.third[c - 1] = self.out[c]

        def last_third_hop(self):
            self.third[PIECES - 1] = outer(self.near_sum(PIECES - 1))

        def middle_sum(self, c):
            mine = self.far[c]
            self.mid[c] = middle(
                kernel_call(
                    f"{self.name}_middle_{c}", sum_kernel, SMALL, (mine, self.out[c]), mine.shape
                )
            )

        def middle_pass(self, c):
            value = self.out[PIECES] if c == 0 else self.back[c]
            shape = (self.spreads, *value.shape[1:])
            value = kernel_call(f"{self.name}_first_{c}", cut_first_kernel, SMALL, (value,), shape)
            self.one[c] = value
            self.mid[PIECES + c] = middle(value)

        def outer_pass(self, c):
            value = self.mid[PIECES + c - 1]
            if c == PIECES:
                value = kernel_call(
                    f"{self.name}_back_{c}", cut_first_kernel, SMALL, (value,), value.shape
                )
            else:
                value = kernel_call(
                    f"{self.name}_back_{c}",
                    end_or_pass_kernel,
                    SMALL,
                    (self.act[c], value),
                    value.shape,
                )
            self.back[c] = outer(value)

        def activated(self, c):
            return self.act[c], self.one[c], self.mid[PIECES + c], self.back[c + 1]

    ahead = Chain("ahead", ahead_rows[0], gates, 1)
    behind = Chain("behind", behind_rows[0], gates, 2)
    grad = Chain("grad", behind_grad[0], downs, 0)
    sent = {}

    def cut(array, c):
        size = height // PIECES
        return array[c * size : (c + 1) * size]

    def activate_ahead(c):
        near = ahead.near[c]
        operands = (near, ahead.third[c])
        ahead.act[c] = kernel_call(f"ahead_act_{c}", ahead_act_kernel, ACT, operands, (1, *ahead.far[c].shape[1:]))

    def activate_behind(c):
        near = behind.near[c]
        operands = (near, behind.third[c], grad.near[c], grad.third[c], cut(scales[1], c))
        behind.act[c] = kernel_call(f"behind_act_{c}", behind_act_kernel, ACT, operands, behind.far[c].shape)

    def output(chain, c):
        forward = chain is ahead
        scale = cut(scales[0], c) if forward else None
        weights = downs if forward else gates
        give, keep = second_product(
            f"{chain.name}_out_{c}", chain.activated(c), scale, weights, list(recent)
        )
        recent[:] = [give]
        return give, keep

    def finish_first(chain):
        give, keep = output(chain, 0)
        sent[chain, 0] = swapped(give), keep

    def send_first(chain):
        share, keep = sent[chain, 0]
        total = kernel_call(
            f"{chain.name}_shares", sum_kernel, SMALL, (keep, share), keep.shape
        )
        sent[chain, 0] = to_section(total, 1 if chain is ahead else -1, 0)

    def finish_last(chain):
        give, keep = output(chain, 1)
        by = 1 if chain is ahead else -1
        sent[chain, 1] = to_section(give, by, 1), to_section(keep, by, 0)

    def result(chain):
        operands = (sent[chain, 0], *sent[chain, 1])
        shape = (height, operands[0].shape[1])
        return kernel_call(f"{chain.name}_result", result_kernel, SMALL, operands, shape)[None]

    for chain in (behind, grad, ahead):
        chain.fetch(0)
    behind.far_product(0)
    behind.first_hop(0)
    behind.fetch(1)
    grad.far_product(0)
    grad.first_hop(0)
    ahead.far_product(0)
    ahead.first_hop(0)
    behind.middle_sum(0)
    grad.fetch(1)
    grad.middle_sum(0)
    behind.far_product(1)
    behind.near_products()
    behind.merged_hop(1, behind.far[1])
    ahead.fetch(1)
    ahead.middle_sum(0)
    grad.far_product(1)
    grad.near_products()
    grad.merged_hop(1, grad.far[1])
    ahead.far_product(1)
    behind.middle_sum(1)
    ahead.near_products()
    ahead.merged_hop(1, ahead.far[1])
    grad.middle_sum(1)
    activate_behind(0)
    behind.merged_hop(2, behind.act[0])
    ahead.middle_sum(1)
    activate_ahead(0)
    grad.last_third_hop()
    behind.middle_pass(0)
    ahead.merged_hop(2, ahead.act[0])
    activate_behind(1)
    behind.outer_pass(1)
    ahead.middle_pass(0)
    activate_ahead(1)
    behind.middle_pass(1)
    ahead.outer_pass(1)
    finish_first(behind)
    behind.outer_pass(2)
    ahead.middle_pass(1)
    finish_first(ahead)
    ahead.outer_pass(2)
    send_first(behind)
    finish_last(behind)
    finish_last(ahead)
    send_first(ahead)
    behind_sent = result(behind)
    ahead_sent = result(ahead)
    return ahead_sent, behind_sent


def body(ahead_rows, behind_rows, behind_grad, route_scores, route_counts, gate_up, down_proj):
    groups = lax.axis_size("expert")
    fgroups = groups // DBLOCKS
    low = [[q * fgroups + f for f in range(fgroups)] for q in range(DBLOCKS)]
    high = [[q * fgroups + f for q in range(DBLOCKS)] for f in range(fgroups)]
    height = ahead_rows.shape[1]
    weights_in = gate_up[0, 0]
    weights_out = down_proj[0, 0]
    units = weights_in.shape[1]
    part = units // DBLOCKS

    def wide(rows):
        return lax.all_gather(rows, "expert", axis_index_groups=low, axis=1, tiled=True)

    def reduced(partials):
        flat = partials.reshape(-1, partials.shape[-1])
        total = lax.psum_scatter(
            flat, "expert", axis_index_groups=high, scatter_dimension=0, tiled=True
        )
        return total.astype(F32).reshape(partials.shape[1:])

    def spread(values):
        return lax.all_gather(values, "expert", axis_index_groups=high, axis=0, tiled=False)

    def narrowed(values):
        return lax.psum_scatter(
            values.astype(BF16), "expert", axis_index_groups=low, scatter_dimension=1, tiled=True
        )

    slot_ids = jnp.arange(height, dtype=jnp.int32)
    scale_ahead = route_scores[0, 0] * (slot_ids < route_counts[0, 0]).astype(F32)
    scale_behind = route_scores[0, 1] * (slot_ids < route_counts[0, 1]).astype(F32)
    gates = weights_in.reshape(2, DBLOCKS, part, -1)
    downs = weights_out.reshape(DBLOCKS, part, -1)

    ahead_wide = wide(ahead_rows[0])
    pre_a = jnp.einsum("cd,kqfd->qkcf", ahead_wide, gates, preferred_element_type=F32).astype(BF16)
    sum_a = reduced(pre_a)
    hidden = (sum_a[0] * jax.nn.sigmoid(sum_a[0]) * sum_a[1]).astype(BF16)
    hidden_all = spread(hidden)

    behind_wide = wide(behind_rows[0])
    grad_wide = wide(behind_grad[0])
    pre_b = jnp.einsum("cd,kqfd->qkcf", behind_wide, gates, preferred_element_type=F32).astype(BF16)
    exp_b = jnp.einsum("cd,qfd->qcf", grad_wide, downs, preferred_element_type=F32).astype(BF16)
    sum_b = reduced(jnp.concatenate([pre_b, exp_b[:, None]], axis=1))
    gate, up, expanded = sum_b[0], sum_b[1], sum_b[2] * scale_behind[:, None]
    sig = jax.nn.sigmoid(gate)
    grad_gate = (expanded * up * sig * (1.0 + gate * (1.0 - sig))).astype(BF16)
    grad_up = (expanded * gate * sig).astype(BF16)
    grads_all = spread(jnp.stack([grad_gate, grad_up]))

    out_a = jnp.einsum("qcf,qfd->cd", hidden_all, downs, preferred_element_type=F32)
    ahead_out = (narrowed(out_a).astype(F32) * scale_ahead[:, None]).astype(BF16)
    moved_ahead = shift(ahead_out, "section", 1)
    out_b = jnp.einsum("qkcf,kqfd->cd", grads_all, gates, preferred_element_type=F32)
    behind_out = narrowed(out_b)
    moved_behind = shift(behind_out, "section", -1)
    return (moved_ahead[None], moved_behind[None])


def solution(mesh):
    in_specs = (
        P("section", None, "expert"),
        P("section", None, "expert"),
        P("section", None, "expert"),
        P("section", None, None),
        P("section", None),
        P("section", "expert", None, None, None),
        P("section", "expert", None, None),
    )
    out_specs = (P("section", None, "expert"), P("section", None, "expert"))
    chosen = chain_body if mesh.shape["expert"] == 2 * DBLOCKS else body
    return jax.shard_map(chosen, mesh=mesh, in_specs=in_specs, out_specs=out_specs, check_vma=False)
```

```python
import functools

import jax
import jax.numpy as jnp
from jax import lax
from jax.experimental import pallas as pl
from jax.experimental.pallas import tpu as pltpu
from jax.sharding import PartitionSpec as P

DBLOCKS = 4
BF16 = jnp.bfloat16
F32 = jnp.float32
MIB = 1024 * 1024
PIECES = 2
ROWS, SMALL, ACT, FIRST, AHEAD_OUT, BEHIND_OUT = 20, 6, 10, 5.2, 3, 20


def shift(shard, axis, by):
    devices = lax.axis_size(axis)
    pairs = [(i, i + by) for i in range(devices) if 0 <= i + by < devices]
    return lax.ppermute(shard, axis, pairs)


def whole(array):
    return pl.BlockSpec(array.shape, functools.partial(lambda n, *_: (0,) * n, array.ndim))


def row_piece(array, c):
    parts, slots, half = array.shape
    return pl.BlockSpec((parts, slots // PIECES, half), lambda *_: (0, c, 0))


def call(kernel, micros, operands, after, out_shape, grid=(1,), in_specs=None, out_specs=None, scratch=(), limit=24, name=None):
    count, unread = len(operands), len(after)

    def run(*refs):
        kernel(*refs[:count], *refs[count + unread :])

    if in_specs is None:
        in_specs = [whole(o) for o in operands]
    if out_specs is None:
        out_specs = jax.tree.map(whole, out_shape)
    return pl.pallas_call(
        run,
        compiler_params=pltpu.CompilerParams(vmem_limit_bytes=limit * MIB),
        cost_estimate=pl.CostEstimate(flops=int(micros * 1e9), bytes_accessed=1024, transcendentals=0),
        out_shape=out_shape,
        name=name,
        grid=grid,
        in_specs=[*in_specs, *[pl.BlockSpec(memory_space=pl.ANY)] * unread],
        out_specs=out_specs,
        scratch_shapes=list(scratch),
    )(*operands, *after)


def cut_kernel(rows, out):
    out[...] = rows[...]


def touch_kernel(gates, downs, out):
    out[...] = gates[0, :16, :128] + downs[0, :16, :128]


def cut_first_kernel(value, out):
    out[...] = value[: out.shape[0]]


def position():
    own = lax.axis_index("expert")
    block = own // 2
    near = jnp.where(block >= DBLOCKS // 2, 1, 0)
    return near, own % 2, (block == 0) | (block == DBLOCKS - 1)


def first_kernel(far, *refs):
    rows, (weights, out, joined) = refs[:-3], refs[-3:]
    near, group, _ = position()
    side = 1 - near if far else near
    parts, _, half = out.shape
    slots, width = rows[0].shape
    at = pl.multiple_of(group * width, 128)
    other = pl.multiple_of((1 - group) * width, 128)
    for piece in range(len(rows) // 2):
        here = pl.ds(piece * slots, slots)
        joined[here, pl.ds(at, width)] = rows[2 * piece][...]
        joined[here, pl.ds(other, width)] = rows[2 * piece + 1][...]
    tile = min(256, half)
    for k in range(parts):
        for j in range(half // tile):
            at = pl.multiple_of(side * half + j * tile, tile)
            out[k, :, j * tile : (j + 1) * tile] = lax.dot_general(
                joined[...],
                weights[k, pl.ds(at, tile)],
                (((1,), (1,)), ((), ())),
                preferred_element_type=F32,
            ).astype(BF16)


def first_product(name, far, rows, weights, after):
    slots = rows[0].shape[0] * len(rows) // 2
    parts, units, features = weights.shape
    return call(
        functools.partial(first_kernel, far),
        FIRST * parts,
        (*rows, weights),
        after,
        jax.ShapeDtypeStruct((parts, slots, units // 2), BF16),
        in_specs=[*[whole(r) for r in rows], pl.BlockSpec(memory_space=pltpu.VMEM)],
        scratch=[pltpu.VMEM((slots, features), BF16)],
        name=name,
    )


def sum_kernel(mine, arrived, out):
    out[...] = (mine[...].astype(F32) + arrived[...].astype(F32)).astype(BF16)


def end_or_sum_kernel(at_end, mine, arrived, out):
    _, _, end = position()

    @pl.when(end)
    def _():
        parts = at_end.shape[0]
        out[:parts] = at_end[...]
        if parts < out.shape[0]:
            out[parts:] = jnp.zeros_like(out[parts:])

    @pl.when(jnp.logical_not(end))
    def _():
        out[...] = (mine[...].astype(F32) + arrived[...].astype(F32)).astype(BF16)


def end_or_pass_kernel(at_end, passed, out):
    _, _, end = position()

    @pl.when(end)
    def _():
        out[...] = at_end[...]

    @pl.when(jnp.logical_not(end))
    def _():
        out[...] = passed[...]


def ahead_act_kernel(near, arrived, out):
    gate = near[0].astype(F32) + arrived[0].astype(F32)
    up = near[1].astype(F32) + arrived[1].astype(F32)
    out[0] = (gate * jax.nn.sigmoid(gate) * up).astype(BF16)


def behind_act_kernel(near, arrived, near_e, arrived_e, scale, out):
    gate = near[0].astype(F32) + arrived[0].astype(F32)
    up = near[1].astype(F32) + arrived[1].astype(F32)
    expanded = (near_e[0].astype(F32) + arrived_e[0].astype(F32)) * scale[...]
    sig = jax.nn.sigmoid(gate)
    out[0] = (expanded * up * sig * (1.0 + gate * (1.0 - sig))).astype(BF16)
    out[1] = (expanded * gate * sig).astype(BF16)


def result_kernel(first, one, two, out):
    size = first.shape[0]
    out[:size] = first[...]
    out[size:] = (one[...].astype(F32) + two[...].astype(F32)).astype(BF16)


def second_kernel(scaled, act, one, two, three, *refs):
    scale, refs = (refs[0], refs[1:]) if scaled else (None, refs)
    weights, give, keep, joined = refs
    near_half, group, end = position()
    kinds, _, half = act.shape
    units = weights.shape[1]
    width = give.shape[1]

    def place(near, far):
        for kind in range(kinds):
            at = pl.multiple_of((2 * kind + near_half) * half, 128)
            other = pl.multiple_of((2 * kind + 1 - near_half) * half, 128)
            joined[:, pl.ds(at, half)] = near[kind]
            joined[:, pl.ds(other, half)] = far[kind]

    @pl.when(end)
    def _():
        place(act, three)

    @pl.when(jnp.logical_not(end))
    def _():
        place(one, two)

    for side, out in ((1 - group, give), (group, keep)):
        at = pl.multiple_of(side * width, 128)
        tile = weights[:, :, pl.ds(at, width)].reshape(kinds * units, width)
        share = jnp.dot(joined[...], tile, preferred_element_type=F32)
        if scaled:
            share = share * scale[...]
        out[...] = share.astype(BF16)


def second_product(name, values, scale, weights, after):
    kinds, units, features = weights.shape
    slots = values[0].shape[1]
    operands = [*values] + ([] if scale is None else [scale])
    share = jax.ShapeDtypeStruct((slots, features // 2), BF16)
    return call(
        functools.partial(second_kernel, scale is not None),
        AHEAD_OUT if kinds == 1 else BEHIND_OUT,
        (*operands, weights),
        after,
        (share, share),
        in_specs=[*[whole(v) for v in operands], pl.BlockSpec(memory_space=pltpu.VMEM)],
        scratch=[pltpu.VMEM((slots, kinds * units), BF16)],
        name=name,
    )


def chain_body(ahead_rows, behind_rows, behind_grad, route_scores, route_counts, gate_up, down_proj):
    height = ahead_rows.shape[1]
    gates = gate_up[0, 0]
    downs = down_proj[0]
    sections = lax.axis_size("section")
    devices = 2 * DBLOCKS
    slot_ids = jnp.arange(height, dtype=jnp.int32)[None]
    live = slot_ids < route_counts[0][:, None]
    scales = jnp.where(live, route_scores[0], 0.0)[:, :, None]

    def between(value, to):
        pairs = [(q * 2 + f, to[q] * 2 + f) for q in range(DBLOCKS) for f in range(2) if to[q] is not None]
        return lax.ppermute(value, "expert", pairs)

    def outer(value):
        return between(value, (1, 0, 3, 2))

    def inward(value):
        return between(value, (1, None, None, 2))

    def outward(value):
        return between(value, (None, 0, 3, None))

    def middle(value):
        return between(value, (0, 2, 1, 3))

    def swapped(value):
        return lax.ppermute(value, "expert", [(i, i ^ 1) for i in range(devices)])

    def to_section(value, by, flip):
        pairs = [
            (s * devices + e, (s + by) * devices + (e ^ flip))
            for s in range(sections)
            if 0 <= s + by < sections
            for e in range(devices)
        ]
        return lax.ppermute(value, ("section", "expert"), pairs)

    recent = []

    def kernel_call(name, kernel, micros, operands, shape):
        specs, arrays = [], []
        for operand in operands:
            array, c = operand if isinstance(operand, tuple) else (operand, None)
            arrays.append(array)
            specs.append(whole(array) if c is None else row_piece(array, c))
        made = call(
            kernel,
            micros,
            arrays,
            list(recent),
            jax.ShapeDtypeStruct(shape, BF16),
            in_specs=specs,
            name=name,
        )
        recent[:] = [made]
        return made

    class Chain:
        def __init__(self, name, rows, weights, spreads):
            self.name = name
            self.rows, self.weights = rows, weights
            self.spreads = spreads
            self.pairs, self.far, self.near, self.act = {}, {}, {}, {}
            self.out, self.mid, self.one, self.back, self.third = {}, {}, {}, {}, {}

        def fetch(self, c):
            size, width = height // PIECES, self.rows.shape[1]
            if c == 0 and self.name == "behind":
                rows = self.rows[:size]
                self.pairs[c] = rows, swapped(rows)
                return
            rows = call(
                cut_kernel,
                SMALL if c else ROWS,
                (self.rows,),
                list(recent),
                jax.ShapeDtypeStruct((size, width), BF16),
                in_specs=[pl.BlockSpec((size, width), lambda i: (c, 0))],
                name=f"{self.name}_rows_{c}",
            )
            recent[:] = [rows]
            self.pairs[c] = rows, swapped(rows)

        def far_product(self, c):
            name = f"{self.name}_far_{c}"
            made = first_product(name, True, self.pairs[c], self.weights, list(recent))
            recent[:] = [made]
            self.far[c] = made

        def near_products(self):
            rows = [row for c in range(PIECES) for row in self.pairs[c]]
            made = first_product(f"{self.name}_near", False, rows, self.weights, list(recent))
            recent[:] = [made]
            self.near = {c: (made, c) for c in range(PIECES)}

        def near_sum(self, c):
            operands = (self.near[c], self.mid[c])
            return kernel_call(f"{self.name}_third_{c}", sum_kernel, SMALL, operands, self.far[c].shape)

        def first_hop(self, c):
            self.out[c] = outer(self.far[c]) if c == 0 else inward(self.far[c])

        def third_hop(self, c):
            self.third[c] = outward(self.near_sum(c))

        def merged_hop(self, c, first):
            operands = (first, self.near[c - 1], self.mid[c - 1])
            shape = self.far[0].shape
            self.out[c] = outer(
                kernel_call(f"{self.name}_outer_{c}", end_or_sum_kernel, SMALL, operands, shape)
            )
            self.third[c - 1] = self.out[c]

        def last_third_hop(self):
            self.third[PIECES - 1] = outer(self.near_sum(PIECES - 1))

        def middle_sum(self, c):
            mine = self.far[c]
            self.mid[c] = middle(
                kernel_call(
                    f"{self.name}_middle_{c}", sum_kernel, SMALL, (mine, self.out[c]), mine.shape
                )
            )

        def middle_pass(self, c):
            value = self.out[PIECES] if c == 0 else self.back[c]
            shape = (self.spreads, *value.shape[1:])
            value = kernel_call(f"{self.name}_first_{c}", cut_first_kernel, SMALL, (value,), shape)
            self.one[c] = value
            self.mid[PIECES + c] = middle(value)

        def outer_pass(self, c):
            value = self.mid[PIECES + c - 1]
            if c == PIECES:
                value = kernel_call(
                    f"{self.name}_back_{c}", cut_first_kernel, SMALL, (value,), value.shape
                )
            else:
                value = kernel_call(
                    f"{self.name}_back_{c}",
                    end_or_pass_kernel,
                    SMALL,
                    (self.act[c], value),
                    value.shape,
                )
            self.back[c] = outer(value)

        def activated(self, c):
            return self.act[c], self.one[c], self.mid[PIECES + c], self.back[c + 1]

    ahead = Chain("ahead", ahead_rows[0], gates, 1)
    behind = Chain("behind", behind_rows[0], gates, 2)
    grad = Chain("grad", behind_grad[0], downs, 0)
    sent = {}

    def cut(array, c):
        size = height // PIECES
        return array[c * size : (c + 1) * size]

    def activate_ahead(c):
        near = ahead.near[c]
        operands = (near, ahead.third[c])
        ahead.act[c] = kernel_call(f"ahead_act_{c}", ahead_act_kernel, ACT, operands, (1, *ahead.far[c].shape[1:]))

    def activate_behind(c):
        near = behind.near[c]
        operands = (near, behind.third[c], grad.near[c], grad.third[c], cut(scales[1], c))
        behind.act[c] = kernel_call(f"behind_act_{c}", behind_act_kernel, ACT, operands, behind.far[c].shape)

    def output(chain, c):
        forward = chain is ahead
        scale = cut(scales[0], c) if forward else None
        weights = downs if forward else gates
        give, keep = second_product(
            f"{chain.name}_out_{c}", chain.activated(c), scale, weights, list(recent)
        )
        recent[:] = [give]
        return give, keep

    def finish_first(chain):
        give, keep = output(chain, 0)
        sent[chain, 0] = swapped(give), keep

    def send_first(chain):
        share, keep = sent[chain, 0]
        total = kernel_call(
            f"{chain.name}_shares", sum_kernel, SMALL, (keep, share), keep.shape
        )
        sent[chain, 0] = to_section(total, 1 if chain is ahead else -1, 0)

    def finish_last(chain):
        give, keep = output(chain, 1)
        by = 1 if chain is ahead else -1
        sent[chain, 1] = to_section(give, by, 1), to_section(keep, by, 0)

    def result(chain):
        operands = (sent[chain, 0], *sent[chain, 1])
        shape = (height, operands[0].shape[1])
        return kernel_call(f"{chain.name}_result", result_kernel, SMALL, operands, shape)[None]

    for chain in (behind, ahead, grad):
        chain.fetch(0)
    weights_spec = pl.BlockSpec(memory_space=pltpu.VMEM)
    touched = call(
        touch_kernel,
        ROWS,
        (gates, downs),
        list(recent),
        jax.ShapeDtypeStruct((16, 128), BF16),
        in_specs=[weights_spec, weights_spec],
        name="touch",
    )
    recent[:] = [touched]
    behind.far_product(0)
    behind.first_hop(0)
    behind.fetch(1)
    ahead.far_product(0)
    ahead.first_hop(0)
    grad.far_product(0)
    grad.first_hop(0)
    behind.middle_sum(0)
    ahead.fetch(1)
    behind.far_product(1)
    behind.near_products()
    ahead.middle_sum(0)
    behind.merged_hop(1, behind.far[1])
    grad.fetch(1)
    grad.middle_sum(0)
    ahead.far_product(1)
    ahead.near_products()
    ahead.merged_hop(1, ahead.far[1])
    behind.middle_sum(1)
    grad.far_product(1)
    grad.near_products()
    grad.merged_hop(1, grad.far[1])
    ahead.middle_sum(1)
    grad.middle_sum(1)
    activate_behind(0)
    behind.merged_hop(2, behind.act[0])
    activate_ahead(0)
    ahead.merged_hop(2, ahead.act[0])
    grad.last_third_hop()
    behind.middle_pass(0)
    ahead.middle_pass(0)
    activate_ahead(1)
    activate_behind(1)
    behind.outer_pass(1)
    ahead.outer_pass(1)
    behind.middle_pass(1)
    ahead.middle_pass(1)
    finish_first(behind)
    finish_first(ahead)
    behind.outer_pass(2)
    ahead.outer_pass(2)
    send_first(behind)
    send_first(ahead)
    finish_last(behind)
    finish_last(ahead)
    behind_sent = result(behind)
    ahead_sent = result(ahead)
    return ahead_sent, behind_sent


def body(ahead_rows, behind_rows, behind_grad, route_scores, route_counts, gate_up, down_proj):
    groups = lax.axis_size("expert")
    fgroups = groups // DBLOCKS
    low = [[q * fgroups + f for f in range(fgroups)] for q in range(DBLOCKS)]
    high = [[q * fgroups + f for q in range(DBLOCKS)] for f in range(fgroups)]
    height = ahead_rows.shape[1]
    weights_in = gate_up[0, 0]
    weights_out = down_proj[0, 0]
    units = weights_in.shape[1]
    part = units // DBLOCKS

    def wide(rows):
        return lax.all_gather(rows, "expert", axis_index_groups=low, axis=1, tiled=True)

    def reduced(partials):
        flat = partials.reshape(-1, partials.shape[-1])
        total = lax.psum_scatter(
            flat, "expert", axis_index_groups=high, scatter_dimension=0, tiled=True
        )
        return total.astype(F32).reshape(partials.shape[1:])

    def spread(values):
        return lax.all_gather(values, "expert", axis_index_groups=high, axis=0, tiled=False)

    def narrowed(values):
        return lax.psum_scatter(
            values.astype(BF16), "expert", axis_index_groups=low, scatter_dimension=1, tiled=True
        )

    slot_ids = jnp.arange(height, dtype=jnp.int32)
    scale_ahead = route_scores[0, 0] * (slot_ids < route_counts[0, 0]).astype(F32)
    scale_behind = route_scores[0, 1] * (slot_ids < route_counts[0, 1]).astype(F32)
    gates = weights_in.reshape(2, DBLOCKS, part, -1)
    downs = weights_out.reshape(DBLOCKS, part, -1)

    ahead_wide = wide(ahead_rows[0])
    pre_a = jnp.einsum("cd,kqfd->qkcf", ahead_wide, gates, preferred_element_type=F32).astype(BF16)
    sum_a = reduced(pre_a)
    hidden = (sum_a[0] * jax.nn.sigmoid(sum_a[0]) * sum_a[1]).astype(BF16)
    hidden_all = spread(hidden)

    behind_wide = wide(behind_rows[0])
    grad_wide = wide(behind_grad[0])
    pre_b = jnp.einsum("cd,kqfd->qkcf", behind_wide, gates, preferred_element_type=F32).astype(BF16)
    exp_b = jnp.einsum("cd,qfd->qcf", grad_wide, downs, preferred_element_type=F32).astype(BF16)
    sum_b = reduced(jnp.concatenate([pre_b, exp_b[:, None]], axis=1))
    gate, up, expanded = sum_b[0], sum_b[1], sum_b[2] * scale_behind[:, None]
    sig = jax.nn.sigmoid(gate)
    grad_gate = (expanded * up * sig * (1.0 + gate * (1.0 - sig))).astype(BF16)
    grad_up = (expanded * gate * sig).astype(BF16)
    grads_all = spread(jnp.stack([grad_gate, grad_up]))

    out_a = jnp.einsum("qcf,qfd->cd", hidden_all, downs, preferred_element_type=F32)
    ahead_out = (narrowed(out_a).astype(F32) * scale_ahead[:, None]).astype(BF16)
    moved_ahead = shift(ahead_out, "section", 1)
    out_b = jnp.einsum("qkcf,kqfd->cd", grads_all, gates, preferred_element_type=F32)
    behind_out = narrowed(out_b)
    moved_behind = shift(behind_out, "section", -1)
    return (moved_ahead[None], moved_behind[None])


def solution(mesh):
    in_specs = (
        P("section", None, "expert"),
        P("section", None, "expert"),
        P("section", None, "expert"),
        P("section", None, None),
        P("section", None),
        P("section", "expert", None, None, None),
        P("section", "expert", None, None),
    )
    out_specs = (P("section", None, "expert"), P("section", None, "expert"))
    chosen = chain_body if mesh.shape["expert"] == 2 * DBLOCKS else body
    return jax.shard_map(chosen, mesh=mesh, in_specs=in_specs, out_specs=out_specs, check_vma=False)
```

```python
import functools

import jax
import jax.numpy as jnp
from jax import lax
from jax.experimental import pallas as pl
from jax.experimental.pallas import tpu as pltpu
from jax.sharding import PartitionSpec as P

DBLOCKS = 4
BF16 = jnp.bfloat16
F32 = jnp.float32
MIB = 1024 * 1024
PIECES = 2
ROWS, SMALL, ACT, FIRST = 20, 6, 10, 5.2
OUT = {(True, 0): 3, (False, 0): 20, (True, 1): 3, (False, 1): 20}


def shift(shard, axis, by):
    devices = lax.axis_size(axis)
    pairs = [(i, i + by) for i in range(devices) if 0 <= i + by < devices]
    return lax.ppermute(shard, axis, pairs)


def whole(array):
    return pl.BlockSpec(array.shape, functools.partial(lambda n, *_: (0,) * n, array.ndim))


def row_piece(array, c):
    parts, slots, half = array.shape
    return pl.BlockSpec((parts, slots // PIECES, half), lambda *_: (0, c, 0))


def call(kernel, micros, operands, after, out_shape, grid=(1,), in_specs=None, out_specs=None, scratch=(), limit=16, name=None):
    count, unread = len(operands), len(after)

    def run(*refs):
        kernel(*refs[:count], *refs[count + unread :])

    if in_specs is None:
        in_specs = [whole(o) for o in operands]
    if out_specs is None:
        out_specs = jax.tree.map(whole, out_shape)
    return pl.pallas_call(
        run,
        compiler_params=pltpu.CompilerParams(vmem_limit_bytes=limit * MIB),
        cost_estimate=pl.CostEstimate(flops=int(micros * 1e9), bytes_accessed=1024, transcendentals=0),
        out_shape=out_shape,
        name=name,
        grid=grid,
        in_specs=[*in_specs, *[pl.BlockSpec(memory_space=pl.ANY)] * unread],
        out_specs=out_specs,
        scratch_shapes=list(scratch),
    )(*operands, *after)


def cut_kernel(rows, out):
    out[...] = rows[...]


def cut_first_kernel(value, out):
    out[...] = value[: out.shape[0]]


def position():
    own = lax.axis_index("expert")
    block = own // 2
    near = jnp.where(block >= DBLOCKS // 2, 1, 0)
    return near, own % 2, (block == 0) | (block == DBLOCKS - 1)


def first_kernel(far, *refs):
    rows, (weights, out, joined) = refs[:-3], refs[-3:]
    near, group, _ = position()
    side = 1 - near if far else near
    parts, _, half = out.shape
    slots, width = rows[0].shape
    at = pl.multiple_of(group * width, 128)
    other = pl.multiple_of((1 - group) * width, 128)
    for piece in range(len(rows) // 2):
        here = pl.ds(piece * slots, slots)
        joined[here, pl.ds(at, width)] = rows[2 * piece][...]
        joined[here, pl.ds(other, width)] = rows[2 * piece + 1][...]
    tile = min(256, half)
    for k in range(parts):
        for j in range(half // tile):
            at = pl.multiple_of(side * half + j * tile, tile)
            out[k, :, j * tile : (j + 1) * tile] = lax.dot_general(
                joined[...],
                weights[k, pl.ds(at, tile)],
                (((1,), (1,)), ((), ())),
                preferred_element_type=F32,
            ).astype(BF16)


def first_product(name, far, rows, weights, after):
    slots = rows[0].shape[0] * len(rows) // 2
    parts, units, features = weights.shape
    return call(
        functools.partial(first_kernel, far),
        FIRST * parts,
        (*rows, weights),
        after,
        jax.ShapeDtypeStruct((parts, slots, units // 2), BF16),
        in_specs=[*[whole(r) for r in rows], pl.BlockSpec(memory_space=pltpu.VMEM)],
        scratch=[pltpu.VMEM((slots, features), BF16)],
        name=name,
    )


def sum_kernel(mine, arrived, out):
    out[...] = (mine[...].astype(F32) + arrived[...].astype(F32)).astype(BF16)


def end_or_sum_kernel(at_end, mine, arrived, out):
    _, _, end = position()

    @pl.when(end)
    def _():
        parts = at_end.shape[0]
        out[:parts] = at_end[...]
        if parts < out.shape[0]:
            out[parts:] = jnp.zeros_like(out[parts:])

    @pl.when(jnp.logical_not(end))
    def _():
        out[...] = (mine[...].astype(F32) + arrived[...].astype(F32)).astype(BF16)


def end_or_pass_kernel(at_end, passed, out):
    _, _, end = position()

    @pl.when(end)
    def _():
        out[...] = at_end[...]

    @pl.when(jnp.logical_not(end))
    def _():
        out[...] = passed[...]


def ahead_act_kernel(near, arrived, out):
    gate = near[0].astype(F32) + arrived[0].astype(F32)
    up = near[1].astype(F32) + arrived[1].astype(F32)
    out[0] = (gate * jax.nn.sigmoid(gate) * up).astype(BF16)


def behind_act_kernel(near, arrived, near_e, arrived_e, scale, out):
    gate = near[0].astype(F32) + arrived[0].astype(F32)
    up = near[1].astype(F32) + arrived[1].astype(F32)
    expanded = (near_e[0].astype(F32) + arrived_e[0].astype(F32)) * scale[...]
    sig = jax.nn.sigmoid(gate)
    out[0] = (expanded * up * sig * (1.0 + gate * (1.0 - sig))).astype(BF16)
    out[1] = (expanded * gate * sig).astype(BF16)


def result_kernel(first, one, two, out):
    size = first.shape[0]
    out[:size] = first[...]
    out[size:] = (one[...].astype(F32) + two[...].astype(F32)).astype(BF16)


def second_kernel(scaled, act, one, two, three, *refs):
    scale, refs = (refs[0], refs[1:]) if scaled else (None, refs)
    weights, give, keep, joined = refs
    near_half, group, end = position()
    kinds, _, half = act.shape
    units = weights.shape[1]
    width = give.shape[1]

    def place(near, far):
        for kind in range(kinds):
            at = pl.multiple_of((2 * kind + near_half) * half, 128)
            other = pl.multiple_of((2 * kind + 1 - near_half) * half, 128)
            joined[:, pl.ds(at, half)] = near[kind]
            joined[:, pl.ds(other, half)] = far[kind]

    @pl.when(end)
    def _():
        place(act, three)

    @pl.when(jnp.logical_not(end))
    def _():
        place(one, two)

    for side, out in ((1 - group, give), (group, keep)):
        at = pl.multiple_of(side * width, 128)
        tile = weights[:, :, pl.ds(at, width)].reshape(kinds * units, width)
        share = jnp.dot(joined[...], tile, preferred_element_type=F32)
        if scaled:
            share = share * scale[...]
        out[...] = share.astype(BF16)


def second_product(name, micros, values, scale, weights, after):
    kinds, units, features = weights.shape
    slots = values[0].shape[1]
    operands = [*values] + ([] if scale is None else [scale])
    share = jax.ShapeDtypeStruct((slots, features // 2), BF16)
    return call(
        functools.partial(second_kernel, scale is not None),
        micros,
        (*operands, weights),
        after,
        (share, share),
        in_specs=[*[whole(v) for v in operands], pl.BlockSpec(memory_space=pltpu.VMEM)],
        scratch=[pltpu.VMEM((slots, kinds * units), BF16)],
        name=name,
    )


def chain_body(ahead_rows, behind_rows, behind_grad, route_scores, route_counts, gate_up, down_proj):
    height = ahead_rows.shape[1]
    gates = gate_up[0, 0]
    downs = down_proj[0]
    sections = lax.axis_size("section")
    devices = 2 * DBLOCKS
    slot_ids = jnp.arange(height, dtype=jnp.int32)[None]
    live = slot_ids < route_counts[0][:, None]
    scales = jnp.where(live, route_scores[0], 0.0)[:, :, None]

    def between(value, to):
        pairs = [(q * 2 + f, to[q] * 2 + f) for q in range(DBLOCKS) for f in range(2) if to[q] is not None]
        return lax.ppermute(value, "expert", pairs)

    def outer(value):
        return between(value, (1, 0, 3, 2))

    def inward(value):
        return between(value, (1, None, None, 2))

    def outward(value):
        return between(value, (None, 0, 3, None))

    def middle(value):
        return between(value, (0, 2, 1, 3))

    def swapped(value):
        return lax.ppermute(value, "expert", [(i, i ^ 1) for i in range(devices)])

    def to_section(value, by, flip):
        pairs = [
            (s * devices + e, (s + by) * devices + (e ^ flip))
            for s in range(sections)
            if 0 <= s + by < sections
            for e in range(devices)
        ]
        return lax.ppermute(value, ("section", "expert"), pairs)

    recent = []

    def kernel_call(name, kernel, micros, operands, shape):
        specs, arrays = [], []
        for operand in operands:
            array, c = operand if isinstance(operand, tuple) else (operand, None)
            arrays.append(array)
            specs.append(whole(array) if c is None else row_piece(array, c))
        made = call(
            kernel,
            micros,
            arrays,
            list(recent),
            jax.ShapeDtypeStruct(shape, BF16),
            in_specs=specs,
            name=name,
        )
        recent[:] = [made]
        return made

    class Chain:
        def __init__(self, name, rows, weights, spreads):
            self.name = name
            self.rows, self.weights = rows, weights
            self.spreads = spreads
            self.pairs, self.far, self.near, self.act = {}, {}, {}, {}
            self.out, self.mid, self.one, self.back, self.third = {}, {}, {}, {}, {}

        def fetch(self, c):
            size, width = height // PIECES, self.rows.shape[1]
            if c == 0 and self.name == "behind":
                rows = self.rows[:size]
                self.pairs[c] = rows, swapped(rows)
                return
            rows = call(
                cut_kernel,
                SMALL if c else ROWS,
                (self.rows,),
                list(recent),
                jax.ShapeDtypeStruct((size, width), BF16),
                in_specs=[pl.BlockSpec((size, width), lambda i: (c, 0))],
                name=f"{self.name}_rows_{c}",
            )
            recent[:] = [rows]
            self.pairs[c] = rows, swapped(rows)

        def far_product(self, c):
            name = f"{self.name}_far_{c}"
            made = first_product(name, True, self.pairs[c], self.weights, list(recent))
            recent[:] = [made]
            self.far[c] = made

        def near_products(self):
            rows = [row for c in range(PIECES) for row in self.pairs[c]]
            made = first_product(f"{self.name}_near", False, rows, self.weights, list(recent))
            recent[:] = [made]
            self.near = {c: (made, c) for c in range(PIECES)}

        def near_sum(self, c):
            operands = (self.near[c], self.mid[c])
            return kernel_call(f"{self.name}_third_{c}", sum_kernel, SMALL, operands, self.far[c].shape)

        def first_hop(self, c):
            self.out[c] = outer(self.far[c]) if c == 0 else inward(self.far[c])

        def third_hop(self, c):
            self.third[c] = outward(self.near_sum(c))

        def merged_hop(self, c, first):
            operands = (first, self.near[c - 1], self.mid[c - 1])
            shape = self.far[0].shape
            self.out[c] = outer(
                kernel_call(f"{self.name}_outer_{c}", end_or_sum_kernel, SMALL, operands, shape)
            )
            self.third[c - 1] = self.out[c]

        def last_third_hop(self):
            self.third[PIECES - 1] = outer(self.near_sum(PIECES - 1))

        def middle_sum(self, c):
            mine = self.far[c]
            self.mid[c] = middle(
                kernel_call(
                    f"{self.name}_middle_{c}", sum_kernel, SMALL, (mine, self.out[c]), mine.shape
                )
            )

        def middle_pass(self, c):
            value = self.out[PIECES] if c == 0 else self.back[c]
            shape = (self.spreads, *value.shape[1:])
            value = kernel_call(f"{self.name}_first_{c}", cut_first_kernel, SMALL, (value,), shape)
            self.one[c] = value
            self.mid[PIECES + c] = middle(value)

        def outer_pass(self, c):
            value = self.mid[PIECES + c - 1]
            if c == PIECES:
                value = kernel_call(
                    f"{self.name}_back_{c}", cut_first_kernel, SMALL, (value,), value.shape
                )
            else:
                value = kernel_call(
                    f"{self.name}_back_{c}",
                    end_or_pass_kernel,
                    SMALL,
                    (self.act[c], value),
                    value.shape,
                )
            self.back[c] = outer(value)

        def activated(self, c):
            return self.act[c], self.one[c], self.mid[PIECES + c], self.back[c + 1]

    ahead = Chain("ahead", ahead_rows[0], gates, 1)
    behind = Chain("behind", behind_rows[0], gates, 2)
    grad = Chain("grad", behind_grad[0], downs, 0)
    sent = {}

    def cut(array, c):
        size = height // PIECES
        return array[c * size : (c + 1) * size]

    def activate_ahead(c):
        near = ahead.near[c]
        operands = (near, ahead.third[c])
        ahead.act[c] = kernel_call(f"ahead_act_{c}", ahead_act_kernel, ACT, operands, (1, *ahead.far[c].shape[1:]))

    def activate_behind(c):
        near = behind.near[c]
        operands = (near, behind.third[c], grad.near[c], grad.third[c], cut(scales[1], c))
        behind.act[c] = kernel_call(f"behind_act_{c}", behind_act_kernel, ACT, operands, behind.far[c].shape)

    def output(chain, c):
        forward = chain is ahead
        scale = cut(scales[0], c) if forward else None
        weights = downs if forward else gates
        give, keep = second_product(
            f"{chain.name}_out_{c}", OUT[forward, c], chain.activated(c), scale, weights, list(recent)
        )
        recent[:] = [give]
        return give, keep

    def finish_first(chain):
        give, keep = output(chain, 0)
        sent[chain, 0] = swapped(give), keep

    def send_first(chain):
        share, keep = sent[chain, 0]
        total = kernel_call(
            f"{chain.name}_shares", sum_kernel, SMALL, (keep, share), keep.shape
        )
        sent[chain, 0] = to_section(total, 1 if chain is ahead else -1, 0)

    def finish_last(chain):
        if chain is ahead:
            recent.append(sent[chain, 0])
        give, keep = output(chain, 1)
        by = 1 if chain is ahead else -1
        sent[chain, 1] = to_section(give, by, 1), to_section(keep, by, 0)

    def result(chain):
        operands = (sent[chain, 0], *sent[chain, 1])
        shape = (height, operands[0].shape[1])
        return kernel_call(f"{chain.name}_result", result_kernel, SMALL, operands, shape)[None]

    for chain in (behind, ahead, grad):
        chain.fetch(0)
    behind.far_product(0)
    behind.first_hop(0)
    behind.fetch(1)
    ahead.far_product(0)
    ahead.first_hop(0)
    grad.far_product(0)
    grad.first_hop(0)
    behind.middle_sum(0)
    ahead.fetch(1)
    behind.far_product(1)
    behind.near_products()
    ahead.middle_sum(0)
    behind.merged_hop(1, behind.far[1])
    grad.fetch(1)
    grad.middle_sum(0)
    ahead.far_product(1)
    ahead.near_products()
    ahead.merged_hop(1, ahead.far[1])
    behind.middle_sum(1)
    grad.far_product(1)
    grad.near_products()
    grad.merged_hop(1, grad.far[1])
    ahead.middle_sum(1)
    activate_behind(0)
    behind.merged_hop(2, behind.act[0])
    grad.middle_sum(1)
    activate_ahead(0)
    ahead.merged_hop(2, ahead.act[0])
    grad.last_third_hop()
    behind.middle_pass(0)
    ahead.middle_pass(0)
    activate_ahead(1)
    activate_behind(1)
    behind.outer_pass(1)
    ahead.outer_pass(1)
    behind.middle_pass(1)
    finish_first(behind)
    finish_first(ahead)
    ahead.middle_pass(1)
    behind.outer_pass(2)
    ahead.outer_pass(2)
    send_first(behind)
    send_first(ahead)
    finish_last(behind)
    finish_last(ahead)
    behind_sent = result(behind)
    ahead_sent = result(ahead)
    return ahead_sent, behind_sent


def body(ahead_rows, behind_rows, behind_grad, route_scores, route_counts, gate_up, down_proj):
    groups = lax.axis_size("expert")
    fgroups = groups // DBLOCKS
    low = [[q * fgroups + f for f in range(fgroups)] for q in range(DBLOCKS)]
    high = [[q * fgroups + f for q in range(DBLOCKS)] for f in range(fgroups)]
    height = ahead_rows.shape[1]
    weights_in = gate_up[0, 0]
    weights_out = down_proj[0, 0]
    units = weights_in.shape[1]
    part = units // DBLOCKS

    def wide(rows):
        return lax.all_gather(rows, "expert", axis_index_groups=low, axis=1, tiled=True)

    def reduced(partials):
        flat = partials.reshape(-1, partials.shape[-1])
        total = lax.psum_scatter(
            flat, "expert", axis_index_groups=high, scatter_dimension=0, tiled=True
        )
        return total.astype(F32).reshape(partials.shape[1:])

    def spread(values):
        return lax.all_gather(values, "expert", axis_index_groups=high, axis=0, tiled=False)

    def narrowed(values):
        return lax.psum_scatter(
            values.astype(BF16), "expert", axis_index_groups=low, scatter_dimension=1, tiled=True
        )

    slot_ids = jnp.arange(height, dtype=jnp.int32)
    scale_ahead = route_scores[0, 0] * (slot_ids < route_counts[0, 0]).astype(F32)
    scale_behind = route_scores[0, 1] * (slot_ids < route_counts[0, 1]).astype(F32)
    gates = weights_in.reshape(2, DBLOCKS, part, -1)
    downs = weights_out.reshape(DBLOCKS, part, -1)

    ahead_wide = wide(ahead_rows[0])
    pre_a = jnp.einsum("cd,kqfd->qkcf", ahead_wide, gates, preferred_element_type=F32).astype(BF16)
    sum_a = reduced(pre_a)
    hidden = (sum_a[0] * jax.nn.sigmoid(sum_a[0]) * sum_a[1]).astype(BF16)
    hidden_all = spread(hidden)

    behind_wide = wide(behind_rows[0])
    grad_wide = wide(behind_grad[0])
    pre_b = jnp.einsum("cd,kqfd->qkcf", behind_wide, gates, preferred_element_type=F32).astype(BF16)
    exp_b = jnp.einsum("cd,qfd->qcf", grad_wide, downs, preferred_element_type=F32).astype(BF16)
    sum_b = reduced(jnp.concatenate([pre_b, exp_b[:, None]], axis=1))
    gate, up, expanded = sum_b[0], sum_b[1], sum_b[2] * scale_behind[:, None]
    sig = jax.nn.sigmoid(gate)
    grad_gate = (expanded * up * sig * (1.0 + gate * (1.0 - sig))).astype(BF16)
    grad_up = (expanded * gate * sig).astype(BF16)
    grads_all = spread(jnp.stack([grad_gate, grad_up]))

    out_a = jnp.einsum("qcf,qfd->cd", hidden_all, downs, preferred_element_type=F32)
    ahead_out = (narrowed(out_a).astype(F32) * scale_ahead[:, None]).astype(BF16)
    moved_ahead = shift(ahead_out, "section", 1)
    out_b = jnp.einsum("qkcf,kqfd->cd", grads_all, gates, preferred_element_type=F32)
    behind_out = narrowed(out_b)
    moved_behind = shift(behind_out, "section", -1)
    return (moved_ahead[None], moved_behind[None])


def solution(mesh):
    in_specs = (
        P("section", None, "expert"),
        P("section", None, "expert"),
        P("section", None, "expert"),
        P("section", None, None),
        P("section", None),
        P("section", "expert", None, None, None),
        P("section", "expert", None, None),
    )
    out_specs = (P("section", None, "expert"), P("section", None, "expert"))
    chosen = chain_body if mesh.shape["expert"] == 2 * DBLOCKS else body
    return jax.shard_map(chosen, mesh=mesh, in_specs=in_specs, out_specs=out_specs, check_vma=False)
```

```python
import functools

import jax
import jax.numpy as jnp
from jax import lax
from jax.experimental import pallas as pl
from jax.experimental.pallas import tpu as pltpu
from jax.sharding import PartitionSpec as P

DBLOCKS = 4
BF16 = jnp.bfloat16
F32 = jnp.float32
MIB = 1024 * 1024
PIECES = 2
ROWS, SMALL, ACT, FIRST = 20, 6, 10, 5.2
OUT = {(True, 0): 3, (False, 0): 20, (True, 1): 3, (False, 1): 20}


def shift(shard, axis, by):
    devices = lax.axis_size(axis)
    pairs = [(i, i + by) for i in range(devices) if 0 <= i + by < devices]
    return lax.ppermute(shard, axis, pairs)


def whole(array):
    return pl.BlockSpec(array.shape, functools.partial(lambda n, *_: (0,) * n, array.ndim))


def row_piece(array, c):
    parts, slots, half = array.shape
    return pl.BlockSpec((parts, slots // PIECES, half), lambda *_: (0, c, 0))


def call(kernel, micros, operands, after, out_shape, grid=(1,), in_specs=None, out_specs=None, scratch=(), limit=16, name=None):
    count, unread = len(operands), len(after)

    def run(*refs):
        kernel(*refs[:count], *refs[count + unread :])

    if in_specs is None:
        in_specs = [whole(o) for o in operands]
    if out_specs is None:
        out_specs = jax.tree.map(whole, out_shape)
    return pl.pallas_call(
        run,
        compiler_params=pltpu.CompilerParams(vmem_limit_bytes=limit * MIB),
        cost_estimate=pl.CostEstimate(flops=int(micros * 1e9), bytes_accessed=1024, transcendentals=0),
        out_shape=out_shape,
        name=name,
        grid=grid,
        in_specs=[*in_specs, *[pl.BlockSpec(memory_space=pl.ANY)] * unread],
        out_specs=out_specs,
        scratch_shapes=list(scratch),
    )(*operands, *after)


def cut_kernel(rows, out):
    out[...] = rows[...]


def cut_first_kernel(value, out):
    out[...] = value[: out.shape[0]]


def position():
    own = lax.axis_index("expert")
    block = own // 2
    near = jnp.where(block >= DBLOCKS // 2, 1, 0)
    return near, own % 2, (block == 0) | (block == DBLOCKS - 1)


def first_kernel(far, *refs):
    rows, (weights, out, joined) = refs[:-3], refs[-3:]
    near, group, _ = position()
    side = 0 if far else near
    parts, _, half = out.shape
    slots, width = rows[0].shape
    at = pl.multiple_of(group * width, 128)
    other = pl.multiple_of((1 - group) * width, 128)
    for piece in range(len(rows) // 2):
        here = pl.ds(piece * slots, slots)
        joined[here, pl.ds(at, width)] = rows[2 * piece][...]
        joined[here, pl.ds(other, width)] = rows[2 * piece + 1][...]
    tile = min(256, half)
    for k in range(parts):
        for j in range(half // tile):
            at = pl.multiple_of(side * half + j * tile, tile)
            out[k, :, j * tile : (j + 1) * tile] = lax.dot_general(
                joined[...],
                weights[k, pl.ds(at, tile)],
                (((1,), (1,)), ((), ())),
                preferred_element_type=F32,
            ).astype(BF16)


def first_product(name, far, rows, weights, after):
    slots = rows[0].shape[0] * len(rows) // 2
    parts, units, features = weights.shape
    half = units if far else units // 2
    return call(
        functools.partial(first_kernel, far),
        FIRST * parts,
        (*rows, weights),
        after,
        jax.ShapeDtypeStruct((parts, slots, half), BF16),
        in_specs=[*[whole(r) for r in rows], pl.BlockSpec(memory_space=pltpu.VMEM)],
        scratch=[pltpu.VMEM((slots, features), BF16)],
        name=name,
    )


def sum_kernel(mine, arrived, out):
    out[...] = (mine[...].astype(F32) + arrived[...].astype(F32)).astype(BF16)


def end_or_sum_kernel(at_end, mine, arrived, out):
    _, _, end = position()

    @pl.when(end)
    def _():
        parts = at_end.shape[0]
        out[:parts] = at_end[...]
        if parts < out.shape[0]:
            out[parts:] = jnp.zeros_like(out[parts:])

    @pl.when(jnp.logical_not(end))
    def _():
        out[...] = (mine[...].astype(F32) + arrived[...].astype(F32)).astype(BF16)


def end_or_pass_kernel(at_end, passed, out):
    _, _, end = position()

    @pl.when(end)
    def _():
        out[...] = at_end[...]

    @pl.when(jnp.logical_not(end))
    def _():
        out[...] = passed[...]


def ahead_act_kernel(near, arrived, out):
    gate = near[0].astype(F32) + arrived[0].astype(F32)
    up = near[1].astype(F32) + arrived[1].astype(F32)
    out[0] = (gate * jax.nn.sigmoid(gate) * up).astype(BF16)


def behind_act_kernel(near, arrived, near_e, arrived_e, scale, out):
    gate = near[0].astype(F32) + arrived[0].astype(F32)
    up = near[1].astype(F32) + arrived[1].astype(F32)
    expanded = (near_e[0].astype(F32) + arrived_e[0].astype(F32)) * scale[...]
    sig = jax.nn.sigmoid(gate)
    out[0] = (expanded * up * sig * (1.0 + gate * (1.0 - sig))).astype(BF16)
    out[1] = (expanded * gate * sig).astype(BF16)


def result_kernel(count, *refs):
    shares, out = refs[:-1], refs[-1]
    size = shares[0].shape[0]
    for at, terms in ((0, shares[:count]), (size, shares[count:])):
        total = terms[0][...].astype(F32)
        for term in terms[1:]:
            total += term[...].astype(F32)
        out[at : at + size] = total.astype(BF16)


def second_kernel(scaled, act, one, two, three, *refs):
    scale, refs = (refs[0], refs[1:]) if scaled else (None, refs)
    weights, give, keep, joined = refs
    near_half, group, end = position()
    kinds, _, half = act.shape
    units = weights.shape[1]
    width = give.shape[1]

    def place(near, far):
        for kind in range(kinds):
            at = pl.multiple_of((2 * kind + near_half) * half, 128)
            other = pl.multiple_of((2 * kind + 1 - near_half) * half, 128)
            joined[:, pl.ds(at, half)] = near[kind]
            joined[:, pl.ds(other, half)] = far[kind]

    @pl.when(end)
    def _():
        place(act, three)

    @pl.when(jnp.logical_not(end))
    def _():
        place(one, two)

    for side, out in ((1 - group, give), (group, keep)):
        at = pl.multiple_of(side * width, 128)
        tile = weights[:, :, pl.ds(at, width)].reshape(kinds * units, width)
        share = jnp.dot(joined[...], tile, preferred_element_type=F32)
        if scaled:
            share = share * scale[...]
        out[...] = share.astype(BF16)


def copying_second_kernel(scaled, act, one, two, three, *refs):
    scale, refs = (refs[0], refs[1:]) if scaled else (None, refs)
    weights, give, keep, joined, tiles, sems = refs
    near_half, group, end = position()
    kinds, _, half = act.shape
    _, _, units, width = tiles.shape
    copies = []
    for own in range(2):
        at = pl.multiple_of((group if own else 1 - group) * width, 128)
        copy = pltpu.make_async_copy(
            weights.at[:, :, pl.ds(at, width)], tiles.at[own], sems.at[own]
        )
        copy.start()
        copies.append(copy)

    def place(near, far):
        for kind in range(kinds):
            at = pl.multiple_of((2 * kind + near_half) * half, 128)
            other = pl.multiple_of((2 * kind + 1 - near_half) * half, 128)
            joined[:, pl.ds(at, half)] = near[kind]
            joined[:, pl.ds(other, half)] = far[kind]

    @pl.when(end)
    def _():
        place(act, three)

    @pl.when(jnp.logical_not(end))
    def _():
        place(one, two)

    for own, out in enumerate((give, keep)):
        copies[own].wait()
        share = jnp.dot(
            joined[...], tiles[own].reshape(kinds * units, width), preferred_element_type=F32
        )
        if scaled:
            share = share * scale[...]
        out[...] = share.astype(BF16)


def second_product(name, micros, values, scale, weights, after):
    kinds, units, features = weights.shape
    slots = values[0].shape[1]
    operands = [*values] + ([] if scale is None else [scale])
    share = jax.ShapeDtypeStruct((slots, features // 2), BF16)
    kernel, space = second_kernel, pltpu.VMEM
    scratch = [pltpu.VMEM((slots, kinds * units), BF16)]
    if kinds == 1:
        kernel, space = copying_second_kernel, pl.ANY
        scratch.append(pltpu.VMEM((2, kinds, units, features // 2), BF16))
        scratch.append(pltpu.SemaphoreType.DMA((2,)))
    return call(
        functools.partial(kernel, scale is not None),
        micros,
        (*operands, weights),
        after,
        (share, share),
        in_specs=[*[whole(v) for v in operands], pl.BlockSpec(memory_space=space)],
        scratch=scratch,
        name=name,
    )


def chain_body(ahead_rows, behind_rows, behind_grad, route_scores, route_counts, gate_up, down_proj):
    height = ahead_rows.shape[1]
    gates = gate_up[0, 0]
    downs = down_proj[0]
    sections = lax.axis_size("section")
    devices = 2 * DBLOCKS
    slot_ids = jnp.arange(height, dtype=jnp.int32)[None]
    live = slot_ids < route_counts[0][:, None]
    scales = jnp.where(live, route_scores[0], 0.0)[:, :, None]

    def between(value, to):
        pairs = [(q * 2 + f, to[q] * 2 + f) for q in range(DBLOCKS) for f in range(2) if to[q] is not None]
        return lax.ppermute(value, "expert", pairs)

    def outer(value):
        return between(value, (1, 0, 3, 2))

    def inward(value):
        return between(value, (1, None, None, 2))

    def outward(value):
        return between(value, (None, 0, 3, None))

    def middle(value):
        return between(value, (0, 2, 1, 3))

    def swapped(value):
        return lax.ppermute(value, "expert", [(i, i ^ 1) for i in range(devices)])

    def to_section(value, by, flip):
        pairs = [
            (s * devices + e, (s + by) * devices + (e ^ flip))
            for s in range(sections)
            if 0 <= s + by < sections
            for e in range(devices)
        ]
        return lax.ppermute(value, ("section", "expert"), pairs)

    recent = []

    def kernel_call(name, kernel, micros, operands, shape):
        specs, arrays = [], []
        for operand in operands:
            array, c = operand if isinstance(operand, tuple) else (operand, None)
            arrays.append(array)
            specs.append(whole(array) if c is None else row_piece(array, c))
        made = call(
            kernel,
            micros,
            arrays,
            list(recent),
            jax.ShapeDtypeStruct(shape, BF16),
            in_specs=specs,
            name=name,
        )
        recent[:] = [made]
        return made

    def far_half(weights):
        parts, units, features = weights.shape
        start = jnp.where(lax.axis_index("expert") // 2 >= DBLOCKS // 2, 0, units // 2)
        return lax.dynamic_slice(weights, (0, start, 0), (parts, units // 2, features))

    gates_far, downs_far = far_half(gates), far_half(downs)

    class Chain:
        def __init__(self, name, rows, weights, far_weights, spreads):
            self.name = name
            self.rows, self.weights, self.far_weights = rows, weights, far_weights
            self.spreads = spreads
            self.pairs, self.far, self.near, self.act = {}, {}, {}, {}
            self.out, self.mid, self.one, self.back, self.third = {}, {}, {}, {}, {}

        def fetch(self, c):
            size, width = height // PIECES, self.rows.shape[1]
            if c == 0 and self.name == "behind":
                rows = self.rows[:size]
                self.pairs[c] = rows, swapped(rows)
                return
            rows = call(
                cut_kernel,
                SMALL if c else ROWS,
                (self.rows,),
                list(recent),
                jax.ShapeDtypeStruct((size, width), BF16),
                in_specs=[pl.BlockSpec((size, width), lambda i: (c, 0))],
                name=f"{self.name}_rows_{c}",
            )
            recent[:] = [rows]
            self.pairs[c] = rows, swapped(rows)

        def far_product(self, c):
            name = f"{self.name}_far_{c}"
            made = first_product(name, True, self.pairs[c], self.far_weights, list(recent))
            recent[:] = [made]
            self.far[c] = made

        def near_products(self):
            rows = [row for c in range(PIECES) for row in self.pairs[c]]
            made = first_product(f"{self.name}_near", False, rows, self.weights, list(recent))
            recent[:] = [made]
            self.near = {c: (made, c) for c in range(PIECES)}

        def near_sum(self, c):
            operands = (self.near[c], self.mid[c])
            return kernel_call(f"{self.name}_third_{c}", sum_kernel, SMALL, operands, self.far[c].shape)

        def first_hop(self, c):
            self.out[c] = outer(self.far[c]) if c == 0 else inward(self.far[c])

        def third_hop(self, c):
            self.third[c] = outward(self.near_sum(c))

        def merged_hop(self, c, first):
            operands = (first, self.near[c - 1], self.mid[c - 1])
            shape = self.far[0].shape
            self.out[c] = outer(
                kernel_call(f"{self.name}_outer_{c}", end_or_sum_kernel, SMALL, operands, shape)
            )
            self.third[c - 1] = self.out[c]

        def last_third_hop(self):
            self.third[PIECES - 1] = outer(self.near_sum(PIECES - 1))

        def middle_sum(self, c):
            mine = self.far[c]
            self.mid[c] = middle(
                kernel_call(
                    f"{self.name}_middle_{c}", sum_kernel, SMALL, (mine, self.out[c]), mine.shape
                )
            )

        def middle_pass(self, c):
            value = self.out[PIECES] if c == 0 else self.back[c]
            shape = (self.spreads, *value.shape[1:])
            value = kernel_call(f"{self.name}_first_{c}", cut_first_kernel, SMALL, (value,), shape)
            self.one[c] = value
            self.mid[PIECES + c] = middle(value)

        def outer_pass(self, c):
            value = self.mid[PIECES + c - 1]
            if c == PIECES:
                value = kernel_call(
                    f"{self.name}_back_{c}", cut_first_kernel, SMALL, (value,), value.shape
                )
            else:
                value = kernel_call(
                    f"{self.name}_back_{c}",
                    end_or_pass_kernel,
                    SMALL,
                    (self.act[c], value),
                    value.shape,
                )
            self.back[c] = outer(value)

        def activated(self, c):
            return self.act[c], self.one[c], self.mid[PIECES + c], self.back[c + 1]

    ahead = Chain("ahead", ahead_rows[0], gates, gates_far, 1)
    behind = Chain("behind", behind_rows[0], gates, gates_far, 2)
    grad = Chain("grad", behind_grad[0], downs, downs_far, 0)
    sent = {}

    def cut(array, c):
        size = height // PIECES
        return array[c * size : (c + 1) * size]

    def activate_ahead(c):
        near = ahead.near[c]
        operands = (near, ahead.third[c])
        ahead.act[c] = kernel_call(f"ahead_act_{c}", ahead_act_kernel, ACT, operands, (1, *ahead.far[c].shape[1:]))

    def activate_behind(c):
        near = behind.near[c]
        operands = (near, behind.third[c], grad.near[c], grad.third[c], cut(scales[1], c))
        behind.act[c] = kernel_call(f"behind_act_{c}", behind_act_kernel, ACT, operands, behind.far[c].shape)

    def output(chain, c):
        forward = chain is ahead
        scale = cut(scales[0], c) if forward else None
        weights = downs if forward else gates
        give, keep = second_product(
            f"{chain.name}_out_{c}", OUT[forward, c], chain.activated(c), scale, weights, list(recent)
        )
        recent[:] = [give]
        return give, keep

    def finish_swapped(chain, c):
        give, keep = output(chain, c)
        sent[chain, c] = swapped(give), keep

    def send_swapped(chain, c):
        share, keep = sent[chain, c]
        total = kernel_call(f"{chain.name}_shares", sum_kernel, SMALL, (keep, share), keep.shape)
        sent[chain, c] = (to_section(total, 1 if chain is ahead else -1, 0),)

    def finish_straight(chain, c):
        give, keep = output(chain, c)
        by = 1 if chain is ahead else -1
        sent[chain, c] = to_section(give, by, 1), to_section(keep, by, 0)

    def result(chain):
        first, second = sent[chain, 0], sent[chain, 1]
        return kernel_call(
            f"{chain.name}_result",
            functools.partial(result_kernel, len(first)),
            SMALL,
            (*first, *second),
            (height, first[0].shape[1]),
        )[None]

    for chain in (behind, ahead, grad):
        chain.fetch(0)
    behind.far_product(0)
    behind.first_hop(0)
    behind.fetch(1)
    ahead.far_product(0)
    ahead.first_hop(0)
    grad.far_product(0)
    grad.first_hop(0)
    behind.middle_sum(0)
    ahead.fetch(1)
    behind.far_product(1)
    behind.near_products()
    ahead.middle_sum(0)
    behind.merged_hop(1, behind.far[1])
    grad.fetch(1)
    grad.middle_sum(0)
    ahead.far_product(1)
    ahead.near_products()
    ahead.merged_hop(1, ahead.far[1])
    behind.middle_sum(1)
    grad.far_product(1)
    grad.near_products()
    grad.merged_hop(1, grad.far[1])
    ahead.middle_sum(1)
    activate_behind(0)
    behind.merged_hop(2, behind.act[0])
    grad.middle_sum(1)
    activate_ahead(0)
    ahead.merged_hop(2, ahead.act[0])
    grad.last_third_hop()
    behind.middle_pass(0)
    ahead.middle_pass(0)
    activate_ahead(1)
    activate_behind(1)
    behind.outer_pass(1)
    ahead.outer_pass(1)
    behind.middle_pass(1)
    ahead.middle_pass(1)
    finish_swapped(behind, 0)
    finish_swapped(ahead, 0)
    behind.outer_pass(2)
    ahead.outer_pass(2)
    send_swapped(behind, 0)
    finish_straight(behind, 1)
    send_swapped(ahead, 0)
    finish_straight(ahead, 1)
    behind_sent = result(behind)
    ahead_sent = result(ahead)
    return ahead_sent, behind_sent


def body(ahead_rows, behind_rows, behind_grad, route_scores, route_counts, gate_up, down_proj):
    groups = lax.axis_size("expert")
    fgroups = groups // DBLOCKS
    low = [[q * fgroups + f for f in range(fgroups)] for q in range(DBLOCKS)]
    high = [[q * fgroups + f for q in range(DBLOCKS)] for f in range(fgroups)]
    height = ahead_rows.shape[1]
    weights_in = gate_up[0, 0]
    weights_out = down_proj[0, 0]
    units = weights_in.shape[1]
    part = units // DBLOCKS

    def wide(rows):
        return lax.all_gather(rows, "expert", axis_index_groups=low, axis=1, tiled=True)

    def reduced(partials):
        flat = partials.reshape(-1, partials.shape[-1])
        total = lax.psum_scatter(
            flat, "expert", axis_index_groups=high, scatter_dimension=0, tiled=True
        )
        return total.astype(F32).reshape(partials.shape[1:])

    def spread(values):
        return lax.all_gather(values, "expert", axis_index_groups=high, axis=0, tiled=False)

    def narrowed(values):
        return lax.psum_scatter(
            values.astype(BF16), "expert", axis_index_groups=low, scatter_dimension=1, tiled=True
        )

    slot_ids = jnp.arange(height, dtype=jnp.int32)
    scale_ahead = route_scores[0, 0] * (slot_ids < route_counts[0, 0]).astype(F32)
    scale_behind = route_scores[0, 1] * (slot_ids < route_counts[0, 1]).astype(F32)
    gates = weights_in.reshape(2, DBLOCKS, part, -1)
    downs = weights_out.reshape(DBLOCKS, part, -1)

    ahead_wide = wide(ahead_rows[0])
    pre_a = jnp.einsum("cd,kqfd->qkcf", ahead_wide, gates, preferred_element_type=F32).astype(BF16)
    sum_a = reduced(pre_a)
    hidden = (sum_a[0] * jax.nn.sigmoid(sum_a[0]) * sum_a[1]).astype(BF16)
    hidden_all = spread(hidden)

    behind_wide = wide(behind_rows[0])
    grad_wide = wide(behind_grad[0])
    pre_b = jnp.einsum("cd,kqfd->qkcf", behind_wide, gates, preferred_element_type=F32).astype(BF16)
    exp_b = jnp.einsum("cd,qfd->qcf", grad_wide, downs, preferred_element_type=F32).astype(BF16)
    sum_b = reduced(jnp.concatenate([pre_b, exp_b[:, None]], axis=1))
    gate, up, expanded = sum_b[0], sum_b[1], sum_b[2] * scale_behind[:, None]
    sig = jax.nn.sigmoid(gate)
    grad_gate = (expanded * up * sig * (1.0 + gate * (1.0 - sig))).astype(BF16)
    grad_up = (expanded * gate * sig).astype(BF16)
    grads_all = spread(jnp.stack([grad_gate, grad_up]))

    out_a = jnp.einsum("qcf,qfd->cd", hidden_all, downs, preferred_element_type=F32)
    ahead_out = (narrowed(out_a).astype(F32) * scale_ahead[:, None]).astype(BF16)
    moved_ahead = shift(ahead_out, "section", 1)
    out_b = jnp.einsum("qkcf,kqfd->cd", grads_all, gates, preferred_element_type=F32)
    behind_out = narrowed(out_b)
    moved_behind = shift(behind_out, "section", -1)
    return (moved_ahead[None], moved_behind[None])


def solution(mesh):
    in_specs = (
        P("section", None, "expert"),
        P("section", None, "expert"),
        P("section", None, "expert"),
        P("section", None, None),
        P("section", None),
        P("section", "expert", None, None, None),
        P("section", "expert", None, None),
    )
    out_specs = (P("section", None, "expert"), P("section", None, "expert"))
    chosen = chain_body if mesh.shape["expert"] == 2 * DBLOCKS else body
    return jax.shard_map(chosen, mesh=mesh, in_specs=in_specs, out_specs=out_specs, check_vma=False)
```

```python
import functools

import jax
import jax.numpy as jnp
from jax import lax
from jax.experimental import pallas as pl
from jax.experimental.pallas import tpu as pltpu
from jax.sharding import PartitionSpec as P

DBLOCKS = 4
BF16 = jnp.bfloat16
F32 = jnp.float32
MIB = 1024 * 1024
PIECES = 2
ROWS, SMALL, ACT, FIRST = 20, 6, 10, 5.2
OUT = {(True, 0): 3, (False, 0): 20, (True, 1): 3, (False, 1): 20}


def shift(shard, axis, by):
    devices = lax.axis_size(axis)
    pairs = [(i, i + by) for i in range(devices) if 0 <= i + by < devices]
    return lax.ppermute(shard, axis, pairs)


def whole(array):
    return pl.BlockSpec(array.shape, functools.partial(lambda n, *_: (0,) * n, array.ndim))


def row_piece(array, c):
    parts, slots, half = array.shape
    return pl.BlockSpec((parts, slots // PIECES, half), lambda *_: (0, c, 0))


def call(kernel, micros, operands, after, out_shape, grid=(1,), in_specs=None, out_specs=None, scratch=(), limit=16, name=None):
    count, unread = len(operands), len(after)

    def run(*refs):
        kernel(*refs[:count], *refs[count + unread :])

    if in_specs is None:
        in_specs = [whole(o) for o in operands]
    if out_specs is None:
        out_specs = jax.tree.map(whole, out_shape)
    return pl.pallas_call(
        run,
        compiler_params=pltpu.CompilerParams(vmem_limit_bytes=limit * MIB),
        cost_estimate=pl.CostEstimate(flops=int(micros * 1e9), bytes_accessed=1024, transcendentals=0),
        out_shape=out_shape,
        name=name,
        grid=grid,
        in_specs=[*in_specs, *[pl.BlockSpec(memory_space=pl.ANY)] * unread],
        out_specs=out_specs,
        scratch_shapes=list(scratch),
    )(*operands, *after)


def cut_kernel(rows, out):
    out[...] = rows[...]


def cut_first_kernel(value, out):
    out[...] = value[: out.shape[0]]


def position():
    own = lax.axis_index("expert")
    block = own // 2
    near = jnp.where(block >= DBLOCKS // 2, 1, 0)
    return near, own % 2, (block == 0) | (block == DBLOCKS - 1)


def first_kernel(far, *refs):
    rows, (weights, out, joined) = refs[:-3], refs[-3:]
    near, group, _ = position()
    side = 0 if far else near
    parts, _, half = out.shape
    slots, width = rows[0].shape
    at = pl.multiple_of(group * width, 128)
    other = pl.multiple_of((1 - group) * width, 128)
    for piece in range(len(rows) // 2):
        here = pl.ds(piece * slots, slots)
        joined[here, pl.ds(at, width)] = rows[2 * piece][...]
        joined[here, pl.ds(other, width)] = rows[2 * piece + 1][...]
    tile = min(256, half)
    for k in range(parts):
        for j in range(half // tile):
            at = pl.multiple_of(side * half + j * tile, tile)
            out[k, :, j * tile : (j + 1) * tile] = lax.dot_general(
                joined[...],
                weights[k, pl.ds(at, tile)],
                (((1,), (1,)), ((), ())),
                preferred_element_type=F32,
            ).astype(BF16)


def first_product(name, far, rows, weights, after):
    slots = rows[0].shape[0] * len(rows) // 2
    parts, units, features = weights.shape
    half = units if far else units // 2
    return call(
        functools.partial(first_kernel, far),
        FIRST * parts,
        (*rows, weights),
        after,
        jax.ShapeDtypeStruct((parts, slots, half), BF16),
        in_specs=[*[whole(r) for r in rows], pl.BlockSpec(memory_space=pltpu.VMEM)],
        scratch=[pltpu.VMEM((slots, features), BF16)],
        name=name,
    )


def sum_kernel(mine, arrived, out):
    out[...] = (mine[...].astype(F32) + arrived[...].astype(F32)).astype(BF16)


def end_or_sum_kernel(at_end, mine, arrived, out):
    _, _, end = position()

    @pl.when(end)
    def _():
        parts = at_end.shape[0]
        out[:parts] = at_end[...]
        if parts < out.shape[0]:
            out[parts:] = jnp.zeros_like(out[parts:])

    @pl.when(jnp.logical_not(end))
    def _():
        out[...] = (mine[...].astype(F32) + arrived[...].astype(F32)).astype(BF16)


def end_or_pass_kernel(at_end, passed, out):
    _, _, end = position()

    @pl.when(end)
    def _():
        out[...] = at_end[...]

    @pl.when(jnp.logical_not(end))
    def _():
        out[...] = passed[...]


def ahead_act_kernel(near, arrived, out):
    gate = near[0].astype(F32) + arrived[0].astype(F32)
    up = near[1].astype(F32) + arrived[1].astype(F32)
    out[0] = (gate * jax.nn.sigmoid(gate) * up).astype(BF16)


def behind_act_kernel(near, arrived, near_e, arrived_e, scale, out):
    gate = near[0].astype(F32) + arrived[0].astype(F32)
    up = near[1].astype(F32) + arrived[1].astype(F32)
    expanded = (near_e[0].astype(F32) + arrived_e[0].astype(F32)) * scale[...]
    sig = jax.nn.sigmoid(gate)
    out[0] = (expanded * up * sig * (1.0 + gate * (1.0 - sig))).astype(BF16)
    out[1] = (expanded * gate * sig).astype(BF16)


def result_kernel(count, *refs):
    shares, out = refs[:-1], refs[-1]
    size = shares[0].shape[0]
    for at, terms in ((0, shares[:count]), (size, shares[count:])):
        total = terms[0][...].astype(F32)
        for term in terms[1:]:
            total += term[...].astype(F32)
        out[at : at + size] = total.astype(BF16)


def second_kernel(scaled, act, one, two, three, *refs):
    scale, refs = (refs[0], refs[1:]) if scaled else (None, refs)
    weights, give, keep, joined = refs
    near_half, group, end = position()
    kinds, _, half = act.shape
    units = weights.shape[1]
    width = give.shape[1]

    def place(near, far):
        for kind in range(kinds):
            at = pl.multiple_of((2 * kind + near_half) * half, 128)
            other = pl.multiple_of((2 * kind + 1 - near_half) * half, 128)
            joined[:, pl.ds(at, half)] = near[kind]
            joined[:, pl.ds(other, half)] = far[kind]

    @pl.when(end)
    def _():
        place(act, three)

    @pl.when(jnp.logical_not(end))
    def _():
        place(one, two)

    for side, out in ((1 - group, give), (group, keep)):
        at = pl.multiple_of(side * width, 128)
        tile = weights[:, :, pl.ds(at, width)].reshape(kinds * units, width)
        share = jnp.dot(joined[...], tile, preferred_element_type=F32)
        if scaled:
            share = share * scale[...]
        out[...] = share.astype(BF16)


def copying_second_kernel(scaled, act, one, two, three, *refs):
    scale, refs = (refs[0], refs[1:]) if scaled else (None, refs)
    weights, give, keep, joined, tiles, sems = refs
    near_half, group, end = position()
    kinds, _, half = act.shape
    _, _, units, width = tiles.shape
    copies = []
    for own in range(2):
        at = pl.multiple_of((group if own else 1 - group) * width, 128)
        copy = pltpu.make_async_copy(
            weights.at[:, :, pl.ds(at, width)], tiles.at[own], sems.at[own]
        )
        copy.start()
        copies.append(copy)

    def place(near, far):
        for kind in range(kinds):
            at = pl.multiple_of((2 * kind + near_half) * half, 128)
            other = pl.multiple_of((2 * kind + 1 - near_half) * half, 128)
            joined[:, pl.ds(at, half)] = near[kind]
            joined[:, pl.ds(other, half)] = far[kind]

    @pl.when(end)
    def _():
        place(act, three)

    @pl.when(jnp.logical_not(end))
    def _():
        place(one, two)

    for own, out in enumerate((give, keep)):
        copies[own].wait()
        share = jnp.dot(
            joined[...], tiles[own].reshape(kinds * units, width), preferred_element_type=F32
        )
        if scaled:
            share = share * scale[...]
        out[...] = share.astype(BF16)


def second_product(name, micros, values, scale, weights, after):
    kinds, units, features = weights.shape
    slots = values[0].shape[1]
    operands = [*values] + ([] if scale is None else [scale])
    share = jax.ShapeDtypeStruct((slots, features // 2), BF16)
    kernel, space = second_kernel, pltpu.VMEM
    scratch = [pltpu.VMEM((slots, kinds * units), BF16)]
    if kinds == 1:
        kernel, space = copying_second_kernel, pl.ANY
        scratch.append(pltpu.VMEM((2, kinds, units, features // 2), BF16))
        scratch.append(pltpu.SemaphoreType.DMA((2,)))
    return call(
        functools.partial(kernel, scale is not None),
        micros,
        (*operands, weights),
        after,
        (share, share),
        in_specs=[*[whole(v) for v in operands], pl.BlockSpec(memory_space=space)],
        scratch=scratch,
        name=name,
    )


def chain_body(ahead_rows, behind_rows, behind_grad, route_scores, route_counts, gate_up, down_proj):
    height = ahead_rows.shape[1]
    gates = gate_up[0, 0]
    downs = down_proj[0]
    sections = lax.axis_size("section")
    devices = 2 * DBLOCKS
    slot_ids = jnp.arange(height, dtype=jnp.int32)[None]
    live = slot_ids < route_counts[0][:, None]
    scales = jnp.where(live, route_scores[0], 0.0)[:, :, None]

    def between(value, to):
        pairs = [(q * 2 + f, to[q] * 2 + f) for q in range(DBLOCKS) for f in range(2) if to[q] is not None]
        return lax.ppermute(value, "expert", pairs)

    def outer(value):
        return between(value, (1, 0, 3, 2))

    def inward(value):
        return between(value, (1, None, None, 2))

    def outward(value):
        return between(value, (None, 0, 3, None))

    def middle(value):
        return between(value, (0, 2, 1, 3))

    def swapped(value):
        return lax.ppermute(value, "expert", [(i, i ^ 1) for i in range(devices)])

    def to_section(value, by, flip):
        pairs = [
            (s * devices + e, (s + by) * devices + (e ^ flip))
            for s in range(sections)
            if 0 <= s + by < sections
            for e in range(devices)
        ]
        return lax.ppermute(value, ("section", "expert"), pairs)

    recent = []

    def kernel_call(name, kernel, micros, operands, shape):
        specs, arrays = [], []
        for operand in operands:
            array, c = operand if isinstance(operand, tuple) else (operand, None)
            arrays.append(array)
            specs.append(whole(array) if c is None else row_piece(array, c))
        made = call(
            kernel,
            micros,
            arrays,
            list(recent),
            jax.ShapeDtypeStruct(shape, BF16),
            in_specs=specs,
            name=name,
        )
        recent[:] = [made]
        return made

    def far_half(weights):
        parts, units, features = weights.shape
        start = jnp.where(lax.axis_index("expert") // 2 >= DBLOCKS // 2, 0, units // 2)
        return lax.dynamic_slice(weights, (0, start, 0), (parts, units // 2, features))

    gates_far, downs_far = far_half(gates), far_half(downs)

    class Chain:
        def __init__(self, name, rows, weights, far_weights, spreads):
            self.name = name
            self.rows, self.weights, self.far_weights = rows, weights, far_weights
            self.spreads = spreads
            self.pairs, self.far, self.near, self.act = {}, {}, {}, {}
            self.out, self.mid, self.one, self.back, self.third = {}, {}, {}, {}, {}

        def fetch(self, c):
            size, width = height // PIECES, self.rows.shape[1]
            if c == 0 and self.name == "behind":
                rows = self.rows[:size]
                self.pairs[c] = rows, swapped(rows)
                return
            rows = call(
                cut_kernel,
                SMALL if c else ROWS,
                (self.rows,),
                list(recent),
                jax.ShapeDtypeStruct((size, width), BF16),
                in_specs=[pl.BlockSpec((size, width), lambda i: (c, 0))],
                name=f"{self.name}_rows_{c}",
            )
            recent[:] = [rows]
            self.pairs[c] = rows, swapped(rows)

        def far_product(self, c):
            name = f"{self.name}_far_{c}"
            made = first_product(name, True, self.pairs[c], self.far_weights, list(recent))
            recent[:] = [made]
            self.far[c] = made

        def near_products(self):
            rows = [row for c in range(PIECES) for row in self.pairs[c]]
            made = first_product(f"{self.name}_near", False, rows, self.weights, list(recent))
            recent[:] = [made]
            self.near = {c: (made, c) for c in range(PIECES)}

        def near_sum(self, c):
            operands = (self.near[c], self.mid[c])
            return kernel_call(f"{self.name}_third_{c}", sum_kernel, SMALL, operands, self.far[c].shape)

        def first_hop(self, c):
            self.out[c] = outer(self.far[c]) if c == 0 else inward(self.far[c])

        def third_hop(self, c):
            self.third[c] = outward(self.near_sum(c))

        def merged_hop(self, c, first):
            operands = (first, self.near[c - 1], self.mid[c - 1])
            shape = self.far[0].shape
            self.out[c] = outer(
                kernel_call(f"{self.name}_outer_{c}", end_or_sum_kernel, SMALL, operands, shape)
            )
            self.third[c - 1] = self.out[c]

        def last_third_hop(self):
            self.third[PIECES - 1] = outer(self.near_sum(PIECES - 1))

        def middle_sum(self, c):
            mine = self.far[c]
            self.mid[c] = middle(
                kernel_call(
                    f"{self.name}_middle_{c}", sum_kernel, SMALL, (mine, self.out[c]), mine.shape
                )
            )

        def middle_pass(self, c):
            value = self.out[PIECES] if c == 0 else self.back[c]
            shape = (self.spreads, *value.shape[1:])
            value = kernel_call(f"{self.name}_first_{c}", cut_first_kernel, SMALL, (value,), shape)
            self.one[c] = value
            self.mid[PIECES + c] = middle(value)

        def outer_pass(self, c):
            value = self.mid[PIECES + c - 1]
            if c == PIECES:
                value = kernel_call(
                    f"{self.name}_back_{c}", cut_first_kernel, SMALL, (value,), value.shape
                )
            else:
                value = kernel_call(
                    f"{self.name}_back_{c}",
                    end_or_pass_kernel,
                    SMALL,
                    (self.act[c], value),
                    value.shape,
                )
            self.back[c] = outer(value)

        def activated(self, c):
            return self.act[c], self.one[c], self.mid[PIECES + c], self.back[c + 1]

    ahead = Chain("ahead", ahead_rows[0], gates, gates_far, 1)
    behind = Chain("behind", behind_rows[0], gates, gates_far, 2)
    grad = Chain("grad", behind_grad[0], downs, downs_far, 0)
    sent = {}

    def cut(array, c):
        size = height // PIECES
        return array[c * size : (c + 1) * size]

    def activate_ahead(c):
        near = ahead.near[c]
        operands = (near, ahead.third[c])
        ahead.act[c] = kernel_call(f"ahead_act_{c}", ahead_act_kernel, ACT, operands, (1, *ahead.far[c].shape[1:]))

    def activate_behind(c):
        near = behind.near[c]
        operands = (near, behind.third[c], grad.near[c], grad.third[c], cut(scales[1], c))
        behind.act[c] = kernel_call(f"behind_act_{c}", behind_act_kernel, ACT, operands, behind.far[c].shape)

    def output(chain, c):
        forward = chain is ahead
        scale = cut(scales[0], c) if forward else None
        weights = downs if forward else gates
        give, keep = second_product(
            f"{chain.name}_out_{c}", OUT[forward, c], chain.activated(c), scale, weights, list(recent)
        )
        recent[:] = [give]
        return give, keep

    def finish_swapped(chain, c):
        give, keep = output(chain, c)
        sent[chain, c] = swapped(give), keep

    def send_swapped(chain, c):
        share, keep = sent[chain, c]
        total = kernel_call(f"{chain.name}_shares", sum_kernel, SMALL, (keep, share), keep.shape)
        sent[chain, c] = (to_section(total, 1 if chain is ahead else -1, 0),)

    def finish_straight(chain, c):
        if chain is ahead:
            recent.extend(sent[chain, 0])
        give, keep = output(chain, c)
        by = 1 if chain is ahead else -1
        sent[chain, c] = to_section(give, by, 1), to_section(keep, by, 0)

    def result(chain):
        first, second = sent[chain, 0], sent[chain, 1]
        return kernel_call(
            f"{chain.name}_result",
            functools.partial(result_kernel, len(first)),
            SMALL,
            (*first, *second),
            (height, first[0].shape[1]),
        )[None]

    for chain in (behind, ahead, grad):
        chain.fetch(0)
    behind.far_product(0)
    behind.first_hop(0)
    behind.fetch(1)
    ahead.far_product(0)
    ahead.first_hop(0)
    behind.middle_sum(0)
    grad.far_product(0)
    grad.first_hop(0)
    ahead.fetch(1)
    behind.far_product(1)
    behind.near_products()
    ahead.middle_sum(0)
    behind.merged_hop(1, behind.far[1])
    grad.fetch(1)
    grad.middle_sum(0)
    ahead.far_product(1)
    ahead.near_products()
    ahead.merged_hop(1, ahead.far[1])
    behind.middle_sum(1)
    grad.far_product(1)
    grad.near_products()
    grad.merged_hop(1, grad.far[1])
    ahead.middle_sum(1)
    activate_behind(0)
    behind.merged_hop(2, behind.act[0])
    grad.middle_sum(1)
    activate_ahead(0)
    ahead.merged_hop(2, ahead.act[0])
    behind.middle_pass(0)
    grad.last_third_hop()
    ahead.middle_pass(0)
    activate_ahead(1)
    activate_behind(1)
    behind.outer_pass(1)
    ahead.outer_pass(1)
    behind.middle_pass(1)
    ahead.middle_pass(1)
    finish_swapped(ahead, 0)
    finish_swapped(behind, 0)
    behind.outer_pass(2)
    ahead.outer_pass(2)
    send_swapped(ahead, 0)
    finish_straight(behind, 1)
    send_swapped(behind, 0)
    finish_straight(ahead, 1)
    behind_sent = result(behind)
    ahead_sent = result(ahead)
    return ahead_sent, behind_sent


def body(ahead_rows, behind_rows, behind_grad, route_scores, route_counts, gate_up, down_proj):
    groups = lax.axis_size("expert")
    fgroups = groups // DBLOCKS
    low = [[q * fgroups + f for f in range(fgroups)] for q in range(DBLOCKS)]
    high = [[q * fgroups + f for q in range(DBLOCKS)] for f in range(fgroups)]
    height = ahead_rows.shape[1]
    weights_in = gate_up[0, 0]
    weights_out = down_proj[0, 0]
    units = weights_in.shape[1]
    part = units // DBLOCKS

    def wide(rows):
        return lax.all_gather(rows, "expert", axis_index_groups=low, axis=1, tiled=True)

    def reduced(partials):
        flat = partials.reshape(-1, partials.shape[-1])
        total = lax.psum_scatter(
            flat, "expert", axis_index_groups=high, scatter_dimension=0, tiled=True
        )
        return total.astype(F32).reshape(partials.shape[1:])

    def spread(values):
        return lax.all_gather(values, "expert", axis_index_groups=high, axis=0, tiled=False)

    def narrowed(values):
        return lax.psum_scatter(
            values.astype(BF16), "expert", axis_index_groups=low, scatter_dimension=1, tiled=True
        )

    slot_ids = jnp.arange(height, dtype=jnp.int32)
    scale_ahead = route_scores[0, 0] * (slot_ids < route_counts[0, 0]).astype(F32)
    scale_behind = route_scores[0, 1] * (slot_ids < route_counts[0, 1]).astype(F32)
    gates = weights_in.reshape(2, DBLOCKS, part, -1)
    downs = weights_out.reshape(DBLOCKS, part, -1)

    ahead_wide = wide(ahead_rows[0])
    pre_a = jnp.einsum("cd,kqfd->qkcf", ahead_wide, gates, preferred_element_type=F32).astype(BF16)
    sum_a = reduced(pre_a)
    hidden = (sum_a[0] * jax.nn.sigmoid(sum_a[0]) * sum_a[1]).astype(BF16)
    hidden_all = spread(hidden)

    behind_wide = wide(behind_rows[0])
    grad_wide = wide(behind_grad[0])
    pre_b = jnp.einsum("cd,kqfd->qkcf", behind_wide, gates, preferred_element_type=F32).astype(BF16)
    exp_b = jnp.einsum("cd,qfd->qcf", grad_wide, downs, preferred_element_type=F32).astype(BF16)
    sum_b = reduced(jnp.concatenate([pre_b, exp_b[:, None]], axis=1))
    gate, up, expanded = sum_b[0], sum_b[1], sum_b[2] * scale_behind[:, None]
    sig = jax.nn.sigmoid(gate)
    grad_gate = (expanded * up * sig * (1.0 + gate * (1.0 - sig))).astype(BF16)
    grad_up = (expanded * gate * sig).astype(BF16)
    grads_all = spread(jnp.stack([grad_gate, grad_up]))

    out_a = jnp.einsum("qcf,qfd->cd", hidden_all, downs, preferred_element_type=F32)
    ahead_out = (narrowed(out_a).astype(F32) * scale_ahead[:, None]).astype(BF16)
    moved_ahead = shift(ahead_out, "section", 1)
    out_b = jnp.einsum("qkcf,kqfd->cd", grads_all, gates, preferred_element_type=F32)
    behind_out = narrowed(out_b)
    moved_behind = shift(behind_out, "section", -1)
    return (moved_ahead[None], moved_behind[None])


def solution(mesh):
    in_specs = (
        P("section", None, "expert"),
        P("section", None, "expert"),
        P("section", None, "expert"),
        P("section", None, None),
        P("section", None),
        P("section", "expert", None, None, None),
        P("section", "expert", None, None),
    )
    out_specs = (P("section", None, "expert"), P("section", None, "expert"))
    chosen = chain_body if mesh.shape["expert"] == 2 * DBLOCKS else body
    return jax.shard_map(chosen, mesh=mesh, in_specs=in_specs, out_specs=out_specs, check_vma=False)
```

```python
import functools

import jax
import jax.numpy as jnp
from jax import lax
from jax.experimental import pallas as pl
from jax.experimental.pallas import tpu as pltpu
from jax.sharding import PartitionSpec as P

DBLOCKS = 4
BF16 = jnp.bfloat16
F32 = jnp.float32
MIB = 1024 * 1024
PIECES = 2
ROWS, SMALL, ACT, FIRST = 20, 6, 10, 5.2
OUT = {(True, 0): 3, (False, 0): 20, (True, 1): 3, (False, 1): 20}


def shift(shard, axis, by):
    devices = lax.axis_size(axis)
    pairs = [(i, i + by) for i in range(devices) if 0 <= i + by < devices]
    return lax.ppermute(shard, axis, pairs)


def whole(array):
    return pl.BlockSpec(array.shape, functools.partial(lambda n, *_: (0,) * n, array.ndim))


def row_piece(array, c):
    parts, slots, half = array.shape
    return pl.BlockSpec((parts, slots // PIECES, half), lambda *_: (0, c, 0))


def call(kernel, micros, operands, after, out_shape, grid=(1,), in_specs=None, out_specs=None, scratch=(), limit=16, name=None):
    count, unread = len(operands), len(after)

    def run(*refs):
        kernel(*refs[:count], *refs[count + unread :])

    if in_specs is None:
        in_specs = [whole(o) for o in operands]
    if out_specs is None:
        out_specs = jax.tree.map(whole, out_shape)
    return pl.pallas_call(
        run,
        compiler_params=pltpu.CompilerParams(vmem_limit_bytes=limit * MIB),
        cost_estimate=pl.CostEstimate(flops=int(micros * 1e9), bytes_accessed=1024, transcendentals=0),
        out_shape=out_shape,
        name=name,
        grid=grid,
        in_specs=[*in_specs, *[pl.BlockSpec(memory_space=pl.ANY)] * unread],
        out_specs=out_specs,
        scratch_shapes=list(scratch),
    )(*operands, *after)


def cut_kernel(rows, out):
    out[...] = rows[...]


def cut_first_kernel(value, out):
    out[...] = value[: out.shape[0]]


def position():
    own = lax.axis_index("expert")
    block = own // 2
    near = jnp.where(block >= DBLOCKS // 2, 1, 0)
    return near, own % 2, (block == 0) | (block == DBLOCKS - 1)


def first_kernel(far, *refs):
    rows, (weights, out, joined) = refs[:-3], refs[-3:]
    near, group, _ = position()
    side = 0 if far else near
    parts, _, half = out.shape
    slots, width = rows[0].shape
    at = pl.multiple_of(group * width, 128)
    other = pl.multiple_of((1 - group) * width, 128)
    for piece in range(len(rows) // 2):
        here = pl.ds(piece * slots, slots)
        joined[here, pl.ds(at, width)] = rows[2 * piece][...]
        joined[here, pl.ds(other, width)] = rows[2 * piece + 1][...]
    tile = min(256, half)
    for k in range(parts):
        for j in range(half // tile):
            at = pl.multiple_of(side * half + j * tile, tile)
            out[k, :, j * tile : (j + 1) * tile] = lax.dot_general(
                joined[...],
                weights[k, pl.ds(at, tile)],
                (((1,), (1,)), ((), ())),
                preferred_element_type=F32,
            ).astype(BF16)


def first_product(name, far, rows, weights, after):
    slots = rows[0].shape[0] * len(rows) // 2
    parts, units, features = weights.shape
    half = units if far else units // 2
    return call(
        functools.partial(first_kernel, far),
        FIRST * parts,
        (*rows, weights),
        after,
        jax.ShapeDtypeStruct((parts, slots, half), BF16),
        in_specs=[*[whole(r) for r in rows], pl.BlockSpec(memory_space=pltpu.VMEM)],
        scratch=[pltpu.VMEM((slots, features), BF16)],
        name=name,
    )


def sum_kernel(mine, arrived, out):
    out[...] = (mine[...].astype(F32) + arrived[...].astype(F32)).astype(BF16)


def end_or_sum_kernel(at_end, mine, arrived, out):
    _, _, end = position()

    @pl.when(end)
    def _():
        parts = at_end.shape[0]
        out[:parts] = at_end[...]
        if parts < out.shape[0]:
            out[parts:] = jnp.zeros_like(out[parts:])

    @pl.when(jnp.logical_not(end))
    def _():
        out[...] = (mine[...].astype(F32) + arrived[...].astype(F32)).astype(BF16)


def end_or_pass_kernel(at_end, passed, out):
    _, _, end = position()

    @pl.when(end)
    def _():
        out[...] = at_end[...]

    @pl.when(jnp.logical_not(end))
    def _():
        out[...] = passed[...]


def ahead_act_kernel(near, arrived, out):
    gate = near[0].astype(F32) + arrived[0].astype(F32)
    up = near[1].astype(F32) + arrived[1].astype(F32)
    out[0] = (gate * jax.nn.sigmoid(gate) * up).astype(BF16)


def behind_act_kernel(near, arrived, near_e, arrived_e, scale, out):
    gate = near[0].astype(F32) + arrived[0].astype(F32)
    up = near[1].astype(F32) + arrived[1].astype(F32)
    expanded = (near_e[0].astype(F32) + arrived_e[0].astype(F32)) * scale[...]
    sig = jax.nn.sigmoid(gate)
    out[0] = (expanded * up * sig * (1.0 + gate * (1.0 - sig))).astype(BF16)
    out[1] = (expanded * gate * sig).astype(BF16)


def result_kernel(count, *refs):
    shares, out = refs[:-1], refs[-1]
    size = shares[0].shape[0]
    for at, terms in ((0, shares[:count]), (size, shares[count:])):
        total = terms[0][...].astype(F32)
        for term in terms[1:]:
            total += term[...].astype(F32)
        out[at : at + size] = total.astype(BF16)


def second_kernel(scaled, act, one, two, three, *refs):
    scale, refs = (refs[0], refs[1:]) if scaled else (None, refs)
    weights, give, keep, joined = refs
    near_half, group, end = position()
    kinds, _, half = act.shape
    units = weights.shape[1]
    width = give.shape[1]

    def place(near, far):
        for kind in range(kinds):
            at = pl.multiple_of((2 * kind + near_half) * half, 128)
            other = pl.multiple_of((2 * kind + 1 - near_half) * half, 128)
            joined[:, pl.ds(at, half)] = near[kind]
            joined[:, pl.ds(other, half)] = far[kind]

    @pl.when(end)
    def _():
        place(act, three)

    @pl.when(jnp.logical_not(end))
    def _():
        place(one, two)

    for side, out in ((1 - group, give), (group, keep)):
        at = pl.multiple_of(side * width, 128)
        tile = weights[:, :, pl.ds(at, width)].reshape(kinds * units, width)
        share = jnp.dot(joined[...], tile, preferred_element_type=F32)
        if scaled:
            share = share * scale[...]
        out[...] = share.astype(BF16)


def copying_second_kernel(scaled, act, one, two, three, *refs):
    scale, refs = (refs[0], refs[1:]) if scaled else (None, refs)
    weights, give, keep, joined, tiles, sems = refs
    near_half, group, end = position()
    kinds, _, half = act.shape
    _, _, units, width = tiles.shape
    copies = []
    for own in range(2):
        at = pl.multiple_of((group if own else 1 - group) * width, 128)
        copy = pltpu.make_async_copy(
            weights.at[:, :, pl.ds(at, width)], tiles.at[own], sems.at[own]
        )
        copy.start()
        copies.append(copy)

    def place(near, far):
        for kind in range(kinds):
            at = pl.multiple_of((2 * kind + near_half) * half, 128)
            other = pl.multiple_of((2 * kind + 1 - near_half) * half, 128)
            joined[:, pl.ds(at, half)] = near[kind]
            joined[:, pl.ds(other, half)] = far[kind]

    @pl.when(end)
    def _():
        place(act, three)

    @pl.when(jnp.logical_not(end))
    def _():
        place(one, two)

    for own, out in enumerate((give, keep)):
        copies[own].wait()
        share = jnp.dot(
            joined[...], tiles[own].reshape(kinds * units, width), preferred_element_type=F32
        )
        if scaled:
            share = share * scale[...]
        out[...] = share.astype(BF16)


def second_product(name, micros, values, scale, weights, after):
    kinds, units, features = weights.shape
    slots = values[0].shape[1]
    operands = [*values] + ([] if scale is None else [scale])
    share = jax.ShapeDtypeStruct((slots, features // 2), BF16)
    kernel, space = second_kernel, pltpu.VMEM
    scratch = [pltpu.VMEM((slots, kinds * units), BF16)]
    if kinds == 1:
        kernel, space = copying_second_kernel, pl.ANY
        scratch.append(pltpu.VMEM((2, kinds, units, features // 2), BF16))
        scratch.append(pltpu.SemaphoreType.DMA((2,)))
    return call(
        functools.partial(kernel, scale is not None),
        micros,
        (*operands, weights),
        after,
        (share, share),
        in_specs=[*[whole(v) for v in operands], pl.BlockSpec(memory_space=space)],
        scratch=scratch,
        name=name,
    )


def chain_body(ahead_rows, behind_rows, behind_grad, route_scores, route_counts, gate_up, down_proj):
    height = ahead_rows.shape[1]
    gates = gate_up[0, 0]
    downs = down_proj[0]
    sections = lax.axis_size("section")
    devices = 2 * DBLOCKS
    slot_ids = jnp.arange(height, dtype=jnp.int32)[None]
    live = slot_ids < route_counts[0][:, None]
    scales = jnp.where(live, route_scores[0], 0.0)[:, :, None]

    def between(value, to):
        pairs = [(q * 2 + f, to[q] * 2 + f) for q in range(DBLOCKS) for f in range(2) if to[q] is not None]
        return lax.ppermute(value, "expert", pairs)

    def outer(value):
        return between(value, (1, 0, 3, 2))

    def inward(value):
        return between(value, (1, None, None, 2))

    def outward(value):
        return between(value, (None, 0, 3, None))

    def middle(value):
        return between(value, (0, 2, 1, 3))

    def swapped(value):
        return lax.ppermute(value, "expert", [(i, i ^ 1) for i in range(devices)])

    def to_section(value, by, flip):
        pairs = [
            (s * devices + e, (s + by) * devices + (e ^ flip))
            for s in range(sections)
            if 0 <= s + by < sections
            for e in range(devices)
        ]
        return lax.ppermute(value, ("section", "expert"), pairs)

    recent = []

    def kernel_call(name, kernel, micros, operands, shape):
        specs, arrays = [], []
        for operand in operands:
            array, c = operand if isinstance(operand, tuple) else (operand, None)
            arrays.append(array)
            specs.append(whole(array) if c is None else row_piece(array, c))
        made = call(
            kernel,
            micros,
            arrays,
            list(recent),
            jax.ShapeDtypeStruct(shape, BF16),
            in_specs=specs,
            name=name,
        )
        recent[:] = [made]
        return made

    def far_half(weights):
        parts, units, features = weights.shape
        start = jnp.where(lax.axis_index("expert") // 2 >= DBLOCKS // 2, 0, units // 2)
        return lax.dynamic_slice(weights, (0, start, 0), (parts, units // 2, features))

    gates_far, downs_far = far_half(gates), far_half(downs)

    class Chain:
        def __init__(self, name, rows, weights, far_weights, spreads):
            self.name = name
            self.rows, self.weights, self.far_weights = rows, weights, far_weights
            self.spreads = spreads
            self.pairs, self.far, self.near, self.act = {}, {}, {}, {}
            self.out, self.mid, self.one, self.back, self.third = {}, {}, {}, {}, {}

        def fetch(self, c):
            size, width = height // PIECES, self.rows.shape[1]
            if c == 0 and self.name == "behind":
                rows = self.rows[:size]
                self.pairs[c] = rows, swapped(rows)
                return
            rows = call(
                cut_kernel,
                SMALL if c else ROWS,
                (self.rows,),
                list(recent),
                jax.ShapeDtypeStruct((size, width), BF16),
                in_specs=[pl.BlockSpec((size, width), lambda i: (c, 0))],
                name=f"{self.name}_rows_{c}",
            )
            recent[:] = [rows]
            self.pairs[c] = rows, swapped(rows)

        def far_product(self, c):
            name = f"{self.name}_far_{c}"
            made = first_product(name, True, self.pairs[c], self.far_weights, list(recent))
            recent[:] = [made]
            self.far[c] = made

        def near_products(self):
            rows = [row for c in range(PIECES) for row in self.pairs[c]]
            made = first_product(f"{self.name}_near", False, rows, self.weights, list(recent))
            recent[:] = [made]
            self.near = {c: (made, c) for c in range(PIECES)}

        def near_sum(self, c):
            operands = (self.near[c], self.mid[c])
            return kernel_call(f"{self.name}_third_{c}", sum_kernel, SMALL, operands, self.far[c].shape)

        def first_hop(self, c):
            self.out[c] = outer(self.far[c]) if c == 0 else inward(self.far[c])

        def third_hop(self, c):
            self.third[c] = outward(self.near_sum(c))

        def merged_hop(self, c, first):
            operands = (first, self.near[c - 1], self.mid[c - 1])
            shape = self.far[0].shape
            self.out[c] = outer(
                kernel_call(f"{self.name}_outer_{c}", end_or_sum_kernel, SMALL, operands, shape)
            )
            self.third[c - 1] = self.out[c]

        def last_third_hop(self):
            self.third[PIECES - 1] = outer(self.near_sum(PIECES - 1))

        def middle_sum(self, c):
            mine = self.far[c]
            self.mid[c] = middle(
                kernel_call(
                    f"{self.name}_middle_{c}", sum_kernel, SMALL, (mine, self.out[c]), mine.shape
                )
            )

        def middle_pass(self, c):
            value = self.out[PIECES] if c == 0 else self.back[c]
            shape = (self.spreads, *value.shape[1:])
            value = kernel_call(f"{self.name}_first_{c}", cut_first_kernel, SMALL, (value,), shape)
            self.one[c] = value
            self.mid[PIECES + c] = middle(value)

        def outer_pass(self, c):
            value = self.mid[PIECES + c - 1]
            if c == PIECES:
                value = kernel_call(
                    f"{self.name}_back_{c}", cut_first_kernel, SMALL, (value,), value.shape
                )
            else:
                value = kernel_call(
                    f"{self.name}_back_{c}",
                    end_or_pass_kernel,
                    SMALL,
                    (self.act[c], value),
                    value.shape,
                )
            self.back[c] = outer(value)

        def activated(self, c):
            return self.act[c], self.one[c], self.mid[PIECES + c], self.back[c + 1]

    ahead = Chain("ahead", ahead_rows[0], gates, gates_far, 1)
    behind = Chain("behind", behind_rows[0], gates, gates_far, 2)
    grad = Chain("grad", behind_grad[0], downs, downs_far, 0)
    sent = {}

    def cut(array, c):
        size = height // PIECES
        return array[c * size : (c + 1) * size]

    def activate_ahead(c):
        near = ahead.near[c]
        operands = (near, ahead.third[c])
        ahead.act[c] = kernel_call(f"ahead_act_{c}", ahead_act_kernel, ACT, operands, (1, *ahead.far[c].shape[1:]))

    def activate_behind(c):
        near = behind.near[c]
        operands = (near, behind.third[c], grad.near[c], grad.third[c], cut(scales[1], c))
        behind.act[c] = kernel_call(f"behind_act_{c}", behind_act_kernel, ACT, operands, behind.far[c].shape)

    def output(chain, c):
        forward = chain is ahead
        scale = cut(scales[0], c) if forward else None
        weights = downs if forward else gates
        give, keep = second_product(
            f"{chain.name}_out_{c}", OUT[forward, c], chain.activated(c), scale, weights, list(recent)
        )
        recent[:] = [give]
        return give, keep

    def finish_swapped(chain, c):
        give, keep = output(chain, c)
        sent[chain, c] = swapped(give), keep

    def send_swapped(chain, c):
        share, keep = sent[chain, c]
        total = kernel_call(f"{chain.name}_shares", sum_kernel, SMALL, (keep, share), keep.shape)
        sent[chain, c] = (to_section(total, 1 if chain is ahead else -1, 0),)

    def finish_straight(chain, c):
        give, keep = output(chain, c)
        by = 1 if chain is ahead else -1
        sent[chain, c] = to_section(give, by, 1), to_section(keep, by, 0)

    def result(chain):
        first, second = sent[chain, 0], sent[chain, 1]
        return kernel_call(
            f"{chain.name}_result",
            functools.partial(result_kernel, len(first)),
            SMALL,
            (*first, *second),
            (height, first[0].shape[1]),
        )[None]

    for chain in (behind, ahead, grad):
        chain.fetch(0)
    behind.far_product(0)
    behind.first_hop(0)
    behind.fetch(1)
    ahead.far_product(0)
    ahead.first_hop(0)
    behind.middle_sum(0)
    grad.far_product(0)
    grad.first_hop(0)
    ahead.fetch(1)
    behind.far_product(1)
    behind.near_products()
    behind.merged_hop(1, behind.far[1])
    ahead.middle_sum(0)
    grad.fetch(1)
    grad.middle_sum(0)
    ahead.far_product(1)
    behind.middle_sum(1)
    ahead.near_products()
    ahead.merged_hop(1, ahead.far[1])
    grad.far_product(1)
    grad.near_products()
    grad.merged_hop(1, grad.far[1])
    ahead.middle_sum(1)
    activate_behind(0)
    behind.merged_hop(2, behind.act[0])
    grad.middle_sum(1)
    activate_ahead(0)
    ahead.merged_hop(2, ahead.act[0])
    behind.middle_pass(0)
    grad.last_third_hop()
    ahead.middle_pass(0)
    activate_ahead(1)
    activate_behind(1)
    behind.outer_pass(1)
    ahead.outer_pass(1)
    behind.middle_pass(1)
    ahead.middle_pass(1)
    finish_swapped(behind, 0)
    finish_swapped(ahead, 0)
    behind.outer_pass(2)
    ahead.outer_pass(2)
    send_swapped(behind, 0)
    finish_straight(behind, 1)
    send_swapped(ahead, 0)
    finish_straight(ahead, 1)
    behind_sent = result(behind)
    ahead_sent = result(ahead)
    return ahead_sent, behind_sent


def body(ahead_rows, behind_rows, behind_grad, route_scores, route_counts, gate_up, down_proj):
    groups = lax.axis_size("expert")
    fgroups = groups // DBLOCKS
    low = [[q * fgroups + f for f in range(fgroups)] for q in range(DBLOCKS)]
    high = [[q * fgroups + f for q in range(DBLOCKS)] for f in range(fgroups)]
    height = ahead_rows.shape[1]
    weights_in = gate_up[0, 0]
    weights_out = down_proj[0, 0]
    units = weights_in.shape[1]
    part = units // DBLOCKS

    def wide(rows):
        return lax.all_gather(rows, "expert", axis_index_groups=low, axis=1, tiled=True)

    def reduced(partials):
        flat = partials.reshape(-1, partials.shape[-1])
        total = lax.psum_scatter(
            flat, "expert", axis_index_groups=high, scatter_dimension=0, tiled=True
        )
        return total.astype(F32).reshape(partials.shape[1:])

    def spread(values):
        return lax.all_gather(values, "expert", axis_index_groups=high, axis=0, tiled=False)

    def narrowed(values):
        return lax.psum_scatter(
            values.astype(BF16), "expert", axis_index_groups=low, scatter_dimension=1, tiled=True
        )

    slot_ids = jnp.arange(height, dtype=jnp.int32)
    scale_ahead = route_scores[0, 0] * (slot_ids < route_counts[0, 0]).astype(F32)
    scale_behind = route_scores[0, 1] * (slot_ids < route_counts[0, 1]).astype(F32)
    gates = weights_in.reshape(2, DBLOCKS, part, -1)
    downs = weights_out.reshape(DBLOCKS, part, -1)

    ahead_wide = wide(ahead_rows[0])
    pre_a = jnp.einsum("cd,kqfd->qkcf", ahead_wide, gates, preferred_element_type=F32).astype(BF16)
    sum_a = reduced(pre_a)
    hidden = (sum_a[0] * jax.nn.sigmoid(sum_a[0]) * sum_a[1]).astype(BF16)
    hidden_all = spread(hidden)

    behind_wide = wide(behind_rows[0])
    grad_wide = wide(behind_grad[0])
    pre_b = jnp.einsum("cd,kqfd->qkcf", behind_wide, gates, preferred_element_type=F32).astype(BF16)
    exp_b = jnp.einsum("cd,qfd->qcf", grad_wide, downs, preferred_element_type=F32).astype(BF16)
    sum_b = reduced(jnp.concatenate([pre_b, exp_b[:, None]], axis=1))
    gate, up, expanded = sum_b[0], sum_b[1], sum_b[2] * scale_behind[:, None]
    sig = jax.nn.sigmoid(gate)
    grad_gate = (expanded * up * sig * (1.0 + gate * (1.0 - sig))).astype(BF16)
    grad_up = (expanded * gate * sig).astype(BF16)
    grads_all = spread(jnp.stack([grad_gate, grad_up]))

    out_a = jnp.einsum("qcf,qfd->cd", hidden_all, downs, preferred_element_type=F32)
    ahead_out = (narrowed(out_a).astype(F32) * scale_ahead[:, None]).astype(BF16)
    moved_ahead = shift(ahead_out, "section", 1)
    out_b = jnp.einsum("qkcf,kqfd->cd", grads_all, gates, preferred_element_type=F32)
    behind_out = narrowed(out_b)
    moved_behind = shift(behind_out, "section", -1)
    return (moved_ahead[None], moved_behind[None])


def solution(mesh):
    in_specs = (
        P("section", None, "expert"),
        P("section", None, "expert"),
        P("section", None, "expert"),
        P("section", None, None),
        P("section", None),
        P("section", "expert", None, None, None),
        P("section", "expert", None, None),
    )
    out_specs = (P("section", None, "expert"), P("section", None, "expert"))
    chosen = chain_body if mesh.shape["expert"] == 2 * DBLOCKS else body
    return jax.shard_map(chosen, mesh=mesh, in_specs=in_specs, out_specs=out_specs, check_vma=False)
```

```python
import functools

import jax
import jax.numpy as jnp
from jax import lax
from jax.experimental import pallas as pl
from jax.experimental.pallas import tpu as pltpu
from jax.sharding import PartitionSpec as P

DBLOCKS = 4
BF16 = jnp.bfloat16
F32 = jnp.float32
MIB = 1024 * 1024
PIECES = 2
ROWS, SMALL, ACT, FIRST = 20, 6, 10, 5.2
OUT = {(True, 0): 3, (False, 0): 20, (True, 1): 3, (False, 1): 20}


def shift(shard, axis, by):
    devices = lax.axis_size(axis)
    pairs = [(i, i + by) for i in range(devices) if 0 <= i + by < devices]
    return lax.ppermute(shard, axis, pairs)


def whole(array):
    return pl.BlockSpec(array.shape, functools.partial(lambda n, *_: (0,) * n, array.ndim))


def row_piece(array, c):
    parts, slots, half = array.shape
    return pl.BlockSpec((parts, slots // PIECES, half), lambda *_: (0, c, 0))


def call(kernel, micros, operands, after, out_shape, grid=(1,), in_specs=None, out_specs=None, scratch=(), limit=16, name=None):
    count, unread = len(operands), len(after)

    def run(*refs):
        kernel(*refs[:count], *refs[count + unread :])

    if in_specs is None:
        in_specs = [whole(o) for o in operands]
    if out_specs is None:
        out_specs = jax.tree.map(whole, out_shape)
    return pl.pallas_call(
        run,
        compiler_params=pltpu.CompilerParams(vmem_limit_bytes=limit * MIB),
        cost_estimate=pl.CostEstimate(flops=int(micros * 1e9), bytes_accessed=1024, transcendentals=0),
        out_shape=out_shape,
        name=name,
        grid=grid,
        in_specs=[*in_specs, *[pl.BlockSpec(memory_space=pl.ANY)] * unread],
        out_specs=out_specs,
        scratch_shapes=list(scratch),
    )(*operands, *after)


def cut_kernel(rows, out):
    out[...] = rows[...]


def cut_first_kernel(value, out):
    out[...] = value[: out.shape[0]]


def position():
    own = lax.axis_index("expert")
    block = own // 2
    near = jnp.where(block >= DBLOCKS // 2, 1, 0)
    return near, own % 2, (block == 0) | (block == DBLOCKS - 1)


def first_kernel(far, *refs):
    rows, (weights, out, joined) = refs[:-3], refs[-3:]
    near, group, _ = position()
    side = 1 - near if far else near
    parts, _, half = out.shape
    slots, width = rows[0].shape
    at = pl.multiple_of(group * width, 128)
    other = pl.multiple_of((1 - group) * width, 128)
    for piece in range(len(rows) // 2):
        here = pl.ds(piece * slots, slots)
        joined[here, pl.ds(at, width)] = rows[2 * piece][...]
        joined[here, pl.ds(other, width)] = rows[2 * piece + 1][...]
    tile = min(256, half)
    for k in range(parts):
        for j in range(half // tile):
            at = pl.multiple_of(side * half + j * tile, tile)
            out[k, :, j * tile : (j + 1) * tile] = lax.dot_general(
                joined[...],
                weights[k, pl.ds(at, tile)],
                (((1,), (1,)), ((), ())),
                preferred_element_type=F32,
            ).astype(BF16)


def first_product(name, far, rows, weights, after):
    slots = rows[0].shape[0] * len(rows) // 2
    parts, units, features = weights.shape
    half = units // 2
    return call(
        functools.partial(first_kernel, far),
        FIRST * parts,
        (*rows, weights),
        after,
        jax.ShapeDtypeStruct((parts, slots, half), BF16),
        in_specs=[*[whole(r) for r in rows], pl.BlockSpec(memory_space=pltpu.VMEM)],
        scratch=[pltpu.VMEM((slots, features), BF16)],
        name=name,
    )


def sum_kernel(mine, arrived, out):
    out[...] = (mine[...].astype(F32) + arrived[...].astype(F32)).astype(BF16)


def end_or_sum_kernel(at_end, mine, arrived, out):
    _, _, end = position()

    @pl.when(end)
    def _():
        parts = at_end.shape[0]
        out[:parts] = at_end[...]
        if parts < out.shape[0]:
            out[parts:] = jnp.zeros_like(out[parts:])

    @pl.when(jnp.logical_not(end))
    def _():
        out[...] = (mine[...].astype(F32) + arrived[...].astype(F32)).astype(BF16)


def end_or_pass_kernel(at_end, passed, out):
    _, _, end = position()

    @pl.when(end)
    def _():
        out[...] = at_end[...]

    @pl.when(jnp.logical_not(end))
    def _():
        out[...] = passed[...]


def ahead_act_kernel(near, arrived, out):
    gate = near[0].astype(F32) + arrived[0].astype(F32)
    up = near[1].astype(F32) + arrived[1].astype(F32)
    out[0] = (gate * jax.nn.sigmoid(gate) * up).astype(BF16)


def behind_act_kernel(near, arrived, near_e, arrived_e, scale, out):
    gate = near[0].astype(F32) + arrived[0].astype(F32)
    up = near[1].astype(F32) + arrived[1].astype(F32)
    expanded = (near_e[0].astype(F32) + arrived_e[0].astype(F32)) * scale[...]
    sig = jax.nn.sigmoid(gate)
    out[0] = (expanded * up * sig * (1.0 + gate * (1.0 - sig))).astype(BF16)
    out[1] = (expanded * gate * sig).astype(BF16)


def result_kernel(count, *refs):
    shares, out = refs[:-1], refs[-1]
    size = shares[0].shape[0]
    for at, terms in ((0, shares[:count]), (size, shares[count:])):
        total = terms[0][...].astype(F32)
        for term in terms[1:]:
            total += term[...].astype(F32)
        out[at : at + size] = total.astype(BF16)


def second_kernel(scaled, act, one, two, three, *refs):
    scale, refs = (refs[0], refs[1:]) if scaled else (None, refs)
    weights, give, keep, joined = refs
    near_half, group, end = position()
    kinds, _, half = act.shape
    units = weights.shape[1]
    width = give.shape[1]

    def place(near, far):
        for kind in range(kinds):
            at = pl.multiple_of((2 * kind + near_half) * half, 128)
            other = pl.multiple_of((2 * kind + 1 - near_half) * half, 128)
            joined[:, pl.ds(at, half)] = near[kind]
            joined[:, pl.ds(other, half)] = far[kind]

    @pl.when(end)
    def _():
        place(act, three)

    @pl.when(jnp.logical_not(end))
    def _():
        place(one, two)

    for side, out in ((1 - group, give), (group, keep)):
        at = pl.multiple_of(side * width, 128)
        tile = weights[:, :, pl.ds(at, width)].reshape(kinds * units, width)
        share = jnp.dot(joined[...], tile, preferred_element_type=F32)
        if scaled:
            share = share * scale[...]
        out[...] = share.astype(BF16)


def copying_second_kernel(scaled, act, one, two, three, *refs):
    scale, refs = (refs[0], refs[1:]) if scaled else (None, refs)
    weights, give, keep, joined, tiles, sems = refs
    near_half, group, end = position()
    kinds, _, half = act.shape
    _, _, units, width = tiles.shape
    copies = []
    for own in range(2):
        at = pl.multiple_of((group if own else 1 - group) * width, 128)
        copy = pltpu.make_async_copy(
            weights.at[:, :, pl.ds(at, width)], tiles.at[own], sems.at[own]
        )
        copy.start()
        copies.append(copy)

    def place(near, far):
        for kind in range(kinds):
            at = pl.multiple_of((2 * kind + near_half) * half, 128)
            other = pl.multiple_of((2 * kind + 1 - near_half) * half, 128)
            joined[:, pl.ds(at, half)] = near[kind]
            joined[:, pl.ds(other, half)] = far[kind]

    @pl.when(end)
    def _():
        place(act, three)

    @pl.when(jnp.logical_not(end))
    def _():
        place(one, two)

    for own, out in enumerate((give, keep)):
        copies[own].wait()
        share = jnp.dot(
            joined[...], tiles[own].reshape(kinds * units, width), preferred_element_type=F32
        )
        if scaled:
            share = share * scale[...]
        out[...] = share.astype(BF16)


def second_product(name, micros, values, scale, weights, after):
    kinds, units, features = weights.shape
    slots = values[0].shape[1]
    operands = [*values] + ([] if scale is None else [scale])
    share = jax.ShapeDtypeStruct((slots, features // 2), BF16)
    kernel, space = second_kernel, pltpu.VMEM
    scratch = [pltpu.VMEM((slots, kinds * units), BF16)]
    if kinds == 1:
        kernel, space = copying_second_kernel, pl.ANY
        scratch.append(pltpu.VMEM((2, kinds, units, features // 2), BF16))
        scratch.append(pltpu.SemaphoreType.DMA((2,)))
    return call(
        functools.partial(kernel, scale is not None),
        micros,
        (*operands, weights),
        after,
        (share, share),
        in_specs=[*[whole(v) for v in operands], pl.BlockSpec(memory_space=space)],
        scratch=scratch,
        name=name,
    )


def chain_body(ahead_rows, behind_rows, behind_grad, route_scores, route_counts, gate_up, down_proj):
    height = ahead_rows.shape[1]
    gates = gate_up[0, 0]
    downs = down_proj[0]
    sections = lax.axis_size("section")
    devices = 2 * DBLOCKS
    slot_ids = jnp.arange(height, dtype=jnp.int32)[None]
    live = slot_ids < route_counts[0][:, None]
    scales = jnp.where(live, route_scores[0], 0.0)[:, :, None]

    def between(value, to):
        pairs = [(q * 2 + f, to[q] * 2 + f) for q in range(DBLOCKS) for f in range(2) if to[q] is not None]
        return lax.ppermute(value, "expert", pairs)

    def outer(value):
        return between(value, (1, 0, 3, 2))

    def inward(value):
        return between(value, (1, None, None, 2))

    def outward(value):
        return between(value, (None, 0, 3, None))

    def middle(value):
        return between(value, (0, 2, 1, 3))

    def swapped(value):
        return lax.ppermute(value, "expert", [(i, i ^ 1) for i in range(devices)])

    def to_section(value, by, flip):
        pairs = [
            (s * devices + e, (s + by) * devices + (e ^ flip))
            for s in range(sections)
            if 0 <= s + by < sections
            for e in range(devices)
        ]
        return lax.ppermute(value, ("section", "expert"), pairs)

    recent = []

    def kernel_call(name, kernel, micros, operands, shape):
        specs, arrays = [], []
        for operand in operands:
            array, c = operand if isinstance(operand, tuple) else (operand, None)
            arrays.append(array)
            specs.append(whole(array) if c is None else row_piece(array, c))
        made = call(
            kernel,
            micros,
            arrays,
            list(recent),
            jax.ShapeDtypeStruct(shape, BF16),
            in_specs=specs,
            name=name,
        )
        recent[:] = [made]
        return made

    class Chain:
        def __init__(self, name, rows, weights, spreads):
            self.name = name
            self.rows, self.weights = rows, weights
            self.spreads = spreads
            self.pairs, self.far, self.near, self.act = {}, {}, {}, {}
            self.out, self.mid, self.one, self.back, self.third = {}, {}, {}, {}, {}

        def fetch(self, c):
            size, width = height // PIECES, self.rows.shape[1]
            if c == 0 and self.name == "behind":
                rows = self.rows[:size]
                self.pairs[c] = rows, swapped(rows)
                return
            rows = call(
                cut_kernel,
                SMALL if c else ROWS,
                (self.rows,),
                list(recent),
                jax.ShapeDtypeStruct((size, width), BF16),
                in_specs=[pl.BlockSpec((size, width), lambda i: (c, 0))],
                name=f"{self.name}_rows_{c}",
            )
            recent[:] = [rows]
            self.pairs[c] = rows, swapped(rows)

        def far_product(self, c):
            name = f"{self.name}_far_{c}"
            made = first_product(name, True, self.pairs[c], self.weights, list(recent))
            recent[:] = [made]
            self.far[c] = made

        def near_products(self):
            rows = [row for c in range(PIECES) for row in self.pairs[c]]
            made = first_product(f"{self.name}_near", False, rows, self.weights, list(recent))
            recent[:] = [made]
            self.near = {c: (made, c) for c in range(PIECES)}

        def near_sum(self, c):
            operands = (self.near[c], self.mid[c])
            return kernel_call(f"{self.name}_third_{c}", sum_kernel, SMALL, operands, self.far[c].shape)

        def first_hop(self, c):
            self.out[c] = outer(self.far[c]) if c == 0 else inward(self.far[c])

        def third_hop(self, c):
            self.third[c] = outward(self.near_sum(c))

        def merged_hop(self, c, first):
            operands = (first, self.near[c - 1], self.mid[c - 1])
            shape = self.far[0].shape
            self.out[c] = outer(
                kernel_call(f"{self.name}_outer_{c}", end_or_sum_kernel, SMALL, operands, shape)
            )
            self.third[c - 1] = self.out[c]

        def last_third_hop(self):
            self.third[PIECES - 1] = outer(self.near_sum(PIECES - 1))

        def middle_sum(self, c):
            mine = self.far[c]
            self.mid[c] = middle(
                kernel_call(
                    f"{self.name}_middle_{c}", sum_kernel, SMALL, (mine, self.out[c]), mine.shape
                )
            )

        def middle_pass(self, c):
            value = self.out[PIECES] if c == 0 else self.back[c]
            shape = (self.spreads, *value.shape[1:])
            value = kernel_call(f"{self.name}_first_{c}", cut_first_kernel, SMALL, (value,), shape)
            self.one[c] = value
            self.mid[PIECES + c] = middle(value)

        def outer_pass(self, c):
            value = self.mid[PIECES + c - 1]
            if c == PIECES:
                value = kernel_call(
                    f"{self.name}_back_{c}", cut_first_kernel, SMALL, (value,), value.shape
                )
            else:
                value = kernel_call(
                    f"{self.name}_back_{c}",
                    end_or_pass_kernel,
                    SMALL,
                    (self.act[c], value),
                    value.shape,
                )
            self.back[c] = outer(value)

        def activated(self, c):
            return self.act[c], self.one[c], self.mid[PIECES + c], self.back[c + 1]

    ahead = Chain("ahead", ahead_rows[0], gates, 1)
    behind = Chain("behind", behind_rows[0], gates, 2)
    grad = Chain("grad", behind_grad[0], downs, 0)
    sent = {}

    def cut(array, c):
        size = height // PIECES
        return array[c * size : (c + 1) * size]

    def activate_ahead(c):
        near = ahead.near[c]
        operands = (near, ahead.third[c])
        ahead.act[c] = kernel_call(f"ahead_act_{c}", ahead_act_kernel, ACT, operands, (1, *ahead.far[c].shape[1:]))

    def activate_behind(c):
        near = behind.near[c]
        operands = (near, behind.third[c], grad.near[c], grad.third[c], cut(scales[1], c))
        behind.act[c] = kernel_call(f"behind_act_{c}", behind_act_kernel, ACT, operands, behind.far[c].shape)

    def output(chain, c):
        forward = chain is ahead
        scale = cut(scales[0], c) if forward else None
        weights = downs if forward else gates
        give, keep = second_product(
            f"{chain.name}_out_{c}", OUT[forward, c], chain.activated(c), scale, weights, list(recent)
        )
        recent[:] = [give]
        return give, keep

    def finish_swapped(chain, c):
        give, keep = output(chain, c)
        sent[chain, c] = swapped(give), keep

    def send_swapped(chain, c):
        share, keep = sent[chain, c]
        total = kernel_call(f"{chain.name}_shares", sum_kernel, SMALL, (keep, share), keep.shape)
        sent[chain, c] = (to_section(total, 1 if chain is ahead else -1, 0),)

    def finish_straight(chain, c):
        give, keep = output(chain, c)
        by = 1 if chain is ahead else -1
        sent[chain, c] = to_section(give, by, 1), to_section(keep, by, 0)

    def result(chain):
        first, second = sent[chain, 0], sent[chain, 1]
        return kernel_call(
            f"{chain.name}_result",
            functools.partial(result_kernel, len(first)),
            SMALL,
            (*first, *second),
            (height, first[0].shape[1]),
        )[None]

    for chain in (behind, ahead, grad):
        chain.fetch(0)
    behind.far_product(0)
    behind.first_hop(0)
    behind.fetch(1)
    ahead.far_product(0)
    ahead.first_hop(0)
    grad.fetch(1)
    behind.middle_sum(0)
    grad.far_product(0)
    grad.first_hop(0)
    behind.far_product(1)
    ahead.fetch(1)
    behind.near_products()
    behind.merged_hop(1, behind.far[1])
    ahead.middle_sum(0)
    grad.middle_sum(0)
    grad.far_product(1)
    grad.near_products()
    behind.middle_sum(1)
    ahead.far_product(1)
    grad.merged_hop(1, grad.far[1])
    ahead.near_products()
    ahead.merged_hop(1, ahead.far[1])
    activate_behind(0)
    behind.merged_hop(2, behind.act[0])
    ahead.middle_sum(1)
    grad.middle_sum(1)
    activate_ahead(0)
    ahead.merged_hop(2, ahead.act[0])
    behind.middle_pass(0)
    grad.last_third_hop()
    ahead.middle_pass(0)
    activate_ahead(1)
    activate_behind(1)
    behind.outer_pass(1)
    ahead.outer_pass(1)
    behind.middle_pass(1)
    ahead.middle_pass(1)
    finish_swapped(behind, 0)
    finish_swapped(ahead, 0)
    behind.outer_pass(2)
    ahead.outer_pass(2)
    send_swapped(behind, 0)
    finish_straight(behind, 1)
    send_swapped(ahead, 0)
    finish_straight(ahead, 1)
    behind_sent = result(behind)
    ahead_sent = result(ahead)
    return ahead_sent, behind_sent


def body(ahead_rows, behind_rows, behind_grad, route_scores, route_counts, gate_up, down_proj):
    groups = lax.axis_size("expert")
    fgroups = groups // DBLOCKS
    low = [[q * fgroups + f for f in range(fgroups)] for q in range(DBLOCKS)]
    high = [[q * fgroups + f for q in range(DBLOCKS)] for f in range(fgroups)]
    height = ahead_rows.shape[1]
    weights_in = gate_up[0, 0]
    weights_out = down_proj[0, 0]
    units = weights_in.shape[1]
    part = units // DBLOCKS

    def wide(rows):
        return lax.all_gather(rows, "expert", axis_index_groups=low, axis=1, tiled=True)

    def reduced(partials):
        flat = partials.reshape(-1, partials.shape[-1])
        total = lax.psum_scatter(
            flat, "expert", axis_index_groups=high, scatter_dimension=0, tiled=True
        )
        return total.astype(F32).reshape(partials.shape[1:])

    def spread(values):
        return lax.all_gather(values, "expert", axis_index_groups=high, axis=0, tiled=False)

    def narrowed(values):
        return lax.psum_scatter(
            values.astype(BF16), "expert", axis_index_groups=low, scatter_dimension=1, tiled=True
        )

    slot_ids = jnp.arange(height, dtype=jnp.int32)
    scale_ahead = route_scores[0, 0] * (slot_ids < route_counts[0, 0]).astype(F32)
    scale_behind = route_scores[0, 1] * (slot_ids < route_counts[0, 1]).astype(F32)
    gates = weights_in.reshape(2, DBLOCKS, part, -1)
    downs = weights_out.reshape(DBLOCKS, part, -1)

    ahead_wide = wide(ahead_rows[0])
    pre_a = jnp.einsum("cd,kqfd->qkcf", ahead_wide, gates, preferred_element_type=F32).astype(BF16)
    sum_a = reduced(pre_a)
    hidden = (sum_a[0] * jax.nn.sigmoid(sum_a[0]) * sum_a[1]).astype(BF16)
    hidden_all = spread(hidden)

    behind_wide = wide(behind_rows[0])
    grad_wide = wide(behind_grad[0])
    pre_b = jnp.einsum("cd,kqfd->qkcf", behind_wide, gates, preferred_element_type=F32).astype(BF16)
    exp_b = jnp.einsum("cd,qfd->qcf", grad_wide, downs, preferred_element_type=F32).astype(BF16)
    sum_b = reduced(jnp.concatenate([pre_b, exp_b[:, None]], axis=1))
    gate, up, expanded = sum_b[0], sum_b[1], sum_b[2] * scale_behind[:, None]
    sig = jax.nn.sigmoid(gate)
    grad_gate = (expanded * up * sig * (1.0 + gate * (1.0 - sig))).astype(BF16)
    grad_up = (expanded * gate * sig).astype(BF16)
    grads_all = spread(jnp.stack([grad_gate, grad_up]))

    out_a = jnp.einsum("qcf,qfd->cd", hidden_all, downs, preferred_element_type=F32)
    ahead_out = (narrowed(out_a).astype(F32) * scale_ahead[:, None]).astype(BF16)
    moved_ahead = shift(ahead_out, "section", 1)
    out_b = jnp.einsum("qkcf,kqfd->cd", grads_all, gates, preferred_element_type=F32)
    behind_out = narrowed(out_b)
    moved_behind = shift(behind_out, "section", -1)
    return (moved_ahead[None], moved_behind[None])


def solution(mesh):
    in_specs = (
        P("section", None, "expert"),
        P("section", None, "expert"),
        P("section", None, "expert"),
        P("section", None, None),
        P("section", None),
        P("section", "expert", None, None, None),
        P("section", "expert", None, None),
    )
    out_specs = (P("section", None, "expert"), P("section", None, "expert"))
    chosen = chain_body if mesh.shape["expert"] == 2 * DBLOCKS else body
    return jax.shard_map(chosen, mesh=mesh, in_specs=in_specs, out_specs=out_specs, check_vma=False)
```

```python
import functools

import jax
import jax.numpy as jnp
from jax import lax
from jax.experimental import pallas as pl
from jax.experimental.pallas import tpu as pltpu
from jax.sharding import PartitionSpec as P

DBLOCKS = 4
BF16 = jnp.bfloat16
F32 = jnp.float32
MIB = 1024 * 1024
PIECES = 2
ROWS, SMALL, ACT, FIRST, AHEAD_OUT, BEHIND_OUT = 20, 6, 10, 5.2, 3, 20


def shift(shard, axis, by):
    devices = lax.axis_size(axis)
    pairs = [(i, i + by) for i in range(devices) if 0 <= i + by < devices]
    return lax.ppermute(shard, axis, pairs)


def whole(array):
    return pl.BlockSpec(array.shape, functools.partial(lambda n, *_: (0,) * n, array.ndim))


def row_piece(array, c):
    parts, slots, half = array.shape
    return pl.BlockSpec((parts, slots // PIECES, half), lambda *_: (0, c, 0))


def call(kernel, micros, operands, after, out_shape, grid=(1,), in_specs=None, out_specs=None, scratch=(), limit=24, name=None):
    count, unread = len(operands), len(after)

    def run(*refs):
        kernel(*refs[:count], *refs[count + unread :])

    if in_specs is None:
        in_specs = [whole(o) for o in operands]
    if out_specs is None:
        out_specs = jax.tree.map(whole, out_shape)
    return pl.pallas_call(
        run,
        compiler_params=pltpu.CompilerParams(vmem_limit_bytes=limit * MIB),
        cost_estimate=pl.CostEstimate(flops=int(micros * 1e9), bytes_accessed=1024, transcendentals=0),
        out_shape=out_shape,
        name=name,
        grid=grid,
        in_specs=[*in_specs, *[pl.BlockSpec(memory_space=pl.ANY)] * unread],
        out_specs=out_specs,
        scratch_shapes=list(scratch),
    )(*operands, *after)


def cut_kernel(rows, out):
    out[...] = rows[...]


def cut_first_kernel(value, out):
    out[...] = value[: out.shape[0]]


def position():
    own = lax.axis_index("expert")
    block = own // 2
    near = jnp.where(block >= DBLOCKS // 2, 1, 0)
    return near, own % 2, (block == 0) | (block == DBLOCKS - 1)


def first_kernel(far, *refs):
    rows, (weights, out, joined) = refs[:-3], refs[-3:]
    near, group, _ = position()
    side = 1 - near if far else near
    parts, _, half = out.shape
    slots, width = rows[0].shape
    at = pl.multiple_of(group * width, 128)
    other = pl.multiple_of((1 - group) * width, 128)
    for piece in range(len(rows) // 2):
        here = pl.ds(piece * slots, slots)
        joined[here, pl.ds(at, width)] = rows[2 * piece][...]
        joined[here, pl.ds(other, width)] = rows[2 * piece + 1][...]
    tile = min(256, half)
    for k in range(parts):
        for j in range(half // tile):
            at = pl.multiple_of(side * half + j * tile, tile)
            out[k, :, j * tile : (j + 1) * tile] = lax.dot_general(
                joined[...],
                weights[k, pl.ds(at, tile)],
                (((1,), (1,)), ((), ())),
                preferred_element_type=F32,
            ).astype(BF16)


def first_product(name, far, rows, weights, after):
    slots = rows[0].shape[0] * len(rows) // 2
    parts, units, features = weights.shape
    return call(
        functools.partial(first_kernel, far),
        FIRST * parts,
        (*rows, weights),
        after,
        jax.ShapeDtypeStruct((parts, slots, units // 2), BF16),
        in_specs=[*[whole(r) for r in rows], pl.BlockSpec(memory_space=pltpu.VMEM)],
        scratch=[pltpu.VMEM((slots, features), BF16)],
        name=name,
    )


def sum_kernel(mine, arrived, out):
    out[...] = (mine[...].astype(F32) + arrived[...].astype(F32)).astype(BF16)


def end_or_sum_kernel(at_end, mine, arrived, out):
    _, _, end = position()

    @pl.when(end)
    def _():
        parts = at_end.shape[0]
        out[:parts] = at_end[...]
        if parts < out.shape[0]:
            out[parts:] = jnp.zeros_like(out[parts:])

    @pl.when(jnp.logical_not(end))
    def _():
        out[...] = (mine[...].astype(F32) + arrived[...].astype(F32)).astype(BF16)


def end_or_pass_kernel(at_end, passed, out):
    _, _, end = position()

    @pl.when(end)
    def _():
        out[...] = at_end[...]

    @pl.when(jnp.logical_not(end))
    def _():
        out[...] = passed[...]


def ahead_act_kernel(near, arrived, out):
    gate = near[0].astype(F32) + arrived[0].astype(F32)
    up = near[1].astype(F32) + arrived[1].astype(F32)
    out[0] = (gate * jax.nn.sigmoid(gate) * up).astype(BF16)


def behind_act_kernel(near, arrived, near_e, arrived_e, scale, out):
    gate = near[0].astype(F32) + arrived[0].astype(F32)
    up = near[1].astype(F32) + arrived[1].astype(F32)
    expanded = (near_e[0].astype(F32) + arrived_e[0].astype(F32)) * scale[...]
    sig = jax.nn.sigmoid(gate)
    out[0] = (expanded * up * sig * (1.0 + gate * (1.0 - sig))).astype(BF16)
    out[1] = (expanded * gate * sig).astype(BF16)


def result_kernel(first, one, two, out):
    size = first.shape[0]
    out[:size] = first[...]
    out[size:] = (one[...].astype(F32) + two[...].astype(F32)).astype(BF16)


def second_kernel(scaled, act, one, two, three, *refs):
    scale, refs = (refs[0], refs[1:]) if scaled else (None, refs)
    weights, give, keep, joined = refs
    near_half, group, end = position()
    kinds, _, half = act.shape
    units = weights.shape[1]
    width = give.shape[1]

    def place(near, far):
        for kind in range(kinds):
            at = pl.multiple_of((2 * kind + near_half) * half, 128)
            other = pl.multiple_of((2 * kind + 1 - near_half) * half, 128)
            joined[:, pl.ds(at, half)] = near[kind]
            joined[:, pl.ds(other, half)] = far[kind]

    @pl.when(end)
    def _():
        place(act, three)

    @pl.when(jnp.logical_not(end))
    def _():
        place(one, two)

    for side, out in ((1 - group, give), (group, keep)):
        at = pl.multiple_of(side * width, 128)
        tile = weights[:, :, pl.ds(at, width)].reshape(kinds * units, width)
        share = jnp.dot(joined[...], tile, preferred_element_type=F32)
        if scaled:
            share = share * scale[...]
        out[...] = share.astype(BF16)


def copying_second_kernel(scaled, act, one, two, three, *refs):
    scale, refs = (refs[0], refs[1:]) if scaled else (None, refs)
    weights, give, keep, joined, tiles, sems = refs
    near_half, group, end = position()
    kinds, _, half = act.shape
    _, _, units, width = tiles.shape
    copies = []
    for own in range(2):
        at = pl.multiple_of((group if own else 1 - group) * width, 128)
        copy = pltpu.make_async_copy(
            weights.at[:, :, pl.ds(at, width)], tiles.at[own], sems.at[own]
        )
        copy.start()
        copies.append(copy)

    def place(near, far):
        for kind in range(kinds):
            at = pl.multiple_of((2 * kind + near_half) * half, 128)
            other = pl.multiple_of((2 * kind + 1 - near_half) * half, 128)
            joined[:, pl.ds(at, half)] = near[kind]
            joined[:, pl.ds(other, half)] = far[kind]

    @pl.when(end)
    def _():
        place(act, three)

    @pl.when(jnp.logical_not(end))
    def _():
        place(one, two)

    for own, out in enumerate((give, keep)):
        copies[own].wait()
        share = jnp.dot(
            joined[...], tiles[own].reshape(kinds * units, width), preferred_element_type=F32
        )
        if scaled:
            share = share * scale[...]
        out[...] = share.astype(BF16)


def second_product(name, values, scale, weights, after):
    kinds, units, features = weights.shape
    slots = values[0].shape[1]
    operands = [*values] + ([] if scale is None else [scale])
    share = jax.ShapeDtypeStruct((slots, features // 2), BF16)
    kernel, space = second_kernel, pltpu.VMEM
    scratch = [pltpu.VMEM((slots, kinds * units), BF16)]
    if kinds == 1:
        kernel, space = copying_second_kernel, pl.ANY
        scratch.append(pltpu.VMEM((2, kinds, units, features // 2), BF16))
        scratch.append(pltpu.SemaphoreType.DMA((2,)))
    return call(
        functools.partial(kernel, scale is not None),
        AHEAD_OUT if kinds == 1 else BEHIND_OUT,
        (*operands, weights),
        after,
        (share, share),
        in_specs=[*[whole(v) for v in operands], pl.BlockSpec(memory_space=space)],
        scratch=scratch,
        name=name,
    )


def chain_body(ahead_rows, behind_rows, behind_grad, route_scores, route_counts, gate_up, down_proj):
    height = ahead_rows.shape[1]
    gates = gate_up[0, 0]
    downs = down_proj[0]
    sections = lax.axis_size("section")
    devices = 2 * DBLOCKS
    slot_ids = jnp.arange(height, dtype=jnp.int32)[None]
    live = slot_ids < route_counts[0][:, None]
    scales = jnp.where(live, route_scores[0], 0.0)[:, :, None]

    def between(value, to):
        pairs = [(q * 2 + f, to[q] * 2 + f) for q in range(DBLOCKS) for f in range(2) if to[q] is not None]
        return lax.ppermute(value, "expert", pairs)

    def outer(value):
        return between(value, (1, 0, 3, 2))

    def inward(value):
        return between(value, (1, None, None, 2))

    def outward(value):
        return between(value, (None, 0, 3, None))

    def middle(value):
        return between(value, (0, 2, 1, 3))

    def swapped(value):
        return lax.ppermute(value, "expert", [(i, i ^ 1) for i in range(devices)])

    def to_section(value, by, flip):
        pairs = [
            (s * devices + e, (s + by) * devices + (e ^ flip))
            for s in range(sections)
            if 0 <= s + by < sections
            for e in range(devices)
        ]
        return lax.ppermute(value, ("section", "expert"), pairs)

    recent = []

    def kernel_call(name, kernel, micros, operands, shape):
        specs, arrays = [], []
        for operand in operands:
            array, c = operand if isinstance(operand, tuple) else (operand, None)
            arrays.append(array)
            specs.append(whole(array) if c is None else row_piece(array, c))
        made = call(
            kernel,
            micros,
            arrays,
            list(recent),
            jax.ShapeDtypeStruct(shape, BF16),
            in_specs=specs,
            name=name,
        )
        recent[:] = [made]
        return made

    class Chain:
        def __init__(self, name, rows, weights, spreads):
            self.name = name
            self.rows, self.weights = rows, weights
            self.spreads = spreads
            self.pairs, self.far, self.near, self.act = {}, {}, {}, {}
            self.out, self.mid, self.one, self.back, self.third = {}, {}, {}, {}, {}

        def fetch(self, c):
            size, width = height // PIECES, self.rows.shape[1]
            if c == 0 and self.name == "behind":
                rows = self.rows[:size]
                self.pairs[c] = rows, swapped(rows)
                return
            rows = call(
                cut_kernel,
                SMALL if c else ROWS,
                (self.rows,),
                list(recent),
                jax.ShapeDtypeStruct((size, width), BF16),
                in_specs=[pl.BlockSpec((size, width), lambda i: (c, 0))],
                name=f"{self.name}_rows_{c}",
            )
            recent[:] = [rows]
            self.pairs[c] = rows, swapped(rows)

        def far_product(self, c):
            name = f"{self.name}_far_{c}"
            made = first_product(name, True, self.pairs[c], self.weights, list(recent))
            recent[:] = [made]
            self.far[c] = made

        def near_products(self):
            rows = [row for c in range(PIECES) for row in self.pairs[c]]
            made = first_product(f"{self.name}_near", False, rows, self.weights, list(recent))
            recent[:] = [made]
            self.near = {c: (made, c) for c in range(PIECES)}

        def near_sum(self, c):
            operands = (self.near[c], self.mid[c])
            return kernel_call(f"{self.name}_third_{c}", sum_kernel, SMALL, operands, self.far[c].shape)

        def first_hop(self, c):
            self.out[c] = outer(self.far[c]) if c == 0 else inward(self.far[c])

        def third_hop(self, c):
            self.third[c] = outward(self.near_sum(c))

        def merged_hop(self, c, first):
            operands = (first, self.near[c - 1], self.mid[c - 1])
            shape = self.far[0].shape
            self.out[c] = outer(
                kernel_call(f"{self.name}_outer_{c}", end_or_sum_kernel, SMALL, operands, shape)
            )
            self.third[c - 1] = self.out[c]

        def last_third_hop(self):
            self.third[PIECES - 1] = outer(self.near_sum(PIECES - 1))

        def middle_sum(self, c):
            mine = self.far[c]
            self.mid[c] = middle(
                kernel_call(
                    f"{self.name}_middle_{c}", sum_kernel, SMALL, (mine, self.out[c]), mine.shape
                )
            )

        def middle_pass(self, c):
            value = self.out[PIECES] if c == 0 else self.back[c]
            shape = (self.spreads, *value.shape[1:])
            value = kernel_call(f"{self.name}_first_{c}", cut_first_kernel, SMALL, (value,), shape)
            self.one[c] = value
            self.mid[PIECES + c] = middle(value)

        def outer_pass(self, c):
            value = self.mid[PIECES + c - 1]
            if c == PIECES:
                value = kernel_call(
                    f"{self.name}_back_{c}", cut_first_kernel, SMALL, (value,), value.shape
                )
            else:
                value = kernel_call(
                    f"{self.name}_back_{c}",
                    end_or_pass_kernel,
                    SMALL,
                    (self.act[c], value),
                    value.shape,
                )
            self.back[c] = outer(value)

        def activated(self, c):
            return self.act[c], self.one[c], self.mid[PIECES + c], self.back[c + 1]

    ahead = Chain("ahead", ahead_rows[0], gates, 1)
    behind = Chain("behind", behind_rows[0], gates, 2)
    grad = Chain("grad", behind_grad[0], downs, 0)
    sent = {}

    def cut(array, c):
        size = height // PIECES
        return array[c * size : (c + 1) * size]

    def activate_ahead(c):
        near = ahead.near[c]
        operands = (near, ahead.third[c])
        ahead.act[c] = kernel_call(f"ahead_act_{c}", ahead_act_kernel, ACT, operands, (1, *ahead.far[c].shape[1:]))

    def activate_behind(c):
        near = behind.near[c]
        operands = (near, behind.third[c], grad.near[c], grad.third[c], cut(scales[1], c))
        behind.act[c] = kernel_call(f"behind_act_{c}", behind_act_kernel, ACT, operands, behind.far[c].shape)

    def output(chain, c):
        forward = chain is ahead
        scale = cut(scales[0], c) if forward else None
        weights = downs if forward else gates
        give, keep = second_product(
            f"{chain.name}_out_{c}", chain.activated(c), scale, weights, list(recent)
        )
        recent[:] = [give]
        return give, keep

    def finish_first(chain):
        give, keep = output(chain, 0)
        sent[chain, 0] = swapped(give), keep

    def send_first(chain):
        share, keep = sent[chain, 0]
        total = kernel_call(
            f"{chain.name}_shares", sum_kernel, SMALL, (keep, share), keep.shape
        )
        sent[chain, 0] = to_section(total, 1 if chain is ahead else -1, 0)

    def finish_last(chain):
        give, keep = output(chain, 1)
        by = 1 if chain is ahead else -1
        sent[chain, 1] = to_section(give, by, 1), to_section(keep, by, 0)

    def result(chain):
        operands = (sent[chain, 0], *sent[chain, 1])
        shape = (height, operands[0].shape[1])
        return kernel_call(f"{chain.name}_result", result_kernel, SMALL, operands, shape)[None]

    for chain in (behind, ahead, grad):
        chain.fetch(0)
    behind.far_product(0)
    behind.first_hop(0)
    behind.fetch(1)
    ahead.far_product(0)
    ahead.first_hop(0)
    grad.far_product(0)
    grad.first_hop(0)
    behind.middle_sum(0)
    ahead.fetch(1)
    behind.far_product(1)
    behind.near_products()
    ahead.middle_sum(0)
    behind.merged_hop(1, behind.far[1])
    grad.fetch(1)
    grad.middle_sum(0)
    ahead.far_product(1)
    ahead.near_products()
    ahead.merged_hop(1, ahead.far[1])
    behind.middle_sum(1)
    grad.far_product(1)
    grad.near_products()
    grad.merged_hop(1, grad.far[1])
    ahead.middle_sum(1)
    grad.middle_sum(1)
    activate_behind(0)
    behind.merged_hop(2, behind.act[0])
    activate_ahead(0)
    ahead.merged_hop(2, ahead.act[0])
    grad.last_third_hop()
    behind.middle_pass(0)
    ahead.middle_pass(0)
    activate_ahead(1)
    activate_behind(1)
    behind.outer_pass(1)
    ahead.outer_pass(1)
    behind.middle_pass(1)
    ahead.middle_pass(1)
    finish_first(behind)
    finish_first(ahead)
    behind.outer_pass(2)
    ahead.outer_pass(2)
    send_first(behind)
    finish_last(behind)
    send_first(ahead)
    finish_last(ahead)
    behind_sent = result(behind)
    ahead_sent = result(ahead)
    return ahead_sent, behind_sent


def body(ahead_rows, behind_rows, behind_grad, route_scores, route_counts, gate_up, down_proj):
    groups = lax.axis_size("expert")
    fgroups = groups // DBLOCKS
    low = [[q * fgroups + f for f in range(fgroups)] for q in range(DBLOCKS)]
    high = [[q * fgroups + f for q in range(DBLOCKS)] for f in range(fgroups)]
    height = ahead_rows.shape[1]
    weights_in = gate_up[0, 0]
    weights_out = down_proj[0, 0]
    units = weights_in.shape[1]
    part = units // DBLOCKS

    def wide(rows):
        return lax.all_gather(rows, "expert", axis_index_groups=low, axis=1, tiled=True)

    def reduced(partials):
        flat = partials.reshape(-1, partials.shape[-1])
        total = lax.psum_scatter(
            flat, "expert", axis_index_groups=high, scatter_dimension=0, tiled=True
        )
        return total.astype(F32).reshape(partials.shape[1:])

    def spread(values):
        return lax.all_gather(values, "expert", axis_index_groups=high, axis=0, tiled=False)

    def narrowed(values):
        return lax.psum_scatter(
            values.astype(BF16), "expert", axis_index_groups=low, scatter_dimension=1, tiled=True
        )

    slot_ids = jnp.arange(height, dtype=jnp.int32)
    scale_ahead = route_scores[0, 0] * (slot_ids < route_counts[0, 0]).astype(F32)
    scale_behind = route_scores[0, 1] * (slot_ids < route_counts[0, 1]).astype(F32)
    gates = weights_in.reshape(2, DBLOCKS, part, -1)
    downs = weights_out.reshape(DBLOCKS, part, -1)

    ahead_wide = wide(ahead_rows[0])
    pre_a = jnp.einsum("cd,kqfd->qkcf", ahead_wide, gates, preferred_element_type=F32).astype(BF16)
    sum_a = reduced(pre_a)
    hidden = (sum_a[0] * jax.nn.sigmoid(sum_a[0]) * sum_a[1]).astype(BF16)
    hidden_all = spread(hidden)

    behind_wide = wide(behind_rows[0])
    grad_wide = wide(behind_grad[0])
    pre_b = jnp.einsum("cd,kqfd->qkcf", behind_wide, gates, preferred_element_type=F32).astype(BF16)
    exp_b = jnp.einsum("cd,qfd->qcf", grad_wide, downs, preferred_element_type=F32).astype(BF16)
    sum_b = reduced(jnp.concatenate([pre_b, exp_b[:, None]], axis=1))
    gate, up, expanded = sum_b[0], sum_b[1], sum_b[2] * scale_behind[:, None]
    sig = jax.nn.sigmoid(gate)
    grad_gate = (expanded * up * sig * (1.0 + gate * (1.0 - sig))).astype(BF16)
    grad_up = (expanded * gate * sig).astype(BF16)
    grads_all = spread(jnp.stack([grad_gate, grad_up]))

    out_a = jnp.einsum("qcf,qfd->cd", hidden_all, downs, preferred_element_type=F32)
    ahead_out = (narrowed(out_a).astype(F32) * scale_ahead[:, None]).astype(BF16)
    moved_ahead = shift(ahead_out, "section", 1)
    out_b = jnp.einsum("qkcf,kqfd->cd", grads_all, gates, preferred_element_type=F32)
    behind_out = narrowed(out_b)
    moved_behind = shift(behind_out, "section", -1)
    return (moved_ahead[None], moved_behind[None])


def solution(mesh):
    in_specs = (
        P("section", None, "expert"),
        P("section", None, "expert"),
        P("section", None, "expert"),
        P("section", None, None),
        P("section", None),
        P("section", "expert", None, None, None),
        P("section", "expert", None, None),
    )
    out_specs = (P("section", None, "expert"), P("section", None, "expert"))
    chosen = chain_body if mesh.shape["expert"] == 2 * DBLOCKS else body
    return jax.shard_map(chosen, mesh=mesh, in_specs=in_specs, out_specs=out_specs, check_vma=False)
```

```python
import functools

import jax
import jax.numpy as jnp
from jax import lax
from jax.experimental import pallas as pl
from jax.experimental.pallas import tpu as pltpu
from jax.sharding import PartitionSpec as P

DBLOCKS = 4
BF16 = jnp.bfloat16
F32 = jnp.float32
MIB = 1024 * 1024
PIECES = 2
ROWS, SMALL, ACT, FIRST, AHEAD_OUT, BEHIND_OUT = 20, 6, 10, 5.2, 3, 20


def shift(shard, axis, by):
    devices = lax.axis_size(axis)
    pairs = [(i, i + by) for i in range(devices) if 0 <= i + by < devices]
    return lax.ppermute(shard, axis, pairs)


def whole(array):
    return pl.BlockSpec(array.shape, functools.partial(lambda n, *_: (0,) * n, array.ndim))


def row_piece(array, c):
    parts, slots, half = array.shape
    return pl.BlockSpec((parts, slots // PIECES, half), lambda *_: (0, c, 0))


def call(kernel, micros, operands, after, out_shape, grid=(1,), in_specs=None, out_specs=None, scratch=(), limit=24, name=None):
    count, unread = len(operands), len(after)

    def run(*refs):
        kernel(*refs[:count], *refs[count + unread :])

    if in_specs is None:
        in_specs = [whole(o) for o in operands]
    if out_specs is None:
        out_specs = jax.tree.map(whole, out_shape)
    return pl.pallas_call(
        run,
        compiler_params=pltpu.CompilerParams(vmem_limit_bytes=limit * MIB),
        cost_estimate=pl.CostEstimate(flops=int(micros * 1e9), bytes_accessed=1024, transcendentals=0),
        out_shape=out_shape,
        name=name,
        grid=grid,
        in_specs=[*in_specs, *[pl.BlockSpec(memory_space=pl.ANY)] * unread],
        out_specs=out_specs,
        scratch_shapes=list(scratch),
    )(*operands, *after)


def cut_kernel(rows, out):
    out[...] = rows[...]


def cut_first_kernel(value, out):
    out[...] = value[: out.shape[0]]


def position():
    own = lax.axis_index("expert")
    block = own // 2
    near = jnp.where(block >= DBLOCKS // 2, 1, 0)
    return near, own % 2, (block == 0) | (block == DBLOCKS - 1)


def first_kernel(far, *refs):
    rows, (weights, out, joined) = refs[:-3], refs[-3:]
    near, group, _ = position()
    side = 1 - near if far else near
    parts, _, half = out.shape
    slots, width = rows[0].shape
    at = pl.multiple_of(group * width, 128)
    other = pl.multiple_of((1 - group) * width, 128)
    for piece in range(len(rows) // 2):
        here = pl.ds(piece * slots, slots)
        joined[here, pl.ds(at, width)] = rows[2 * piece][...]
        joined[here, pl.ds(other, width)] = rows[2 * piece + 1][...]
    tile = min(256, half)
    for k in range(parts):
        for j in range(half // tile):
            at = pl.multiple_of(side * half + j * tile, tile)
            out[k, :, j * tile : (j + 1) * tile] = lax.dot_general(
                joined[...],
                weights[k, pl.ds(at, tile)],
                (((1,), (1,)), ((), ())),
                preferred_element_type=F32,
            ).astype(BF16)


def first_product(name, far, rows, weights, after):
    slots = rows[0].shape[0] * len(rows) // 2
    parts, units, features = weights.shape
    return call(
        functools.partial(first_kernel, far),
        FIRST * parts,
        (*rows, weights),
        after,
        jax.ShapeDtypeStruct((parts, slots, units // 2), BF16),
        in_specs=[*[whole(r) for r in rows], pl.BlockSpec(memory_space=pltpu.VMEM)],
        scratch=[pltpu.VMEM((slots, features), BF16)],
        name=name,
    )


def sum_kernel(mine, arrived, out):
    out[...] = (mine[...].astype(F32) + arrived[...].astype(F32)).astype(BF16)


def end_or_sum_kernel(at_end, mine, arrived, out):
    _, _, end = position()

    @pl.when(end)
    def _():
        parts = at_end.shape[0]
        out[:parts] = at_end[...]
        if parts < out.shape[0]:
            out[parts:] = jnp.zeros_like(out[parts:])

    @pl.when(jnp.logical_not(end))
    def _():
        out[...] = (mine[...].astype(F32) + arrived[...].astype(F32)).astype(BF16)


def end_or_pass_kernel(at_end, passed, out):
    _, _, end = position()

    @pl.when(end)
    def _():
        out[...] = at_end[...]

    @pl.when(jnp.logical_not(end))
    def _():
        out[...] = passed[...]


def ahead_act_kernel(near, arrived, out):
    gate = near[0].astype(F32) + arrived[0].astype(F32)
    up = near[1].astype(F32) + arrived[1].astype(F32)
    out[0] = (gate * jax.nn.sigmoid(gate) * up).astype(BF16)


def behind_act_kernel(near, arrived, near_e, arrived_e, scale, out):
    gate = near[0].astype(F32) + arrived[0].astype(F32)
    up = near[1].astype(F32) + arrived[1].astype(F32)
    expanded = (near_e[0].astype(F32) + arrived_e[0].astype(F32)) * scale[...]
    sig = jax.nn.sigmoid(gate)
    out[0] = (expanded * up * sig * (1.0 + gate * (1.0 - sig))).astype(BF16)
    out[1] = (expanded * gate * sig).astype(BF16)


def result_kernel(first, one, two, out):
    size = first.shape[0]
    out[:size] = first[...]
    out[size:] = (one[...].astype(F32) + two[...].astype(F32)).astype(BF16)


def second_kernel(scaled, act, one, two, three, *refs):
    scale, refs = (refs[0], refs[1:]) if scaled else (None, refs)
    weights, give, keep, joined = refs
    near_half, group, end = position()
    kinds, _, half = act.shape
    units = weights.shape[1]
    width = give.shape[1]

    def place(near, far):
        for kind in range(kinds):
            at = pl.multiple_of((2 * kind + near_half) * half, 128)
            other = pl.multiple_of((2 * kind + 1 - near_half) * half, 128)
            joined[:, pl.ds(at, half)] = near[kind]
            joined[:, pl.ds(other, half)] = far[kind]

    @pl.when(end)
    def _():
        place(act, three)

    @pl.when(jnp.logical_not(end))
    def _():
        place(one, two)

    for side, out in ((1 - group, give), (group, keep)):
        at = pl.multiple_of(side * width, 128)
        tile = weights[:, :, pl.ds(at, width)].reshape(kinds * units, width)
        share = jnp.dot(joined[...], tile, preferred_element_type=F32)
        if scaled:
            share = share * scale[...]
        out[...] = share.astype(BF16)


def copying_second_kernel(scaled, act, one, two, three, *refs):
    scale, refs = (refs[0], refs[1:]) if scaled else (None, refs)
    weights, give, keep, joined, tiles, sems = refs
    near_half, group, end = position()
    kinds, _, half = act.shape
    _, _, units, width = tiles.shape
    copies = []
    for own in range(2):
        at = pl.multiple_of((group if own else 1 - group) * width, 128)
        copy = pltpu.make_async_copy(
            weights.at[:, :, pl.ds(at, width)], tiles.at[own], sems.at[own]
        )
        copy.start()
        copies.append(copy)

    def place(near, far):
        for kind in range(kinds):
            at = pl.multiple_of((2 * kind + near_half) * half, 128)
            other = pl.multiple_of((2 * kind + 1 - near_half) * half, 128)
            joined[:, pl.ds(at, half)] = near[kind]
            joined[:, pl.ds(other, half)] = far[kind]

    @pl.when(end)
    def _():
        place(act, three)

    @pl.when(jnp.logical_not(end))
    def _():
        place(one, two)

    for own, out in enumerate((give, keep)):
        copies[own].wait()
        share = jnp.dot(
            joined[...], tiles[own].reshape(kinds * units, width), preferred_element_type=F32
        )
        if scaled:
            share = share * scale[...]
        out[...] = share.astype(BF16)


def second_product(name, values, scale, weights, after):
    kinds, units, features = weights.shape
    slots = values[0].shape[1]
    operands = [*values] + ([] if scale is None else [scale])
    share = jax.ShapeDtypeStruct((slots, features // 2), BF16)
    kernel, space = second_kernel, pltpu.VMEM
    scratch = [pltpu.VMEM((slots, kinds * units), BF16)]
    if kinds == 1:
        kernel, space = copying_second_kernel, pl.ANY
        scratch.append(pltpu.VMEM((2, kinds, units, features // 2), BF16))
        scratch.append(pltpu.SemaphoreType.DMA((2,)))
    return call(
        functools.partial(kernel, scale is not None),
        AHEAD_OUT if kinds == 1 else BEHIND_OUT,
        (*operands, weights),
        after,
        (share, share),
        in_specs=[*[whole(v) for v in operands], pl.BlockSpec(memory_space=space)],
        scratch=scratch,
        name=name,
    )


def chain_body(ahead_rows, behind_rows, behind_grad, route_scores, route_counts, gate_up, down_proj):
    height = ahead_rows.shape[1]
    gates = gate_up[0, 0]
    downs = down_proj[0]
    sections = lax.axis_size("section")
    devices = 2 * DBLOCKS
    slot_ids = jnp.arange(height, dtype=jnp.int32)[None]
    live = slot_ids < route_counts[0][:, None]
    scales = jnp.where(live, route_scores[0], 0.0)[:, :, None]

    def between(value, to):
        pairs = [(q * 2 + f, to[q] * 2 + f) for q in range(DBLOCKS) for f in range(2) if to[q] is not None]
        return lax.ppermute(value, "expert", pairs)

    def outer(value):
        return between(value, (1, 0, 3, 2))

    def inward(value):
        return between(value, (1, None, None, 2))

    def outward(value):
        return between(value, (None, 0, 3, None))

    def middle(value):
        return between(value, (0, 2, 1, 3))

    def swapped(value):
        return lax.ppermute(value, "expert", [(i, i ^ 1) for i in range(devices)])

    def to_section(value, by, flip):
        pairs = [
            (s * devices + e, (s + by) * devices + (e ^ flip))
            for s in range(sections)
            if 0 <= s + by < sections
            for e in range(devices)
        ]
        return lax.ppermute(value, ("section", "expert"), pairs)

    recent = []

    def kernel_call(name, kernel, micros, operands, shape):
        specs, arrays = [], []
        for operand in operands:
            array, c = operand if isinstance(operand, tuple) else (operand, None)
            arrays.append(array)
            specs.append(whole(array) if c is None else row_piece(array, c))
        made = call(
            kernel,
            micros,
            arrays,
            list(recent),
            jax.ShapeDtypeStruct(shape, BF16),
            in_specs=specs,
            name=name,
        )
        recent[:] = [made]
        return made

    class Chain:
        def __init__(self, name, rows, weights, spreads):
            self.name = name
            self.rows, self.weights = rows, weights
            self.spreads = spreads
            self.pairs, self.far, self.near, self.act = {}, {}, {}, {}
            self.out, self.mid, self.one, self.back, self.third = {}, {}, {}, {}, {}

        def fetch(self, c):
            size, width = height // PIECES, self.rows.shape[1]
            if c == 0 and self.name == "behind":
                rows = self.rows[:size]
                self.pairs[c] = rows, swapped(rows)
                return
            rows = call(
                cut_kernel,
                SMALL if c else ROWS,
                (self.rows,),
                list(recent),
                jax.ShapeDtypeStruct((size, width), BF16),
                in_specs=[pl.BlockSpec((size, width), lambda i: (c, 0))],
                name=f"{self.name}_rows_{c}",
            )
            recent[:] = [rows]
            self.pairs[c] = rows, swapped(rows)

        def far_product(self, c):
            name = f"{self.name}_far_{c}"
            made = first_product(name, True, self.pairs[c], self.weights, list(recent))
            recent[:] = [made]
            self.far[c] = made

        def near_products(self):
            rows = [row for c in range(PIECES) for row in self.pairs[c]]
            made = first_product(f"{self.name}_near", False, rows, self.weights, list(recent))
            recent[:] = [made]
            self.near = {c: (made, c) for c in range(PIECES)}

        def near_sum(self, c):
            operands = (self.near[c], self.mid[c])
            return kernel_call(f"{self.name}_third_{c}", sum_kernel, SMALL, operands, self.far[c].shape)

        def first_hop(self, c):
            self.out[c] = outer(self.far[c]) if c == 0 else inward(self.far[c])

        def third_hop(self, c):
            self.third[c] = outward(self.near_sum(c))

        def merged_hop(self, c, first):
            operands = (first, self.near[c - 1], self.mid[c - 1])
            shape = self.far[0].shape
            self.out[c] = outer(
                kernel_call(f"{self.name}_outer_{c}", end_or_sum_kernel, SMALL, operands, shape)
            )
            self.third[c - 1] = self.out[c]

        def last_third_hop(self):
            self.third[PIECES - 1] = outer(self.near_sum(PIECES - 1))

        def middle_sum(self, c):
            mine = self.far[c]
            self.mid[c] = middle(
                kernel_call(
                    f"{self.name}_middle_{c}", sum_kernel, SMALL, (mine, self.out[c]), mine.shape
                )
            )

        def middle_pass(self, c):
            value = self.out[PIECES] if c == 0 else self.back[c]
            shape = (self.spreads, *value.shape[1:])
            value = kernel_call(f"{self.name}_first_{c}", cut_first_kernel, SMALL, (value,), shape)
            self.one[c] = value
            self.mid[PIECES + c] = middle(value)

        def outer_pass(self, c):
            value = self.mid[PIECES + c - 1]
            if c == PIECES:
                value = kernel_call(
                    f"{self.name}_back_{c}", cut_first_kernel, SMALL, (value,), value.shape
                )
            else:
                value = kernel_call(
                    f"{self.name}_back_{c}",
                    end_or_pass_kernel,
                    SMALL,
                    (self.act[c], value),
                    value.shape,
                )
            self.back[c] = outer(value)

        def activated(self, c):
            return self.act[c], self.one[c], self.mid[PIECES + c], self.back[c + 1]

    ahead = Chain("ahead", ahead_rows[0], gates, 1)
    behind = Chain("behind", behind_rows[0], gates, 2)
    grad = Chain("grad", behind_grad[0], downs, 0)
    sent = {}

    def cut(array, c):
        size = height // PIECES
        return array[c * size : (c + 1) * size]

    def activate_ahead(c):
        near = ahead.near[c]
        operands = (near, ahead.third[c])
        ahead.act[c] = kernel_call(f"ahead_act_{c}", ahead_act_kernel, ACT, operands, (1, *ahead.far[c].shape[1:]))

    def activate_behind(c):
        near = behind.near[c]
        operands = (near, behind.third[c], grad.near[c], grad.third[c], cut(scales[1], c))
        behind.act[c] = kernel_call(f"behind_act_{c}", behind_act_kernel, ACT, operands, behind.far[c].shape)

    def output(chain, c):
        forward = chain is ahead
        scale = cut(scales[0], c) if forward else None
        weights = downs if forward else gates
        give, keep = second_product(
            f"{chain.name}_out_{c}", chain.activated(c), scale, weights, list(recent)
        )
        recent[:] = [give]
        return give, keep

    def finish_first(chain):
        give, keep = output(chain, 0)
        sent[chain, 0] = swapped(give), keep

    def send_first(chain):
        share, keep = sent[chain, 0]
        total = kernel_call(
            f"{chain.name}_shares", sum_kernel, SMALL, (keep, share), keep.shape
        )
        sent[chain, 0] = to_section(total, 1 if chain is ahead else -1, 0)

    def finish_last(chain):
        give, keep = output(chain, 1)
        by = 1 if chain is ahead else -1
        sent[chain, 1] = to_section(give, by, 1), to_section(keep, by, 0)

    def result(chain):
        operands = (sent[chain, 0], *sent[chain, 1])
        shape = (height, operands[0].shape[1])
        return kernel_call(f"{chain.name}_result", result_kernel, SMALL, operands, shape)[None]

    for chain in (behind, ahead, grad):
        chain.fetch(0)
    behind.far_product(0)
    behind.first_hop(0)
    behind.fetch(1)
    ahead.far_product(0)
    ahead.first_hop(0)
    grad.far_product(0)
    grad.first_hop(0)
    behind.middle_sum(0)
    ahead.fetch(1)
    behind.far_product(1)
    behind.near_products()
    ahead.middle_sum(0)
    behind.merged_hop(1, behind.far[1])
    grad.fetch(1)
    grad.middle_sum(0)
    ahead.far_product(1)
    ahead.near_products()
    ahead.merged_hop(1, ahead.far[1])
    behind.middle_sum(1)
    grad.far_product(1)
    grad.near_products()
    grad.merged_hop(1, grad.far[1])
    ahead.middle_sum(1)
    activate_behind(0)
    behind.merged_hop(2, behind.act[0])
    grad.middle_sum(1)
    activate_ahead(0)
    ahead.merged_hop(2, ahead.act[0])
    grad.last_third_hop()
    behind.middle_pass(0)
    activate_behind(1)
    behind.outer_pass(1)
    ahead.middle_pass(0)
    activate_ahead(1)
    behind.middle_pass(1)
    ahead.outer_pass(1)
    finish_first(behind)
    ahead.middle_pass(1)
    behind.outer_pass(2)
    finish_first(ahead)
    ahead.outer_pass(2)
    send_first(behind)
    finish_last(behind)
    finish_last(ahead)
    send_first(ahead)
    behind_sent = result(behind)
    ahead_sent = result(ahead)
    return ahead_sent, behind_sent


def body(ahead_rows, behind_rows, behind_grad, route_scores, route_counts, gate_up, down_proj):
    groups = lax.axis_size("expert")
    fgroups = groups // DBLOCKS
    low = [[q * fgroups + f for f in range(fgroups)] for q in range(DBLOCKS)]
    high = [[q * fgroups + f for q in range(DBLOCKS)] for f in range(fgroups)]
    height = ahead_rows.shape[1]
    weights_in = gate_up[0, 0]
    weights_out = down_proj[0, 0]
    units = weights_in.shape[1]
    part = units // DBLOCKS

    def wide(rows):
        return lax.all_gather(rows, "expert", axis_index_groups=low, axis=1, tiled=True)

    def reduced(partials):
        flat = partials.reshape(-1, partials.shape[-1])
        total = lax.psum_scatter(
            flat, "expert", axis_index_groups=high, scatter_dimension=0, tiled=True
        )
        return total.astype(F32).reshape(partials.shape[1:])

    def spread(values):
        return lax.all_gather(values, "expert", axis_index_groups=high, axis=0, tiled=False)

    def narrowed(values):
        return lax.psum_scatter(
            values.astype(BF16), "expert", axis_index_groups=low, scatter_dimension=1, tiled=True
        )

    slot_ids = jnp.arange(height, dtype=jnp.int32)
    scale_ahead = route_scores[0, 0] * (slot_ids < route_counts[0, 0]).astype(F32)
    scale_behind = route_scores[0, 1] * (slot_ids < route_counts[0, 1]).astype(F32)
    gates = weights_in.reshape(2, DBLOCKS, part, -1)
    downs = weights_out.reshape(DBLOCKS, part, -1)

    ahead_wide = wide(ahead_rows[0])
    pre_a = jnp.einsum("cd,kqfd->qkcf", ahead_wide, gates, preferred_element_type=F32).astype(BF16)
    sum_a = reduced(pre_a)
    hidden = (sum_a[0] * jax.nn.sigmoid(sum_a[0]) * sum_a[1]).astype(BF16)
    hidden_all = spread(hidden)

    behind_wide = wide(behind_rows[0])
    grad_wide = wide(behind_grad[0])
    pre_b = jnp.einsum("cd,kqfd->qkcf", behind_wide, gates, preferred_element_type=F32).astype(BF16)
    exp_b = jnp.einsum("cd,qfd->qcf", grad_wide, downs, preferred_element_type=F32).astype(BF16)
    sum_b = reduced(jnp.concatenate([pre_b, exp_b[:, None]], axis=1))
    gate, up, expanded = sum_b[0], sum_b[1], sum_b[2] * scale_behind[:, None]
    sig = jax.nn.sigmoid(gate)
    grad_gate = (expanded * up * sig * (1.0 + gate * (1.0 - sig))).astype(BF16)
    grad_up = (expanded * gate * sig).astype(BF16)
    grads_all = spread(jnp.stack([grad_gate, grad_up]))

    out_a = jnp.einsum("qcf,qfd->cd", hidden_all, downs, preferred_element_type=F32)
    ahead_out = (narrowed(out_a).astype(F32) * scale_ahead[:, None]).astype(BF16)
    moved_ahead = shift(ahead_out, "section", 1)
    out_b = jnp.einsum("qkcf,kqfd->cd", grads_all, gates, preferred_element_type=F32)
    behind_out = narrowed(out_b)
    moved_behind = shift(behind_out, "section", -1)
    return (moved_ahead[None], moved_behind[None])


def solution(mesh):
    in_specs = (
        P("section", None, "expert"),
        P("section", None, "expert"),
        P("section", None, "expert"),
        P("section", None, None),
        P("section", None),
        P("section", "expert", None, None, None),
        P("section", "expert", None, None),
    )
    out_specs = (P("section", None, "expert"), P("section", None, "expert"))
    chosen = chain_body if mesh.shape["expert"] == 2 * DBLOCKS else body
    return jax.shard_map(chosen, mesh=mesh, in_specs=in_specs, out_specs=out_specs, check_vma=False)
```

```python
import functools

import jax
import jax.numpy as jnp
from jax import lax
from jax.experimental import pallas as pl
from jax.experimental.pallas import tpu as pltpu
from jax.sharding import PartitionSpec as P

DBLOCKS = 4
BF16 = jnp.bfloat16
F32 = jnp.float32
MIB = 1024 * 1024
PIECES = 2
ROWS, SMALL, ACT, FIRST, AHEAD_OUT, BEHIND_OUT, RESULT = 20, 6, 10, 5.2, 20, 60, 60


def shift(shard, axis, by):
    devices = lax.axis_size(axis)
    pairs = [(i, i + by) for i in range(devices) if 0 <= i + by < devices]
    return lax.ppermute(shard, axis, pairs)


def whole(array):
    return pl.BlockSpec(array.shape, functools.partial(lambda n, *_: (0,) * n, array.ndim))


def row_piece(array, c):
    parts, slots, half = array.shape
    return pl.BlockSpec((parts, slots // PIECES, half), lambda *_: (0, c, 0))


def call(kernel, micros, operands, after, out_shape, grid=(1,), in_specs=None, out_specs=None, scratch=(), limit=24, name=None):
    count, unread = len(operands), len(after)

    def run(*refs):
        kernel(*refs[:count], *refs[count + unread :])

    if in_specs is None:
        in_specs = [whole(o) for o in operands]
    if out_specs is None:
        out_specs = jax.tree.map(whole, out_shape)
    return pl.pallas_call(
        run,
        compiler_params=pltpu.CompilerParams(vmem_limit_bytes=limit * MIB),
        cost_estimate=pl.CostEstimate(flops=int(micros * 1e9), bytes_accessed=1024, transcendentals=0),
        out_shape=out_shape,
        name=name,
        grid=grid,
        in_specs=[*in_specs, *[pl.BlockSpec(memory_space=pl.ANY)] * unread],
        out_specs=out_specs,
        scratch_shapes=list(scratch),
    )(*operands, *after)


def cut_kernel(rows, out):
    out[...] = rows[...]


def cut_first_kernel(value, out):
    out[...] = value[: out.shape[0]]


def position():
    own = lax.axis_index("expert")
    block = own // 2
    near = jnp.where(block >= DBLOCKS // 2, 1, 0)
    return near, own % 2, (block == 0) | (block == DBLOCKS - 1)


def first_kernel(far, *refs):
    rows, (weights, out, joined) = refs[:-3], refs[-3:]
    near, group, _ = position()
    side = 1 - near if far else near
    parts, _, half = out.shape
    slots, width = rows[0].shape
    at = pl.multiple_of(group * width, 128)
    other = pl.multiple_of((1 - group) * width, 128)
    for piece in range(len(rows) // 2):
        here = pl.ds(piece * slots, slots)
        joined[here, pl.ds(at, width)] = rows[2 * piece][...]
        joined[here, pl.ds(other, width)] = rows[2 * piece + 1][...]
    tile = min(256, half)
    for k in range(parts):
        for j in range(half // tile):
            at = pl.multiple_of(side * half + j * tile, tile)
            out[k, :, j * tile : (j + 1) * tile] = lax.dot_general(
                joined[...],
                weights[k, pl.ds(at, tile)],
                (((1,), (1,)), ((), ())),
                preferred_element_type=F32,
            ).astype(BF16)


def first_product(name, far, rows, weights, after):
    slots = rows[0].shape[0] * len(rows) // 2
    parts, units, features = weights.shape
    return call(
        functools.partial(first_kernel, far),
        FIRST * parts,
        (*rows, weights),
        after,
        jax.ShapeDtypeStruct((parts, slots, units // 2), BF16),
        in_specs=[*[whole(r) for r in rows], pl.BlockSpec(memory_space=pltpu.VMEM)],
        scratch=[pltpu.VMEM((slots, features), BF16)],
        name=name,
    )


def sum_kernel(mine, arrived, out):
    out[...] = (mine[...].astype(F32) + arrived[...].astype(F32)).astype(BF16)


def end_or_sum_kernel(at_end, mine, arrived, out):
    _, _, end = position()

    @pl.when(end)
    def _():
        parts = at_end.shape[0]
        out[:parts] = at_end[...]
        if parts < out.shape[0]:
            out[parts:] = jnp.zeros_like(out[parts:])

    @pl.when(jnp.logical_not(end))
    def _():
        out[...] = (mine[...].astype(F32) + arrived[...].astype(F32)).astype(BF16)


def end_or_pass_kernel(at_end, passed, out):
    _, _, end = position()

    @pl.when(end)
    def _():
        out[...] = at_end[...]

    @pl.when(jnp.logical_not(end))
    def _():
        out[...] = passed[...]


def ahead_act_kernel(near, arrived, out):
    gate = near[0].astype(F32) + arrived[0].astype(F32)
    up = near[1].astype(F32) + arrived[1].astype(F32)
    out[0] = (gate * jax.nn.sigmoid(gate) * up).astype(BF16)


def behind_act_kernel(near, arrived, near_e, arrived_e, scale, out):
    gate = near[0].astype(F32) + arrived[0].astype(F32)
    up = near[1].astype(F32) + arrived[1].astype(F32)
    expanded = (near_e[0].astype(F32) + arrived_e[0].astype(F32)) * scale[...]
    sig = jax.nn.sigmoid(gate)
    out[0] = (expanded * up * sig * (1.0 + gate * (1.0 - sig))).astype(BF16)
    out[1] = (expanded * gate * sig).astype(BF16)


def result_kernel(first, one, two, out):
    size = first.shape[0]
    out[:size] = first[...]
    out[size:] = (one[...].astype(F32) + two[...].astype(F32)).astype(BF16)


def second_kernel(scaled, act, one, two, three, *refs):
    scale, refs = (refs[0], refs[1:]) if scaled else (None, refs)
    weights, give, keep, joined = refs
    near_half, group, end = position()
    kinds, _, half = act.shape
    units = weights.shape[1]
    width = give.shape[1]

    def place(near, far):
        for kind in range(kinds):
            at = pl.multiple_of((2 * kind + near_half) * half, 128)
            other = pl.multiple_of((2 * kind + 1 - near_half) * half, 128)
            joined[:, pl.ds(at, half)] = near[kind]
            joined[:, pl.ds(other, half)] = far[kind]

    @pl.when(end)
    def _():
        place(act, three)

    @pl.when(jnp.logical_not(end))
    def _():
        place(one, two)

    for side, out in ((1 - group, give), (group, keep)):
        at = pl.multiple_of(side * width, 128)
        tile = weights[:, :, pl.ds(at, width)].reshape(kinds * units, width)
        share = jnp.dot(joined[...], tile, preferred_element_type=F32)
        if scaled:
            share = share * scale[...]
        out[...] = share.astype(BF16)


def copying_second_kernel(scaled, act, one, two, three, *refs):
    scale, refs = (refs[0], refs[1:]) if scaled else (None, refs)
    weights, give, keep, joined, tiles, sems = refs
    near_half, group, end = position()
    kinds, _, half = act.shape
    _, _, units, width = tiles.shape
    copies = []
    for own in range(2):
        at = pl.multiple_of((group if own else 1 - group) * width, 128)
        copy = pltpu.make_async_copy(
            weights.at[:, :, pl.ds(at, width)], tiles.at[own], sems.at[own]
        )
        copy.start()
        copies.append(copy)

    def place(near, far):
        for kind in range(kinds):
            at = pl.multiple_of((2 * kind + near_half) * half, 128)
            other = pl.multiple_of((2 * kind + 1 - near_half) * half, 128)
            joined[:, pl.ds(at, half)] = near[kind]
            joined[:, pl.ds(other, half)] = far[kind]

    @pl.when(end)
    def _():
        place(act, three)

    @pl.when(jnp.logical_not(end))
    def _():
        place(one, two)

    for own, out in enumerate((give, keep)):
        copies[own].wait()
        share = jnp.dot(
            joined[...], tiles[own].reshape(kinds * units, width), preferred_element_type=F32
        )
        if scaled:
            share = share * scale[...]
        out[...] = share.astype(BF16)


def second_product(name, values, scale, weights, after):
    kinds, units, features = weights.shape
    slots = values[0].shape[1]
    operands = [*values] + ([] if scale is None else [scale])
    share = jax.ShapeDtypeStruct((slots, features // 2), BF16)
    kernel, space = second_kernel, pltpu.VMEM
    scratch = [pltpu.VMEM((slots, kinds * units), BF16)]
    if kinds == 1:
        kernel, space = copying_second_kernel, pl.ANY
        scratch.append(pltpu.VMEM((2, kinds, units, features // 2), BF16))
        scratch.append(pltpu.SemaphoreType.DMA((2,)))
    return call(
        functools.partial(kernel, scale is not None),
        AHEAD_OUT if kinds == 1 else BEHIND_OUT,
        (*operands, weights),
        after,
        (share, share),
        in_specs=[*[whole(v) for v in operands], pl.BlockSpec(memory_space=space)],
        scratch=scratch,
        name=name,
    )


def chain_body(ahead_rows, behind_rows, behind_grad, route_scores, route_counts, gate_up, down_proj):
    height = ahead_rows.shape[1]
    gates = gate_up[0, 0]
    downs = down_proj[0]
    sections = lax.axis_size("section")
    devices = 2 * DBLOCKS
    slot_ids = jnp.arange(height, dtype=jnp.int32)[None]
    live = slot_ids < route_counts[0][:, None]
    scales = jnp.where(live, route_scores[0], 0.0)[:, :, None]

    def between(value, to):
        pairs = [(q * 2 + f, to[q] * 2 + f) for q in range(DBLOCKS) for f in range(2) if to[q] is not None]
        return lax.ppermute(value, "expert", pairs)

    def outer(value):
        return between(value, (1, 0, 3, 2))

    def inward(value):
        return between(value, (1, None, None, 2))

    def outward(value):
        return between(value, (None, 0, 3, None))

    def middle(value):
        return between(value, (0, 2, 1, 3))

    def swapped(value):
        return lax.ppermute(value, "expert", [(i, i ^ 1) for i in range(devices)])

    def to_section(value, by, flip):
        pairs = [
            (s * devices + e, (s + by) * devices + (e ^ flip))
            for s in range(sections)
            if 0 <= s + by < sections
            for e in range(devices)
        ]
        return lax.ppermute(value, ("section", "expert"), pairs)

    recent = []

    def kernel_call(name, kernel, micros, operands, shape):
        specs, arrays = [], []
        for operand in operands:
            array, c = operand if isinstance(operand, tuple) else (operand, None)
            arrays.append(array)
            specs.append(whole(array) if c is None else row_piece(array, c))
        made = call(
            kernel,
            micros,
            arrays,
            list(recent),
            jax.ShapeDtypeStruct(shape, BF16),
            in_specs=specs,
            name=name,
        )
        recent[:] = [made]
        return made

    class Chain:
        def __init__(self, name, rows, weights, spreads):
            self.name = name
            self.rows, self.weights = rows, weights
            self.spreads = spreads
            self.pairs, self.far, self.near, self.act = {}, {}, {}, {}
            self.out, self.mid, self.one, self.back, self.third = {}, {}, {}, {}, {}

        def fetch(self, c):
            size, width = height // PIECES, self.rows.shape[1]
            if c == 0 and self.name == "behind":
                rows = self.rows[:size]
                self.pairs[c] = rows, swapped(rows)
                return
            rows = call(
                cut_kernel,
                SMALL if c else ROWS,
                (self.rows,),
                list(recent),
                jax.ShapeDtypeStruct((size, width), BF16),
                in_specs=[pl.BlockSpec((size, width), lambda i: (c, 0))],
                name=f"{self.name}_rows_{c}",
            )
            recent[:] = [rows]
            self.pairs[c] = rows, swapped(rows)

        def far_product(self, c):
            name = f"{self.name}_far_{c}"
            made = first_product(name, True, self.pairs[c], self.weights, list(recent))
            recent[:] = [made]
            self.far[c] = made

        def near_products(self):
            rows = [row for c in range(PIECES) for row in self.pairs[c]]
            made = first_product(f"{self.name}_near", False, rows, self.weights, list(recent))
            recent[:] = [made]
            self.near = {c: (made, c) for c in range(PIECES)}

        def near_sum(self, c):
            operands = (self.near[c], self.mid[c])
            return kernel_call(f"{self.name}_third_{c}", sum_kernel, SMALL, operands, self.far[c].shape)

        def first_hop(self, c):
            self.out[c] = outer(self.far[c]) if c == 0 else inward(self.far[c])

        def third_hop(self, c):
            self.third[c] = outward(self.near_sum(c))

        def merged_hop(self, c, first):
            operands = (first, self.near[c - 1], self.mid[c - 1])
            shape = self.far[0].shape
            self.out[c] = outer(
                kernel_call(f"{self.name}_outer_{c}", end_or_sum_kernel, SMALL, operands, shape)
            )
            self.third[c - 1] = self.out[c]

        def last_third_hop(self):
            self.third[PIECES - 1] = outer(self.near_sum(PIECES - 1))

        def middle_sum(self, c):
            mine = self.far[c]
            self.mid[c] = middle(
                kernel_call(
                    f"{self.name}_middle_{c}", sum_kernel, SMALL, (mine, self.out[c]), mine.shape
                )
            )

        def middle_pass(self, c):
            value = self.out[PIECES] if c == 0 else self.back[c]
            shape = (self.spreads, *value.shape[1:])
            value = kernel_call(f"{self.name}_first_{c}", cut_first_kernel, SMALL, (value,), shape)
            self.one[c] = value
            self.mid[PIECES + c] = middle(value)

        def outer_pass(self, c):
            value = self.mid[PIECES + c - 1]
            if c == PIECES:
                value = kernel_call(
                    f"{self.name}_back_{c}", cut_first_kernel, SMALL, (value,), value.shape
                )
            else:
                value = kernel_call(
                    f"{self.name}_back_{c}",
                    end_or_pass_kernel,
                    SMALL,
                    (self.act[c], value),
                    value.shape,
                )
            self.back[c] = outer(value)

        def activated(self, c):
            return self.act[c], self.one[c], self.mid[PIECES + c], self.back[c + 1]

    ahead = Chain("ahead", ahead_rows[0], gates, 1)
    behind = Chain("behind", behind_rows[0], gates, 2)
    grad = Chain("grad", behind_grad[0], downs, 0)
    sent = {}

    def cut(array, c):
        size = height // PIECES
        return array[c * size : (c + 1) * size]

    def activate_ahead(c):
        near = ahead.near[c]
        operands = (near, ahead.third[c])
        ahead.act[c] = kernel_call(f"ahead_act_{c}", ahead_act_kernel, ACT, operands, (1, *ahead.far[c].shape[1:]))

    def activate_behind(c):
        near = behind.near[c]
        operands = (near, behind.third[c], grad.near[c], grad.third[c], cut(scales[1], c))
        behind.act[c] = kernel_call(f"behind_act_{c}", behind_act_kernel, ACT, operands, behind.far[c].shape)

    def output(chain, c):
        forward = chain is ahead
        scale = cut(scales[0], c) if forward else None
        weights = downs if forward else gates
        give, keep = second_product(
            f"{chain.name}_out_{c}", chain.activated(c), scale, weights, list(recent)
        )
        recent[:] = [give]
        return give, keep

    def finish_first(chain):
        give, keep = output(chain, 0)
        sent[chain, 0] = swapped(give), keep

    def send_first(chain):
        share, keep = sent[chain, 0]
        total = kernel_call(
            f"{chain.name}_shares", sum_kernel, SMALL, (keep, share), keep.shape
        )
        sent[chain, 0] = to_section(total, 1 if chain is ahead else -1, 0)

    def finish_last(chain):
        give, keep = output(chain, 1)
        by = 1 if chain is ahead else -1
        sent[chain, 1] = to_section(give, by, 1), to_section(keep, by, 0)

    def result(chain):
        operands = (sent[chain, 0], *sent[chain, 1])
        shape = (height, operands[0].shape[1])
        return kernel_call(f"{chain.name}_result", result_kernel, RESULT, operands, shape)[None]

    for chain in (behind, ahead, grad):
        chain.fetch(0)
    behind.far_product(0)
    behind.first_hop(0)
    behind.fetch(1)
    ahead.far_product(0)
    ahead.first_hop(0)
    grad.far_product(0)
    grad.first_hop(0)
    behind.middle_sum(0)
    ahead.fetch(1)
    behind.far_product(1)
    behind.near_products()
    ahead.middle_sum(0)
    behind.merged_hop(1, behind.far[1])
    grad.fetch(1)
    grad.middle_sum(0)
    ahead.far_product(1)
    ahead.near_products()
    ahead.merged_hop(1, ahead.far[1])
    behind.middle_sum(1)
    grad.far_product(1)
    grad.near_products()
    grad.merged_hop(1, grad.far[1])
    ahead.middle_sum(1)
    activate_behind(0)
    behind.merged_hop(2, behind.act[0])
    grad.middle_sum(1)
    activate_ahead(0)
    ahead.merged_hop(2, ahead.act[0])
    grad.last_third_hop()
    behind.middle_pass(0)
    ahead.middle_pass(0)
    activate_ahead(1)
    activate_behind(1)
    behind.outer_pass(1)
    ahead.outer_pass(1)
    behind.middle_pass(1)
    ahead.middle_pass(1)
    finish_first(ahead)
    finish_first(behind)
    behind.outer_pass(2)
    ahead.outer_pass(2)
    send_first(ahead)
    finish_last(behind)
    send_first(behind)
    finish_last(ahead)
    behind_sent = result(behind)
    ahead_sent = result(ahead)
    return ahead_sent, behind_sent


def body(ahead_rows, behind_rows, behind_grad, route_scores, route_counts, gate_up, down_proj):
    groups = lax.axis_size("expert")
    fgroups = groups // DBLOCKS
    low = [[q * fgroups + f for f in range(fgroups)] for q in range(DBLOCKS)]
    high = [[q * fgroups + f for q in range(DBLOCKS)] for f in range(fgroups)]
    height = ahead_rows.shape[1]
    weights_in = gate_up[0, 0]
    weights_out = down_proj[0, 0]
    units = weights_in.shape[1]
    part = units // DBLOCKS

    def wide(rows):
        return lax.all_gather(rows, "expert", axis_index_groups=low, axis=1, tiled=True)

    def reduced(partials):
        flat = partials.reshape(-1, partials.shape[-1])
        total = lax.psum_scatter(
            flat, "expert", axis_index_groups=high, scatter_dimension=0, tiled=True
        )
        return total.astype(F32).reshape(partials.shape[1:])

    def spread(values):
        return lax.all_gather(values, "expert", axis_index_groups=high, axis=0, tiled=False)

    def narrowed(values):
        return lax.psum_scatter(
            values.astype(BF16), "expert", axis_index_groups=low, scatter_dimension=1, tiled=True
        )

    slot_ids = jnp.arange(height, dtype=jnp.int32)
    scale_ahead = route_scores[0, 0] * (slot_ids < route_counts[0, 0]).astype(F32)
    scale_behind = route_scores[0, 1] * (slot_ids < route_counts[0, 1]).astype(F32)
    gates = weights_in.reshape(2, DBLOCKS, part, -1)
    downs = weights_out.reshape(DBLOCKS, part, -1)

    ahead_wide = wide(ahead_rows[0])
    pre_a = jnp.einsum("cd,kqfd->qkcf", ahead_wide, gates, preferred_element_type=F32).astype(BF16)
    sum_a = reduced(pre_a)
    hidden = (sum_a[0] * jax.nn.sigmoid(sum_a[0]) * sum_a[1]).astype(BF16)
    hidden_all = spread(hidden)

    behind_wide = wide(behind_rows[0])
    grad_wide = wide(behind_grad[0])
    pre_b = jnp.einsum("cd,kqfd->qkcf", behind_wide, gates, preferred_element_type=F32).astype(BF16)
    exp_b = jnp.einsum("cd,qfd->qcf", grad_wide, downs, preferred_element_type=F32).astype(BF16)
    sum_b = reduced(jnp.concatenate([pre_b, exp_b[:, None]], axis=1))
    gate, up, expanded = sum_b[0], sum_b[1], sum_b[2] * scale_behind[:, None]
    sig = jax.nn.sigmoid(gate)
    grad_gate = (expanded * up * sig * (1.0 + gate * (1.0 - sig))).astype(BF16)
    grad_up = (expanded * gate * sig).astype(BF16)
    grads_all = spread(jnp.stack([grad_gate, grad_up]))

    out_a = jnp.einsum("qcf,qfd->cd", hidden_all, downs, preferred_element_type=F32)
    ahead_out = (narrowed(out_a).astype(F32) * scale_ahead[:, None]).astype(BF16)
    moved_ahead = shift(ahead_out, "section", 1)
    out_b = jnp.einsum("qkcf,kqfd->cd", grads_all, gates, preferred_element_type=F32)
    behind_out = narrowed(out_b)
    moved_behind = shift(behind_out, "section", -1)
    return (moved_ahead[None], moved_behind[None])


def solution(mesh):
    in_specs = (
        P("section", None, "expert"),
        P("section", None, "expert"),
        P("section", None, "expert"),
        P("section", None, None),
        P("section", None),
        P("section", "expert", None, None, None),
        P("section", "expert", None, None),
    )
    out_specs = (P("section", None, "expert"), P("section", None, "expert"))
    chosen = chain_body if mesh.shape["expert"] == 2 * DBLOCKS else body
    return jax.shard_map(chosen, mesh=mesh, in_specs=in_specs, out_specs=out_specs, check_vma=False)
```

```python
import functools

import jax
import jax.numpy as jnp
from jax import lax
from jax.experimental import pallas as pl
from jax.experimental.pallas import tpu as pltpu
from jax.sharding import PartitionSpec as P

DBLOCKS = 4
BF16 = jnp.bfloat16
F32 = jnp.float32
MIB = 1024 * 1024
PIECES = 2
ROWS, SMALL, ACT, FIRST, AHEAD_OUT, BEHIND_OUT = 20, 6, 10, 5.2, 3, 20


def shift(shard, axis, by):
    devices = lax.axis_size(axis)
    pairs = [(i, i + by) for i in range(devices) if 0 <= i + by < devices]
    return lax.ppermute(shard, axis, pairs)


def whole(array):
    return pl.BlockSpec(array.shape, functools.partial(lambda n, *_: (0,) * n, array.ndim))


def row_piece(array, c):
    parts, slots, half = array.shape
    return pl.BlockSpec((parts, slots // PIECES, half), lambda *_: (0, c, 0))


def call(kernel, micros, operands, after, out_shape, grid=(1,), in_specs=None, out_specs=None, scratch=(), limit=24, name=None):
    count, unread = len(operands), len(after)

    def run(*refs):
        kernel(*refs[:count], *refs[count + unread :])

    if in_specs is None:
        in_specs = [whole(o) for o in operands]
    if out_specs is None:
        out_specs = jax.tree.map(whole, out_shape)
    return pl.pallas_call(
        run,
        compiler_params=pltpu.CompilerParams(vmem_limit_bytes=limit * MIB),
        cost_estimate=pl.CostEstimate(flops=int(micros * 1e9), bytes_accessed=1024, transcendentals=0),
        out_shape=out_shape,
        name=name,
        grid=grid,
        in_specs=[*in_specs, *[pl.BlockSpec(memory_space=pl.ANY)] * unread],
        out_specs=out_specs,
        scratch_shapes=list(scratch),
    )(*operands, *after)


def cut_kernel(rows, out):
    out[...] = rows[...]


def cut_first_kernel(value, out):
    out[...] = value[: out.shape[0]]


def position():
    own = lax.axis_index("expert")
    block = own // 2
    near = jnp.where(block >= DBLOCKS // 2, 1, 0)
    return near, own % 2, (block == 0) | (block == DBLOCKS - 1)


def first_kernel(far, *refs):
    rows, (weights, out, joined) = refs[:-3], refs[-3:]
    near, group, _ = position()
    side = 1 - near if far else near
    parts, _, half = out.shape
    slots, width = rows[0].shape
    at = pl.multiple_of(group * width, 128)
    other = pl.multiple_of((1 - group) * width, 128)
    for piece in range(len(rows) // 2):
        here = pl.ds(piece * slots, slots)
        joined[here, pl.ds(at, width)] = rows[2 * piece][...]
        joined[here, pl.ds(other, width)] = rows[2 * piece + 1][...]
    tile = min(256, half)
    for k in range(parts):
        for j in range(half // tile):
            at = pl.multiple_of(side * half + j * tile, tile)
            out[k, :, j * tile : (j + 1) * tile] = lax.dot_general(
                joined[...],
                weights[k, pl.ds(at, tile)],
                (((1,), (1,)), ((), ())),
                preferred_element_type=F32,
            ).astype(BF16)


def first_product(name, far, rows, weights, after):
    slots = rows[0].shape[0] * len(rows) // 2
    parts, units, features = weights.shape
    return call(
        functools.partial(first_kernel, far),
        FIRST * parts,
        (*rows, weights),
        after,
        jax.ShapeDtypeStruct((parts, slots, units // 2), BF16),
        in_specs=[*[whole(r) for r in rows], pl.BlockSpec(memory_space=pltpu.VMEM)],
        scratch=[pltpu.VMEM((slots, features), BF16)],
        name=name,
    )


def sum_kernel(mine, arrived, out):
    out[...] = (mine[...].astype(F32) + arrived[...].astype(F32)).astype(BF16)


def end_or_sum_kernel(at_end, mine, arrived, out):
    _, _, end = position()

    @pl.when(end)
    def _():
        parts = at_end.shape[0]
        out[:parts] = at_end[...]
        if parts < out.shape[0]:
            out[parts:] = jnp.zeros_like(out[parts:])

    @pl.when(jnp.logical_not(end))
    def _():
        out[...] = (mine[...].astype(F32) + arrived[...].astype(F32)).astype(BF16)


def end_or_pass_kernel(at_end, passed, out):
    _, _, end = position()

    @pl.when(end)
    def _():
        out[...] = at_end[...]

    @pl.when(jnp.logical_not(end))
    def _():
        out[...] = passed[...]


def ahead_act_kernel(near, arrived, out):
    gate = near[0].astype(F32) + arrived[0].astype(F32)
    up = near[1].astype(F32) + arrived[1].astype(F32)
    out[0] = (gate * jax.nn.sigmoid(gate) * up).astype(BF16)


def behind_act_kernel(near, arrived, near_e, arrived_e, scale, out):
    gate = near[0].astype(F32) + arrived[0].astype(F32)
    up = near[1].astype(F32) + arrived[1].astype(F32)
    expanded = (near_e[0].astype(F32) + arrived_e[0].astype(F32)) * scale[...]
    sig = jax.nn.sigmoid(gate)
    out[0] = (expanded * up * sig * (1.0 + gate * (1.0 - sig))).astype(BF16)
    out[1] = (expanded * gate * sig).astype(BF16)


def result_kernel(first, one, two, out):
    size = first.shape[0]
    out[:size] = first[...]
    out[size:] = (one[...].astype(F32) + two[...].astype(F32)).astype(BF16)


def second_kernel(scaled, act, one, two, three, *refs):
    scale, refs = (refs[0], refs[1:]) if scaled else (None, refs)
    weights, give, keep, joined = refs
    near_half, group, end = position()
    kinds, _, half = act.shape
    units = weights.shape[1]
    width = give.shape[1]

    def place(near, far):
        for kind in range(kinds):
            at = pl.multiple_of((2 * kind + near_half) * half, 128)
            other = pl.multiple_of((2 * kind + 1 - near_half) * half, 128)
            joined[:, pl.ds(at, half)] = near[kind]
            joined[:, pl.ds(other, half)] = far[kind]

    @pl.when(end)
    def _():
        place(act, three)

    @pl.when(jnp.logical_not(end))
    def _():
        place(one, two)

    for side, out in ((1 - group, give), (group, keep)):
        at = pl.multiple_of(side * width, 128)
        tile = weights[:, :, pl.ds(at, width)].reshape(kinds * units, width)
        share = jnp.dot(joined[...], tile, preferred_element_type=F32)
        if scaled:
            share = share * scale[...]
        out[...] = share.astype(BF16)


def copying_second_kernel(scaled, act, one, two, three, *refs):
    scale, refs = (refs[0], refs[1:]) if scaled else (None, refs)
    weights, give, keep, joined, tiles, sems = refs
    near_half, group, end = position()
    kinds, _, half = act.shape
    _, _, units, width = tiles.shape
    copies = []
    for own in range(2):
        at = pl.multiple_of((group if own else 1 - group) * width, 128)
        copy = pltpu.make_async_copy(
            weights.at[:, :, pl.ds(at, width)], tiles.at[own], sems.at[own]
        )
        copy.start()
        copies.append(copy)

    def place(near, far):
        for kind in range(kinds):
            at = pl.multiple_of((2 * kind + near_half) * half, 128)
            other = pl.multiple_of((2 * kind + 1 - near_half) * half, 128)
            joined[:, pl.ds(at, half)] = near[kind]
            joined[:, pl.ds(other, half)] = far[kind]

    @pl.when(end)
    def _():
        place(act, three)

    @pl.when(jnp.logical_not(end))
    def _():
        place(one, two)

    for own, out in enumerate((give, keep)):
        copies[own].wait()
        share = jnp.dot(
            joined[...], tiles[own].reshape(kinds * units, width), preferred_element_type=F32
        )
        if scaled:
            share = share * scale[...]
        out[...] = share.astype(BF16)


def second_product(name, values, scale, weights, after):
    kinds, units, features = weights.shape
    slots = values[0].shape[1]
    operands = [*values] + ([] if scale is None else [scale])
    share = jax.ShapeDtypeStruct((slots, features // 2), BF16)
    kernel, space = second_kernel, pltpu.VMEM
    scratch = [pltpu.VMEM((slots, kinds * units), BF16)]
    if kinds == 1:
        kernel, space = copying_second_kernel, pl.ANY
        scratch.append(pltpu.VMEM((2, kinds, units, features // 2), BF16))
        scratch.append(pltpu.SemaphoreType.DMA((2,)))
    return call(
        functools.partial(kernel, scale is not None),
        AHEAD_OUT if kinds == 1 else BEHIND_OUT,
        (*operands, weights),
        after,
        (share, share),
        in_specs=[*[whole(v) for v in operands], pl.BlockSpec(memory_space=space)],
        scratch=scratch,
        name=name,
    )


def chain_body(ahead_rows, behind_rows, behind_grad, route_scores, route_counts, gate_up, down_proj):
    height = ahead_rows.shape[1]
    gates = gate_up[0, 0]
    downs = down_proj[0]
    sections = lax.axis_size("section")
    devices = 2 * DBLOCKS
    slot_ids = jnp.arange(height, dtype=jnp.int32)[None]
    live = slot_ids < route_counts[0][:, None]
    scales = jnp.where(live, route_scores[0], 0.0)[:, :, None]

    def between(value, to):
        pairs = [(q * 2 + f, to[q] * 2 + f) for q in range(DBLOCKS) for f in range(2) if to[q] is not None]
        return lax.ppermute(value, "expert", pairs)

    def outer(value):
        return between(value, (1, 0, 3, 2))

    def inward(value):
        return between(value, (1, None, None, 2))

    def outward(value):
        return between(value, (None, 0, 3, None))

    def middle(value):
        return between(value, (0, 2, 1, 3))

    def swapped(value):
        return lax.ppermute(value, "expert", [(i, i ^ 1) for i in range(devices)])

    def to_section(value, by, flip):
        pairs = [
            (s * devices + e, (s + by) * devices + (e ^ flip))
            for s in range(sections)
            if 0 <= s + by < sections
            for e in range(devices)
        ]
        return lax.ppermute(value, ("section", "expert"), pairs)

    recent = []

    def kernel_call(name, kernel, micros, operands, shape):
        specs, arrays = [], []
        for operand in operands:
            array, c = operand if isinstance(operand, tuple) else (operand, None)
            arrays.append(array)
            specs.append(whole(array) if c is None else row_piece(array, c))
        made = call(
            kernel,
            micros,
            arrays,
            list(recent),
            jax.ShapeDtypeStruct(shape, BF16),
            in_specs=specs,
            name=name,
        )
        recent[:] = [made]
        return made

    class Chain:
        def __init__(self, name, rows, weights, spreads):
            self.name = name
            self.rows, self.weights = rows, weights
            self.spreads = spreads
            self.pairs, self.far, self.near, self.act = {}, {}, {}, {}
            self.out, self.mid, self.one, self.back, self.third = {}, {}, {}, {}, {}

        def fetch(self, c):
            size, width = height // PIECES, self.rows.shape[1]
            if c == 0 and self.name == "behind":
                rows = self.rows[:size]
                self.pairs[c] = rows, swapped(rows)
                return
            rows = call(
                cut_kernel,
                SMALL if c else ROWS,
                (self.rows,),
                list(recent),
                jax.ShapeDtypeStruct((size, width), BF16),
                in_specs=[pl.BlockSpec((size, width), lambda i: (c, 0))],
                name=f"{self.name}_rows_{c}",
            )
            recent[:] = [rows]
            self.pairs[c] = rows, swapped(rows)

        def far_product(self, c):
            name = f"{self.name}_far_{c}"
            made = first_product(name, True, self.pairs[c], self.weights, list(recent))
            recent[:] = [made]
            self.far[c] = made

        def near_products(self):
            rows = [row for c in range(PIECES) for row in self.pairs[c]]
            made = first_product(f"{self.name}_near", False, rows, self.weights, list(recent))
            recent[:] = [made]
            self.near = {c: (made, c) for c in range(PIECES)}

        def near_sum(self, c):
            operands = (self.near[c], self.mid[c])
            return kernel_call(f"{self.name}_third_{c}", sum_kernel, SMALL, operands, self.far[c].shape)

        def first_hop(self, c):
            self.out[c] = outer(self.far[c]) if c == 0 else inward(self.far[c])

        def third_hop(self, c):
            self.third[c] = outward(self.near_sum(c))

        def merged_hop(self, c, first):
            operands = (first, self.near[c - 1], self.mid[c - 1])
            shape = self.far[0].shape
            self.out[c] = outer(
                kernel_call(f"{self.name}_outer_{c}", end_or_sum_kernel, SMALL, operands, shape)
            )
            self.third[c - 1] = self.out[c]

        def last_third_hop(self):
            self.third[PIECES - 1] = outer(self.near_sum(PIECES - 1))

        def middle_sum(self, c):
            mine = self.far[c]
            self.mid[c] = middle(
                kernel_call(
                    f"{self.name}_middle_{c}", sum_kernel, SMALL, (mine, self.out[c]), mine.shape
                )
            )

        def middle_pass(self, c):
            value = self.out[PIECES] if c == 0 else self.back[c]
            shape = (self.spreads, *value.shape[1:])
            value = kernel_call(f"{self.name}_first_{c}", cut_first_kernel, SMALL, (value,), shape)
            self.one[c] = value
            self.mid[PIECES + c] = middle(value)

        def outer_pass(self, c):
            value = self.mid[PIECES + c - 1]
            if c == PIECES:
                value = kernel_call(
                    f"{self.name}_back_{c}", cut_first_kernel, SMALL, (value,), value.shape
                )
            else:
                value = kernel_call(
                    f"{self.name}_back_{c}",
                    end_or_pass_kernel,
                    SMALL,
                    (self.act[c], value),
                    value.shape,
                )
            self.back[c] = outer(value)

        def activated(self, c):
            return self.act[c], self.one[c], self.mid[PIECES + c], self.back[c + 1]

    ahead = Chain("ahead", ahead_rows[0], gates, 1)
    behind = Chain("behind", behind_rows[0], gates, 2)
    grad = Chain("grad", behind_grad[0], downs, 0)
    sent = {}

    def cut(array, c):
        size = height // PIECES
        return array[c * size : (c + 1) * size]

    def activate_ahead(c):
        near = ahead.near[c]
        operands = (near, ahead.third[c])
        ahead.act[c] = kernel_call(f"ahead_act_{c}", ahead_act_kernel, ACT, operands, (1, *ahead.far[c].shape[1:]))

    def activate_behind(c):
        near = behind.near[c]
        operands = (near, behind.third[c], grad.near[c], grad.third[c], cut(scales[1], c))
        behind.act[c] = kernel_call(f"behind_act_{c}", behind_act_kernel, ACT, operands, behind.far[c].shape)

    def output(chain, c):
        forward = chain is ahead
        scale = cut(scales[0], c) if forward else None
        weights = downs if forward else gates
        give, keep = second_product(
            f"{chain.name}_out_{c}", chain.activated(c), scale, weights, list(recent)
        )
        recent[:] = [give]
        return give, keep

    def finish_first(chain):
        give, keep = output(chain, 0)
        sent[chain, 0] = swapped(give), keep

    def send_first(chain):
        share, keep = sent[chain, 0]
        total = kernel_call(
            f"{chain.name}_shares", sum_kernel, SMALL, (keep, share), keep.shape
        )
        sent[chain, 0] = to_section(total, 1 if chain is ahead else -1, 0)

    def finish_last(chain):
        give, keep = output(chain, 1)
        by = 1 if chain is ahead else -1
        sent[chain, 1] = to_section(give, by, 1), to_section(keep, by, 0)

    def result(chain):
        operands = (sent[chain, 0], *sent[chain, 1])
        shape = (height, operands[0].shape[1])
        return kernel_call(f"{chain.name}_result", result_kernel, SMALL, operands, shape)[None]

    for chain in (behind, ahead, grad):
        chain.fetch(0)
    behind.far_product(0)
    behind.first_hop(0)
    behind.fetch(1)
    recent.append(behind.out[0])
    ahead.far_product(0)
    ahead.first_hop(0)
    grad.far_product(0)
    grad.first_hop(0)
    behind.middle_sum(0)
    ahead.fetch(1)
    behind.far_product(1)
    behind.near_products()
    ahead.middle_sum(0)
    behind.merged_hop(1, behind.far[1])
    grad.fetch(1)
    grad.middle_sum(0)
    ahead.far_product(1)
    ahead.near_products()
    ahead.merged_hop(1, ahead.far[1])
    behind.middle_sum(1)
    grad.far_product(1)
    grad.near_products()
    grad.merged_hop(1, grad.far[1])
    ahead.middle_sum(1)
    grad.middle_sum(1)
    activate_behind(0)
    behind.merged_hop(2, behind.act[0])
    activate_ahead(0)
    ahead.merged_hop(2, ahead.act[0])
    grad.last_third_hop()
    behind.middle_pass(0)
    ahead.middle_pass(0)
    activate_ahead(1)
    activate_behind(1)
    behind.outer_pass(1)
    ahead.outer_pass(1)
    behind.middle_pass(1)
    ahead.middle_pass(1)
    finish_first(behind)
    finish_first(ahead)
    behind.outer_pass(2)
    ahead.outer_pass(2)
    send_first(behind)
    finish_last(behind)
    send_first(ahead)
    finish_last(ahead)
    behind_sent = result(behind)
    ahead_sent = result(ahead)
    return ahead_sent, behind_sent


def body(ahead_rows, behind_rows, behind_grad, route_scores, route_counts, gate_up, down_proj):
    groups = lax.axis_size("expert")
    fgroups = groups // DBLOCKS
    low = [[q * fgroups + f for f in range(fgroups)] for q in range(DBLOCKS)]
    high = [[q * fgroups + f for q in range(DBLOCKS)] for f in range(fgroups)]
    height = ahead_rows.shape[1]
    weights_in = gate_up[0, 0]
    weights_out = down_proj[0, 0]
    units = weights_in.shape[1]
    part = units // DBLOCKS

    def wide(rows):
        return lax.all_gather(rows, "expert", axis_index_groups=low, axis=1, tiled=True)

    def reduced(partials):
        flat = partials.reshape(-1, partials.shape[-1])
        total = lax.psum_scatter(
            flat, "expert", axis_index_groups=high, scatter_dimension=0, tiled=True
        )
        return total.astype(F32).reshape(partials.shape[1:])

    def spread(values):
        return lax.all_gather(values, "expert", axis_index_groups=high, axis=0, tiled=False)

    def narrowed(values):
        return lax.psum_scatter(
            values.astype(BF16), "expert", axis_index_groups=low, scatter_dimension=1, tiled=True
        )

    slot_ids = jnp.arange(height, dtype=jnp.int32)
    scale_ahead = route_scores[0, 0] * (slot_ids < route_counts[0, 0]).astype(F32)
    scale_behind = route_scores[0, 1] * (slot_ids < route_counts[0, 1]).astype(F32)
    gates = weights_in.reshape(2, DBLOCKS, part, -1)
    downs = weights_out.reshape(DBLOCKS, part, -1)

    ahead_wide = wide(ahead_rows[0])
    pre_a = jnp.einsum("cd,kqfd->qkcf", ahead_wide, gates, preferred_element_type=F32).astype(BF16)
    sum_a = reduced(pre_a)
    hidden = (sum_a[0] * jax.nn.sigmoid(sum_a[0]) * sum_a[1]).astype(BF16)
    hidden_all = spread(hidden)

    behind_wide = wide(behind_rows[0])
    grad_wide = wide(behind_grad[0])
    pre_b = jnp.einsum("cd,kqfd->qkcf", behind_wide, gates, preferred_element_type=F32).astype(BF16)
    exp_b = jnp.einsum("cd,qfd->qcf", grad_wide, downs, preferred_element_type=F32).astype(BF16)
    sum_b = reduced(jnp.concatenate([pre_b, exp_b[:, None]], axis=1))
    gate, up, expanded = sum_b[0], sum_b[1], sum_b[2] * scale_behind[:, None]
    sig = jax.nn.sigmoid(gate)
    grad_gate = (expanded * up * sig * (1.0 + gate * (1.0 - sig))).astype(BF16)
    grad_up = (expanded * gate * sig).astype(BF16)
    grads_all = spread(jnp.stack([grad_gate, grad_up]))

    out_a = jnp.einsum("qcf,qfd->cd", hidden_all, downs, preferred_element_type=F32)
    ahead_out = (narrowed(out_a).astype(F32) * scale_ahead[:, None]).astype(BF16)
    moved_ahead = shift(ahead_out, "section", 1)
    out_b = jnp.einsum("qkcf,kqfd->cd", grads_all, gates, preferred_element_type=F32)
    behind_out = narrowed(out_b)
    moved_behind = shift(behind_out, "section", -1)
    return (moved_ahead[None], moved_behind[None])


def solution(mesh):
    in_specs = (
        P("section", None, "expert"),
        P("section", None, "expert"),
        P("section", None, "expert"),
        P("section", None, None),
        P("section", None),
        P("section", "expert", None, None, None),
        P("section", "expert", None, None),
    )
    out_specs = (P("section", None, "expert"), P("section", None, "expert"))
    chosen = chain_body if mesh.shape["expert"] == 2 * DBLOCKS else body
    return jax.shard_map(chosen, mesh=mesh, in_specs=in_specs, out_specs=out_specs, check_vma=False)
```

```python
import functools

import jax
import jax.numpy as jnp
from jax import lax
from jax.experimental import pallas as pl
from jax.experimental.pallas import tpu as pltpu
from jax.sharding import PartitionSpec as P

DBLOCKS = 4
BF16 = jnp.bfloat16
F32 = jnp.float32
MIB = 1024 * 1024
PIECES = 2
ROWS, SMALL, ACT, FIRST, AHEAD_OUT, BEHIND_OUT = 20, 6, 10, 5.2, 3, 20


def shift(shard, axis, by):
    devices = lax.axis_size(axis)
    pairs = [(i, i + by) for i in range(devices) if 0 <= i + by < devices]
    return lax.ppermute(shard, axis, pairs)


def whole(array):
    return pl.BlockSpec(array.shape, functools.partial(lambda n, *_: (0,) * n, array.ndim))


def row_piece(array, c):
    parts, slots, half = array.shape
    return pl.BlockSpec((parts, slots // PIECES, half), lambda *_: (0, c, 0))


def call(kernel, micros, operands, after, out_shape, grid=(1,), in_specs=None, out_specs=None, scratch=(), limit=24, name=None):
    count, unread = len(operands), len(after)

    def run(*refs):
        kernel(*refs[:count], *refs[count + unread :])

    if in_specs is None:
        in_specs = [whole(o) for o in operands]
    if out_specs is None:
        out_specs = jax.tree.map(whole, out_shape)
    return pl.pallas_call(
        run,
        compiler_params=pltpu.CompilerParams(vmem_limit_bytes=limit * MIB),
        cost_estimate=pl.CostEstimate(flops=int(micros * 1e9), bytes_accessed=1024, transcendentals=0),
        out_shape=out_shape,
        name=name,
        grid=grid,
        in_specs=[*in_specs, *[pl.BlockSpec(memory_space=pl.ANY)] * unread],
        out_specs=out_specs,
        scratch_shapes=list(scratch),
    )(*operands, *after)


def cut_kernel(rows, out):
    out[...] = rows[...]


def cut_first_kernel(value, out):
    out[...] = value[: out.shape[0]]


def position():
    own = lax.axis_index("expert")
    block = own // 2
    near = jnp.where(block >= DBLOCKS // 2, 1, 0)
    return near, own % 2, (block == 0) | (block == DBLOCKS - 1)


def first_kernel(far, *refs):
    rows, (weights, out, joined) = refs[:-3], refs[-3:]
    near, group, _ = position()
    side = 1 - near if far else near
    parts, _, half = out.shape
    slots, width = rows[0].shape
    at = pl.multiple_of(group * width, 128)
    other = pl.multiple_of((1 - group) * width, 128)
    for piece in range(len(rows) // 2):
        here = pl.ds(piece * slots, slots)
        joined[here, pl.ds(at, width)] = rows[2 * piece][...]
        joined[here, pl.ds(other, width)] = rows[2 * piece + 1][...]
    tile = min(256, half)
    for k in range(parts):
        for j in range(half // tile):
            at = pl.multiple_of(side * half + j * tile, tile)
            out[k, :, j * tile : (j + 1) * tile] = lax.dot_general(
                joined[...],
                weights[k, pl.ds(at, tile)],
                (((1,), (1,)), ((), ())),
                preferred_element_type=F32,
            ).astype(BF16)


def first_product(name, far, rows, weights, after):
    slots = rows[0].shape[0] * len(rows) // 2
    parts, units, features = weights.shape
    return call(
        functools.partial(first_kernel, far),
        FIRST * parts,
        (*rows, weights),
        after,
        jax.ShapeDtypeStruct((parts, slots, units // 2), BF16),
        in_specs=[*[whole(r) for r in rows], pl.BlockSpec(memory_space=pltpu.VMEM)],
        scratch=[pltpu.VMEM((slots, features), BF16)],
        name=name,
    )


def sum_kernel(mine, arrived, out):
    out[...] = (mine[...].astype(F32) + arrived[...].astype(F32)).astype(BF16)


def end_or_sum_kernel(at_end, mine, arrived, out):
    _, _, end = position()

    @pl.when(end)
    def _():
        parts = at_end.shape[0]
        out[:parts] = at_end[...]
        if parts < out.shape[0]:
            out[parts:] = jnp.zeros_like(out[parts:])

    @pl.when(jnp.logical_not(end))
    def _():
        out[...] = (mine[...].astype(F32) + arrived[...].astype(F32)).astype(BF16)


def end_or_pass_kernel(at_end, passed, out):
    _, _, end = position()

    @pl.when(end)
    def _():
        out[...] = at_end[...]

    @pl.when(jnp.logical_not(end))
    def _():
        out[...] = passed[...]


def ahead_act_kernel(near, arrived, out):
    gate = near[0].astype(F32) + arrived[0].astype(F32)
    up = near[1].astype(F32) + arrived[1].astype(F32)
    out[0] = (gate * jax.nn.sigmoid(gate) * up).astype(BF16)


def behind_act_kernel(near, arrived, near_e, arrived_e, scale, out):
    gate = near[0].astype(F32) + arrived[0].astype(F32)
    up = near[1].astype(F32) + arrived[1].astype(F32)
    expanded = (near_e[0].astype(F32) + arrived_e[0].astype(F32)) * scale[...]
    sig = jax.nn.sigmoid(gate)
    out[0] = (expanded * up * sig * (1.0 + gate * (1.0 - sig))).astype(BF16)
    out[1] = (expanded * gate * sig).astype(BF16)


def result_kernel(first, one, two, out):
    size = first.shape[0]
    out[:size] = first[...]
    out[size:] = (one[...].astype(F32) + two[...].astype(F32)).astype(BF16)


def second_kernel(scaled, act, one, two, three, *refs):
    scale, refs = (refs[0], refs[1:]) if scaled else (None, refs)
    weights, give, keep, joined = refs
    near_half, group, end = position()
    kinds, _, half = act.shape
    units = weights.shape[1]
    width = give.shape[1]

    def place(near, far):
        for kind in range(kinds):
            at = pl.multiple_of((2 * kind + near_half) * half, 128)
            other = pl.multiple_of((2 * kind + 1 - near_half) * half, 128)
            joined[:, pl.ds(at, half)] = near[kind]
            joined[:, pl.ds(other, half)] = far[kind]

    @pl.when(end)
    def _():
        place(act, three)

    @pl.when(jnp.logical_not(end))
    def _():
        place(one, two)

    for side, out in ((1 - group, give), (group, keep)):
        at = pl.multiple_of(side * width, 128)
        tile = weights[:, :, pl.ds(at, width)].reshape(kinds * units, width)
        share = jnp.dot(joined[...], tile, preferred_element_type=F32)
        if scaled:
            share = share * scale[...]
        out[...] = share.astype(BF16)


def copying_second_kernel(scaled, act, one, two, three, *refs):
    scale, refs = (refs[0], refs[1:]) if scaled else (None, refs)
    weights, give, keep, joined, tiles, sems = refs
    near_half, group, end = position()
    kinds, _, half = act.shape
    _, _, units, width = tiles.shape
    copies = []
    for own in range(2):
        at = pl.multiple_of((group if own else 1 - group) * width, 128)
        copy = pltpu.make_async_copy(
            weights.at[:, :, pl.ds(at, width)], tiles.at[own], sems.at[own]
        )
        copy.start()
        copies.append(copy)

    def place(near, far):
        for kind in range(kinds):
            at = pl.multiple_of((2 * kind + near_half) * half, 128)
            other = pl.multiple_of((2 * kind + 1 - near_half) * half, 128)
            joined[:, pl.ds(at, half)] = near[kind]
            joined[:, pl.ds(other, half)] = far[kind]

    @pl.when(end)
    def _():
        place(act, three)

    @pl.when(jnp.logical_not(end))
    def _():
        place(one, two)

    for own, out in enumerate((give, keep)):
        copies[own].wait()
        share = jnp.dot(
            joined[...], tiles[own].reshape(kinds * units, width), preferred_element_type=F32
        )
        if scaled:
            share = share * scale[...]
        out[...] = share.astype(BF16)


def second_product(name, values, scale, weights, after):
    kinds, units, features = weights.shape
    slots = values[0].shape[1]
    operands = [*values] + ([] if scale is None else [scale])
    share = jax.ShapeDtypeStruct((slots, features // 2), BF16)
    kernel, space = second_kernel, pltpu.VMEM
    scratch = [pltpu.VMEM((slots, kinds * units), BF16)]
    if kinds == 1:
        kernel, space = copying_second_kernel, pl.ANY
        scratch.append(pltpu.VMEM((2, kinds, units, features // 2), BF16))
        scratch.append(pltpu.SemaphoreType.DMA((2,)))
    return call(
        functools.partial(kernel, scale is not None),
        AHEAD_OUT if kinds == 1 else BEHIND_OUT,
        (*operands, weights),
        after,
        (share, share),
        in_specs=[*[whole(v) for v in operands], pl.BlockSpec(memory_space=space)],
        scratch=scratch,
        name=name,
    )


def chain_body(ahead_rows, behind_rows, behind_grad, route_scores, route_counts, gate_up, down_proj):
    height = ahead_rows.shape[1]
    gates = gate_up[0, 0]
    downs = down_proj[0]
    sections = lax.axis_size("section")
    devices = 2 * DBLOCKS
    slot_ids = jnp.arange(height, dtype=jnp.int32)[None]
    live = slot_ids < route_counts[0][:, None]
    scales = jnp.where(live, route_scores[0], 0.0)[:, :, None]

    def between(value, to):
        pairs = [(q * 2 + f, to[q] * 2 + f) for q in range(DBLOCKS) for f in range(2) if to[q] is not None]
        return lax.ppermute(value, "expert", pairs)

    def outer(value):
        return between(value, (1, 0, 3, 2))

    def inward(value):
        return between(value, (1, None, None, 2))

    def outward(value):
        return between(value, (None, 0, 3, None))

    def middle(value):
        return between(value, (0, 2, 1, 3))

    def swapped(value):
        return lax.ppermute(value, "expert", [(i, i ^ 1) for i in range(devices)])

    def to_section(value, by, flip):
        pairs = [
            (s * devices + e, (s + by) * devices + (e ^ flip))
            for s in range(sections)
            if 0 <= s + by < sections
            for e in range(devices)
        ]
        return lax.ppermute(value, ("section", "expert"), pairs)

    recent = []

    def kernel_call(name, kernel, micros, operands, shape):
        specs, arrays = [], []
        for operand in operands:
            array, c = operand if isinstance(operand, tuple) else (operand, None)
            arrays.append(array)
            specs.append(whole(array) if c is None else row_piece(array, c))
        made = call(
            kernel,
            micros,
            arrays,
            list(recent),
            jax.ShapeDtypeStruct(shape, BF16),
            in_specs=specs,
            name=name,
        )
        recent[:] = [made]
        return made

    class Chain:
        def __init__(self, name, rows, weights, spreads):
            self.name = name
            self.rows, self.weights = rows, weights
            self.spreads = spreads
            self.pairs, self.far, self.near, self.act = {}, {}, {}, {}
            self.out, self.mid, self.one, self.back, self.third = {}, {}, {}, {}, {}

        def fetch(self, c):
            size, width = height // PIECES, self.rows.shape[1]
            if c == 0 and self.name == "behind":
                rows = self.rows[:size]
                self.pairs[c] = rows, swapped(rows)
                return
            rows = call(
                cut_kernel,
                SMALL if c else ROWS,
                (self.rows,),
                list(recent),
                jax.ShapeDtypeStruct((size, width), BF16),
                in_specs=[pl.BlockSpec((size, width), lambda i: (c, 0))],
                name=f"{self.name}_rows_{c}",
            )
            recent[:] = [rows]
            self.pairs[c] = rows, swapped(rows)

        def far_product(self, c):
            name = f"{self.name}_far_{c}"
            made = first_product(name, True, self.pairs[c], self.weights, list(recent))
            recent[:] = [made]
            self.far[c] = made

        def near_products(self):
            rows = [row for c in range(PIECES) for row in self.pairs[c]]
            made = first_product(f"{self.name}_near", False, rows, self.weights, list(recent))
            recent[:] = [made]
            self.near = {c: (made, c) for c in range(PIECES)}

        def near_sum(self, c):
            operands = (self.near[c], self.mid[c])
            return kernel_call(f"{self.name}_third_{c}", sum_kernel, SMALL, operands, self.far[c].shape)

        def first_hop(self, c):
            self.out[c] = outer(self.far[c]) if c == 0 else inward(self.far[c])

        def third_hop(self, c):
            self.third[c] = outward(self.near_sum(c))

        def merged_hop(self, c, first):
            operands = (first, self.near[c - 1], self.mid[c - 1])
            shape = self.far[0].shape
            self.out[c] = outer(
                kernel_call(f"{self.name}_outer_{c}", end_or_sum_kernel, SMALL, operands, shape)
            )
            self.third[c - 1] = self.out[c]

        def last_third_hop(self):
            self.third[PIECES - 1] = outer(self.near_sum(PIECES - 1))

        def middle_sum(self, c):
            mine = self.far[c]
            self.mid[c] = middle(
                kernel_call(
                    f"{self.name}_middle_{c}", sum_kernel, SMALL, (mine, self.out[c]), mine.shape
                )
            )

        def middle_pass(self, c):
            value = self.out[PIECES] if c == 0 else self.back[c]
            shape = (self.spreads, *value.shape[1:])
            value = kernel_call(f"{self.name}_first_{c}", cut_first_kernel, SMALL, (value,), shape)
            self.one[c] = value
            self.mid[PIECES + c] = middle(value)

        def outer_pass(self, c):
            value = self.mid[PIECES + c - 1]
            if c == PIECES:
                value = kernel_call(
                    f"{self.name}_back_{c}", cut_first_kernel, SMALL, (value,), value.shape
                )
            else:
                value = kernel_call(
                    f"{self.name}_back_{c}",
                    end_or_pass_kernel,
                    SMALL,
                    (self.act[c], value),
                    value.shape,
                )
            self.back[c] = outer(value)

        def activated(self, c):
            return self.act[c], self.one[c], self.mid[PIECES + c], self.back[c + 1]

    ahead = Chain("ahead", ahead_rows[0], gates, 1)
    behind = Chain("behind", behind_rows[0], gates, 2)
    grad = Chain("grad", behind_grad[0], downs, 0)
    sent = {}

    def cut(array, c):
        size = height // PIECES
        return array[c * size : (c + 1) * size]

    def activate_ahead(c):
        near = ahead.near[c]
        operands = (near, ahead.third[c])
        ahead.act[c] = kernel_call(f"ahead_act_{c}", ahead_act_kernel, ACT, operands, (1, *ahead.far[c].shape[1:]))

    def activate_behind(c):
        near = behind.near[c]
        operands = (near, behind.third[c], grad.near[c], grad.third[c], cut(scales[1], c))
        behind.act[c] = kernel_call(f"behind_act_{c}", behind_act_kernel, ACT, operands, behind.far[c].shape)

    def output(chain, c):
        forward = chain is ahead
        scale = cut(scales[0], c) if forward else None
        weights = downs if forward else gates
        give, keep = second_product(
            f"{chain.name}_out_{c}", chain.activated(c), scale, weights, list(recent)
        )
        recent[:] = [give]
        return give, keep

    def finish_first(chain):
        give, keep = output(chain, 0)
        sent[chain, 0] = swapped(give), keep

    def send_first(chain):
        share, keep = sent[chain, 0]
        total = kernel_call(
            f"{chain.name}_shares", sum_kernel, SMALL, (keep, share), keep.shape
        )
        sent[chain, 0] = to_section(total, 1 if chain is ahead else -1, 0)

    def finish_last(chain):
        give, keep = output(chain, 1)
        by = 1 if chain is ahead else -1
        sent[chain, 1] = to_section(give, by, 1), to_section(keep, by, 0)

    def result(chain):
        operands = (sent[chain, 0], *sent[chain, 1])
        shape = (height, operands[0].shape[1])
        return kernel_call(f"{chain.name}_result", result_kernel, SMALL, operands, shape)[None]

    for chain in (behind, ahead, grad):
        chain.fetch(0)
    behind.far_product(0)
    behind.first_hop(0)
    behind.fetch(1)
    recent.append(behind.out[0])
    ahead.far_product(0)
    ahead.first_hop(0)
    behind.middle_sum(0)
    grad.far_product(0)
    grad.first_hop(0)
    ahead.fetch(1)
    behind.far_product(1)
    behind.near_products()
    ahead.middle_sum(0)
    behind.merged_hop(1, behind.far[1])
    grad.fetch(1)
    grad.middle_sum(0)
    ahead.far_product(1)
    ahead.near_products()
    ahead.merged_hop(1, ahead.far[1])
    behind.middle_sum(1)
    grad.far_product(1)
    grad.near_products()
    grad.merged_hop(1, grad.far[1])
    ahead.middle_sum(1)
    grad.middle_sum(1)
    activate_behind(0)
    behind.merged_hop(2, behind.act[0])
    activate_ahead(0)
    ahead.merged_hop(2, ahead.act[0])
    grad.last_third_hop()
    behind.middle_pass(0)
    ahead.middle_pass(0)
    activate_ahead(1)
    activate_behind(1)
    behind.outer_pass(1)
    ahead.outer_pass(1)
    behind.middle_pass(1)
    ahead.middle_pass(1)
    finish_first(behind)
    finish_first(ahead)
    behind.outer_pass(2)
    ahead.outer_pass(2)
    send_first(behind)
    finish_last(behind)
    send_first(ahead)
    finish_last(ahead)
    behind_sent = result(behind)
    ahead_sent = result(ahead)
    return ahead_sent, behind_sent


def body(ahead_rows, behind_rows, behind_grad, route_scores, route_counts, gate_up, down_proj):
    groups = lax.axis_size("expert")
    fgroups = groups // DBLOCKS
    low = [[q * fgroups + f for f in range(fgroups)] for q in range(DBLOCKS)]
    high = [[q * fgroups + f for q in range(DBLOCKS)] for f in range(fgroups)]
    height = ahead_rows.shape[1]
    weights_in = gate_up[0, 0]
    weights_out = down_proj[0, 0]
    units = weights_in.shape[1]
    part = units // DBLOCKS

    def wide(rows):
        return lax.all_gather(rows, "expert", axis_index_groups=low, axis=1, tiled=True)

    def reduced(partials):
        flat = partials.reshape(-1, partials.shape[-1])
        total = lax.psum_scatter(
            flat, "expert", axis_index_groups=high, scatter_dimension=0, tiled=True
        )
        return total.astype(F32).reshape(partials.shape[1:])

    def spread(values):
        return lax.all_gather(values, "expert", axis_index_groups=high, axis=0, tiled=False)

    def narrowed(values):
        return lax.psum_scatter(
            values.astype(BF16), "expert", axis_index_groups=low, scatter_dimension=1, tiled=True
        )

    slot_ids = jnp.arange(height, dtype=jnp.int32)
    scale_ahead = route_scores[0, 0] * (slot_ids < route_counts[0, 0]).astype(F32)
    scale_behind = route_scores[0, 1] * (slot_ids < route_counts[0, 1]).astype(F32)
    gates = weights_in.reshape(2, DBLOCKS, part, -1)
    downs = weights_out.reshape(DBLOCKS, part, -1)

    ahead_wide = wide(ahead_rows[0])
    pre_a = jnp.einsum("cd,kqfd->qkcf", ahead_wide, gates, preferred_element_type=F32).astype(BF16)
    sum_a = reduced(pre_a)
    hidden = (sum_a[0] * jax.nn.sigmoid(sum_a[0]) * sum_a[1]).astype(BF16)
    hidden_all = spread(hidden)

    behind_wide = wide(behind_rows[0])
    grad_wide = wide(behind_grad[0])
    pre_b = jnp.einsum("cd,kqfd->qkcf", behind_wide, gates, preferred_element_type=F32).astype(BF16)
    exp_b = jnp.einsum("cd,qfd->qcf", grad_wide, downs, preferred_element_type=F32).astype(BF16)
    sum_b = reduced(jnp.concatenate([pre_b, exp_b[:, None]], axis=1))
    gate, up, expanded = sum_b[0], sum_b[1], sum_b[2] * scale_behind[:, None]
    sig = jax.nn.sigmoid(gate)
    grad_gate = (expanded * up * sig * (1.0 + gate * (1.0 - sig))).astype(BF16)
    grad_up = (expanded * gate * sig).astype(BF16)
    grads_all = spread(jnp.stack([grad_gate, grad_up]))

    out_a = jnp.einsum("qcf,qfd->cd", hidden_all, downs, preferred_element_type=F32)
    ahead_out = (narrowed(out_a).astype(F32) * scale_ahead[:, None]).astype(BF16)
    moved_ahead = shift(ahead_out, "section", 1)
    out_b = jnp.einsum("qkcf,kqfd->cd", grads_all, gates, preferred_element_type=F32)
    behind_out = narrowed(out_b)
    moved_behind = shift(behind_out, "section", -1)
    return (moved_ahead[None], moved_behind[None])


def solution(mesh):
    in_specs = (
        P("section", None, "expert"),
        P("section", None, "expert"),
        P("section", None, "expert"),
        P("section", None, None),
        P("section", None),
        P("section", "expert", None, None, None),
        P("section", "expert", None, None),
    )
    out_specs = (P("section", None, "expert"), P("section", None, "expert"))
    chosen = chain_body if mesh.shape["expert"] == 2 * DBLOCKS else body
    return jax.shard_map(chosen, mesh=mesh, in_specs=in_specs, out_specs=out_specs, check_vma=False)
```
